32 devices in a mesh: dp: 8 (over z, x), fsdp: 4 (over y, core).
Axes of the slice: x: 2, y: 2, z: 4, core: 2. Of those that a mesh axis runs over, the one named last changes fastest.
Arguments:
- hidden_in: bfloat16 [2, 8, 1024, 1024], P(None, 'dp', 'fsdp'), may hold values from -6 to 6
- segment_ids: int32 [2, 8, 1024], P(None, 'dp', 'fsdp'), may hold values from 0 to 1023, as said below
- norm1_gain: bfloat16 [1024], P(('dp', 'fsdp')), may hold values from 0.5 to 1.5
- w_gate_z: bfloat16 [1024, 1536], P(('dp', 'fsdp')), may hold values from -0.1875 to 0.1875
- w_xbc: bfloat16 [1024, 1792], P(('dp', 'fsdp')), may hold values from -0.1875 to 0.1875
- w_step: bfloat16 [1024, 24], P(('dp', 'fsdp')), may hold values from -0.1875 to 0.1875
- conv_weight: bfloat16 [4, 1792], P(None, ('dp', 'fsdp')), may hold values from -3 to 3
- conv_bias: bfloat16 [1792], P(('dp', 'fsdp')), may hold values from -3 to 3
- step_bias: float32 [24], replicated, may hold values from -1 to 0.5
- decay_log: float32 [24], replicated, may hold values from -12 to -2
- skip_gain: float32 [24], replicated, may hold values from 0.5 to 1.5
- mixer_gain: bfloat16 [1536], P(('dp', 'fsdp')), may hold values from 0.5 to 1.5
- w_mix_out: bfloat16 [1536, 1024], P(('dp', 'fsdp')), may hold values from -0.15625 to 0.15625
- w_query: bfloat16 [1024, 512], P(('dp', 'fsdp')), may hold values from -0.1875 to 0.1875
- key_value_weight: bfloat16 [1024, 256], P(('dp', 'fsdp')), may hold values from -0.1875 to 0.1875
- w_attn_out: bfloat16 [512, 1024], P(('dp', 'fsdp')), may hold values from -1 to 1
- norm2_gain: bfloat16 [1024], P(('dp', 'fsdp')), may hold values from 0.5 to 1.5
- w_gate_up: bfloat16 [1024, 4096], P(('dp', 'fsdp')), may hold values from -0.1875 to 0.1875
- w_down: bfloat16 [2048, 1024], P(('dp', 'fsdp')), may hold values from -0.125 to 0.125
- out_grad: bfloat16 [2, 8, 1024, 1024], P(None, 'dp', 'fsdp'), may hold values from -6 to 6
Outputs:
- hidden_out: bfloat16 [2, 8, 1024, 1024], P(None, 'dp', 'fsdp')
- input_grad: float32 [2, 8, 1024, 1024], P(None, 'dp', 'fsdp')
- grad_norm1_gain: float32 [1024], P(('dp', 'fsdp'))
- grad_w_gate_z: float32 [1024, 1536], P(('dp', 'fsdp'))
- grad_w_xbc: float32 [1024, 1792], P(('dp', 'fsdp'))
- grad_w_step: float32 [1024, 24], P(('dp', 'fsdp'))
- grad_conv_weight: float32 [4, 1792], P(None, ('dp', 'fsdp'))
- grad_conv_bias: float32 [1792], P(('dp', 'fsdp'))
- grad_step_bias: float32 [24], replicated
- grad_decay_log: float32 [24], replicated
- grad_skip_gain: float32 [24], replicated
- grad_mixer_gain: float32 [1536], P(('dp', 'fsdp'))
- grad_w_mix_out: float32 [1536, 1024], P(('dp', 'fsdp'))
- grad_w_query: float32 [1024, 512], P(('dp', 'fsdp'))
- grad_w_keyval: float32 [1024, 256], P(('dp', 'fsdp'))
- grad_w_attn_out: float32 [512, 1024], P(('dp', 'fsdp'))
- grad_norm2_gain: float32 [1024], P(('dp', 'fsdp'))
- grad_w_gate_up: float32 [1024, 4096], P(('dp', 'fsdp'))
- grad_w_down: float32 [2048, 1024], P(('dp', 'fsdp'))
The draws below stay inside these ranges and needn't reach their ends.
Inputs may be any that keep to these rules, and one draw needn't show every extreme that they name: `segment_ids`: ids start at 0 and never fall along a sequence, and the last document of every sequence has id 1024 - 1; in every sequence one document covers 1024 - 255 or more positions.
All inputs are finite; a program needn't handle non-finite values.
Results may differ from the reference program's by a relative error of at most 0.034.
Values may be sent and summed in bfloat16 or wider, within the bound.
No kernel may reach another device: no remote copies, remote signals or barrier semaphores. Data moves between devices by JAX's collectives and lax.ppermute only.
A program may use at most 256 MiB of HBM per device.

```python
import jax
import jax.numpy as jnp
from jax import lax

MODEL_WIDTH = 1024
FF = 2048
H = 24
P_SIZE = 64
NS = 128
QUERY_HEADS = 8
KEY_VALUE_HEADS = 2
HEAD_WIDTH = 64
KC = 4
MB = 2
LEN = 1024
TOK_MB = 256
DI = 1536
SEQS = 8


def draw_segment_ids(key, part):
    key = jax.random.fold_in(key, 11)
    first_key, second_key, third_key = jax.random.split(key, 3)
    row_count = MB * SEQS
    extra_len = jax.random.randint(first_key, (row_count, 1), 0, TOK_MB // 2 + 1)
    long_span = LEN - TOK_MB + 1 + extra_len
    long_begin = jax.random.randint(second_key, (row_count, 1), 0, LEN - long_span + 1)
    position = jnp.arange(LEN, dtype=jnp.int32)[None, :]
    random_cut = jax.random.randint(third_key, (row_count, LEN), 0, 12) == 0
    outside = (position < long_begin) | (position >= long_begin + long_span)
    boundary = ((position == long_begin) | (position == long_begin + long_span) | random_cut & outside) & (position > 0)
    counted = jnp.cumsum(boundary.astype(jnp.int32), axis=1)
    final_count = counted[:, LEN - 1:LEN]
    doc_ids = jnp.where(counted == final_count, LEN - 1, counted).astype(jnp.int32)
    return doc_ids.reshape(MB, SEQS, LEN)


def draw_decay_log(key, part):
    key = jax.random.fold_in(key, 23)
    first_key, second_key, third_key = jax.random.split(key, 3)
    slow_share = 0.5
    slow_head = jax.random.uniform(first_key, (H,)) < slow_share
    slow_rate = jax.random.uniform(second_key, (H,), minval=jnp.log(0.3 / LEN), maxval=jnp.log(1.5 / LEN))
    fast_rate = jax.random.uniform(third_key, (H,), minval=jnp.log(1.0 / 40.0), maxval=jnp.log(1.0 / 12.0))
    return jnp.where(slow_head, slow_rate, fast_rate).astype(jnp.float32)


def block_levels(stream_key, extent, pieces, low, high):
    def one(axis_at, shards_of):
        steps = jax.random.uniform(jax.random.fold_in(jax.random.fold_in(stream_key, 6), axis_at), (shards_of,), jnp.float32, low / len(pieces), high / len(pieces))
        return jnp.repeat(jnp.exp(steps), extent[axis_at] // shards_of).reshape((-1,) + (1,) * (len(extent) - axis_at - 1))

    gain = one(*pieces[0])
    for cut in pieces[1:]:
        gain = gain * one(*cut)
    return gain


def normal_values(rng, dims, scale, most, cuts=(), held_as=jnp.bfloat16):
    drawn = scale * jax.random.normal(rng, dims, jnp.float32)
    if cuts:
        drawn = drawn * block_levels(rng, dims, cuts, -0.22, 0.18)
    return jnp.clip(drawn, -most, most).astype(held_as)


def setup_inputs(seed: int = 0) -> dict:
    key_of = jax.random.split(jax.random.key(seed), 21)
    hidden_in = normal_values(key_of[0], (MB, SEQS, LEN, MODEL_WIDTH), 1.0, 6.0, ((1, 8), (2, 4)))
    segment_ids = draw_segment_ids(jax.random.fold_in(key_of[20], 71), 0)
    norm1_gain = jnp.clip(1.0 + 0.1 * jax.random.normal(key_of[2], (MODEL_WIDTH,), jnp.float32), 0.5, 1.5).astype(jnp.bfloat16)
    w_gate_z = normal_values(key_of[3], (MODEL_WIDTH, DI), MODEL_WIDTH ** -0.5, 0.1875, ((0, 32),))
    w_xbc = normal_values(key_of[4], (MODEL_WIDTH, DI + 2 * NS), MODEL_WIDTH ** -0.5, 0.1875, ((0, 32),))
    w_step = normal_values(key_of[5], (MODEL_WIDTH, H), MODEL_WIDTH ** -0.5, 0.1875, ((0, 32),))
    conv_weight = normal_values(key_of[6], (KC, DI + 2 * NS), KC ** -0.5, 3.0, ((1, 32),))
    conv_bias = normal_values(key_of[7], (DI + 2 * NS,), 0.5, 3.0, ((0, 32),))
    step_bias = jnp.clip(jax.random.uniform(key_of[8], (H,), jnp.float32, -1.0, 0.5), -1.0, 0.5)
    decay_log = draw_decay_log(jax.random.fold_in(key_of[20], 71), 0)
    skip_gain = jnp.clip(jax.random.uniform(key_of[10], (H,), jnp.float32, 0.5, 1.5), 0.5, 1.5)
    mixer_gain = jnp.clip(1.0 + 0.1 * jax.random.normal(key_of[11], (DI,), jnp.float32), 0.5, 1.5).astype(jnp.bfloat16)
    w_mix_out = normal_values(key_of[12], (DI, MODEL_WIDTH), DI ** -0.5, 0.15625, ((0, 32),))
    w_query = normal_values(key_of[13], (MODEL_WIDTH, QUERY_HEADS * HEAD_WIDTH), MODEL_WIDTH ** -0.5, 0.1875, ((0, 32),))
    key_value_weight = normal_values(key_of[14], (MODEL_WIDTH, 2 * KEY_VALUE_HEADS * HEAD_WIDTH), MODEL_WIDTH ** -0.5, 0.1875, ((0, 32),))
    w_attn_out = normal_values(key_of[15], (QUERY_HEADS * HEAD_WIDTH, MODEL_WIDTH), (QUERY_HEADS * HEAD_WIDTH // 16) ** -0.5, 1.0, ((0, 32),))
    norm2_gain = jnp.clip(1.0 + 0.1 * jax.random.normal(key_of[16], (MODEL_WIDTH,), jnp.float32), 0.5, 1.5).astype(jnp.bfloat16)
    w_gate_up = normal_values(key_of[17], (MODEL_WIDTH, 2 * FF), MODEL_WIDTH ** -0.5, 0.1875, ((0, 32),))
    w_down = normal_values(key_of[18], (FF, MODEL_WIDTH), FF ** -0.5, 0.125, ((0, 32),))
    out_grad = normal_values(key_of[19], (MB, SEQS, LEN, MODEL_WIDTH), 1.0, 6.0, ((1, 8), (2, 4)))
    return dict(hidden_in=hidden_in, segment_ids=segment_ids, norm1_gain=norm1_gain, w_gate_z=w_gate_z, w_xbc=w_xbc, w_step=w_step, conv_weight=conv_weight, conv_bias=conv_bias, step_bias=step_bias, decay_log=decay_log, skip_gain=skip_gain, mixer_gain=mixer_gain, w_mix_out=w_mix_out, w_query=w_query, key_value_weight=key_value_weight, w_attn_out=w_attn_out, norm2_gain=norm2_gain, w_gate_up=w_gate_up, w_down=w_down, out_grad=out_grad)


EPSILON = 1e-06
NEGATIVE = -1e+30
HIGHEST = lax.Precision.HIGHEST

@jax.custom_vjp
def low(v):
    return lax.optimization_barrier(v.astype(jnp.bfloat16)).astype(jnp.float32)

@jax.custom_vjp
def low_back(v):
    return v

def low_keep(v):
    return (low(v), None)

def low_pass(kept, grad):
    return (grad,)

def back_keep(v):
    return (v, None)

def back_low(kept, grad):
    return (low(grad),)
low.defvjp(low_keep, low_pass)
low_back.defvjp(back_keep, back_low)

def matmul(first_op, second_op):
    return jnp.dot(first_op, second_op, precision=HIGHEST, preferred_element_type=jnp.float32)

def rms_gain(values, gain_in):
    return values * lax.rsqrt(lax.optimization_barrier(jnp.mean(values * values, axis=-1, keepdims=True)) + EPSILON) * gain_in

def conv_mix(extended, seg_ext, kernel, offset):
    sequence_length = extended.shape[0] - (KC - 1)
    summed = jnp.zeros((sequence_length, extended.shape[1]), jnp.float32) + offset[None, :]
    for tap_index in range(KC):
        same_doc = (seg_ext[tap_index:tap_index + sequence_length] == seg_ext[KC - 1:]).astype(jnp.float32)
        summed = summed + kernel[tap_index][None, :] * extended[tap_index:tap_index + sequence_length] * same_doc[:, None]
    return jax.nn.silu(summed)

def split_parts(conv_out):
    sequence_length = conv_out.shape[0]
    inputs = conv_out[:, :H * P_SIZE].reshape(sequence_length, H, P_SIZE)
    b_rows = conv_out[:, H * P_SIZE:H * P_SIZE + NS]
    c_rows = conv_out[:, H * P_SIZE + NS:]
    return (inputs, b_rows, c_rows)

def decay_terms(raw_step, step_bias, decay_log):
    step_size = jax.nn.softplus(raw_step + step_bias[None, :])
    cumulated = jnp.cumsum(-step_size * jnp.exp(decay_log)[None, :], axis=0)
    return (step_size, cumulated)

def state_local(conv_out, raw_step, step_bias, decay_log, seg_ids):
    inputs, b_rows, c_rows = split_parts(conv_out)
    step_size, cumulated = decay_terms(raw_step, step_bias, decay_log)
    keep_end = (seg_ids == seg_ids[-1]).astype(jnp.float32)
    weight_set = jnp.exp(cumulated[-1][None, :] - cumulated) * step_size * keep_end[:, None]
    weighted = inputs * weight_set[:, :, None]
    end_state = jnp.einsum('shp,sn->hpn', weighted, b_rows, precision=HIGHEST)
    carry_gate = jnp.exp(cumulated[-1]) * (seg_ids[0] == seg_ids[-1]).astype(jnp.float32)
    return (end_state, carry_gate)

def mixer_output(conv_out, raw_step, step_bias, decay_log, skip_gain, seg_ids, prev_state, prev_last):
    inputs, b_rows, c_rows = split_parts(conv_out)
    step_size, cumulated = decay_terms(raw_step, step_bias, decay_log)
    sequence_length = conv_out.shape[0]
    places = lax.iota(jnp.int32, sequence_length)
    allowed = (seg_ids[:, None] == seg_ids[None, :]) & (places[:, None] >= places[None, :])
    by_head = cumulated.T
    spread = jnp.where(allowed[None], by_head[:, :, None] - by_head[:, None, :], NEGATIVE)
    couple = jnp.dot(c_rows, b_rows.T, precision=HIGHEST, preferred_element_type=jnp.float32)
    mixing = jnp.exp(spread) * couple[None] * step_size.T[:, None, :]
    inside = jnp.einsum('hts,shp->thp', mixing, inputs, precision=HIGHEST)
    inflow = jnp.exp(cumulated) * (seg_ids == prev_last).astype(jnp.float32)[:, None]
    carried = jnp.einsum('tn,hpn->thp', c_rows, prev_state, precision=HIGHEST) * inflow[:, :, None]
    result = inside + carried + skip_gain[None, :, None] * inputs
    return result.reshape(sequence_length, H * P_SIZE)

def gated_norm(mixer_out, gate_in, gain_in):
    return rms_gain(mixer_out * jax.nn.silu(gate_in), gain_in)

def swiglu(gate_up):
    return jax.nn.silu(gate_up[:, :FF]) * gate_up[:, FF:]

def mixer_sequence(conv_out, raw_step, seg_ids, step_bias, decay_log, skip_gain):
    blocks = conv_out.shape[0] // TOK_MB

    def block_step(carry_in, block_in):
        ssm_state, last_id = carry_in
        mix_in, raw_in, seg_in = block_in
        result = mixer_output(mix_in, raw_in, step_bias, decay_log, skip_gain, seg_in, ssm_state, last_id)
        end_state, carry_gate = state_local(mix_in, raw_in, step_bias, decay_log, seg_in)
        linked = carry_gate * (last_id == seg_in[0]).astype(jnp.float32)
        return ((end_state + linked[:, None, None] * ssm_state, seg_in[-1]), result)
    start_carry = (jnp.zeros((H, P_SIZE, NS), jnp.float32), jnp.array(-1, jnp.int32))
    blocks_in = (conv_out.reshape(blocks, TOK_MB, conv_out.shape[1]), raw_step.reshape(blocks, TOK_MB, H), seg_ids.reshape(blocks, TOK_MB))
    _, results = lax.scan(jax.checkpoint(block_step), start_carry, blocks_in)
    return results.reshape(conv_out.shape[0], H * P_SIZE)

def attention(queries, key_value_rows, seg_ids):
    sequence_length = queries.shape[0]
    head_groups = QUERY_HEADS // KEY_VALUE_HEADS
    query_head_rows = queries.reshape(sequence_length, QUERY_HEADS, HEAD_WIDTH)
    key_head_rows = jnp.repeat(key_value_rows[:, :KEY_VALUE_HEADS * HEAD_WIDTH].reshape(sequence_length, KEY_VALUE_HEADS, HEAD_WIDTH), head_groups, axis=1)
    value_head_rows = jnp.repeat(key_value_rows[:, KEY_VALUE_HEADS * HEAD_WIDTH:].reshape(sequence_length, KEY_VALUE_HEADS, HEAD_WIDTH), head_groups, axis=1)
    places = lax.iota(jnp.int32, sequence_length)
    allowed = (seg_ids[:, None] == seg_ids[None, :]) & (places[:, None] >= places[None, :])
    scores = low_back(jnp.einsum('qhd,khd->hqk', query_head_rows, key_head_rows, precision=HIGHEST) * HEAD_WIDTH ** (-0.5))
    scores = jnp.where(allowed[None], scores, NEGATIVE)
    weight_set = low(jax.nn.softmax(scores, axis=-1))
    combined = jnp.einsum('hqk,khd->qhd', weight_set, value_head_rows, precision=HIGHEST)
    return low(low_back(combined)).reshape(sequence_length, QUERY_HEADS * HEAD_WIDTH)

def seq_forward(tokens, seg_ids, params):
    gain_one, gate_z_w, xbc_w, step_w, kernel, offset, step_bias, decay_log, skip_gain, mix_gain, mix_out_w, query_w, keyval_w, attn_out_w, gain_two, gate_up_w, down_w = params
    normed = low(rms_gain(tokens, gain_one))
    gate_z = low_back(matmul(normed, gate_z_w))
    conv_in = low(low_back(matmul(normed, xbc_w)))
    raw_step = low_back(matmul(normed, step_w))
    queries = low(low_back(matmul(normed, query_w)))
    key_value_rows = low(low_back(matmul(normed, keyval_w)))
    halo_rows = KC - 1
    extended = jnp.concatenate([jnp.zeros((halo_rows, conv_in.shape[1]), jnp.float32), conv_in])
    seg_ext = jnp.concatenate([jnp.zeros((halo_rows,), jnp.int32), seg_ids])
    conv_out = conv_mix(extended, seg_ext, kernel, offset)
    mixer_out = mixer_sequence(conv_out, raw_step, seg_ids, step_bias, decay_log, skip_gain)
    normed_mix = low(gated_norm(mixer_out, gate_z, mix_gain))
    attn_low = attention(queries, key_value_rows, seg_ids)
    residual = tokens + low_back(matmul(normed_mix, mix_out_w) + matmul(attn_low, attn_out_w))
    normed_two = low(rms_gain(residual, gain_two))
    gate_up = low_back(matmul(normed_two, gate_up_w))
    activated = low(swiglu(gate_up))
    return residual + matmul(activated, down_w)

def reference(hidden_in, segment_ids, norm1_gain, w_gate_z, w_xbc, w_step, conv_weight, conv_bias, step_bias, decay_log, skip_gain, mixer_gain, w_mix_out, w_query, key_value_weight, w_attn_out, norm2_gain, w_gate_up, w_down, out_grad):
    params = tuple((weight_in.astype(jnp.float32) for weight_in in (norm1_gain, w_gate_z, w_xbc, w_step, conv_weight, conv_bias, step_bias, decay_log, skip_gain, mixer_gain, w_mix_out, w_query, key_value_weight, w_attn_out, norm2_gain, w_gate_up, w_down)))
    seq_count = MB * SEQS
    tokens_all = hidden_in.astype(jnp.float32).reshape(seq_count, LEN, MODEL_WIDTH)
    seg_all = segment_ids.reshape(seq_count, LEN)

    def forward(tokens_in, params_in):

        def seq_item(carry_in, pair_in):
            return (carry_in, jax.checkpoint(seq_forward)(pair_in[0], pair_in[1], params_in))
        _, results = lax.scan(seq_item, jnp.zeros((), jnp.float32), (tokens_in, seg_all))
        return results
    block_out, pull_back = jax.vjp(forward, tokens_all, params)
    grad_tokens, grad_params = pull_back(out_grad.astype(jnp.float32).reshape(seq_count, LEN, MODEL_WIDTH))
    return (block_out.reshape(MB, SEQS, LEN, MODEL_WIDTH).astype(jnp.bfloat16), grad_tokens.reshape(MB, SEQS, LEN, MODEL_WIDTH), grad_params[0], grad_params[1], grad_params[2], grad_params[3], grad_params[4], grad_params[5], grad_params[6], grad_params[7], grad_params[8], grad_params[9], grad_params[10], grad_params[11], grad_params[12], grad_params[13], grad_params[14], grad_params[15], grad_params[16])
```

```python
import jax
import jax.numpy as jnp
from jax import lax
from jax.experimental import pallas as pl
from jax.experimental.pallas import tpu as pltpu
from jax.sharding import PartitionSpec as P

MODEL_WIDTH = 1024
FF = 2048
H = 24
P_SIZE = 64
NS = 128
QUERY_HEADS = 8
KEY_VALUE_HEADS = 2
HEAD_WIDTH = 64
KC = 4
MB = 2
DI = 1536


EPSILON = 1e-06
NEGATIVE = -1e30
HIGHEST = lax.Precision.HIGHEST


def from_behind(block, axis, distance):
    devices = range(lax.axis_size(axis))
    route = [(i - distance, i) for i in devices if i - distance in devices]
    return lax.ppermute(block, axis, route)


def entering(value, axis, join, neutral):
    place = lax.axis_index(axis)
    gathered = jax.tree.map(
        lambda a, kind: lax.all_gather(a.astype(kind), axis),
        value,
        (jnp.bfloat16, jnp.bfloat16, jnp.int32, jnp.int32),
    )
    state = jax.tree.map(lambda a, e: jnp.zeros_like(a) + jnp.asarray(e, a.dtype), value, neutral)

    def one(step, state):
        return join(
            state,
            jax.tree.map(
                lambda a, own: lax.dynamic_index_in_dim(a, step, 0, False).astype(own.dtype),
                gathered,
                value,
            ),
        )

    return lax.fori_loop(0, place, one, state)


def entering_2(value, axis, join, neutral):
    count = lax.axis_size(axis)
    place = lax.axis_index(axis)
    ahead = count - 1 - place
    gathered = jax.tree.map(
        lambda a, kind: lax.all_gather(a.astype(kind), axis),
        value,
        jax.tree.map(lambda a: jnp.bfloat16 if a.dtype == jnp.float32 else a.dtype, value),
    )
    state = jax.tree.map(lambda a, e: jnp.zeros_like(a) + jnp.asarray(e, a.dtype), value, neutral)

    def one(step, state):
        source = count - 1 - step
        return join(
            state,
            jax.tree.map(
                lambda a, own: lax.dynamic_index_in_dim(a, source, 0, False).astype(own.dtype),
                gathered,
                value,
            ),
        )

    return lax.fori_loop(0, ahead, one, state)


def matmul(first_op, second_op):
    return jnp.dot(first_op, second_op, preferred_element_type=jnp.float32)


def left_t(first_op, second_op):
    return jnp.einsum("ti,tj->ij", first_op, second_op, preferred_element_type=jnp.float32)


def right_t(first_op, second_op):
    return jnp.einsum("ti,ji->tj", first_op, second_op, preferred_element_type=jnp.float32)


def rms_gain(values, gain_in):
    return values * lax.rsqrt(jnp.mean(values * values, axis=-1, keepdims=True) + EPSILON) * gain_in


def conv_mix(extended, seg_ext, kernel, offset):
    sequence_length = extended.shape[0] - (KC - 1)
    summed = jnp.zeros((sequence_length, extended.shape[1]), jnp.float32) + offset[None, :]
    for tap_index in range(KC):
        same_doc = (seg_ext[tap_index : tap_index + sequence_length] == seg_ext[KC - 1 :]).astype(
            jnp.float32
        )
        summed = (
            summed
            + kernel[tap_index][None, :]
            * extended[tap_index : tap_index + sequence_length]
            * same_doc[:, None]
        )
    return jax.nn.silu(summed)


def split_parts(conv_out):
    sequence_length = conv_out.shape[0]
    inputs = conv_out[:, : H * P_SIZE].reshape(sequence_length, H, P_SIZE)
    b_rows = conv_out[:, H * P_SIZE : H * P_SIZE + NS]
    c_rows = conv_out[:, H * P_SIZE + NS :]
    return (inputs, b_rows, c_rows)


def decay_terms(raw_step, step_bias, decay_log):
    step_size = jax.nn.softplus(raw_step + step_bias[None, :])
    cumulated = jnp.cumsum(-step_size * jnp.exp(decay_log)[None, :], axis=0)
    return (step_size, cumulated)


def state_local(conv_out, raw_step, step_bias, decay_log, seg_ids):
    inputs, b_rows, c_rows = split_parts(conv_out)
    step_size, cumulated = decay_terms(raw_step, step_bias, decay_log)
    keep_end = (seg_ids == seg_ids[-1]).astype(jnp.float32)
    weight_set = jnp.exp(cumulated[-1][None, :] - cumulated) * step_size * keep_end[:, None]
    weighted = inputs * weight_set[:, :, None]
    end_state = jnp.einsum("shp,sn->hpn", weighted, b_rows, precision=HIGHEST)
    carry_gate = jnp.exp(cumulated[-1]) * (seg_ids[0] == seg_ids[-1]).astype(jnp.float32)
    return (end_state, carry_gate)


def mixer_output(
    conv_out, raw_step, step_bias, decay_log, skip_gain, seg_ids, prev_state, prev_last
):
    inputs, b_rows, c_rows = split_parts(conv_out)
    step_size, cumulated = decay_terms(raw_step, step_bias, decay_log)
    sequence_length = conv_out.shape[0]
    places = lax.iota(jnp.int32, sequence_length)
    allowed = (seg_ids[:, None] == seg_ids[None, :]) & (places[:, None] >= places[None, :])
    by_head = cumulated.T
    spread = jnp.where(allowed[None], by_head[:, :, None] - by_head[:, None, :], NEGATIVE)
    couple = jnp.dot(c_rows, b_rows.T, precision=HIGHEST, preferred_element_type=jnp.float32)
    mixing = jnp.exp(spread) * couple[None] * step_size.T[:, None, :]
    inside = jnp.einsum("hts,shp->thp", mixing, inputs, precision=HIGHEST)
    inflow = jnp.exp(cumulated) * (seg_ids == prev_last).astype(jnp.float32)[:, None]
    carried = jnp.einsum("tn,hpn->thp", c_rows, prev_state, precision=HIGHEST) * inflow[:, :, None]
    result = inside + carried + skip_gain[None, :, None] * inputs
    return result.reshape(sequence_length, H * P_SIZE)


def gated_norm(mixer_out, gate_in, gain_in):
    return rms_gain(mixer_out * jax.nn.silu(gate_in), gain_in)


def swiglu(gate_up):
    return jax.nn.silu(gate_up[:, :FF]) * gate_up[:, FF:]


def join_states(earlier, later_in):
    gate_early, state_early, first_early, last_early = earlier
    gate_late, state_late, first_late, last_late = later_in
    linked = ((last_early == first_late) | (last_early < 0) | (first_late < 0)).astype(jnp.float32)
    through = gate_late * linked
    return (
        gate_early * through,
        state_late + through[:, None, None] * state_early,
        jnp.where(first_early < 0, first_late, first_early),
        jnp.where(last_late < 0, last_early, last_late),
    )


def join_back(earlier, later_in):
    gate_early, grad_early = earlier
    gate_late, grad_late = later_in
    return (gate_early * gate_late, grad_late + gate_late[:, None, None] * grad_early)


def head_scores(query_head_rows, segment_key_value, piece_seg, query_pos, query_seg):
    segment_length = segment_key_value.shape[0]
    local_rows = query_head_rows.shape[0]
    head_groups = QUERY_HEADS // KEY_VALUE_HEADS
    segment_key_rows = segment_key_value[:, : KEY_VALUE_HEADS * HEAD_WIDTH].reshape(
        segment_length, KEY_VALUE_HEADS, HEAD_WIDTH
    )
    segment_value_rows = segment_key_value[:, KEY_VALUE_HEADS * HEAD_WIDTH :].reshape(
        segment_length, KEY_VALUE_HEADS, HEAD_WIDTH
    )
    key_pos = lax.iota(jnp.int32, segment_length)
    allowed = (piece_seg[None, :] == query_seg[:, None]) & (key_pos[None, :] <= query_pos[:, None])
    grouped_heads = query_head_rows.reshape(local_rows, KEY_VALUE_HEADS, head_groups, HEAD_WIDTH)
    scores = jnp.einsum(
        "qgjd,kgd->gjqk", grouped_heads, segment_key_rows, preferred_element_type=jnp.float32
    ) * HEAD_WIDTH ** (-0.5)
    scores = jnp.where(
        allowed[None], scores.reshape(QUERY_HEADS, local_rows, segment_length), NEGATIVE
    )
    return (scores, allowed, segment_key_rows, segment_value_rows, grouped_heads)


def mixer_forward(conv_seq, seg_ids, raw_seq, kernel_f, offset_f, step_bias, decay_log, skip_gain):
    local_rows = conv_seq.shape[0]
    halo_rows = KC - 1
    prev_rows, prev_ids = from_behind(
        (conv_seq[local_rows - halo_rows :], seg_ids[local_rows - halo_rows :]), "fsdp", 1
    )
    seg_ext = jnp.concatenate([prev_ids, seg_ids])
    extended = jnp.concatenate([prev_rows, conv_seq]).astype(jnp.float32)
    conv_out, pull_conv = jax.vjp(
        lambda ext_in, kernel, offset: conv_mix(ext_in, seg_ext, kernel, offset),
        extended,
        kernel_f,
        offset_f,
    )
    (end_state, carry_gate), pull_state = jax.vjp(
        lambda mix_in, raw_in, bias_in, decay_in: state_local(
            mix_in, raw_in, bias_in, decay_in, seg_ids
        ),
        conv_out,
        raw_seq,
        step_bias,
        decay_log,
    )
    identity = (
        jnp.ones((H,), jnp.float32),
        jnp.zeros((H, P_SIZE, NS), jnp.float32),
        jnp.array(-1, jnp.int32),
        jnp.array(-1, jnp.int32),
    )
    prefix = entering(
        (carry_gate, end_state, seg_ids[0], seg_ids[local_rows - 1]), "fsdp", join_states, identity
    )
    prev_state = prefix[1]
    prev_last = prefix[3]
    mixer_out, pull_mixer = jax.vjp(
        lambda mix_in, raw_in, bias_in, decay_in, skip_in, state_in: mixer_output(
            mix_in, raw_in, bias_in, decay_in, skip_in, seg_ids, state_in, prev_last
        ),
        conv_out,
        raw_seq,
        step_bias,
        decay_log,
        skip_gain,
        prev_state,
    )
    saved_terms = (pull_conv, pull_state, pull_mixer, carry_gate, prev_state, prev_last, seg_ids)
    return (mixer_out, saved_terms)


def mixer_backward(saved_terms, grad_mixer):
    pull_conv, pull_state, pull_mixer, carry_gate, prev_state, prev_last, seg_ids = saved_terms
    local_rows = seg_ids.shape[0]
    halo_rows = KC - 1
    grad_mix_b, grad_raw_b, grad_bias_b, grad_decay_b, grad_skip, grad_prev = pull_mixer(grad_mixer)
    linked = (prev_last == seg_ids[0]).astype(jnp.float32)
    back_identity = (jnp.ones((H,), jnp.float32), jnp.zeros((H, P_SIZE, NS), jnp.float32))
    from_later = entering_2((carry_gate * linked, grad_prev), "fsdp", join_back, back_identity)[1]
    grad_gate = linked * jnp.sum(from_later * prev_state, axis=(1, 2))
    grad_mix_a, grad_raw_a, grad_bias_a, grad_decay_a = pull_state((from_later, grad_gate))
    grad_ext, grad_kernel, grad_offset = pull_conv(grad_mix_a + grad_mix_b)
    back_rows = from_behind(grad_ext[:halo_rows], "fsdp", -1)
    grad_conv_seq = jnp.concatenate(
        [grad_ext[halo_rows:local_rows], grad_ext[local_rows:] + back_rows]
    ).astype(jnp.bfloat16)
    return (
        grad_conv_seq,
        grad_raw_a + grad_raw_b,
        grad_kernel,
        grad_offset,
        grad_bias_a + grad_bias_b,
        grad_decay_a + grad_decay_b,
        grad_skip,
    )


def attend_forward(queries, key_value_rows, seg_ids, query_pos):
    local_rows = queries.shape[0]
    head_groups = QUERY_HEADS // KEY_VALUE_HEADS
    run_max = jnp.full((QUERY_HEADS, local_rows), NEGATIVE, jnp.float32)
    accumulated = jnp.zeros((local_rows, QUERY_HEADS, HEAD_WIDTH), jnp.float32)
    scores, allowed, segment_key_rows, segment_value_rows, grouped_heads = head_scores(
        queries,
        lax.all_gather(key_value_rows, "fsdp", axis=0, tiled=True),
        lax.all_gather(seg_ids, "fsdp", axis=0, tiled=True),
        query_pos,
        seg_ids,
    )
    segment_length = segment_key_rows.shape[0]
    new_max = jnp.maximum(run_max, jnp.max(scores, axis=-1))
    weight_set = jnp.where(allowed[None], jnp.exp(scores - new_max[:, :, None]), 0.0)
    factor = jnp.exp(run_max - new_max)
    new_sum = jnp.sum(weight_set, axis=-1)
    weight_set_reduced = weight_set.astype(jnp.bfloat16).reshape(
        KEY_VALUE_HEADS, head_groups, local_rows, segment_length
    )
    added = jnp.einsum(
        "gjqk,kgd->qgjd", weight_set_reduced, segment_value_rows, preferred_element_type=jnp.float32
    ).reshape(local_rows, QUERY_HEADS, HEAD_WIDTH)
    run_max, run_sum, accumulated = (new_max, new_sum, accumulated * factor.T[:, :, None] + added)
    attn_vals = accumulated / run_sum.T[:, :, None]
    log_sum = run_max + jnp.log(run_sum)
    return (attn_vals, log_sum)


def attend_backward(
    queries, key_value_rows, seg_ids, query_pos, log_sum, attn_vals, gradient_attention_values
):
    local_rows = queries.shape[0]
    head_groups = QUERY_HEADS // KEY_VALUE_HEADS
    score_scale = HEAD_WIDTH ** (-0.5)
    row_dot = jnp.sum(gradient_attention_values.astype(jnp.float32) * attn_vals, axis=-1).T
    gradient_attention_grouped = gradient_attention_values.reshape(
        local_rows, KEY_VALUE_HEADS, head_groups, HEAD_WIDTH
    )
    scores, allowed, segment_key_rows, segment_value_rows, grouped_heads = head_scores(
        queries,
        lax.all_gather(key_value_rows, "fsdp", axis=0, tiled=True),
        lax.all_gather(seg_ids, "fsdp", axis=0, tiled=True),
        query_pos,
        seg_ids,
    )
    segment_length = segment_key_rows.shape[0]
    weight_set = jnp.where(allowed[None], jnp.exp(scores - log_sum[:, :, None]), 0.0)
    weight_set_reduced = weight_set.astype(jnp.bfloat16).reshape(
        KEY_VALUE_HEADS, head_groups, local_rows, segment_length
    )
    gradient_value_rows = jnp.einsum(
        "gjqk,qgjd->kgd",
        weight_set_reduced,
        gradient_attention_grouped,
        preferred_element_type=jnp.float32,
    )
    grad_weights = jnp.einsum(
        "qgjd,kgd->gjqk",
        gradient_attention_grouped,
        segment_value_rows,
        preferred_element_type=jnp.float32,
    ).reshape(QUERY_HEADS, local_rows, segment_length)
    grad_scores = (
        (weight_set * (grad_weights - row_dot[:, :, None]))
        .astype(jnp.bfloat16)
        .reshape(KEY_VALUE_HEADS, head_groups, local_rows, segment_length)
    )
    grad_query = (
        jnp.einsum(
            "gjqk,kgd->qgjd", grad_scores, segment_key_rows, preferred_element_type=jnp.float32
        ).reshape(local_rows, QUERY_HEADS, HEAD_WIDTH)
        * score_scale
    )
    gradient_key_rows = (
        jnp.einsum("gjqk,qgjd->kgd", grad_scores, grouped_heads, preferred_element_type=jnp.float32)
        * score_scale
    )
    update = jnp.concatenate(
        [
            gradient_key_rows.reshape(segment_length, KEY_VALUE_HEADS * HEAD_WIDTH),
            gradient_value_rows.reshape(segment_length, KEY_VALUE_HEADS * HEAD_WIDTH),
        ],
        axis=1,
    )
    grad_query, grad_kv_all = (grad_query, update)
    grad_kv = lax.psum_scatter(
        grad_kv_all.astype(jnp.bfloat16), "fsdp", scatter_dimension=0, tiled=True
    )
    return (grad_query.astype(jnp.bfloat16).reshape(local_rows, QUERY_HEADS * HEAD_WIDTH), grad_kv)


BOTH = ("dp", "fsdp")


def exchange(block, bit):
    count = lax.axis_size(BOTH)
    return lax.ppermute(block, BOTH, [(i, i ^ (1 << bit)) for i in range(count)])


def bit_count():
    return lax.axis_size(BOTH).bit_length() - 1


def place_of():
    return lax.axis_index(BOTH)


def gather_pieces(packed):
    grown = packed[None]
    offsets = [0]
    for bit in range(bit_count() - 1, 2, -1):
        grown = jnp.concatenate([grown, exchange(grown, bit)], 0)
        offsets = offsets + [o ^ (1 << bit) for o in offsets]
    halves = []
    for half, (first, second) in enumerate(((2, 1), (1, 2))):
        own = grown[:, half]
        eight = jnp.concatenate([own, exchange(own, first)], 0)
        near = offsets + [o ^ (1 << first) for o in offsets]
        far_block = exchange(eight, second)
        far = [o ^ (1 << second) for o in near]
        halves.append(
            [
                (eight, near),
                (far_block, far),
                (exchange(eight, 0), [o ^ 1 for o in near]),
                (exchange(far_block, 0), [o ^ 1 for o in far]),
            ]
        )
    return halves


def assemble(halves, outs, moves):
    flat, meta = [], []
    for half, pieces in enumerate(halves):
        for piece, offsets in pieces:
            flat.append(piece)
            meta.append((half, offsets))
    jobs = []
    for at, (half, offsets) in enumerate(meta):
        for j, offset in enumerate(offsets):
            for move in moves:
                if move[0] == half:
                    jobs.append((at, j, offset, move))
    jobs.sort(key=lambda job: job[3][3])
    n_in, n_out = len(flat), len(outs)

    def kernel(place_ref, *refs):
        ins, results = refs[:n_in], refs[n_in : n_in + n_out]
        held, sems, out_sems = refs[n_in + n_out : -2], refs[-2], refs[-1]
        place = place_ref[0]
        copies = [[] for _ in outs]
        for number, (at, j, offset, (_, r0, rows, c0, columns, out, row, column)) in enumerate(jobs):
            copy = pltpu.make_async_copy(
                ins[at].at[j, pl.ds(r0, rows), pl.ds(c0, columns)],
                held[out].at[place ^ offset, pl.ds(row, rows), pl.ds(column, columns)],
                sems.at[number],
            )
            copy.start()
            copies[out].append(copy)
        back = []
        for out in range(n_out):
            for copy in copies[out]:
                copy.wait()
            copy = pltpu.make_async_copy(held[out], results[out], out_sems.at[out])
            copy.start()
            back.append(copy)
        for copy in back:
            copy.wait()

    return pl.pallas_call(
        kernel,
        out_shape=[jax.ShapeDtypeStruct(s, jnp.bfloat16) for s in outs],
        in_specs=[pl.BlockSpec(memory_space=pltpu.SMEM)]
        + [pl.BlockSpec(memory_space=pl.ANY)] * n_in,
        out_specs=[pl.BlockSpec(memory_space=pl.ANY)] * n_out,
        scratch_shapes=[pltpu.VMEM(s, jnp.bfloat16) for s in outs]
        + [pltpu.SemaphoreType.DMA((len(jobs),)), pltpu.SemaphoreType.DMA((n_out,))],
        compiler_params=pltpu.CompilerParams(vmem_limit_bytes=24 * 2**20),
        name="assemble",
    )(place_of().reshape(1).astype(jnp.int32), *flat)


def halve(block, axis, bit, last=False):
    own_bit = (place_of() >> bit) & 1
    mine = lax.dynamic_index_in_dim(block, own_bit, axis, False)
    other = lax.dynamic_index_in_dim(block, 1 - own_bit, axis, False)
    summed = mine.astype(jnp.float32) + exchange(other, bit).astype(jnp.float32)
    return summed if last else summed.astype(jnp.bfloat16)


def scatter_sum(first_half, second_half):
    bits = bit_count()
    count = 1 << bits
    halves = []
    for block, first in ((first_half, 2), (second_half, 1)):
        rows, columns = block.shape[0] // count, block.shape[1]
        block = block.astype(jnp.bfloat16).reshape((2,) * bits + (rows, columns))
        block = halve(block, bits - 1, 0)
        if first == 2:
            block = halve(halve(block, bits - 3, 2), bits - 3, 1)
        else:
            block = halve(halve(block, bits - 2, 1), bits - 3, 2)
        halves.append(block)
    block = jnp.stack(halves)
    for bit in range(3, bits):
        block = halve(block, bits - bit, bit, last=bit == bits - 1)
    return block


def gather_weights(w_gate_z, w_xbc, w_step, w_query, key_value_weight, w_mix_out, w_attn_out, w_gate_up, w_down):
    count = lax.axis_size(BOTH)
    r = w_xbc.shape[0]
    rm, ra, rd = w_mix_out.shape[0], w_attn_out.shape[0], w_down.shape[0]
    step_pad = jnp.pad(w_step, ((0, 0), (0, 128 - H)))
    one = jnp.concatenate([w_xbc, step_pad, w_query, key_value_weight], 1)
    n1 = one.shape[1]
    pad1 = -n1 % 256
    one = jnp.pad(one, ((0, 0), (0, pad1)))
    h1 = (n1 + pad1) // 2
    one = jnp.stack([one[:, :h1], one[:, h1:]])
    (first_full,) = assemble(
        gather_pieces(one),
        [(count, r, n1 + pad1)],
        [(0, 0, r, 0, h1, 0, 0, 0), (1, 0, r, 0, h1, 0, 0, h1)],
    )
    z2 = jnp.stack([w_gate_z[:, : DI // 2], w_gate_z[:, DI // 2 :]])
    (z_full,) = assemble(
        gather_pieces(z2),
        [(count, r, DI)],
        [(0, 0, r, 0, DI // 2, 0, 0, 0), (1, 0, r, 0, DI // 2, 0, 0, DI // 2)],
    )
    hw = MODEL_WIDTH // 2
    out2 = jnp.concatenate([w_mix_out, w_attn_out], 0)
    out2 = jnp.stack([out2[:, :hw], out2[:, hw:]])
    mix_full, attn_full = assemble(
        gather_pieces(out2),
        [(count, rm, MODEL_WIDTH), (count, ra, MODEL_WIDTH)],
        [
            (0, 0, rm, 0, hw, 0, 0, 0),
            (1, 0, rm, 0, hw, 0, 0, hw),
            (0, rm, ra, 0, hw, 1, 0, 0),
            (1, rm, ra, 0, hw, 1, 0, hw),
        ],
    )
    gu2 = jnp.stack([w_gate_up[:, :FF], w_gate_up[:, FF:]])
    (gate_up_full,) = assemble(
        gather_pieces(gu2),
        [(count, r, 2 * FF)],
        [(0, 0, r, 0, FF, 0, 0, 0), (1, 0, r, 0, FF, 0, 0, FF)],
    )
    d2 = jnp.stack([w_down[:, :hw], w_down[:, hw:]])
    (down_full,) = assemble(
        gather_pieces(d2),
        [(count, rd, MODEL_WIDTH)],
        [(0, 0, rd, 0, hw, 0, 0, 0), (1, 0, rd, 0, hw, 0, 0, hw)],
    )
    return tuple(
        a.reshape(-1, a.shape[2])
        for a in (first_full, z_full, mix_full, attn_full, gate_up_full, down_full)
    )


def per_device(
    hidden_in,
    segment_ids,
    norm1_gain,
    w_gate_z,
    w_xbc,
    w_step,
    conv_weight,
    conv_bias,
    step_bias,
    decay_log,
    skip_gain,
    mixer_gain,
    w_mix_out,
    w_query,
    key_value_weight,
    w_attn_out,
    norm2_gain,
    w_gate_up,
    w_down,
    out_grad,
):
    local_rows = hidden_in.shape[2]
    seqs = hidden_in.shape[0] * hidden_in.shape[1]
    flat_rows = seqs * local_rows
    conv_width = DI + 2 * NS
    query_width = QUERY_HEADS * HEAD_WIDTH
    kv_width = 2 * KEY_VALUE_HEADS * HEAD_WIDTH
    query_pos = lax.axis_index("fsdp") * local_rows + lax.iota(jnp.int32, local_rows)
    pieces = [norm1_gain, norm2_gain, mixer_gain, conv_bias, conv_weight.reshape(-1)]
    sizes = [p.shape[0] for p in pieces]
    small = jnp.concatenate(pieces)
    small_pad = -small.shape[0] % 128
    small = jnp.pad(small, (0, small_pad))[None]
    small_all = lax.all_gather(small, BOTH, axis=0, tiled=True).astype(jnp.float32)
    vectors = []
    at = 0
    for size in sizes:
        vectors.append(small_all[:, at : at + size])
        at += size
    gain_one, gain_two, mix_gain_full, offset_f = (v.reshape(-1) for v in vectors[:4])
    kernel_f = vectors[4].reshape(vectors[4].shape[0], KC, -1).transpose(1, 0, 2).reshape(KC, -1)
    first_full, z_full, mix_out_full, attn_out_full, gate_up_full, down_full = gather_weights(
        w_gate_z, w_xbc, w_step, w_query, key_value_weight, w_mix_out, w_attn_out, w_gate_up, w_down
    )
    tokens = hidden_in.reshape(flat_rows, MODEL_WIDTH).astype(jnp.float32)
    seg_block = segment_ids.reshape(seqs, local_rows)
    normed, pull_norm_one = jax.vjp(rms_gain, tokens, gain_one)
    normed_low = normed.astype(jnp.bfloat16)
    first_out = matmul(normed_low, first_full)
    conv_in = first_out[:, :conv_width].astype(jnp.bfloat16).reshape(seqs, local_rows, conv_width)
    raw_step = first_out[:, conv_width : conv_width + H].reshape(seqs, local_rows, H)
    q0 = conv_width + 128
    queries = first_out[:, q0 : q0 + query_width].astype(jnp.bfloat16)
    queries = queries.reshape(seqs, local_rows, query_width)
    k0 = q0 + query_width
    key_value_rows = first_out[:, k0 : k0 + kv_width].astype(jnp.bfloat16)
    key_value_rows = key_value_rows.reshape(seqs, local_rows, kv_width)
    gate_z = matmul(normed_low, z_full)
    mixers, saved, attns, log_sums = [], [], [], []
    for s in range(seqs):
        mixer_out, saved_terms = mixer_forward(
            conv_in[s], seg_block[s], raw_step[s], kernel_f, offset_f, step_bias, decay_log, skip_gain
        )
        mixers.append(mixer_out)
        saved.append(saved_terms)
        attn_vals, log_sum = attend_forward(queries[s], key_value_rows[s], seg_block[s], query_pos)
        attns.append(attn_vals)
        log_sums.append(log_sum)
    mixer_out = jnp.concatenate(mixers)
    normed_mix, pull_gated = jax.vjp(gated_norm, mixer_out, gate_z, mix_gain_full)
    normed_mix_low = normed_mix.astype(jnp.bfloat16)
    attn_low = jnp.concatenate(attns).astype(jnp.bfloat16).reshape(flat_rows, query_width)
    residual = tokens + (matmul(normed_mix_low, mix_out_full) + matmul(attn_low, attn_out_full))
    normed_two, pull_norm_two = jax.vjp(rms_gain, residual, gain_two)
    normed_two_low = normed_two.astype(jnp.bfloat16)
    gate_up = matmul(normed_two_low, gate_up_full)
    activated, pull_swiglu = jax.vjp(swiglu, gate_up)
    act_low = activated.astype(jnp.bfloat16)
    block_out = (residual + matmul(act_low, down_full)).astype(jnp.bfloat16)
    grad_out = out_grad.reshape(flat_rows, MODEL_WIDTH)
    grad_down = left_t(act_low, grad_out)
    (grad_gate_up,) = pull_swiglu(right_t(grad_out, down_full))
    grad_gate_up_low = grad_gate_up.astype(jnp.bfloat16)
    grad_gate_up_w = left_t(normed_two_low, grad_gate_up_low)
    hw = MODEL_WIDTH // 2
    sum_down = scatter_sum(grad_down[:, :hw], grad_down[:, hw:])
    sum_gate_up = scatter_sum(grad_gate_up_w[:, :FF], grad_gate_up_w[:, FF:])
    grad_resid_norm, grad_gain_two = pull_norm_two(right_t(grad_gate_up_low, gate_up_full))
    grad_resid = grad_out.astype(jnp.float32) + grad_resid_norm
    grad_branch = grad_resid.astype(jnp.bfloat16)
    grad_attn_w = left_t(attn_low, grad_branch)
    grad_mix_out_w = left_t(normed_mix_low, grad_branch)
    count = lax.axis_size(BOTH)
    out_w = jnp.concatenate(
        [
            grad_mix_out_w.astype(jnp.bfloat16).reshape(count, -1, MODEL_WIDTH),
            grad_attn_w.astype(jnp.bfloat16).reshape(count, -1, MODEL_WIDTH),
        ],
        1,
    ).reshape(-1, MODEL_WIDTH)
    sum_out = scatter_sum(out_w[:, :hw], out_w[:, hw:])
    grad_attn = right_t(grad_branch, attn_out_full).astype(jnp.bfloat16)
    grad_attn = grad_attn.reshape(seqs, local_rows, QUERY_HEADS, HEAD_WIDTH)
    grad_mixer, grad_gate_z, grad_mix_gain = pull_gated(right_t(grad_branch, mix_out_full))
    grad_gate_z_low = grad_gate_z.astype(jnp.bfloat16)
    grad_gate_z_w = left_t(normed_low, grad_gate_z_low)
    sum_z = scatter_sum(grad_gate_z_w[:, : DI // 2], grad_gate_z_w[:, DI // 2 :])
    grad_mixer = grad_mixer.reshape(seqs, local_rows, DI)
    rows_out = []
    totals = None
    for s in range(seqs):
        grad_query, grad_kv = attend_backward(
            queries[s], key_value_rows[s], seg_block[s], query_pos, log_sums[s], attns[s], grad_attn[s]
        )
        conv_seq, raw_seq, *parts = mixer_backward(saved[s], grad_mixer[s])
        totals = parts if totals is None else jax.tree.map(jnp.add, totals, parts)
        raw_low = jnp.pad(raw_seq.astype(jnp.bfloat16), ((0, 0), (0, 128 - H)))
        rows_out.append(jnp.concatenate([conv_seq, raw_low, grad_query, grad_kv], 1))
    kernel_part, offset_part, bias_part, decay_part, skip_part = totals
    grad_first = jnp.concatenate(rows_out)
    grad_first = jnp.pad(grad_first, ((0, 0), (0, first_full.shape[1] - grad_first.shape[1])))
    grad_first_w = left_t(normed_low, grad_first)
    h1 = grad_first.shape[1] // 2
    sum_first = scatter_sum(grad_first_w[:, :h1], grad_first_w[:, h1:])
    grad_normed = right_t(grad_gate_z_low, z_full) + right_t(grad_first, first_full)
    grad_tokens, grad_gain_one = pull_norm_one(grad_normed)
    input_grad = grad_resid + grad_tokens
    parts = [
        grad_gain_one.reshape(count, -1),
        grad_gain_two.reshape(count, -1),
        grad_mix_gain.reshape(count, -1),
        offset_part.reshape(count, -1),
        kernel_part.reshape(KC, count, -1).transpose(1, 0, 2).reshape(count, -1),
    ]
    small_grads = jnp.concatenate(parts, 1)
    small_grads = jnp.pad(small_grads, ((0, 0), (0, small_pad)))
    own_small = lax.psum_scatter(small_grads, BOTH, scatter_dimension=0, tiled=True)[0]
    own = []
    at = 0
    for size in sizes:
        own.append(own_small[at : at + size])
        at += size
    head_sums = lax.psum(jnp.stack([bias_part, decay_part, skip_part]), BOTH)
    sum_first = jnp.concatenate([sum_first[0], sum_first[1]], 1)
    rm = w_mix_out.shape[0]
    sum_out = jnp.concatenate([sum_out[0], sum_out[1]], 1)
    return (
        block_out.reshape(hidden_in.shape),
        input_grad.reshape(hidden_in.shape),
        own[0],
        jnp.concatenate([sum_z[0], sum_z[1]], 1),
        sum_first[:, :conv_width],
        sum_first[:, conv_width : conv_width + H],
        own[4].reshape(KC, -1),
        own[3],
        head_sums[0],
        head_sums[1],
        head_sums[2],
        own[2],
        sum_out[:rm],
        sum_first[:, q0 : q0 + query_width],
        sum_first[:, k0 : k0 + kv_width],
        sum_out[rm:],
        own[1],
        jnp.concatenate([sum_gate_up[0], sum_gate_up[1]], 1),
        jnp.concatenate([sum_down[0], sum_down[1]], 1),
    )


def solution(mesh):
    placed = (
        P(None, "dp", "fsdp", None),
        P(None, "dp", "fsdp"),
        P(("dp", "fsdp")),
        P(("dp", "fsdp"), None),
        P(("dp", "fsdp"), None),
        P(("dp", "fsdp"), None),
        P(None, ("dp", "fsdp")),
        P(("dp", "fsdp")),
        P(),
        P(),
        P(),
        P(("dp", "fsdp")),
        P(("dp", "fsdp"), None),
        P(("dp", "fsdp"), None),
        P(("dp", "fsdp"), None),
        P(("dp", "fsdp"), None),
        P(("dp", "fsdp")),
        P(("dp", "fsdp"), None),
        P(("dp", "fsdp"), None),
        P(None, "dp", "fsdp", None),
    )
    return jax.shard_map(
        per_device,
        mesh=mesh,
        in_specs=placed,
        out_specs=(
            P(None, "dp", "fsdp", None),
            P(None, "dp", "fsdp", None),
            P(("dp", "fsdp")),
            P(("dp", "fsdp"), None),
            P(("dp", "fsdp"), None),
            P(("dp", "fsdp"), None),
            P(None, ("dp", "fsdp")),
            P(("dp", "fsdp")),
            P(),
            P(),
            P(),
            P(("dp", "fsdp")),
            P(("dp", "fsdp"), None),
            P(("dp", "fsdp"), None),
            P(("dp", "fsdp"), None),
            P(("dp", "fsdp"), None),
            P(("dp", "fsdp")),
            P(("dp", "fsdp"), None),
            P(("dp", "fsdp"), None),
        ),
        check_vma=False,
    )
```

```python
import functools

import jax
import jax.numpy as jnp
from jax import lax
from jax.experimental import pallas as pl
from jax.experimental.pallas import tpu as pltpu
from jax.sharding import PartitionSpec as P

MODEL_WIDTH = 1024
FF = 2048
H = 24
P_SIZE = 64
NS = 128
QUERY_HEADS = 8
KEY_VALUE_HEADS = 2
HEAD_WIDTH = 64
KC = 4
DI = 1536


EPSILON = 1e-06
NEGATIVE = -1e30


def matmul(first_op, second_op):
    return jnp.dot(first_op, second_op, preferred_element_type=jnp.float32)


def left_t(first_op, second_op):
    return jnp.einsum("ti,tj->ij", first_op, second_op, preferred_element_type=jnp.float32)


def right_t(first_op, second_op):
    return jnp.einsum("ti,ji->tj", first_op, second_op, preferred_element_type=jnp.float32)


def rms_gain(values, gain_in):
    return values * lax.rsqrt(jnp.mean(values * values, axis=-1, keepdims=True) + EPSILON) * gain_in


def swiglu(gate_up):
    return jax.nn.silu(gate_up[:, :FF]) * gate_up[:, FF:]


BOTH = ("dp", "fsdp")


def exchange_mask(block, mask):
    count = lax.axis_size(BOTH)
    return lax.ppermute(block, BOTH, [(i, i ^ mask) for i in range(count)])


def exchange(block, bit):
    return exchange_mask(block, 1 << bit)


def bit_count():
    return lax.axis_size(BOTH).bit_length() - 1


def place_of():
    return lax.axis_index(BOTH)


def spec_any(count):
    return [pl.BlockSpec(memory_space=pl.ANY)] * count


def copies_kernel(n_in, n_after, n_out, n_hold, jobs, place_ref, *refs):
    ins, refs = refs[:n_in], refs[n_in + n_hold + n_after :]
    outs, refs = refs[:n_out], refs[n_out + n_hold :]
    held, sems, out_sems = refs[:n_out], refs[-2], refs[-1]
    place = place_ref[0]
    copies = [[] for _ in outs]
    for number, (out, source, source_at, target_at) in enumerate(jobs):
        copy = pltpu.make_async_copy(
            ins[source].at[source_at], held[out].at[target_at(place)], sems.at[number]
        )
        copy.start()
        copies[out].append(copy)
    back = []
    for out in range(n_out):
        for copy in copies[out]:
            copy.wait()
        copy = pltpu.make_async_copy(held[out], outs[out], out_sems.at[out])
        copy.start()
        back.append(copy)
    for copy in back:
        copy.wait()


def copies(name, ins, outs, jobs, after=(), hold=()):
    jobs = sorted(jobs, key=lambda job: job[0])
    return pl.pallas_call(
        functools.partial(copies_kernel, len(ins), len(after), len(outs), len(hold), jobs),
        out_shape=[jax.ShapeDtypeStruct(s, jnp.bfloat16) for s in outs]
        + [jax.ShapeDtypeStruct(a.shape, a.dtype) for a in hold],
        in_specs=[pl.BlockSpec(memory_space=pltpu.SMEM)] + spec_any(len(ins) + len(hold) + len(after)),
        out_specs=spec_any(len(outs) + len(hold)),
        input_output_aliases={1 + len(ins) + n: len(outs) + n for n in range(len(hold))},
        scratch_shapes=[pltpu.VMEM(s, jnp.bfloat16) for s in outs]
        + [pltpu.SemaphoreType.DMA((len(jobs),)), pltpu.SemaphoreType.DMA((len(outs),))],
        compiler_params=pltpu.CompilerParams(vmem_limit_bytes=24 * 2**20),
        name=name,
    )(place_of().reshape(1).astype(jnp.int32), *ins, *hold, *after)


class Part:
    def __init__(self, block, offsets=(0,)):
        self.pieces = [(block, list(offsets))]

    def step(self, bit):
        ((block, offsets),) = self.pieces
        self.pieces.append((exchange(block, bit), [o ^ (1 << bit) for o in offsets]))

    def steps(self, bits):
        for n, bit in enumerate(bits):
            if n:
                join([self])
            self.step(bit)

    def core(self):
        self.pieces += [(exchange(a, 0), [o ^ 1 for o in offsets]) for a, offsets in self.pieces]


def join(parts, after=(), split=(), hold=()):
    ins, outs, jobs, made = [], [], [], []
    for part in parts:
        first = part.pieces[0][0]
        blocks = sum(len(offsets) for _, offsets in part.pieces)
        offsets = sum((o for _, o in part.pieces), [])
        halves = (0, 1) if part in split else (None,)
        for half in halves:
            at = 0
            for number, (array, own) in enumerate(part.pieces):
                source = len(ins) + number
                source_at = (slice(None),) if half is None else (slice(None), half)
                target = (slice(at, at + len(own)),)
                jobs.append((len(outs), source, source_at, lambda place, target=target: target))
                at += len(own)
            outs.append((blocks,) + (first.shape[1:] if half is None else first.shape[2:]))
            made.append((part, half, offsets))
        ins += [array for array, _ in part.pieces]
    cut = []
    held = [part.pieces[0][0] for part in hold]
    found = copies("join", ins, outs, jobs, after, held)
    for array, part in zip(found[len(outs) :], hold):
        part.pieces = [(array, part.pieces[0][1])]
    for array, (part, half, offsets) in zip(found, made):
        if half is None:
            part.pieces = [(array, offsets)]
        else:
            cut.append(Part(array, offsets))
    return cut


def assemble(parts, outs, moves, after=()):
    ins, jobs = [], []
    for at, part in enumerate(parts):
        for piece, offsets in part.pieces:
            for j, offset in enumerate(offsets):
                for of, r0, rows, c0, columns, out, row, column in moves:
                    if of == at:
                        source_at = (j, pl.ds(r0, rows), pl.ds(c0, columns))
                        target = (pl.ds(row, rows), pl.ds(column, columns))
                        jobs.append(
                            (out, len(ins), source_at, lambda place, o=offset, t=target: (place ^ o,) + t)
                        )
            ins.append(piece)
    return [a.reshape(-1, a.shape[2]) for a in copies("assemble", ins, outs, jobs, after)]


def turned_offsets(bits):
    offsets = [0]
    for bit in list(range(bits - 1, 2, -1)) + [1, 2]:
        offsets = offsets + [o ^ (1 << bit) for o in offsets]
    return offsets


def turn_kernel(n_x, n_hold, n_after, rows, offsets, place_ref, *refs):
    xs, refs = refs[:n_x], refs[n_x + n_hold + n_after :]
    keep_ref, send_ref, turned = refs[0], refs[1], refs[2 + n_hold :]
    place = place_ref[0]
    total = sum(rows)
    for x_ref, t_ref in zip(xs, turned):
        t_ref[...] = x_ref[...].T
    for t, offset in enumerate(offsets):
        at = t * total
        for t_ref, size in zip(turned, rows):
            begin = pl.multiple_of((place ^ offset) * size, size)
            keep_ref[at : at + size] = t_ref[pl.ds(begin, size)]
            begin = pl.multiple_of((place ^ (offset ^ 1)) * size, size)
            send_ref[at : at + size] = t_ref[pl.ds(begin, size)]
            at += size


def turn(*xs, after=(), hold=()):
    bits = bit_count()
    rows = [x.shape[1] >> bits for x in xs]
    tokens, half = xs[0].shape[0], sum(x.shape[1] for x in xs) // 2
    if any(r % 16 for r in rows):
        blocks = jnp.concatenate([x.T.reshape(1 << bits, r, tokens) for x, r in zip(xs, rows)], 1)
        offsets = jnp.asarray(turned_offsets(bits), jnp.int32) ^ place_of()
        sides = [jnp.take(blocks, o, axis=0).reshape(half, tokens) for o in (offsets, offsets ^ 1)]
        return (*sides, *hold)
    vmem = pl.BlockSpec(memory_space=pltpu.VMEM)
    return pl.pallas_call(
        functools.partial(turn_kernel, len(xs), len(hold), len(after), rows, turned_offsets(bits)),
        in_specs=[pl.BlockSpec(memory_space=pltpu.SMEM)] + [vmem] * len(xs) + spec_any(len(hold) + len(after)),
        out_specs=[vmem] * 2 + spec_any(len(hold)),
        out_shape=[jax.ShapeDtypeStruct((half, tokens), jnp.bfloat16)] * 2
        + [jax.ShapeDtypeStruct(a.shape, a.dtype) for a in hold],
        input_output_aliases={1 + len(xs) + n: 2 + n for n in range(len(hold))},
        scratch_shapes=[pltpu.VMEM((x.shape[1], x.shape[0]), jnp.bfloat16) for x in xs],
        compiler_params=pltpu.CompilerParams(vmem_limit_bytes=24 * 2**20),
        name="turn",
    )(place_of().reshape(1).astype(jnp.int32), *xs, *hold, *after)


def grad_kernel(n_pairs, half, *refs):
    pairs, (keep_ref, send_ref) = refs[: 2 * n_pairs], refs[-2:]
    total = None
    for x_ref, g_ref in zip(pairs[:n_pairs], pairs[n_pairs:]):
        part = jnp.dot(x_ref[...], g_ref[...], preferred_element_type=jnp.float32)
        total = part if total is None else total + part
    total = total.astype(jnp.bfloat16)
    rows = keep_ref.shape[1]
    for second in range(2):
        for first, ref in enumerate((keep_ref, send_ref)):
            quarter = 2 * first + second if half == 0 else 2 * second + first
            ref[second] = total[quarter * rows : (quarter + 1) * rows]


def weight_grad(xs, gs, half, after=()):
    k, n = xs[0].shape[0], gs[0].shape[1]
    width = next(w for w in (512, 384, 256, 128) if n % w == 0)
    block = pl.BlockSpec((2, k // 4, width), lambda i: (0, 0, i))
    return pl.pallas_call(
        functools.partial(grad_kernel, len(xs), half),
        grid=(n // width,),
        in_specs=[pl.BlockSpec((k, g.shape[0]), lambda i: (0, 0)) for g in gs]
        + [pl.BlockSpec((g.shape[0], width), lambda i: (0, i)) for g in gs]
        + spec_any(len(after)),
        out_specs=[block, block],
        out_shape=[jax.ShapeDtypeStruct((2, k // 4, n), jnp.bfloat16)] * 2,
        compiler_params=pltpu.CompilerParams(vmem_limit_bytes=48 * 2**20),
        name="weight_grad",
    )(*xs, *gs, *after)


def both_kernel(n_pairs, half, *refs):
    outs = refs[-2:]
    gs = refs[2 * n_pairs : 3 * n_pairs]
    for xs, out_ref in ((refs[:n_pairs], outs[0]), (refs[n_pairs : 2 * n_pairs], outs[1])):
        total = None
        for x_ref, g_ref in zip(xs, gs):
            part = jnp.dot(x_ref[...], g_ref[...], preferred_element_type=jnp.float32)
            total = part if total is None else total + part
        total = total.astype(jnp.bfloat16)
        rows = out_ref.shape[1] // 4
        for quarter in range(4):
            place = quarter if half == 0 else 2 * (quarter % 2) + quarter // 2
            out_ref[0, place * rows : (place + 1) * rows] = total[quarter * rows : (quarter + 1) * rows]


def both_grads(keeps, sends, gs, half, after=()):
    k, n = keeps[0].shape[0], gs[0].shape[1]
    width = next(w for w in (256, 128) if n % w == 0)
    block = pl.BlockSpec((1, k, width), lambda i: (0, 0, i))
    return pl.pallas_call(
        functools.partial(both_kernel, len(gs), half),
        grid=(n // width,),
        in_specs=[pl.BlockSpec((k, g.shape[0]), lambda i: (0, 0)) for g in gs] * 2
        + [pl.BlockSpec((g.shape[0], width), lambda i: (0, i)) for g in gs]
        + spec_any(len(after)),
        out_specs=[block, block],
        out_shape=[jax.ShapeDtypeStruct((1, k, n), jnp.bfloat16)] * 2,
        compiler_params=pltpu.CompilerParams(vmem_limit_bytes=48 * 2**20),
        name="both_grads",
    )(*keeps, *sends, *gs, *after)


def add_kernel(shape, last, n_after, *refs):
    n_in = sum(len(counts) for counts in shape)
    keeps, gots, outs = refs[:n_in], refs[n_in : 2 * n_in], refs[2 * n_in + n_after :]
    at = 0
    for item, counts in enumerate(shape):
        slot = 0
        for count in counts:
            for s in range(count):
                total = keeps[at][s].astype(jnp.float32) + gots[at][s].astype(jnp.float32)
                if last:
                    outs[item][slot] = total
                else:
                    total = total.astype(jnp.bfloat16)
                    half = total.shape[0] // 2
                    outs[2 * item][slot] = total[:half]
                    outs[2 * item + 1][slot] = total[half:]
                slot += 1
            at += 1


def add_up(items, after=(), last=False):
    shape = [[own.shape[0] for own, _ in item] for item in items]
    keeps = [own for item in items for own, _ in item]
    gots = [got for item in items for _, got in item]
    widths = {a.shape[2] for a in keeps}
    steps = next(g for g in (4, 2, 3, 1) if all(w % (g * 128) == 0 for w in widths))
    blocks, outs = [], []
    for a in keeps:
        blocks.append(pl.BlockSpec(a.shape[:2] + (a.shape[2] // steps,), lambda i: (0, 0, i)))
    out_blocks = []
    for item, counts in zip(items, shape):
        rows, n = item[0][0].shape[1:]
        rows = rows if last else rows // 2
        for _ in range(1 if last else 2):
            out_blocks.append(pl.BlockSpec((sum(counts), rows, n // steps), lambda i: (0, 0, i)))
            outs.append(
                jax.ShapeDtypeStruct((sum(counts), rows, n), jnp.float32 if last else jnp.bfloat16)
            )
    return pl.pallas_call(
        functools.partial(add_kernel, shape, last, len(after)),
        grid=(steps,),
        in_specs=blocks + blocks + spec_any(len(after)),
        out_specs=out_blocks,
        out_shape=outs,
        compiler_params=pltpu.CompilerParams(vmem_limit_bytes=48 * 2**20),
        name="add_up",
    )(*keeps, *gots, *after)


class Sum:
    def __init__(self, xs, gs, half, after=()):
        self.first = (2, 1)[half]
        keep, send = weight_grad(xs, gs, half, after)
        self.keep, self.send = (a.reshape(1, -1, a.shape[2]) for a in (keep, send))

    def start(self, bit):
        self.got = exchange(self.send, bit)

    def near(self):
        self.start(self.first)

    def second(self):
        self.start(3 - self.first)


class CoreSum(Sum):
    def __init__(self, keeps, sends, gs, half, after=()):
        self.first = (2, 1)[half]
        self.keep, self.send = both_grads(keeps, sends, gs, half, after)

    def core(self):
        self.start(0)


class Pair:
    def start(self, bit):
        self.got = exchange(self.send, bit)


def advance(steps, after=()):
    items = [[(s.keep, s.got) for s in (step if isinstance(step, tuple) else (step,))] for step in steps]
    found = add_up(items, after)
    made = []
    for n, step in enumerate(steps):
        step = Pair() if isinstance(step, tuple) else step
        step.keep, step.send = found[2 * n : 2 * n + 2]
        made.append(step)
    return made


def finish(pairs, after=()):
    return add_up([[(p.keep, p.got)] for p in pairs], after, last=True)


def parts_kernel(n_in, parts, n_after, *refs):
    ins, outs = refs[:n_in], refs[n_in + n_after :]
    total = ins[0][0].astype(jnp.float32)
    for ref in ins[1:]:
        total = total + ref[0].astype(jnp.float32)
    rows = total.shape[0] // parts
    for n in range(parts):
        outs[n][0] = total[n * rows : (n + 1) * rows].astype(outs[n].dtype)


def add_parts(arrays, parts, kind=jnp.bfloat16, after=()):
    _, rows, n = arrays[0].shape
    steps = next(g for g in (4, 2, 1) if n % (g * 128) == 0)
    spec = lambda rows: pl.BlockSpec((1, rows, n // steps), lambda i: (0, 0, i))
    return pl.pallas_call(
        functools.partial(parts_kernel, len(arrays), parts, len(after)),
        grid=(steps,),
        in_specs=[spec(rows)] * len(arrays) + spec_any(len(after)),
        out_specs=[spec(rows // parts)] * parts,
        out_shape=[jax.ShapeDtypeStruct((1, rows // parts, n), kind)] * parts,
        compiler_params=pltpu.CompilerParams(vmem_limit_bytes=48 * 2**20),
        name="add_parts",
    )(*arrays, *after)


class Direct:
    def __init__(self, keeps, sends, gs, after=()):
        self.keep, self.send = both_grads(keeps, sends, gs, 0, after)

    def core(self):
        self.got = [exchange(self.send, 0)]

    def planes(self, after=()):
        quarters = add_parts([self.keep] + self.got, 4, after=after)
        self.keep = quarters[0]
        self.got = [exchange_mask(q, mask) for q, mask in zip(quarters[1:], (2, 4, 6))]
        return quarters[0]

    def lines(self, after=()):
        bits = bit_count()
        arrays = [self.keep] + self.got
        if bits == 5:
            quarters = add_parts(arrays, 4, after=after)
            self.keep = quarters[0]
            self.got = [exchange_mask(q, mask) for q, mask in zip(quarters[1:], (16, 8, 24))]
            return
        for bit in range(3, bits):
            self.keep, send = add_parts(arrays, 2, after=after)
            self.got = [exchange(send, bit)]
            arrays = [self.keep] + self.got

    def done(self):
        return add_parts([self.keep] + self.got, 1, jnp.float32)[0][0]


F32 = jnp.float32
BF16 = jnp.bfloat16
LANES = 128
HALO = 16
STATE_ROWS = NS + 16
LEFT = 1024
SLOTS = 2
CONV_WIDTH = DI + 2 * NS
VMEM_LIMIT = 48 * 2**20


def dot_nn(a, b):
    return jnp.dot(a, b, preferred_element_type=F32)


def dot_nt(a, b):
    return lax.dot_general(a, b, (((1,), (1,)), ((), ())), preferred_element_type=F32)


def dot_tn(a, b):
    return lax.dot_general(a, b, (((0,), (0,)), ((), ())), preferred_element_type=F32)


def split_two(v):
    high = v.astype(BF16)
    return high, (v - high.astype(F32)).astype(BF16)


def sum_heads(v, spread):
    high, low = split_two(v)
    return dot_nt(high, spread) + dot_nt(low, spread)


def tile_of(i):
    return slice(i * LANES, (i + 1) * LANES)


def two_heads(v, i):
    rows = v.shape[0]
    lane = lax.broadcasted_iota(jnp.int32, (rows, LANES), 1)
    left = jnp.broadcast_to(v[:, 2 * i : 2 * i + 1], (rows, LANES))
    right = jnp.broadcast_to(v[:, 2 * i + 1 : 2 * i + 2], (rows, LANES))
    return jnp.where(lane < P_SIZE, left, right)


def all_heads(v):
    v = jnp.broadcast_to(v, (16, LANES))
    return jnp.concatenate([two_heads(v, i) for i in range(DI // LANES)], 1)


def triangle(size, lower):
    rows = lax.broadcasted_iota(jnp.int32, (size, size), 0)
    cols = lax.broadcasted_iota(jnp.int32, (size, size), 1)
    return jnp.where(rows >= cols if lower else rows <= cols, 1.0, 0.0).astype(BF16)


def exact_sum(ones, v):
    high = v.astype(BF16)
    rest = v - high.astype(F32)
    mid = rest.astype(BF16)
    low = (rest - mid.astype(F32)).astype(BF16)
    return dot_nn(ones, high) + (dot_nn(ones, mid) + dot_nn(ones, low))


def soft_plus(z):
    return jnp.maximum(z, 0.0) + jnp.log1p(jnp.exp(-jnp.abs(z)))


def sigmoid(v):
    return 0.5 * jnp.tanh(0.5 * v) + 0.5


def conv_tile(left_ref, right_ref, i):
    tiles = LEFT // LANES
    if i < tiles:
        return left_ref[0, :, tile_of(i)].astype(F32)
    return right_ref[0, :, tile_of(i - tiles)].astype(BF16).astype(F32)


def raw_tile(right_ref):
    return right_ref[0, :, CONV_WIDTH - LEFT : CONV_WIDTH - LEFT + LANES]


def mix_begin_kernel(
    left_ref, right_ref, halo_ref, cols_ref, heads_ref, conv_ref,
    xbc_ref, slope_ref, xd_ref, step_ref, cum_ref, msg_ref,
):
    rows = left_ref.shape[1]
    masks = cols_ref[0]
    step = soft_plus(raw_tile(right_ref) + heads_ref[0:1])
    cum = exact_sum(triangle(rows, True), step * heads_ref[1:2])
    step_ref[0] = step
    cum_ref[0] = cum
    last = cum[rows - 1 : rows]
    ends = jnp.exp(last - cum) * masks[:, 3:4]
    msg_ref[0, NS:STATE_ROWS, :] = all_heads(jnp.exp(last)).astype(BF16)
    wide = [jnp.broadcast_to(masks[:, k : k + 1], (rows, LANES)) for k in range(KC - 1)]

    def conv(i):
        lanes = tile_of(i)
        own = conv_tile(left_ref, right_ref, i)
        ext = jnp.concatenate([halo_ref[0, :, lanes].astype(F32), own], 0)
        taps = conv_ref[:, lanes]
        total = taps[4:5] + taps[3:4] * own
        for k in range(KC - 1):
            at = HALO - (KC - 1) + k
            total = total + taps[k : k + 1] * (ext[at : at + rows] * wide[k])
        sig = sigmoid(total)
        x = total * sig
        slope_ref[0, :, lanes] = (sig + x * (1.0 - sig)).astype(BF16)
        low = x.astype(BF16)
        xbc_ref[0, :, lanes] = low
        return x, low

    tiles = DI // LANES
    b_turned = conv(tiles)[1].T
    conv(tiles + 1)
    for i in range(tiles):
        xd = conv(i)[0] * two_heads(step, i)
        xd_ref[0, :, tile_of(i)] = xd.astype(BF16)
        weighted = (xd * two_heads(ends, i)).astype(BF16)
        msg_ref[0, 0:NS, tile_of(i)] = dot_nn(b_turned, weighted).astype(BF16)


def seq_block(*shape):
    return pl.BlockSpec((1,) + shape, lambda s: (s,) + (0,) * len(shape))


def whole_block(*shape):
    return pl.BlockSpec(shape, lambda s: (0,) * len(shape))


def call(kernel, name, seqs, ins, in_specs, outs, out_specs, scratch=(), after=()):
    n_in, n_after = len(ins), len(after)

    def run(*refs):
        kernel(*refs[:n_in], *refs[n_in + n_after :])

    ins = tuple(ins) + tuple(after)
    in_specs = list(in_specs) + [pl.BlockSpec(memory_space=pl.ANY)] * n_after
    return pl.pallas_call(
        run,
        grid=(seqs,),
        in_specs=in_specs,
        out_specs=out_specs,
        out_shape=[jax.ShapeDtypeStruct(s, d) for s, d in outs],
        scratch_shapes=list(scratch),
        compiler_params=pltpu.CompilerParams(vmem_limit_bytes=VMEM_LIMIT),
        name=name,
    )(*ins)


def mix_begin(left, right, halo, cols, heads, conv, after=()):
    seqs, rows, _ = left.shape
    width = CONV_WIDTH
    return call(
        mix_begin_kernel,
        "mix_begin",
        seqs,
        (left, right, halo, cols, heads, conv),
        [
            seq_block(rows, LEFT),
            seq_block(rows, LEFT),
            seq_block(HALO, halo.shape[2]),
            seq_block(rows, LANES),
            whole_block(8, LANES),
            whole_block(8, width),
        ],
        [
            ((seqs, rows, width), BF16),
            ((seqs, rows, width), BF16),
            ((seqs, rows, DI), BF16),
            ((seqs, rows, LANES), F32),
            ((seqs, rows, LANES), F32),
            ((seqs, STATE_ROWS, DI), BF16),
        ],
        [
            seq_block(rows, width),
            seq_block(rows, width),
            seq_block(rows, DI),
            seq_block(rows, LANES),
            seq_block(rows, LANES),
            seq_block(STATE_ROWS, DI),
        ],
        after=after,
    )


def row_parts(rows):
    if rows < 256:
        return [(0, rows, rows)]
    return [(a, a + LANES, a + LANES) for a in range(0, rows, LANES)]


def side_by_side(pair):
    lane = lax.broadcasted_iota(jnp.int32, pair.shape, 1)
    blank = jnp.zeros_like(pair)
    return jnp.where(lane < P_SIZE, pair, blank), jnp.where(lane < P_SIZE, blank, pair)


def mix_inside_kernel(xbc_ref, xd_ref, cum_ref, cols_ref, rows_ref, skip_ref, y_ref):
    rows = xbc_ref.shape[1]
    b_rows, c_rows = xbc_ref[0, :, DI : DI + NS], xbc_ref[0, :, DI + NS :]
    seg_col, seg_row = cols_ref[0, :, 5:6], rows_ref[0, 0:1, :]
    row_at = lax.broadcasted_iota(jnp.int32, (rows, rows), 0)
    col_at = lax.broadcasted_iota(jnp.int32, (rows, rows), 1)
    couple = jnp.where((seg_col == seg_row) & (row_at >= col_at), dot_nt(c_rows, b_rows), 0.0)
    cum = cum_ref[0]
    cum_rows = cum.T
    for first in range(0, H, 2):
        lanes = slice(first * P_SIZE, (first + 2) * P_SIZE)
        sides = side_by_side(xd_ref[0, :, lanes])
        for begin, end, upto in row_parts(rows):
            y = xbc_ref[0, begin:end, lanes].astype(F32) * skip_ref[0:1, lanes]
            for h, side in zip((first, first + 1), sides):
                gap = jnp.minimum(cum[begin:end, h : h + 1] - cum_rows[h : h + 1, :upto], 0.0)
                mixing = (jnp.exp(gap) * couple[begin:end, :upto]).astype(BF16)
                y = y + dot_nn(mixing, side[:upto])
            y_ref[0, begin:end, lanes] = y


def mix_inside(xbc, xd, cum, cols, rows_in, skip, after=()):
    seqs, rows, width = xbc.shape
    return call(
        mix_inside_kernel,
        "mix_inside",
        seqs,
        (xbc, xd, cum, cols, rows_in, skip),
        [
            seq_block(rows, width),
            seq_block(rows, DI),
            seq_block(rows, LANES),
            seq_block(rows, LANES),
            seq_block(8, rows),
            whole_block(8, DI),
        ],
        [((seqs, rows, DI), F32)],
        [seq_block(rows, DI)],
        after=after,
    )[0]


def mix_finish_kernel(y_ref, c_ref, prev_ref, cum_ref, cols_ref, z_ref, gain_ref, mo_ref, nm_ref, g_ref):
    rows = y_ref.shape[1]
    flow = jnp.exp(cum_ref[0]) * cols_ref[0, :, 4:5]
    c_rows = c_ref[0]
    total = jnp.zeros((rows, LANES), F32)
    for i in range(DI // LANES):
        lanes = tile_of(i)
        mo = y_ref[0, :, lanes] + dot_nn(c_rows, prev_ref[0, :, lanes]) * two_heads(flow, i)
        mo_ref[0, :, lanes] = mo
        z = z_ref[0, :, lanes]
        g = mo * (z * sigmoid(z))
        g_ref[:, lanes] = g
        total = total + g * g
    scale = lax.rsqrt(jnp.sum(total, axis=1, keepdims=True) / DI + EPSILON)
    scale = jnp.broadcast_to(scale, (rows, LANES))
    for i in range(DI // LANES):
        lanes = tile_of(i)
        nm_ref[0, :, lanes] = (g_ref[:, lanes] * scale * gain_ref[0:1, lanes]).astype(BF16)


def c_block(rows):
    return pl.BlockSpec((1, rows, NS), lambda s: (s, 0, (DI + NS) // NS))


def mix_finish(y, xbc, prev, cum, cols, z, gain, after=()):
    seqs, rows, _ = y.shape
    return call(
        mix_finish_kernel,
        "mix_finish",
        seqs,
        (y, xbc, prev, cum, cols, z, gain),
        [
            seq_block(rows, DI),
            c_block(rows),
            seq_block(NS, DI),
            seq_block(rows, LANES),
            seq_block(rows, LANES),
            seq_block(rows, DI),
            whole_block(1, DI),
        ],
        [((seqs, rows, DI), F32), ((seqs, rows, DI), BF16)],
        [seq_block(rows, DI), seq_block(rows, DI)],
        [pltpu.VMEM((rows, DI), F32)],
        after=after,
    )


def gated_back_kernel(
    dn_ref, mo_ref, z_ref, gain_ref, c_ref, cum_ref, cols_ref, dy_ref, dza_ref, dzb_ref, msg_ref, sig_ref
):
    rows = dn_ref.shape[1]
    squares = jnp.zeros((rows, LANES), F32)
    mixed = jnp.zeros((rows, LANES), F32)
    for i in range(DI // LANES):
        lanes = tile_of(i)
        z = z_ref[0, :, lanes]
        sig = sigmoid(z)
        sig_ref[:, lanes] = sig
        g = mo_ref[0, :, lanes] * (z * sig)
        squares = squares + g * g
        mixed = mixed + g * (dn_ref[0, :, lanes] * gain_ref[0:1, lanes])
    scale = lax.rsqrt(jnp.sum(squares, axis=1, keepdims=True) / DI + EPSILON)
    back = jnp.sum(mixed, axis=1, keepdims=True) / DI * scale * scale * scale
    scale = jnp.broadcast_to(scale, (rows, LANES))
    back = jnp.broadcast_to(back, (rows, LANES))
    cum = cum_ref[0]
    flow = jnp.exp(cum) * cols_ref[0, :, 4:5]
    msg_ref[0, NS:STATE_ROWS, :] = all_heads(jnp.exp(cum[rows - 1 : rows])).astype(BF16)
    c_turned = c_ref[0].T
    for i in range(DI // LANES):
        lanes = tile_of(i)
        z = z_ref[0, :, lanes]
        mo = mo_ref[0, :, lanes]
        sig = sig_ref[:, lanes]
        swish = z * sig
        g = mo * swish
        dn = dn_ref[0, :, lanes] * scale
        dg = dn * gain_ref[0:1, lanes] - g * back
        dy = (dg * swish).astype(BF16)
        dy_ref[0, :, lanes] = dy
        dz = (dg * mo * (sig + swish * (1.0 - sig))).astype(BF16)
        split = dza_ref.shape[2] // LANES
        if i < split:
            dza_ref[0, :, lanes] = dz
        else:
            dzb_ref[0, :, tile_of(i - split)] = dz
        flowed = (dy.astype(F32) * two_heads(flow, i)).astype(BF16)
        msg_ref[0, 0:NS, lanes] = dot_nn(c_turned, flowed).astype(BF16)


def gated_back(dn, mo, z, gain, xbc, cum, cols, split, after=()):
    seqs, rows, _ = dn.shape
    return call(
        gated_back_kernel,
        "gated_back",
        seqs,
        (dn, mo, z, gain, xbc, cum, cols),
        [
            seq_block(rows, DI),
            seq_block(rows, DI),
            seq_block(rows, DI),
            whole_block(1, DI),
            c_block(rows),
            seq_block(rows, LANES),
            seq_block(rows, LANES),
        ],
        [
            ((seqs, rows, DI), BF16),
            ((seqs, rows, split), BF16),
            ((seqs, rows, DI - split), BF16),
            ((seqs, STATE_ROWS, DI), BF16),
        ],
        [
            seq_block(rows, DI),
            seq_block(rows, split),
            seq_block(rows, DI - split),
            seq_block(STATE_ROWS, DI),
        ],
        [pltpu.VMEM((rows, DI), F32)],
        after=after,
    )


def inside_back_kernel(
    xbc_ref, xd_ref, cum_ref, cols_ref, rows_ref, skip_ref, spread_ref, dy_ref, mo_ref, prev_ref,
    dxd_ref, dbc_ref, sums_ref, dcouple_ref,
):
    rows = xbc_ref.shape[1]
    cum = cum_ref[0]
    flow = jnp.exp(cum) * cols_ref[0, :, 4:5]
    sums = jnp.zeros((rows, LANES), F32)
    dc = jnp.zeros((rows, NS), F32)
    for i in range(DI // LANES):
        lanes = tile_of(i)
        dy = dy_ref[0, :, lanes].astype(F32)
        plain = mo_ref[0, :, lanes] - xbc_ref[0, :, lanes].astype(F32) * skip_ref[0:1, lanes]
        sums = sums + sum_heads(dy * plain, spread_ref[:, lanes])
        dc = dc + dot_nt((dy * two_heads(flow, i)).astype(BF16), prev_ref[0, :, lanes])
    sums_ref[0] = sums
    b_rows, c_rows = xbc_ref[0, :, DI : DI + NS], xbc_ref[0, :, DI + NS :]
    seg_col, seg_row = cols_ref[0, :, 5:6], rows_ref[0, 0:1, :]
    row_at = lax.broadcasted_iota(jnp.int32, (rows, rows), 0)
    col_at = lax.broadcasted_iota(jnp.int32, (rows, rows), 1)
    keep = (seg_col == seg_row) & (row_at <= col_at)
    couple = jnp.where(keep, dot_nt(b_rows, c_rows), 0.0)
    dcouple_ref[...] = jnp.zeros_like(dcouple_ref)
    cum_rows = cum.T
    for first in range(0, H, 2):
        lanes = slice(first * P_SIZE, (first + 2) * P_SIZE)
        dy_sides = side_by_side(dy_ref[0, :, lanes])
        xd = xd_ref[0, :, lanes]
        for begin, end, _ in row_parts(rows):
            dxd, added = [], []
            for h, dy in zip((first, first + 1), dy_sides):
                decay = jnp.exp(jnp.minimum(cum_rows[h : h + 1, begin:] - cum[begin:end, h : h + 1], 0.0))
                mixing = (decay * couple[begin:end, begin:]).astype(BF16)
                dxd.append(dot_nn(mixing, dy[begin:]))
                added.append(dot_nt(xd[begin:end], dy[begin:]) * decay)
            dcouple_ref[begin:end, begin:] += added[0] + added[1]
            dxd_ref[0, begin:end, lanes] = dxd[0] + dxd[1]
    dcouple = jnp.where(keep, dcouple_ref[...], 0.0).astype(BF16)
    dbc_ref[0, :, :NS] = dot_nn(dcouple, c_rows)
    dbc_ref[0, :, NS:] = dc + dot_tn(dcouple, b_rows)


def inside_back(xbc, xd, cum, cols, rows_in, skip, spread, dy, mo, prev, after=()):
    seqs, rows, width = xbc.shape
    return call(
        inside_back_kernel,
        "inside_back",
        seqs,
        (xbc, xd, cum, cols, rows_in, skip, spread, dy, mo, prev),
        [
            seq_block(rows, width),
            seq_block(rows, DI),
            seq_block(rows, LANES),
            seq_block(rows, LANES),
            seq_block(8, rows),
            whole_block(8, DI),
            whole_block(LANES, DI),
            seq_block(rows, DI),
            seq_block(rows, DI),
            seq_block(NS, DI),
        ],
        [((seqs, rows, DI), F32), ((seqs, rows, 2 * NS), F32), ((seqs, rows, LANES), F32)],
        [seq_block(rows, DI), seq_block(rows, 2 * NS), seq_block(rows, LANES)],
        [pltpu.VMEM((rows, rows), F32)],
        after=after,
    )


def mix_end_kernel(
    left_ref, right_ref, halo_ref, xbc_ref, slope_ref, xd_ref, step_ref, cum_ref, cols_ref, heads_ref, skip_ref,
    conv_ref, spread_ref, dy_ref, dxd_ref, dbc_ref, sums_ref, later_ref, prev_ref,
    grad_ref, gconv_ref, gheads_ref, dco_ref, tops_ref,
):
    rows = xbc_ref.shape[1]
    cum = cum_ref[0]
    step = step_ref[0]
    masks = cols_ref[0]
    last = cum[rows - 1 : rows]
    ends = jnp.exp(last - cum) * masks[:, 3:4]
    b_rows = xbc_ref[0, :, DI : DI + NS]
    direct = jnp.zeros((rows, LANES), F32)
    db = dbc_ref[0, :, :NS]
    for i in range(DI // LANES):
        lanes = tile_of(i)
        x = xbc_ref[0, :, lanes].astype(F32)
        xd = xd_ref[0, :, lanes].astype(F32)
        dy = dy_ref[0, :, lanes].astype(F32)
        later = later_ref[0, :, lanes]
        to_end = two_heads(ends, i)
        from_end = dot_nn(b_rows, later) * to_end
        dxd = dxd_ref[0, :, lanes] + from_end
        dco_ref[:, lanes] = dxd * two_heads(step, i) + dy * skip_ref[0:1, lanes]
        db = db + dot_nt((xd * to_end).astype(BF16), later)
        direct = direct + sum_heads(x * dxd, spread_ref[:, lanes])
        tops_ref[:, lanes] = jnp.concatenate(
            [
                jnp.sum(xd * from_end, axis=0, keepdims=True),
                jnp.sum(dy * x, axis=0, keepdims=True),
                jnp.sum(later.astype(F32) * prev_ref[0, :, lanes].astype(F32), axis=0, keepdims=True),
                jnp.zeros((13, LANES), F32),
            ],
            0,
        )
    dco_ref[:, DI : DI + NS] = db
    dco_ref[:, DI + NS :] = dbc_ref[0, :, NS:]
    tops = sum_heads(tops_ref[...], spread_ref[...])
    ended, skipped, carried = tops[0:1], tops[1:2], tops[2:3]
    at = lax.broadcasted_iota(jnp.int32, (rows, LANES), 0)
    dcum = sums_ref[0] - step * direct
    dcum = dcum + jnp.where(at == rows - 1, ended + jnp.exp(last) * carried, 0.0)
    da = exact_sum(triangle(rows, False), dcum)
    rate = heads_ref[1:2]
    graw = (direct + da * rate) * sigmoid(raw_tile(right_ref) + heads_ref[0:1])
    seqs = grad_ref.shape[0] // (rows + HALO)
    seq = pl.program_id(0)
    main = pl.ds(pl.multiple_of(seq * rows, rows), rows)
    edge = pl.ds(pl.multiple_of(seqs * rows + seq * HALO, HALO), HALO)
    end = CONV_WIDTH + LANES
    grad_ref[main, CONV_WIDTH:end] = graw.astype(BF16)
    grad_ref[edge, CONV_WIDTH:end] = jnp.zeros((HALO, LANES), BF16)
    grad_ref[main, end:] = jnp.zeros((rows, grad_ref.shape[1] - end), BF16)
    grad_ref[edge, end:] = jnp.zeros((HALO, grad_ref.shape[1] - end), BF16)
    gheads_ref[0] = jnp.concatenate(
        [
            jnp.sum(graw, axis=0, keepdims=True),
            jnp.sum(da * step, axis=0, keepdims=True) * rate,
            skipped,
            jnp.zeros((5, LANES), F32),
        ],
        0,
    )
    wide = [jnp.broadcast_to(masks[:, k : k + 1], (rows, LANES)) for k in range(KC - 1)]
    blank = jnp.zeros((HALO, LANES), F32)
    for i in range(CONV_WIDTH // LANES):
        lanes = tile_of(i)
        du = dco_ref[:, lanes] * slope_ref[0, :, lanes].astype(F32)
        own = conv_tile(left_ref, right_ref, i)
        ext = jnp.concatenate([halo_ref[0, :, lanes].astype(F32), own], 0)
        taps = conv_ref[:, lanes]
        grads = []
        total = jnp.zeros((rows + HALO, LANES), F32)
        for k in range(KC):
            part = du * wide[k] if k < KC - 1 else du
            at_ext = HALO - (KC - 1) + k
            grads.append(jnp.sum(part * ext[at_ext : at_ext + rows], axis=0, keepdims=True))
            padded = jnp.concatenate([blank, part, blank], 0)
            total = total + taps[k : k + 1] * padded[KC - 1 - k : KC - 1 - k + rows + HALO]
        grad_ref[main, lanes] = total[HALO:].astype(BF16)
        grad_ref[edge, lanes] = total[:HALO].astype(BF16)
        gconv_ref[0, :, lanes] = jnp.concatenate(
            grads + [jnp.sum(du, axis=0, keepdims=True), jnp.zeros((3, LANES), F32)], 0
        )


def mix_end(
    left, right, halo, xbc, slope, xd, step, cum, cols, heads, skip, conv, spread, dy, dxd, dbc, sums, later, prev,
    after=(),
):
    seqs, rows, width = xbc.shape
    tokens = seqs * (rows + HALO)
    return call(
        mix_end_kernel,
        "mix_end",
        seqs,
        (left, right, halo, xbc, slope, xd, step, cum, cols, heads, skip, conv, spread, dy, dxd, dbc, sums, later, prev),
        [
            seq_block(rows, LEFT),
            seq_block(rows, LEFT),
            seq_block(HALO, halo.shape[2]),
            seq_block(rows, width),
            seq_block(rows, width),
            seq_block(rows, DI),
            seq_block(rows, LANES),
            seq_block(rows, LANES),
            seq_block(rows, LANES),
            whole_block(8, LANES),
            whole_block(8, DI),
            whole_block(8, width),
            whole_block(LANES, DI),
            seq_block(rows, DI),
            seq_block(rows, DI),
            seq_block(rows, 2 * NS),
            seq_block(rows, LANES),
            seq_block(NS, DI),
            seq_block(NS, DI),
        ],
        [
            ((tokens, 2 * LEFT), BF16),
            ((seqs, 8, width), F32),
            ((seqs, 8, LANES), F32),
        ],
        [
            whole_block(tokens, 2 * LEFT),
            seq_block(8, width),
            seq_block(8, LANES),
        ],
        [pltpu.VMEM((rows, width), F32), pltpu.VMEM((16, DI), F32)],
        after=after,
    )


def attend_bias(slot, rest, cols_ref, rows_ref, kv_ref, offsets):
    rows = cols_ref.shape[1]
    found = []
    for before in range(slot + 1):
        for j, offset in enumerate(offsets):
            if before == slot and offset == 0:
                row_at = lax.broadcasted_iota(jnp.int32, (rows, rows), 0)
                col_at = lax.broadcasted_iota(jnp.int32, (rows, rows), 1)
                same = cols_ref[slot, :, 5:6] == rows_ref[slot, 0:1, :]
                allowed = same & (row_at >= col_at)
            else:
                keys = kv_ref[j][before, rows : rows + 16, :rows].astype(F32)[0:1]
                if before == slot:
                    keys = keys * jnp.where((rest ^ offset) < rest, 1.0, 0.0)
                allowed = cols_ref[slot, :, 4:5] * keys > 0.5
            found.append((j, before, jnp.where(allowed, 0.0, NEGATIVE)))
    return found


def swap_halves(pair):
    return jnp.concatenate([pair[:, P_SIZE:], pair[:, :P_SIZE]], 1)


def to_side(pair, group):
    pair_sides, swapped = side_by_side(pair), side_by_side(swap_halves(pair))
    return (pair_sides[0], swapped[0]) if group == 0 else (swapped[1], pair_sides[1])


def from_side(left, right, group):
    lane = lax.broadcasted_iota(jnp.int32, left.shape, 1)
    if group == 0:
        right = swap_halves(right)
    else:
        left = swap_halves(left)
    return jnp.where(lane < P_SIZE, left, right)


def attend_kernel(offsets, rest_ref, q_ref, cols_ref, rows_ref, *refs):
    kv_ref, (out_ref, lse_ref) = refs[:-2], refs[-2:]
    rows = q_ref.shape[1]
    for slot in range(SLOTS):
        blocks = attend_bias(slot, rest_ref[0], cols_ref, rows_ref, kv_ref, offsets)
        sums = []
        for i in range(QUERY_HEADS // 2):
            lanes, group = tile_of(i), (2 * i) // (QUERY_HEADS // KEY_VALUE_HEADS)
            outs = []
            for q in to_side(q_ref[slot, :, lanes] * jnp.asarray(HEAD_WIDTH**-0.5, BF16), group):
                scores = [dot_nt(q, kv_ref[j][n, :rows, :LANES]) + bias for j, n, bias in blocks]
                top = jnp.max(functools.reduce(jnp.maximum, scores), axis=1, keepdims=True)
                weights = [jnp.exp(s - top) for s in scores]
                total = jnp.sum(functools.reduce(jnp.add, weights), axis=1, keepdims=True)
                out = [
                    dot_nn(w.astype(BF16), kv_ref[j][n, :rows, LANES:]) for (j, n, _), w in zip(blocks, weights)
                ]
                outs.append(functools.reduce(jnp.add, out) / total)
                sums.append(top + jnp.log(total))
            out_ref[slot, :, lanes] = from_side(*outs, group).astype(BF16)
        lse_ref[slot] = jnp.concatenate(sums + [jnp.zeros((rows, LANES - QUERY_HEADS), F32)], 1)


def call_whole(kernel, name, scalars, ins, outs, scratch=(), after=()):
    vmem = pl.BlockSpec(memory_space=pltpu.VMEM)
    n_in = len(scalars) + len(ins)

    def run(*refs):
        kernel(*refs[:n_in], *refs[n_in + len(after) :])

    return pl.pallas_call(
        run,
        in_specs=[pl.BlockSpec(memory_space=pltpu.SMEM)] * len(scalars) + [vmem] * len(ins) + spec_any(len(after)),
        out_specs=[vmem] * len(outs),
        out_shape=[jax.ShapeDtypeStruct(s, d) for s, d in outs],
        scratch_shapes=list(scratch),
        compiler_params=pltpu.CompilerParams(vmem_limit_bytes=VMEM_LIMIT),
        name=name,
    )(*scalars, *ins, *after)


def attend(rest, q, kv, cols, rows_in, offsets, after=()):
    outs = [(q.shape, BF16), (q.shape[:2] + (LANES,), F32)]
    return call_whole(
        functools.partial(attend_kernel, offsets), "attend", (rest,), (q, cols, rows_in, *kv), outs, after=after
    )


def attend_back_kernel(
    offsets, rest_ref, q_ref, cols_ref, rows_ref, out_ref, lse_ref, dout_ref, *refs
):
    count = len(offsets)
    kv_ref, dq_ref, dkv_ref, acc_ref = refs[:count], refs[count], refs[count + 1 : -1], refs[-1]
    rows = q_ref.shape[1]
    scale = HEAD_WIDTH**-0.5
    acc_ref[...] = jnp.zeros_like(acc_ref)
    for slot in range(SLOTS):
        blocks = attend_bias(slot, rest_ref[0], cols_ref, rows_ref, kv_ref, offsets)
        for i in range(QUERY_HEADS // 2):
            lanes, group = tile_of(i), (2 * i) // (QUERY_HEADS // KEY_VALUE_HEADS)
            q_pair = q_ref[slot, :, lanes] * jnp.asarray(scale, BF16)
            dout_pair = dout_ref[slot, :, lanes]
            q_turned, dout_turned = q_pair.T, dout_pair.T
            product = dout_pair.astype(F32) * out_ref[slot, :, lanes].astype(F32)
            q_sides, dout_sides = to_side(q_pair, group), to_side(dout_pair, group)
            k_rows = slice(group * HEAD_WIDTH, (group + 1) * HEAD_WIDTH)
            v_rows = slice(LANES + group * HEAD_WIDTH, LANES + (group + 1) * HEAD_WIDTH)
            dqs = []
            for n in range(2):
                own = slice(n * HEAD_WIDTH, (n + 1) * HEAD_WIDTH)
                q, dout = q_sides[n], dout_sides[n]
                delta = jnp.sum(side_by_side(product)[n], axis=1, keepdims=True)
                lse = lse_ref[slot, :, 2 * i + n : 2 * i + n + 1]
                dq = None
                for j, before, bias in blocks:
                    k, v = kv_ref[j][before, :rows, :LANES], kv_ref[j][before, :rows, LANES:]
                    p = jnp.exp(dot_nt(q, k) + bias - lse)
                    ds = (p * (dot_nt(dout, v) - delta)).astype(BF16)
                    part = dot_nn(ds, k)
                    dq = part if dq is None else dq + part
                    acc_ref[j, before, k_rows, :] += dot_nn(q_turned[own], ds)
                    acc_ref[j, before, v_rows, :] += dot_nn(dout_turned[own], p.astype(BF16))
                dqs.append(dq * scale)
            dq_ref[slot, :, lanes] = from_side(*dqs, group).astype(BF16)
    for j in range(len(offsets)):
        for before in range(SLOTS):
            dkv_ref[j][before] = acc_ref[j, before].T.astype(BF16)


def attend_back(rest, q, kv, cols, rows_in, out, lse, dout, offsets, after=()):
    rows, blocks, (slots, _, kv_width) = q.shape[1], len(kv), kv[0].shape
    found = call_whole(
        functools.partial(attend_back_kernel, offsets),
        "attend_back",
        (rest,),
        (q, cols, rows_in, out, lse, dout, *kv),
        [(q.shape, BF16)] + [((slots, rows, kv_width), BF16)] * blocks,
        [pltpu.VMEM((blocks, slots, kv_width, rows), F32)],
        after=after,
    )
    return found[0], found[1:]


def pick_offset(rest, number, group, offsets, pieces, slot):
    wanted = (number % group) ^ rest
    found = None
    for offset, piece in zip(offsets, pieces):
        part = piece[slot].astype(F32)
        found = part if found is None else jnp.where(wanted == offset, part, found)
    return found


def halo_kernel(offsets, rest_ref, *refs):
    pieces, out_ref = refs[:-1], refs[-1]
    rest, group = rest_ref[0], len(pieces)
    for slot in range(SLOTS):
        found = jnp.zeros(out_ref.shape[1:], F32)
        for number in range(group * slot, group * (slot + 1)):
            if number > 0:
                before = number - 1
                part = pick_offset(rest, before, group, offsets, pieces, before // group)
                found = jnp.where(rest == number % group, part, found)
        out_ref[slot] = found.astype(out_ref.dtype)


def take_halo(rest, pieces, offsets):
    return call_whole(
        functools.partial(halo_kernel, offsets), "halo", (rest,), pieces, [(pieces[0].shape, pieces[0].dtype)]
    )[0]


def scan_kernel(offsets, from_earlier, rest_ref, *refs):
    pieces, out_ref = refs[:-1], refs[-1]
    rest, group = rest_ref[0], len(pieces)
    order = list(range(SLOTS * group))
    width = 4 * LANES

    def column(i, _):
        lanes = pl.ds(pl.multiple_of(i * width, width), width)
        state = jnp.zeros((NS, width), F32)
        found = [state] * SLOTS
        for number in order if from_earlier else order[::-1]:
            slot = number // group
            found[slot] = jnp.where(rest == number % group, state, found[slot])
            part = pick_offset(rest, number, group, offsets, [p.at[:, :, lanes] for p in pieces], slot)
            state = part[:NS] + part[NS : NS + 1] * state
        for slot in range(SLOTS):
            out_ref[slot, :, lanes] = found[slot].astype(BF16)
        return 0

    lax.fori_loop(0, DI // width, column, 0)


def scan_states(rest, pieces, offsets, from_earlier, after=()):
    return call_whole(
        functools.partial(scan_kernel, offsets, from_earlier),
        "scan_states",
        (rest,),
        pieces,
        [((SLOTS, NS, DI), BF16)],
        after=after,
    )[0]


def join_grads_kernel(zb_ref, q_ref, own_ref, got_ref, out_ref):
    slots, rows, width = own_ref.shape
    at = zb_ref.shape[1] + q_ref.shape[1]
    out_ref[:, : zb_ref.shape[1]] = zb_ref[...]
    out_ref[:, zb_ref.shape[1] : at] = q_ref[...]
    for s in range(slots):
        total = own_ref[s].astype(F32) + got_ref[s].astype(F32)
        out_ref[s * rows : (s + 1) * rows, at:] = total.astype(BF16)


def join_grads(zb, q, own, got, after=()):
    tokens = zb.shape[0]
    width = zb.shape[1] + q.shape[1] + own.shape[2]
    return call_whole(
        join_grads_kernel, "join_grads", (), (zb, q, own, got), [((tokens, width), BF16)], after=after
    )[0]


def line_place(j, count, r):
    stride = LANES // -(-count // r)
    return j % r, stride * (j // r)


def pack_lines(rows_of, r):
    count = len(rows_of)
    stride = LANES // -(-count // r)
    groups = []
    for begin in range(0, count, r):
        part = [
            jnp.concatenate([v, jnp.zeros((1, stride - v.shape[1]), F32)], 1) for v in rows_of[begin : begin + r]
        ]
        if len(part) < r:
            part.append(jnp.zeros((r - len(part), stride), F32))
        groups.append(jnp.concatenate(part, 0))
    tile = jnp.concatenate(groups, 1) if len(groups) > 1 else groups[0]
    if tile.shape[1] < LANES:
        tile = jnp.concatenate([tile, jnp.zeros((r, LANES - tile.shape[1]), F32)], 1)
    return tile


def pack_first_kernel(xbc_ref, step_ref, conv_ref, bias_ref, mix_ref, one_ref, two_ref, out_ref):
    r = xbc_ref.shape[0]
    over = CONV_WIDTH - LEFT
    out_ref[0] = xbc_ref[:, :LEFT]
    out_ref[1, :, :over] = xbc_ref[:, LEFT:]
    blank = jnp.zeros((r, LANES - H), BF16)
    out_ref[1, :, over : over + LANES] = jnp.concatenate([step_ref[...], blank], 1)
    taps = conv_ref[...].astype(F32)
    vectors = [taps[k : k + 1] for k in range(KC)]
    vectors += [ref[...].astype(F32) for ref in (bias_ref, mix_ref, one_ref, two_ref)]
    out_ref[1, :, over + LANES :] = pack_lines(vectors, r).astype(BF16)


def pack_first(w_xbc, w_step, conv_weight, conv_bias, mixer_gain, norm1_gain, norm2_gain):
    r = w_xbc.shape[0]
    vmem = pl.BlockSpec(memory_space=pltpu.VMEM)
    return pl.pallas_call(
        pack_first_kernel,
        in_specs=[vmem] * 7,
        out_specs=vmem,
        out_shape=jax.ShapeDtypeStruct((2, r, LEFT), BF16),
        name="pack_first",
    )(w_xbc, w_step, conv_weight, conv_bias[None], mixer_gain[None], norm1_gain[None], norm2_gain[None])


def pack_two_kernel(z_ref, query_ref, kv_ref, two_ref):
    width = two_ref.shape[2]
    two_ref[0] = z_ref[:, :width]
    two_ref[1, :, : DI - width] = z_ref[:, width:]
    at = DI - width + query_ref.shape[1]
    two_ref[1, :, DI - width : at] = query_ref[...]
    two_ref[1, :, at:] = kv_ref[...]


def pack_two(w_gate_z, w_query, key_value_weight, after=()):
    width = (DI + w_query.shape[1] + key_value_weight.shape[1]) // 2
    ins = (w_gate_z, w_query, key_value_weight)
    return call_whole(pack_two_kernel, "pack_two", (), ins, [((2, w_gate_z.shape[0], width), BF16)], after=after)[0]


def pack_units_kernel(gate_up_ref, down_ref, units_ref):
    r, half = gate_up_ref.shape[0], down_ref.shape[0] // 2
    for n in range(2):
        for q in range(2):
            column = (2 * n + q) * MODEL_WIDTH
            units_ref[n, q * r : (q + 1) * r] = gate_up_ref[:, column : column + MODEL_WIDTH]
        units_ref[n, 2 * r :] = down_ref[n * half : (n + 1) * half]


def pack_units(w_gate_up, w_down, after=()):
    shape = (2, 2 * w_gate_up.shape[0] + w_down.shape[0] // 2, MODEL_WIDTH)
    return call_whole(pack_units_kernel, "pack_units", (), (w_gate_up, w_down), [(shape, BF16)], after=after)[0]


def pack_out_kernel(mix_ref, attn_ref, out_ref):
    out_ref[0, : mix_ref.shape[0]] = mix_ref[...]
    out_ref[0, mix_ref.shape[0] :] = attn_ref[...]


def pack_out(w_mix_out, w_attn_out, after=()):
    shape = (1, w_mix_out.shape[0] + w_attn_out.shape[0], MODEL_WIDTH)
    return call_whole(pack_out_kernel, "pack_out", (), (w_mix_out, w_attn_out), [(shape, BF16)], after=after)[0]


def unpack_small_kernel(r, small_ref, conv_ref, mix_ref, gain_ref):
    count = small_ref.shape[0] // r
    widths = [CONV_WIDTH // count] * (KC + 1) + [DI // count] + [MODEL_WIDTH // count] * 2
    found = [[] for _ in widths]
    for i in range(count):
        tile = small_ref[i * r : (i + 1) * r, :].astype(F32)
        for j, width in enumerate(widths):
            row, lane = line_place(j, len(widths), r)
            found[j].append(tile[row : row + 1, lane : lane + width])
    found = [jnp.concatenate(v, 1) for v in found]
    conv_ref[...] = jnp.concatenate(found[: KC + 1] + [jnp.zeros((3, CONV_WIDTH), F32)], 0)
    mix_ref[...] = found[KC + 1]
    gain_ref[...] = jnp.concatenate(found[KC + 2 :], 0)


def unpack_small(small, r):
    vmem = pl.BlockSpec(memory_space=pltpu.VMEM)
    return pl.pallas_call(
        functools.partial(unpack_small_kernel, r),
        in_specs=[vmem],
        out_specs=[vmem] * 3,
        out_shape=[jax.ShapeDtypeStruct(s, F32) for s in ((8, CONV_WIDTH), (1, DI), (2, MODEL_WIDTH))],
        name="unpack_small",
    )(small)


def small_grads_kernel(r, offsets, place_ref, conv_ref, heads_ref, keep_ref, send_ref, tile_ref):
    count = tile_ref.shape[0]
    conv = jnp.sum(conv_ref[...], 0)
    heads = jnp.sum(heads_ref[...], 0)
    width = CONV_WIDTH // count
    shared = [heads[k : k + 1, :H] for k in range(3)]
    for i in range(count):
        own = [conv[k : k + 1, i * width : (i + 1) * width] for k in range(KC + 1)]
        tile_ref[i] = pack_lines(own + shared, r)
    place = place_ref[0]
    for t, offset in enumerate(offsets):
        keep_ref[t * r : (t + 1) * r] = tile_ref[place ^ offset].astype(BF16)
        send_ref[t * r : (t + 1) * r] = tile_ref[place ^ (offset ^ 1)].astype(BF16)


def small_grads(r, conv, heads):
    bits = bit_count()
    count = 1 << bits
    vmem = pl.BlockSpec(memory_space=pltpu.VMEM)
    return pl.pallas_call(
        functools.partial(small_grads_kernel, r, turned_offsets(bits)),
        in_specs=[pl.BlockSpec(memory_space=pltpu.SMEM)] + [vmem] * 2,
        out_specs=[vmem] * 2,
        out_shape=[jax.ShapeDtypeStruct((count // 2 * r, LANES), BF16)] * 2,
        scratch_shapes=[pltpu.VMEM((count, r, LANES), F32)],
        name="small_grads",
    )(place_of().reshape(1).astype(jnp.int32), conv, heads)


def tiles_spec(shape, axis, width):
    block = tuple(width if n == axis else size for n, size in enumerate(shape))
    return pl.BlockSpec(block, lambda i: tuple(i if n == axis else 0 for n in range(len(shape))))


def fixed(*shape):
    return pl.BlockSpec(shape, lambda i: (0,) * len(shape))


def dense(kernel, name, steps, ins, in_specs, outs, out_specs, scratch=(), after=()):
    n_in, n_after = len(ins), len(after)

    def run(*refs):
        kernel(*refs[:n_in], *refs[n_in + n_after :])

    return pl.pallas_call(
        run,
        grid=(steps,),
        in_specs=list(in_specs) + spec_any(n_after),
        out_specs=out_specs,
        out_shape=[jax.ShapeDtypeStruct(s, d) for s, d in outs],
        scratch_shapes=list(scratch),
        compiler_params=pltpu.CompilerParams(vmem_limit_bytes=VMEM_LIMIT),
        name=name,
    )(*ins, *after)


def row_scale(values):
    return lax.rsqrt(jnp.mean(values * values, axis=1, keepdims=True) + EPSILON)


def first_proj_kernel(x_ref, gain_ref, left_w, right_w, cols_ref, normed_ref, left_ref, right_ref, tails_ref):
    step, tile = pl.program_id(0), left_w.shape[1]

    @pl.when(step == 0)
    def _():
        x = x_ref[...].astype(F32)
        normed_ref[...] = (x * row_scale(x) * gain_ref[...]).astype(BF16)

    left = dot_nn(normed_ref[...], left_w[...]).astype(BF16)
    right = dot_nn(normed_ref[...], right_w[...])
    left_ref[...] = left
    right_ref[...] = right
    slots, rows, _ = cols_ref.shape
    lanes = pl.ds(pl.multiple_of(step * tile, tile), tile)
    for s in range(slots):
        begin, end = (s + 1) * rows - HALO, (s + 1) * rows
        edge = cols_ref[s, rows - HALO :, 3:4]
        tails_ref[s, :, lanes] = (left[begin:end].astype(F32) * edge).astype(BF16)
        normed = normed_ref[begin:end, lanes].astype(F32)
        tails_ref[s, :, pl.ds(pl.multiple_of(CONV_WIDTH + step * tile, tile), tile)] = (normed * edge).astype(BF16)

        @pl.when(step < (CONV_WIDTH - LEFT) // tile)
        def _():
            at = pl.ds(pl.multiple_of(LEFT + step * tile, tile), tile)
            tails_ref[s, :, at] = (right[begin:end].astype(BF16).astype(F32) * edge).astype(BF16)


def first_proj(x, gain, left_full, right_full, cols, after=()):
    tokens, width = x.shape
    tile = LEFT // 4
    tails = (cols.shape[0], HALO, CONV_WIDTH + width)
    return dense(
        first_proj_kernel,
        "first_proj",
        4,
        (x, gain, left_full, right_full, cols),
        [
            fixed(tokens, width),
            fixed(1, width),
            tiles_spec((width, LEFT), 1, tile),
            tiles_spec((width, LEFT), 1, tile),
            fixed(*cols.shape),
        ],
        [((tokens, width), BF16), ((tokens, LEFT), BF16), ((tokens, LEFT), F32), (tails, BF16)],
        [
            fixed(tokens, width),
            tiles_spec((tokens, LEFT), 1, tile),
            tiles_spec((tokens, LEFT), 1, tile),
            fixed(*tails),
        ],
        after=after,
    )


def second_proj_kernel(normed_ref, z_w, qkv_w, rows_ref, z_ref, q_ref, kv_ref):
    step = pl.program_id(0)
    z_ref[...] = dot_nn(normed_ref[...], z_w[...])
    part = dot_nn(normed_ref[...], qkv_w[...]).astype(BF16)
    slots, extended, width = kv_ref.shape
    rows = extended - 16

    @pl.when(step < 2)
    def _():
        q_ref[...] = part

    @pl.when(step == 2)
    def _():
        for s in range(slots):
            kv_ref[s, :rows] = part[s * rows : (s + 1) * rows]
            keys = jnp.broadcast_to(rows_ref[s, 1:2], (16, rows))
            if rows < width:
                keys = jnp.concatenate([keys, jnp.zeros((16, width - rows), F32)], 1)
            kv_ref[s, rows:] = keys.astype(BF16)


def second_proj(normed, z_full, qkv_full, rows_in, after=()):
    tokens, width = normed.shape
    slots, _, rows = rows_in.shape
    query, kv = QUERY_HEADS * HEAD_WIDTH, 2 * KEY_VALUE_HEADS * HEAD_WIDTH
    return dense(
        second_proj_kernel,
        "second_proj",
        3,
        (normed, z_full, qkv_full, rows_in),
        [
            fixed(tokens, width),
            tiles_spec((width, DI), 1, DI // 3),
            tiles_spec((width, query + kv), 1, kv),
            fixed(slots, 8, rows),
        ],
        [((tokens, DI), F32), ((tokens, query), BF16), ((slots, rows + 16, kv), BF16)],
        [
            tiles_spec((tokens, DI), 1, DI // 3),
            pl.BlockSpec((tokens, kv), lambda i: (0, jnp.minimum(i, 1))),
            fixed(slots, rows + 16, kv),
        ],
        after=after,
    )


def out_proj_kernel(x_ref, nm_ref, attn_ref, mix_w, attn_w, gain_ref, resid_ref, normed_ref):
    step = pl.program_id(0)
    part = dot_nn(nm_ref[...], mix_w[...]) + dot_nn(attn_ref[...], attn_w[...])

    @pl.when(step == 0)
    def _():
        resid_ref[...] = x_ref[...].astype(F32) + part

    @pl.when(step > 0)
    def _():
        resid_ref[...] += part

    @pl.when(step == pl.num_programs(0) - 1)
    def _():
        resid = resid_ref[...]
        normed_ref[...] = (resid * row_scale(resid) * gain_ref[...]).astype(BF16)


def out_proj(x, nm, attn, mix_full, attn_full, gain, after=()):
    tokens, width = x.shape
    query = attn.shape[1]
    steps = 4
    return dense(
        out_proj_kernel,
        "out_proj",
        steps,
        (x, nm, attn, mix_full, attn_full, gain),
        [
            fixed(tokens, width),
            tiles_spec(nm.shape, 1, DI // steps),
            tiles_spec(attn.shape, 1, query // steps),
            tiles_spec(mix_full.shape, 0, DI // steps),
            tiles_spec(attn_full.shape, 0, query // steps),
            fixed(1, width),
        ],
        [((tokens, width), F32), ((tokens, width), BF16)],
        [fixed(tokens, width), fixed(tokens, width)],
        after=after,
    )


def gate_up_kernel(normed_ref, gate_w, up_w, act_ref, swish_ref, slope_ref):
    gate = dot_nn(normed_ref[...], gate_w[...])
    up = dot_nn(normed_ref[...], up_w[...])
    sig = sigmoid(gate)
    swish = gate * sig
    act_ref[...] = (swish * up).astype(BF16)
    swish_ref[...] = swish.astype(BF16)
    slope_ref[...] = ((sig + swish * (1.0 - sig)) * up).astype(BF16)


def gate_up(normed, gate_full, up_full, after=()):
    tokens, width = normed.shape
    tile = FF // 4
    spec = tiles_spec((tokens, FF), 1, tile)
    return dense(
        gate_up_kernel,
        "gate_up",
        4,
        (normed, gate_full, up_full),
        [fixed(tokens, width), tiles_spec((width, FF), 1, tile), tiles_spec((width, FF), 1, tile)],
        [((tokens, FF), BF16)] * 3,
        [spec] * 3,
        after=after,
    )


def down_kernel(act_ref, swish_ref, slope_ref, down_w, resid_ref, grad_ref, out_ref, dgate_ref, dup_ref, total_ref):
    step = pl.program_id(0)
    weights = down_w[...]
    part = dot_nn(act_ref[...], weights)

    @pl.when(step == 0)
    def _():
        total_ref[...] = resid_ref[...] + part

    @pl.when(step > 0)
    def _():
        total_ref[...] += part

    @pl.when(step == pl.num_programs(0) - 1)
    def _():
        out_ref[...] = total_ref[...].astype(BF16)

    dact = dot_nt(grad_ref[...], weights)
    dgate_ref[...] = (dact * slope_ref[...].astype(F32)).astype(BF16)
    dup_ref[...] = (dact * swish_ref[...].astype(F32)).astype(BF16)


def down(act, swish, slope, down_full, resid, grad_out, after=()):
    tokens, width = resid.shape
    tile = FF // 4
    spec = tiles_spec((tokens, FF), 1, tile)
    return dense(
        down_kernel,
        "down",
        4,
        (act, swish, slope, down_full, resid, grad_out),
        [spec, spec, spec, tiles_spec((FF, width), 0, tile), fixed(tokens, width), fixed(tokens, width)],
        [((tokens, width), BF16), ((tokens, FF), BF16), ((tokens, FF), BF16)],
        [fixed(tokens, width), spec, spec],
        [pltpu.VMEM((tokens, width), F32)],
        after=after,
    )


def gate_up_back_kernel(
    dgate_ref, dup_ref, gate_w, up_w, resid_ref, gain_ref, grad_ref, back_ref, branch_ref, total_ref
):
    step = pl.program_id(0)
    part = dot_nt(dgate_ref[...], gate_w[...]) + dot_nt(dup_ref[...], up_w[...])

    @pl.when(step == 0)
    def _():
        total_ref[...] = part

    @pl.when(step > 0)
    def _():
        total_ref[...] += part

    @pl.when(step == pl.num_programs(0) - 1)
    def _():
        resid = resid_ref[...]
        scale = row_scale(resid)
        scaled = resid * scale
        dnormed = total_ref[...]
        dscaled = dnormed * gain_ref[...]
        mean = jnp.mean(dscaled * scaled, axis=1, keepdims=True)
        back = grad_ref[...].astype(F32) + (dscaled - scaled * mean) * scale
        back_ref[...] = back
        branch_ref[...] = back.astype(BF16)


def gate_up_back(dgate, dup, gate_full, up_full, resid, gain, grad_out, after=()):
    tokens, width = resid.shape
    tile = FF // 4
    spec, w_spec, whole = tiles_spec((tokens, FF), 1, tile), tiles_spec((width, FF), 1, tile), fixed(tokens, width)
    return dense(
        gate_up_back_kernel,
        "gate_up_back",
        4,
        (dgate, dup, gate_full, up_full, resid, gain, grad_out),
        [spec, spec, w_spec, w_spec, whole, fixed(1, width), whole],
        [((tokens, width), F32), ((tokens, width), BF16)],
        [whole, whole],
        [pltpu.VMEM((tokens, width), F32)],
        after=after,
    )


def out_back_kernel(branch_ref, mix_w, attn_w, dnm_ref, dattn_ref):
    dnm_ref[...] = dot_nt(branch_ref[...], mix_w[...])
    dattn_ref[...] = dot_nt(branch_ref[...], attn_w[...]).astype(BF16)


def out_back(branch, mix_full, attn_full, after=()):
    tokens, width = branch.shape
    query = attn_full.shape[0]
    steps = 4
    return dense(
        out_back_kernel,
        "out_back",
        steps,
        (branch, mix_full, attn_full),
        [
            fixed(tokens, width),
            tiles_spec(mix_full.shape, 0, DI // steps),
            tiles_spec(attn_full.shape, 0, query // steps),
        ],
        [((tokens, DI), F32), ((tokens, query), BF16)],
        [tiles_spec((tokens, DI), 1, DI // steps), tiles_spec((tokens, query), 1, query // steps)],
        after=after,
    )


def second_back_kernel(za_ref, zq_ref, z_w, qkv_w, out_ref):
    split = za_ref.shape[1]
    rest = DI - split
    out_ref[...] = (
        dot_nt(za_ref[...], z_w[:, :split])
        + dot_nt(zq_ref[:, :rest], z_w[:, split:])
        + dot_nt(zq_ref[:, rest:], qkv_w[...])
    )


def second_back(za, zq, z_full, qkv_full, after=()):
    tokens, width = za.shape[0], z_full.shape[0]
    tile = width // 4
    return dense(
        second_back_kernel,
        "second_back",
        4,
        (za, zq, z_full, qkv_full),
        [fixed(*za.shape), fixed(*zq.shape), tiles_spec(z_full.shape, 0, tile), tiles_spec(qkv_full.shape, 0, tile)],
        [((tokens, width), F32)],
        [tiles_spec((tokens, width), 1, tile)],
        after=after,
    )[0]


def first_back_kernel(grad_ref, left_w, right_w, part_ref, out_ref, edge_ref):
    tokens = part_ref.shape[0]
    total = dot_nt(grad_ref[:, :LEFT], left_w[...]) + dot_nt(grad_ref[:, LEFT:], right_w[...])
    out_ref[...] = total[:tokens] + part_ref[...]
    edge_ref[...] = total[tokens:]


def first_back(grad, left_full, right_full, part, after=()):
    tokens, width = part.shape
    ext = grad.shape[0]
    tile = width // 4
    w_spec = tiles_spec((width, LEFT), 0, tile)
    return dense(
        first_back_kernel,
        "first_back",
        4,
        (grad, left_full, right_full, part),
        [fixed(*grad.shape), w_spec, w_spec, tiles_spec((tokens, width), 1, tile)],
        [((tokens, width), F32), ((ext - tokens, width), F32)],
        [tiles_spec((tokens, width), 1, tile), tiles_spec((ext - tokens, width), 1, tile)],
        after=after,
    )


def input_back_kernel(gn_ref, next_ref, x_ref, gain_ref, resid_ref, out_ref, low_ref):
    rows = gn_ref.shape[0]
    x = x_ref[...].astype(F32)
    scale = row_scale(x)
    scaled = x * scale
    tail = gn_ref[rows - HALO :] + next_ref[0]
    dscaled = jnp.concatenate([gn_ref[: rows - HALO], tail], 0) * gain_ref[...]
    mean = jnp.mean(dscaled * scaled, axis=1, keepdims=True)
    total = resid_ref[...] + (dscaled - scaled * mean) * scale
    out_ref[0] = total
    low_ref[0] = total.astype(BF16)


def input_back(gn, from_next, x, gain, resid, after=()):
    slots = from_next.shape[0]
    rows, width = gn.shape[0] // slots, gn.shape[1]
    spec = pl.BlockSpec((rows, width), lambda s: (s, 0))
    return dense(
        input_back_kernel,
        "input_back",
        slots,
        (gn, from_next, x, gain, resid),
        [spec, seq_block(HALO, width), spec, fixed(1, width), spec],
        [((slots, rows, width), F32), ((slots, rows, width), BF16)],
        [seq_block(rows, width)] * 2,
        after=after,
    )


def pick_kernel(index_ref, block_ref, out_ref):
    out_ref[...] = block_ref[0]


def pick(block, index, after=()):
    n_after = len(after)

    def run(index_ref, block_ref, *refs):
        pick_kernel(index_ref, block_ref, refs[n_after])

    return pl.pallas_call(
        run,
        grid_spec=pltpu.PrefetchScalarGridSpec(
            num_scalar_prefetch=1,
            grid=(1,),
            in_specs=[pl.BlockSpec((1,) + block.shape[1:], lambda i, index: (index[0], 0, 0))] + spec_any(n_after),
            out_specs=pl.BlockSpec(block.shape[1:], lambda i, index: (0, 0)),
        ),
        out_shape=jax.ShapeDtypeStruct(block.shape[1:], block.dtype),
        name="pick",
    )(index.reshape(1).astype(jnp.int32), block, *after)


def merge_kernel(side_ref, block_ref, got_ref, out_ref):
    keep = pl.program_id(0) == side_ref[0]

    @pl.when(keep)
    def _():
        out_ref[0] = block_ref[0]

    @pl.when(jnp.logical_not(keep))
    def _():
        out_ref[0] = got_ref[...]


def merge(block, got, side, after=()):
    slots, rows, width = block.shape
    n_after = len(after)

    def run(side_ref, block_ref, got_ref, *refs):
        merge_kernel(side_ref, block_ref, got_ref, refs[n_after])

    return pl.pallas_call(
        run,
        grid=(slots,),
        in_specs=[
            pl.BlockSpec(memory_space=pltpu.SMEM),
            seq_block(rows, width),
            pl.BlockSpec((rows, width), lambda s: (0, 0)),
        ]
        + spec_any(n_after),
        out_specs=seq_block(rows, width),
        out_shape=jax.ShapeDtypeStruct(block.shape, block.dtype),
        name="merge",
    )(side.reshape(1).astype(jnp.int32), block, got, *after)


def fsdp_bits():
    return lax.axis_size("fsdp").bit_length() - 1


def fsdp_exchange(block, bit):
    return lax.ppermute(block, "fsdp", [(i, i ^ (1 << bit)) for i in range(lax.axis_size("fsdp"))])


def side_of():
    return lax.axis_index("fsdp") >> (fsdp_bits() - 1)


def swap_start(block):
    return fsdp_exchange(lax.dynamic_index_in_dim(block, 1 - side_of(), 0, False), fsdp_bits() - 1)


def swap_end(block, got):
    return lax.dynamic_update_index_in_dim(block, got.astype(block.dtype), 1 - side_of(), 0)


def gather_sequence(block):
    pieces, offsets = [block], [0]
    for bit in range(fsdp_bits() - 1):
        pieces = pieces + [fsdp_exchange(a, bit) for a in pieces]
        offsets = offsets + [o ^ (1 << bit) for o in offsets]
    return pieces, tuple(offsets)


def sum_sequence(blocks):
    blocks = list(blocks)
    for bit in range(fsdp_bits() - 2, -1, -1):
        half = len(blocks) // 2
        got = [fsdp_exchange(a, bit) for a in blocks[half:]]
        if half > 1:
            blocks = [(a.astype(F32) + b.astype(F32)).astype(BF16) for a, b in zip(blocks, got)]
        else:
            blocks = [blocks[0], got[0]]
    return blocks


def rest_place():
    return lax.axis_index("fsdp") & (lax.axis_size("fsdp") // 2 - 1)


def from_next_part(block):
    pieces, offsets = gather_sequence(block)
    group, rest = len(pieces), rest_place()
    found = [jnp.zeros(block.shape[1:], block.dtype)] * SLOTS
    for number in range(SLOTS * group - 1):
        slot, after = number // group, number + 1
        for offset, piece in zip(offsets, pieces):
            match = (rest == number % group) & ((after % group) ^ rest == offset)
            found[slot] = jnp.where(match, piece[after // group], found[slot])
    return jnp.stack(found)


def sequence_masks(segs):
    slots, rows = segs.shape
    behind = (lax.iota(jnp.int32, slots)[:, None] > 0) | (rest_place() > 0)
    first = (segs == segs[:, :1]) & behind
    keep_end = segs == segs[:, -1:]
    columns = []
    for k in range(KC - 1):
        back = KC - 1 - k
        inside = segs[:, back:] == segs[:, : rows - back]
        columns.append(jnp.concatenate([first[:, :back], inside], 1).astype(F32))
    columns += [keep_end.astype(F32), first.astype(F32), segs.astype(F32)]
    cols = jnp.stack(columns, 2)
    cols = jnp.pad(cols, ((0, 0), (0, 0), (0, LANES - cols.shape[2])))
    rows_in = jnp.pad(jnp.stack([segs, keep_end.astype(segs.dtype)], 1).astype(F32), ((0, 0), (0, 6), (0, 0)))
    return cols, rows_in, keep_end


def per_device(
    hidden_in,
    segment_ids,
    norm1_gain,
    w_gate_z,
    w_xbc,
    w_step,
    conv_weight,
    conv_bias,
    step_bias,
    decay_log,
    skip_gain,
    mixer_gain,
    w_mix_out,
    w_query,
    key_value_weight,
    w_attn_out,
    norm2_gain,
    w_gate_up,
    w_down,
    out_grad,
):
    rows = hidden_in.shape[2]
    seqs = hidden_in.shape[0] * hidden_in.shape[1]
    flat_rows = seqs * rows
    count = lax.axis_size(BOTH)
    query_width = QUERY_HEADS * HEAD_WIDTH
    kv_width = 2 * KEY_VALUE_HEADS * HEAD_WIDTH
    by_seq = lambda a: a.reshape(seqs, rows, a.shape[1])
    flat = lambda a: a.reshape(flat_rows, a.shape[2])
    r, rm, ra, rd = w_xbc.shape[0], w_mix_out.shape[0], w_attn_out.shape[0], w_down.shape[0]
    bits = bit_count()
    top = list(range(bits - 1, 2, -1))
    half = (DI + query_width + kv_width) // 2

    heads = jnp.stack([step_bias, -jnp.exp(decay_log), skip_gain])
    heads = jnp.pad(heads, ((0, 5), (0, LANES - H)))
    spread = jnp.repeat(jnp.eye(LANES, H, dtype=BF16), P_SIZE, axis=1)
    skip_row = jnp.broadcast_to(jnp.repeat(skip_gain, P_SIZE)[None], (8, DI))
    picks = jnp.eye(LANES, 2 * LEFT, 2 * LEFT - LANES, dtype=BF16)
    rest = rest_place().reshape(1).astype(jnp.int32)

    first = Part(
        pack_first(w_xbc, w_step, conv_weight, conv_bias, mixer_gain, norm1_gain, norm2_gain)[None]
    )
    first.step(top[0])
    out = Part(pack_out(w_mix_out, w_attn_out))
    x_got = swap_start(hidden_in[:, 0])
    segs_got = swap_start(segment_ids[:, 0])
    out.step(2)
    for n, bit in enumerate(top[1:]):
        join([first] if n else [first, out])
        first.step(bit)
    out.step(1)
    first_halves = join([first, out], split=(first,), after=(heads, spread, skip_row, picks))
    [p.step(bit) for p, bit in zip(first_halves, (2, 1))]
    two = Part(pack_two(w_gate_z, w_query, key_value_weight, after=(first_halves[0].pieces[0][0],))[None])
    two.step(top[0])
    cols, rows_in, keep_end = sequence_masks(swap_end(segment_ids[:, 0], segs_got))
    join(first_halves + [two])
    [p.step(bit) for p, bit in zip(first_halves, (1, 2))]
    two.steps(top[1:])
    x = swap_end(hidden_in[:, 0], x_got).reshape(flat_rows, MODEL_WIDTH)
    [p.core() for p in first_halves]
    two_halves = join([two], split=(two,), after=[p.pieces[1][0] for p in first_halves])
    [p.step(bit) for p, bit in zip(two_halves, (2, 1))]
    units = Part(pack_units(w_gate_up, w_down, after=(two_halves[0].pieces[0][0],))[None])
    units.step(top[0])
    left_full, right_full, small_full = assemble(
        first_halves,
        [(count, r, LEFT), (count, r, LEFT), (count, r, LANES)],
        [
            (0, 0, r, 0, LEFT, 0, 0, 0),
            (1, 0, r, 0, LEFT, 1, 0, 0),
            (1, 0, r, LEFT - LANES, LANES, 2, 0, 0),
        ],
        after=(units.pieces[0][0],),
    )

    conv, mix_gain, gains = unpack_small(small_full, r)
    gain_one, gain_two = gains[:1], gains[1:]
    normed, left, right, tails = first_proj(x, gain_one, left_full, right_full, cols, after=(rows_in,))
    left, right = by_seq(left), by_seq(right)
    tail_pieces, offsets = gather_sequence(tails)
    join(two_halves + [units], after=(left,))
    [p.step(bit) for p, bit in zip(two_halves, (1, 2))]
    units.steps(top[1:])
    out.step(top[0])
    halo = take_halo(rest, tail_pieces, offsets)
    xbc, slope, xd, step, cum, msg = mix_begin(
        left, right, halo, cols, heads, conv, after=(two_halves[0].pieces[0][0],)
    )
    msg_pieces, _ = gather_sequence(msg)
    units_halves = join([units, out], after=(cum,), split=(units,))
    [p.step(bit) for p, bit in zip(units_halves, (2, 1))]
    out.steps(top[1:])
    [p.core() for p in two_halves]
    inside = mix_inside(xbc, xd, cum, cols, rows_in, skip_row, after=(out.pieces[0][0],))
    z_full, qkv_full = assemble(
        two_halves,
        [(count, r, DI), (count, r, query_width + kv_width)],
        [
            (0, 0, r, 0, half, 0, 0, 0),
            (1, 0, r, 0, DI - half, 0, 0, half),
            (1, 0, r, DI - half, query_width + kv_width, 1, 0, 0),
        ],
        after=(inside,),
    )
    gate_z, queries, keyvals = second_proj(normed, z_full, qkv_full, rows_in)
    gate_z, queries = by_seq(gate_z), by_seq(queries)
    prev = scan_states(rest, msg_pieces, offsets, True, after=(gate_z,))
    join(units_halves, after=(prev, out.pieces[1][0]))
    [p.step(bit) for p, bit in zip(units_halves, (1, 2))]
    out.core()
    kv_pieces, _ = gather_sequence(keyvals)
    mixer_out, normed_mix = mix_finish(
        inside, xbc, prev, cum, cols, gate_z, mix_gain, after=(units_halves[0].pieces[0][0],)
    )
    attn_low, log_sums = attend(rest, queries, kv_pieces, cols, rows_in, offsets, after=(normed_mix,))

    out_keep, out_send = turn(flat(normed_mix), flat(attn_low))
    x_halo = halo[:, :, CONV_WIDTH:].reshape(seqs * HALO, MODEL_WIDTH)
    normed_keep, normed_send = turn(jnp.concatenate([normed, x_halo]), after=(out_keep,))

    mix_out_full, attn_out_full = assemble(
        [out],
        [(count, rm, MODEL_WIDTH), (count, ra, MODEL_WIDTH)],
        [(0, 0, rm, 0, MODEL_WIDTH, 0, 0, 0), (0, rm, ra, 0, MODEL_WIDTH, 1, 0, 0)],
        after=(normed_keep,),
    )
    residual, normed_two = out_proj(x, flat(normed_mix), flat(attn_low), mix_out_full, attn_out_full, gain_two)
    two_keep, two_send, *held = turn(normed_two, hold=[p.pieces[1][0] for p in units_halves])
    for p, got in zip(units_halves, held):
        p.pieces[1] = (got, p.pieces[1][1])
        p.core()
    moves = [(n, q * r, r, 0, MODEL_WIDTH, n, 0, q * MODEL_WIDTH) for n in range(2) for q in range(2)]
    moves += [(n, 2 * r, rd // 2, 0, MODEL_WIDTH, 2, n * (rd // 2), 0) for n in range(2)]
    gate_full, up_full, down_full = assemble(
        units_halves, [(count, r, FF), (count, r, FF), (count, rd, MODEL_WIDTH)], moves, after=(two_keep,)
    )
    out_turned = [out_keep, exchange(out_send, 0)]
    x_turned = [normed_keep, exchange(normed_send, 0)]
    two_turned = [two_keep, exchange(two_send, 0)]
    grad_got = fsdp_exchange(pick(out_grad[:, 0], 1 - side_of(), after=(gate_full,)), fsdp_bits() - 1)
    act, swish, gate_slope = gate_up(normed_two, gate_full, up_full)
    act_keep, act_send = turn(act)
    grad_out = merge(out_grad[:, 0], grad_got, side_of(), after=(act_keep,)).reshape(flat_rows, MODEL_WIDTH)
    act_turned = [act_keep, exchange(act_send, 0)]
    grad_out_got = exchange(grad_out, 0)

    block_out, grad_gate, grad_up = down(
        act, swish, gate_slope, down_full, residual, grad_out, after=(act_keep,)
    )
    gate_got, up_got = exchange(grad_gate, 0), exchange(grad_up, 0)
    hidden_got = swap_start(by_seq(block_out))
    sum_down = Sum(act_turned, [grad_out, grad_out_got], 0, after=(block_out,))
    sum_down.near()
    sum_gate = Sum(two_turned, [grad_gate, gate_got], 0, after=(sum_down.send,))
    sum_up = Sum(two_turned, [grad_up, up_got], 1, after=(sum_gate.send,))
    grad_resid, grad_branch = gate_up_back(
        grad_gate, grad_up, gate_full, up_full, residual, gain_two, grad_out, after=(sum_up.send,)
    )
    advance([sum_down], after=(grad_branch,))
    hidden_out = swap_end(by_seq(block_out), hidden_got)
    branch_got = exchange(grad_branch, 0)
    sum_gate.near(), sum_up.near()
    grad_normed_mix, grad_attn = out_back(
        grad_branch, mix_out_full, attn_out_full, after=(sum_down.send, hidden_out)
    )
    grad_normed_mix, grad_attn = by_seq(grad_normed_mix), by_seq(grad_attn)
    sum_out = Sum(out_turned, [grad_branch, branch_got], 0, after=(grad_normed_mix,))

    grad_queries, grad_kv_pieces = attend_back(
        rest, queries, kv_pieces, cols, rows_in, attn_low, log_sums, grad_attn, offsets, after=(sum_out.send,)
    )
    advance([sum_gate, sum_up], after=(grad_queries,))
    sum_gate.second(), sum_up.second()
    kv_own, kv_got = sum_sequence(grad_kv_pieces)
    dy, grad_za, grad_zb, back_msg = gated_back(
        grad_normed_mix, mixer_out, gate_z, mix_gain, xbc, cum, cols, half, after=(sum_gate.send, sum_up.send)
    )
    grad_za = flat(grad_za)
    grad_zq = join_grads(flat(grad_zb), flat(grad_queries), kv_own, kv_got)
    (pair_gate_up,) = advance([(sum_gate, sum_up)], after=(grad_zq,))
    za_got, zq_got = exchange(grad_za, 0), exchange(grad_zq, 0)
    back_pieces, _ = gather_sequence(back_msg)
    pair_gate_up.start(3)
    sum_out.near(), sum_down.second()
    dxd, dbc, sums = inside_back(
        xbc, xd, cum, cols, rows_in, skip_row, spread, dy, mixer_out, prev, after=(pair_gate_up.send,)
    )
    sum_z = Sum(x_turned, [grad_za, za_got], 0, after=(sums,))
    sum_zq = Sum(x_turned, [grad_zq, zq_got], 1, after=(sum_z.send,))
    later = scan_states(rest, back_pieces, offsets, False, after=(sum_zq.send,))
    for bit in range(4, bits):
        advance([sum_out, pair_gate_up] if bit == 4 else [pair_gate_up], after=(later,))
        pair_gate_up.start(bit)
    sum_out.second()
    sum_z.near(), sum_zq.near()
    grad_second = second_back(grad_za, grad_zq, z_full, qkv_full, after=(sum_out.send,))
    grad_first, conv_sums, head_sums = mix_end(
        left, right, halo, xbc, slope, xd, step, cum, cols, heads, skip_row, conv, spread,
        dy, dxd, dbc, sums, later, prev, after=(grad_second,),
    )
    _, _, pair_out_down = advance([sum_z, sum_zq, (sum_out, sum_down)], after=(head_sums,))
    small_keep, small_send = small_grads(r, conv_sums, head_sums)
    sum_x = Direct(
        [normed_keep, small_keep], [normed_send, small_send], [grad_first, picks], after=(pair_out_down.send,)
    )
    grad_normed, grad_halo = first_back(
        grad_first, left_full, right_full, grad_second, after=(sum_x.send,)
    )
    sum_x.core()
    sum_z.second(), sum_zq.second()
    pair_out_down.start(3)
    edge = keep_end[:, rows - HALO :, None]
    from_next = jnp.where(edge, from_next_part(grad_halo.reshape(seqs, HALO, MODEL_WIDTH)), 0.0)
    quarter = sum_x.planes(after=(grad_normed,))
    input_grad, input_low = input_back(grad_normed, from_next, x, gain_one, grad_resid, after=(quarter,))
    input_got = swap_start(input_low)
    input_grad = swap_end(input_grad, input_got)

    (own_gate_up,) = finish([pair_gate_up], after=(grad_normed,))
    far = list(range(4, bits))
    (pair_z,) = advance([(sum_z, sum_zq)], after=(input_low,))
    pair_z.start(3)
    for bit in far:
        advance([pair_out_down], after=(pair_z.send,))
        pair_out_down.start(bit)
    sum_x.lines(after=(pair_out_down.send,))
    (own_out_down,) = finish([pair_out_down], after=(sum_x.keep,))
    for bit in far:
        advance([pair_z], after=(sum_x.keep,))
        pair_z.start(bit)
    (own_zq,) = finish([pair_z], after=(sum_x.keep,))
    own_first = sum_x.done()
    own_small = own_first[:, 2 * LEFT - LANES :]
    widths = [conv_weight.shape[1]] * KC + [conv_bias.shape[0]] + [H] * 3
    own = []
    for j, width in enumerate(widths):
        row, lane = line_place(j, len(widths), r)
        own.append(own_small[row, lane : lane + width])
    gain_grad = lambda weights, grads, gain: sum(
        jnp.sum(w.astype(F32) * g, 1) for w, g in zip(weights, grads)
    ) / gain.astype(F32)
    zq = jnp.concatenate([own_zq[0], own_zq[1]], 1)
    grad_z, grad_query, grad_keyval = jnp.split(zq, (DI, DI + query_width), 1)
    grad_xbc = own_first[:, :CONV_WIDTH]
    grad_step = own_first[:, CONV_WIDTH : CONV_WIDTH + H]
    grad_gate_up = jnp.concatenate([own_gate_up[0], own_gate_up[1]], 1)
    grad_out_w, grad_down = own_out_down[0], own_out_down[1]
    first_w = (w_gate_z, w_xbc, w_step, w_query, key_value_weight)
    first_g = (grad_z, grad_xbc, grad_step, grad_query, grad_keyval)
    return (
        hidden_out.reshape(hidden_in.shape),
        input_grad.reshape(hidden_in.shape),
        gain_grad(first_w, first_g, norm1_gain),
        grad_z,
        grad_xbc,
        grad_step,
        jnp.stack(own[:KC]),
        own[KC],
        own[KC + 1],
        own[KC + 2],
        own[KC + 3],
        gain_grad([w_mix_out], [grad_out_w[:rm]], mixer_gain),
        grad_out_w[:rm],
        grad_query,
        grad_keyval,
        grad_out_w[rm:],
        gain_grad([w_gate_up], [grad_gate_up], norm2_gain),
        grad_gate_up,
        grad_down,
    )


def solution(mesh):
    placed = (
        P(None, "dp", "fsdp", None),
        P(None, "dp", "fsdp"),
        P(("dp", "fsdp")),
        P(("dp", "fsdp"), None),
        P(("dp", "fsdp"), None),
        P(("dp", "fsdp"), None),
        P(None, ("dp", "fsdp")),
        P(("dp", "fsdp")),
        P(),
        P(),
        P(),
        P(("dp", "fsdp")),
        P(("dp", "fsdp"), None),
        P(("dp", "fsdp"), None),
        P(("dp", "fsdp"), None),
        P(("dp", "fsdp"), None),
        P(("dp", "fsdp")),
        P(("dp", "fsdp"), None),
        P(("dp", "fsdp"), None),
        P(None, "dp", "fsdp", None),
    )
    return jax.shard_map(
        per_device,
        mesh=mesh,
        in_specs=placed,
        out_specs=(
            P(None, "dp", "fsdp", None),
            P(None, "dp", "fsdp", None),
            P(("dp", "fsdp")),
            P(("dp", "fsdp"), None),
            P(("dp", "fsdp"), None),
            P(("dp", "fsdp"), None),
            P(None, ("dp", "fsdp")),
            P(("dp", "fsdp")),
            P(),
            P(),
            P(),
            P(("dp", "fsdp")),
            P(("dp", "fsdp"), None),
            P(("dp", "fsdp"), None),
            P(("dp", "fsdp"), None),
            P(("dp", "fsdp"), None),
            P(("dp", "fsdp")),
            P(("dp", "fsdp"), None),
            P(("dp", "fsdp"), None),
        ),
        check_vma=False,
    )
```

```python
import functools

import jax
import jax.numpy as jnp
from jax import lax
from jax.experimental import pallas as pl
from jax.experimental.pallas import tpu as pltpu
from jax.sharding import PartitionSpec as P

MODEL_WIDTH = 1024
FF = 2048
H = 24
P_SIZE = 64
NS = 128
QUERY_HEADS = 8
KEY_VALUE_HEADS = 2
HEAD_WIDTH = 64
KC = 4
DI = 1536


EPSILON = 1e-06
NEGATIVE = -1e30


def matmul(first_op, second_op):
    return jnp.dot(first_op, second_op, preferred_element_type=jnp.float32)


def left_t(first_op, second_op):
    return jnp.einsum("ti,tj->ij", first_op, second_op, preferred_element_type=jnp.float32)


def right_t(first_op, second_op):
    return jnp.einsum("ti,ji->tj", first_op, second_op, preferred_element_type=jnp.float32)


def rms_gain(values, gain_in):
    return values * lax.rsqrt(jnp.mean(values * values, axis=-1, keepdims=True) + EPSILON) * gain_in


def swiglu(gate_up):
    return jax.nn.silu(gate_up[:, :FF]) * gate_up[:, FF:]


BOTH = ("dp", "fsdp")


def exchange_mask(block, mask):
    count = lax.axis_size(BOTH)
    return lax.ppermute(block, BOTH, [(i, i ^ mask) for i in range(count)])


def exchange(block, bit):
    return exchange_mask(block, 1 << bit)


def bit_count():
    return lax.axis_size(BOTH).bit_length() - 1


def place_of():
    return lax.axis_index(BOTH)


def in_hbm(array):
    return pltpu.with_memory_space_constraint(array, pltpu.HBM)


def spec_any(count):
    return [pl.BlockSpec(memory_space=pl.ANY)] * count


def copies_kernel(n_in, n_after, n_out, n_hold, jobs, place_ref, *refs):
    ins, refs = refs[:n_in], refs[n_in + n_hold + n_after :]
    outs, refs = refs[:n_out], refs[n_out + n_hold :]
    held, sems, out_sems = refs[:n_out], refs[-2], refs[-1]
    place = place_ref[0]
    copies = [[] for _ in outs]
    for number, (out, source, source_at, target_at) in enumerate(jobs):
        copy = pltpu.make_async_copy(
            ins[source].at[source_at], held[out].at[target_at(place)], sems.at[number]
        )
        copy.start()
        copies[out].append(copy)
    back = []
    for out in range(n_out):
        for copy in copies[out]:
            copy.wait()
        copy = pltpu.make_async_copy(held[out], outs[out], out_sems.at[out])
        copy.start()
        back.append(copy)
    for copy in back:
        copy.wait()


def copies(name, ins, outs, jobs, after=(), hold=(), limit=24):
    jobs = sorted(jobs, key=lambda job: job[0])
    ins = [in_hbm(a) for a in ins]
    return pl.pallas_call(
        functools.partial(copies_kernel, len(ins), len(after), len(outs), len(hold), jobs),
        out_shape=[jax.ShapeDtypeStruct(s, jnp.bfloat16) for s in outs]
        + [jax.ShapeDtypeStruct(a.shape, a.dtype) for a in hold],
        in_specs=[pl.BlockSpec(memory_space=pltpu.SMEM)] + spec_any(len(ins) + len(hold) + len(after)),
        out_specs=spec_any(len(outs) + len(hold)),
        input_output_aliases={1 + len(ins) + n: len(outs) + n for n in range(len(hold))},
        scratch_shapes=[pltpu.VMEM(s, jnp.bfloat16) for s in outs]
        + [pltpu.SemaphoreType.DMA((len(jobs),)), pltpu.SemaphoreType.DMA((len(outs),))],
        compiler_params=pltpu.CompilerParams(vmem_limit_bytes=limit * 2**20),
        name=name,
    )(place_of().reshape(1).astype(jnp.int32), *ins, *hold, *after)


class Part:
    def __init__(self, block, offsets=(0,)):
        self.pieces = [(block, list(offsets))]

    def step(self, bit):
        ((block, offsets),) = self.pieces
        self.pieces.append((exchange(block, bit), [o ^ (1 << bit) for o in offsets]))

    def steps(self, bits):
        for n, bit in enumerate(bits):
            if n:
                join([self])
            self.step(bit)

    def direct(self, masks):
        ((block, offsets),) = self.pieces
        self.pieces += [(exchange_mask(block, mask), [o ^ mask for o in offsets]) for mask in masks]

    def core(self):
        self.pieces += [(exchange(a, 0), [o ^ 1 for o in offsets]) for a, offsets in self.pieces]


def join_all(parts, after=(), hold=()):
    ins, jobs = [], []
    for p, part in enumerate(parts):
        at = 0
        for array, own in part.pieces:
            target = (p, slice(at, at + len(own)))
            jobs.append((0, len(ins), (slice(None),), lambda place, target=target: target))
            ins.append(array)
            at += len(own)
    shape = (len(parts), at) + ins[0].shape[1:]
    return copies("join_all", ins, [shape], jobs, after, hold)


def join(parts, after=(), split=(), hold=()):
    ins, outs, jobs, made = [], [], [], []
    for part in parts:
        first = part.pieces[0][0]
        blocks = sum(len(offsets) for _, offsets in part.pieces)
        offsets = sum((o for _, o in part.pieces), [])
        halves = (0, 1) if part in split else (None,)
        for half in halves:
            at = 0
            for number, (array, own) in enumerate(part.pieces):
                source = len(ins) + number
                source_at = (slice(None),) if half is None else (slice(None), half)
                target = (slice(at, at + len(own)),)
                jobs.append((len(outs), source, source_at, lambda place, target=target: target))
                at += len(own)
            outs.append((blocks,) + (first.shape[1:] if half is None else first.shape[2:]))
            made.append((part, half, offsets))
        ins += [array for array, _ in part.pieces]
    cut = []
    held = [part.pieces[-1][0] for part in hold]
    found = copies("join", ins, outs, jobs, after, held)
    for array, part in zip(found[len(outs) :], hold):
        part.pieces[-1] = (array, part.pieces[-1][1])
    for array, (part, half, offsets) in zip(found, made):
        if half is None:
            part.pieces = [(array, offsets)]
        else:
            cut.append(Part(array, offsets))
    return cut


def assemble(parts, outs, moves, after=(), limit=24):
    ins, jobs = [], []
    for at, part in enumerate(parts):
        for piece, offsets, *of_part in part.pieces:
            for j, offset in enumerate(offsets):
                for of, r0, rows, c0, columns, out, row, column in moves:
                    if of == at:
                        source_at = (*of_part, j, pl.ds(r0, rows), pl.ds(c0, columns))
                        target = (pl.ds(row, rows), pl.ds(column, columns))
                        jobs.append(
                            (out, len(ins), source_at, lambda place, o=offset, t=target: (place ^ o,) + t)
                        )
            ins.append(piece)
    return [a.reshape(-1, a.shape[2]) for a in copies("assemble", ins, outs, jobs, after, limit=limit)]


def turned_offsets(bits):
    offsets = [0]
    for bit in list(range(bits - 1, 2, -1)) + [1, 2]:
        offsets = offsets + [o ^ (1 << bit) for o in offsets]
    return offsets


def turn_kernel(n_x, n_hold, n_after, rows, offsets, place_ref, *refs):
    xs, refs = refs[:n_x], refs[n_x + n_hold + n_after :]
    keep_ref, send_ref, turned = refs[0], refs[1], refs[2 + n_hold :]
    place = place_ref[0]
    total = sum(rows)
    for x_ref, t_ref in zip(xs, turned):
        t_ref[...] = x_ref[...].T
    for t, offset in enumerate(offsets):
        at = t * total
        for t_ref, size in zip(turned, rows):
            begin = pl.multiple_of((place ^ offset) * size, size)
            keep_ref[at : at + size] = t_ref[pl.ds(begin, size)]
            begin = pl.multiple_of((place ^ (offset ^ 1)) * size, size)
            send_ref[at : at + size] = t_ref[pl.ds(begin, size)]
            at += size


def turn(*xs, after=(), hold=()):
    bits = bit_count()
    rows = [x.shape[1] >> bits for x in xs]
    tokens, half = xs[0].shape[0], sum(x.shape[1] for x in xs) // 2
    if any(r % 16 for r in rows):
        blocks = jnp.concatenate([x.T.reshape(1 << bits, r, tokens) for x, r in zip(xs, rows)], 1)
        offsets = jnp.asarray(turned_offsets(bits), jnp.int32) ^ place_of()
        sides = [jnp.take(blocks, o, axis=0).reshape(half, tokens) for o in (offsets, offsets ^ 1)]
        return (*sides, *hold)
    vmem = pl.BlockSpec(memory_space=pltpu.VMEM)
    return pl.pallas_call(
        functools.partial(turn_kernel, len(xs), len(hold), len(after), rows, turned_offsets(bits)),
        in_specs=[pl.BlockSpec(memory_space=pltpu.SMEM)] + [vmem] * len(xs) + spec_any(len(hold) + len(after)),
        out_specs=[vmem] * 2 + spec_any(len(hold)),
        out_shape=[jax.ShapeDtypeStruct((half, tokens), jnp.bfloat16)] * 2
        + [jax.ShapeDtypeStruct(a.shape, a.dtype) for a in hold],
        input_output_aliases={1 + len(xs) + n: 2 + n for n in range(len(hold))},
        scratch_shapes=[pltpu.VMEM((x.shape[1], x.shape[0]), jnp.bfloat16) for x in xs],
        compiler_params=pltpu.CompilerParams(vmem_limit_bytes=24 * 2**20),
        name="turn",
    )(place_of().reshape(1).astype(jnp.int32), *xs, *hold, *after)


def grad_kernel(n_pairs, half, *refs):
    pairs, (keep_ref, send_ref) = refs[: 2 * n_pairs], refs[-2:]
    total = None
    for x_ref, g_ref in zip(pairs[:n_pairs], pairs[n_pairs:]):
        part = jnp.dot(x_ref[...], g_ref[...], preferred_element_type=jnp.float32)
        total = part if total is None else total + part
    total = total.astype(jnp.bfloat16)
    rows = keep_ref.shape[1]
    for second in range(2):
        for first, ref in enumerate((keep_ref, send_ref)):
            quarter = 2 * first + second if half == 0 else 2 * second + first
            ref[second] = total[quarter * rows : (quarter + 1) * rows]


def weight_grad(xs, gs, half, after=(), columns=None):
    k, (first, n) = xs[0].shape[0], columns or (0, gs[0].shape[1])
    width = next(w for w in (1024, 512, 384, 256, 128) if n % w == 0 and first % w == 0)
    at = first // width
    block = pl.BlockSpec((2, k // 4, width), lambda i: (0, 0, i))
    return pl.pallas_call(
        functools.partial(grad_kernel, len(xs), half),
        grid=(n // width,),
        in_specs=[pl.BlockSpec((k, g.shape[0]), lambda i: (0, 0)) for g in gs]
        + [pl.BlockSpec((g.shape[0], width), lambda i: (0, at + i)) for g in gs]
        + spec_any(len(after)),
        out_specs=[block, block],
        out_shape=[jax.ShapeDtypeStruct((2, k // 4, n), jnp.bfloat16)] * 2,
        compiler_params=pltpu.CompilerParams(vmem_limit_bytes=48 * 2**20),
        name="weight_grad",
    )(*xs, *gs, *after)


def both_kernel(n_pairs, half, *refs):
    outs = refs[-2:]
    gs = refs[2 * n_pairs : 3 * n_pairs]
    for xs, out_ref in ((refs[:n_pairs], outs[0]), (refs[n_pairs : 2 * n_pairs], outs[1])):
        total = None
        for x_ref, g_ref in zip(xs, gs):
            part = jnp.dot(x_ref[...], g_ref[...], preferred_element_type=jnp.float32)
            total = part if total is None else total + part
        total = total.astype(jnp.bfloat16)
        rows = out_ref.shape[1] // 4
        for quarter in range(4):
            place = quarter if half == 0 else 2 * (quarter % 2) + quarter // 2
            out_ref[0, place * rows : (place + 1) * rows] = total[quarter * rows : (quarter + 1) * rows]


def both_grads(keeps, sends, gs, half, after=()):
    k, n = keeps[0].shape[0], gs[0].shape[1]
    width = next(w for w in (512, 256, 128) if n % w == 0)
    block = pl.BlockSpec((1, k, width), lambda i: (0, 0, i))
    return pl.pallas_call(
        functools.partial(both_kernel, len(gs), half),
        grid=(n // width,),
        in_specs=[pl.BlockSpec((k, g.shape[0]), lambda i: (0, 0)) for g in gs] * 2
        + [pl.BlockSpec((g.shape[0], width), lambda i: (0, i)) for g in gs]
        + spec_any(len(after)),
        out_specs=[block, block],
        out_shape=[jax.ShapeDtypeStruct((1, k, n), jnp.bfloat16)] * 2,
        compiler_params=pltpu.CompilerParams(vmem_limit_bytes=48 * 2**20),
        name="both_grads",
    )(*keeps, *sends, *gs, *after)


def add_kernel(shape, last, n_after, *refs):
    n_in = sum(len(counts) for counts in shape)
    keeps, gots, outs = refs[:n_in], refs[n_in : 2 * n_in], refs[2 * n_in + n_after :]
    at = 0
    for item, counts in enumerate(shape):
        slot = 0
        for count in counts:
            for s in range(count):
                total = keeps[at][s].astype(jnp.float32) + gots[at][s].astype(jnp.float32)
                if last:
                    outs[item][slot] = total
                else:
                    total = total.astype(jnp.bfloat16)
                    half = total.shape[0] // 2
                    outs[2 * item][slot] = total[:half]
                    outs[2 * item + 1][slot] = total[half:]
                slot += 1
            at += 1


def add_up(items, after=(), last=False):
    shape = [[own.shape[0] for own, _ in item] for item in items]
    keeps = [own for item in items for own, _ in item]
    gots = [in_hbm(got) for item in items for _, got in item]
    widths = {a.shape[2] for a in keeps}
    steps = next(g for g in (2, 3, 1) if all(w % (g * 128) == 0 for w in widths))
    blocks, outs = [], []
    for a in keeps:
        blocks.append(pl.BlockSpec(a.shape[:2] + (a.shape[2] // steps,), lambda i: (0, 0, i)))
    out_blocks = []
    for item, counts in zip(items, shape):
        rows, n = item[0][0].shape[1:]
        rows = rows if last else rows // 2
        for _ in range(1 if last else 2):
            out_blocks.append(pl.BlockSpec((sum(counts), rows, n // steps), lambda i: (0, 0, i)))
            outs.append(
                jax.ShapeDtypeStruct((sum(counts), rows, n), jnp.float32 if last else jnp.bfloat16)
            )
    return pl.pallas_call(
        functools.partial(add_kernel, shape, last, len(after)),
        grid=(steps,),
        in_specs=blocks + blocks + spec_any(len(after)),
        out_specs=out_blocks,
        out_shape=outs,
        compiler_params=pltpu.CompilerParams(vmem_limit_bytes=48 * 2**20),
        name="add_up",
    )(*keeps, *gots, *after)


class Sum:
    def __init__(self, xs, gs, half, after=(), columns=None):
        self.first = (2, 1)[half]
        keep, send = weight_grad(xs, gs, half, after, columns)
        self.keep, self.send = (a.reshape(1, -1, a.shape[2]) for a in (keep, send))

    def start(self, bit):
        self.got = exchange(self.send, bit)

    def near(self):
        self.start(self.first)

    def second(self):
        self.start(3 - self.first)


class CoreSum(Sum):
    def __init__(self, keeps, sends, gs, half, after=()):
        self.first = (2, 1)[half]
        self.keep, self.send = both_grads(keeps, sends, gs, half, after)

    def core(self):
        self.start(0)


class Pair:
    def start(self, bit):
        self.got = exchange(self.send, bit)


def advance(steps, after=()):
    items = [[(s.keep, s.got) for s in (step if isinstance(step, tuple) else (step,))] for step in steps]
    found = add_up(items, after)
    made = []
    for n, step in enumerate(steps):
        step = Pair() if isinstance(step, tuple) else step
        step.keep, step.send = found[2 * n : 2 * n + 2]
        made.append(step)
    return made


def finish(pairs, after=()):
    return add_up([[(p.keep, p.got)] for p in pairs], after, last=True)


def parts_kernel(n_in, parts, n_skip, *refs):
    ins, outs = refs[:n_in], refs[n_in + n_skip :]
    total = ins[0][0].astype(jnp.float32)
    for ref in ins[1:]:
        total = total + ref[0].astype(jnp.float32)
    rows = total.shape[0] // parts
    for n in range(parts):
        outs[n][0] = total[n * rows : (n + 1) * rows].astype(outs[n].dtype)


def add_parts(arrays, parts, kind=jnp.bfloat16, after=(), hold=()):
    _, rows, n = arrays[0].shape
    steps = next(g for g in (2, 1) if n % (g * 128) == 0)
    spec = lambda rows: pl.BlockSpec((1, rows, n // steps), lambda i: (0, 0, i))
    return pl.pallas_call(
        functools.partial(parts_kernel, len(arrays), parts, len(hold) + len(after)),
        grid=(steps,),
        in_specs=[spec(rows)] * len(arrays) + spec_any(len(hold) + len(after)),
        out_specs=[spec(rows // parts)] * parts + spec_any(len(hold)),
        out_shape=[jax.ShapeDtypeStruct((1, rows // parts, n), kind)] * parts
        + [jax.ShapeDtypeStruct(a.shape, a.dtype) for a in hold],
        input_output_aliases={len(arrays) + n: parts + n for n in range(len(hold))},
        compiler_params=pltpu.CompilerParams(vmem_limit_bytes=48 * 2**20),
        name="add_parts",
    )(arrays[0], *[in_hbm(a) for a in arrays[1:]], *hold, *after)


class Direct:
    def __init__(self, keeps, sends, gs, after=()):
        self.keep, self.send = both_grads(keeps, sends, gs, 0, after)

    def core(self):
        self.got = [exchange(self.send, 0)]

    def planes(self, after=()):
        quarters = add_parts([self.keep] + self.got, 4, after=after)
        self.keep = quarters[0]
        self.got = [exchange_mask(q, mask) for q, mask in zip(quarters[1:], (2, 4, 6))]
        return quarters[0]

    def lines(self, after=(), hold=()):
        bits = bit_count()
        arrays = [self.keep] + self.got
        if bits == 5:
            quarters = add_parts(arrays, 4, after=after, hold=hold)
            self.keep = quarters[0]
            self.got = [exchange_mask(q, mask) for q, mask in zip(quarters[1:4], (16, 8, 24))]
            return quarters[4:]
        for bit in range(3, bits):
            self.keep, send = add_parts(arrays, 2, after=after)
            self.got = [exchange(send, bit)]
            arrays = [self.keep] + self.got
        return hold

    def done(self):
        return add_parts([self.keep] + self.got, 1, jnp.float32)[0][0]


F32 = jnp.float32
BF16 = jnp.bfloat16
LANES = 128
HALO = 16
STATE_ROWS = NS + 16
LEFT = 1024
SLOTS = 2
CONV_WIDTH = DI + 2 * NS
VMEM_LIMIT = 48 * 2**20


def dot_nn(a, b):
    return jnp.dot(a, b, preferred_element_type=F32)


def dot_nt(a, b):
    return lax.dot_general(a, b, (((1,), (1,)), ((), ())), preferred_element_type=F32)


def dot_tn(a, b):
    return lax.dot_general(a, b, (((0,), (0,)), ((), ())), preferred_element_type=F32)


def split_two(v):
    high = v.astype(BF16)
    return high, (v - high.astype(F32)).astype(BF16)


def sum_heads(v, spread):
    high, low = split_two(v)
    return dot_nt(high, spread) + dot_nt(low, spread)


def tile_of(i):
    return slice(i * LANES, (i + 1) * LANES)


def two_heads(v, i):
    rows = v.shape[0]
    lane = lax.broadcasted_iota(jnp.int32, (rows, LANES), 1)
    left = jnp.broadcast_to(v[:, 2 * i : 2 * i + 1], (rows, LANES))
    right = jnp.broadcast_to(v[:, 2 * i + 1 : 2 * i + 2], (rows, LANES))
    return jnp.where(lane < P_SIZE, left, right)


def all_heads(v):
    v = jnp.broadcast_to(v, (16, LANES))
    return jnp.concatenate([two_heads(v, i) for i in range(DI // LANES)], 1)


def triangle(size, lower):
    rows = lax.broadcasted_iota(jnp.int32, (size, size), 0)
    cols = lax.broadcasted_iota(jnp.int32, (size, size), 1)
    return jnp.where(rows >= cols if lower else rows <= cols, 1.0, 0.0).astype(BF16)


def exact_sum(ones, v):
    high = v.astype(BF16)
    rest = v - high.astype(F32)
    mid = rest.astype(BF16)
    low = (rest - mid.astype(F32)).astype(BF16)
    return dot_nn(ones, high) + (dot_nn(ones, mid) + dot_nn(ones, low))


def soft_plus(z):
    return jnp.maximum(z, 0.0) + jnp.log1p(jnp.exp(-jnp.abs(z)))


def sigmoid(v):
    return 0.5 * jnp.tanh(0.5 * v) + 0.5


def conv_tile(left_ref, right_ref, i):
    tiles = LEFT // LANES
    if i < tiles:
        return left_ref[0, :, tile_of(i)].astype(F32)
    return right_ref[0, :, tile_of(i - tiles)].astype(BF16).astype(F32)


def raw_tile(right_ref):
    return right_ref[0, :, CONV_WIDTH - LEFT : CONV_WIDTH - LEFT + LANES]


def mix_begin_kernel(
    left_ref, right_ref, halo_ref, cols_ref, heads_ref, conv_ref,
    xbc_ref, slope_ref, xd_ref, step_ref, cum_ref, msg_ref,
):
    rows = left_ref.shape[1]
    masks = cols_ref[0]
    step = soft_plus(raw_tile(right_ref) + heads_ref[0:1])
    cum = exact_sum(triangle(rows, True), step * heads_ref[1:2])
    step_ref[0] = step
    cum_ref[0] = cum
    last = cum[rows - 1 : rows]
    ends = jnp.exp(last - cum) * masks[:, 3:4]
    msg_ref[0, NS:STATE_ROWS, :] = all_heads(jnp.exp(last)).astype(BF16)
    wide = [jnp.broadcast_to(masks[:, k : k + 1], (rows, LANES)) for k in range(KC - 1)]

    def conv(i):
        lanes = tile_of(i)
        own = conv_tile(left_ref, right_ref, i)
        ext = jnp.concatenate([halo_ref[0, :, lanes].astype(F32), own], 0)
        taps = conv_ref[:, lanes]
        total = taps[4:5] + taps[3:4] * own
        for k in range(KC - 1):
            at = HALO - (KC - 1) + k
            total = total + taps[k : k + 1] * (ext[at : at + rows] * wide[k])
        sig = sigmoid(total)
        x = total * sig
        slope_ref[0, :, lanes] = (sig + x * (1.0 - sig)).astype(BF16)
        low = x.astype(BF16)
        xbc_ref[0, :, lanes] = low
        return x, low

    tiles = DI // LANES
    b_turned = conv(tiles)[1].T
    conv(tiles + 1)
    for i in range(tiles):
        xd = conv(i)[0] * two_heads(step, i)
        xd_ref[0, :, tile_of(i)] = xd.astype(BF16)
        weighted = (xd * two_heads(ends, i)).astype(BF16)
        msg_ref[0, 0:NS, tile_of(i)] = dot_nn(b_turned, weighted).astype(BF16)


def seq_block(*shape):
    return pl.BlockSpec((1,) + shape, lambda s: (s,) + (0,) * len(shape))


def whole_block(*shape):
    return pl.BlockSpec(shape, lambda s: (0,) * len(shape))


def call(kernel, name, seqs, ins, in_specs, outs, out_specs, scratch=(), after=()):
    n_in, n_after = len(ins), len(after)

    def run(*refs):
        kernel(*refs[:n_in], *refs[n_in + n_after :])

    ins = tuple(ins) + tuple(after)
    in_specs = list(in_specs) + [pl.BlockSpec(memory_space=pl.ANY)] * n_after
    return pl.pallas_call(
        run,
        grid=(seqs,),
        in_specs=in_specs,
        out_specs=out_specs,
        out_shape=[jax.ShapeDtypeStruct(s, d) for s, d in outs],
        scratch_shapes=list(scratch),
        compiler_params=pltpu.CompilerParams(vmem_limit_bytes=VMEM_LIMIT),
        name=name,
    )(*ins)


def mix_begin(left, right, halo, cols, heads, conv, after=()):
    seqs, rows, _ = left.shape
    width = CONV_WIDTH
    return call(
        mix_begin_kernel,
        "mix_begin",
        seqs,
        (left, right, halo, cols, heads, conv),
        [
            seq_block(rows, LEFT),
            seq_block(rows, LEFT),
            seq_block(HALO, halo.shape[2]),
            seq_block(rows, LANES),
            whole_block(8, LANES),
            whole_block(8, width),
        ],
        [
            ((seqs, rows, width), BF16),
            ((seqs, rows, width), BF16),
            ((seqs, rows, DI), BF16),
            ((seqs, rows, LANES), F32),
            ((seqs, rows, LANES), F32),
            ((seqs, STATE_ROWS, DI), BF16),
        ],
        [
            seq_block(rows, width),
            seq_block(rows, width),
            seq_block(rows, DI),
            seq_block(rows, LANES),
            seq_block(rows, LANES),
            seq_block(STATE_ROWS, DI),
        ],
        after=after,
    )


def row_parts(rows):
    if rows < 256:
        return [(0, rows, rows)]
    return [(a, a + LANES, a + LANES) for a in range(0, rows, LANES)]


def side_by_side(pair):
    lane = lax.broadcasted_iota(jnp.int32, pair.shape, 1)
    blank = jnp.zeros_like(pair)
    return jnp.where(lane < P_SIZE, pair, blank), jnp.where(lane < P_SIZE, blank, pair)


def mix_inside_kernel(xbc_ref, xd_ref, cum_ref, cols_ref, rows_ref, skip_ref, y_ref):
    rows = xbc_ref.shape[1]
    b_rows, c_rows = xbc_ref[0, :, DI : DI + NS], xbc_ref[0, :, DI + NS :]
    seg_col, seg_row = cols_ref[0, :, 5:6], rows_ref[0, 0:1, :]
    row_at = lax.broadcasted_iota(jnp.int32, (rows, rows), 0)
    col_at = lax.broadcasted_iota(jnp.int32, (rows, rows), 1)
    couple = jnp.where((seg_col == seg_row) & (row_at >= col_at), dot_nt(c_rows, b_rows), 0.0)
    cum = cum_ref[0]
    cum_rows = cum.T
    for first in range(0, H, 2):
        lanes = slice(first * P_SIZE, (first + 2) * P_SIZE)
        sides = side_by_side(xd_ref[0, :, lanes])
        for begin, end, upto in row_parts(rows):
            y = xbc_ref[0, begin:end, lanes].astype(F32) * skip_ref[0:1, lanes]
            for h, side in zip((first, first + 1), sides):
                gap = jnp.minimum(cum[begin:end, h : h + 1] - cum_rows[h : h + 1, :upto], 0.0)
                mixing = (jnp.exp(gap) * couple[begin:end, :upto]).astype(BF16)
                y = y + dot_nn(mixing, side[:upto])
            y_ref[0, begin:end, lanes] = y


def mix_inside(xbc, xd, cum, cols, rows_in, skip, after=()):
    seqs, rows, width = xbc.shape
    return call(
        mix_inside_kernel,
        "mix_inside",
        seqs,
        (xbc, xd, cum, cols, rows_in, skip),
        [
            seq_block(rows, width),
            seq_block(rows, DI),
            seq_block(rows, LANES),
            seq_block(rows, LANES),
            seq_block(8, rows),
            whole_block(8, DI),
        ],
        [((seqs, rows, DI), F32)],
        [seq_block(rows, DI)],
        after=after,
    )[0]


def mix_finish_kernel(y_ref, c_ref, prev_ref, cum_ref, cols_ref, z_ref, gain_ref, mo_ref, nm_ref, g_ref):
    rows = y_ref.shape[1]
    flow = jnp.exp(cum_ref[0]) * cols_ref[0, :, 4:5]
    c_rows = c_ref[0]
    total = jnp.zeros((rows, LANES), F32)
    for i in range(DI // LANES):
        lanes = tile_of(i)
        mo = y_ref[0, :, lanes] + dot_nn(c_rows, prev_ref[0, :, lanes]) * two_heads(flow, i)
        mo_ref[0, :, lanes] = mo
        z = z_ref[0, :, lanes]
        g = mo * (z * sigmoid(z))
        g_ref[:, lanes] = g
        total = total + g * g
    scale = lax.rsqrt(jnp.sum(total, axis=1, keepdims=True) / DI + EPSILON)
    scale = jnp.broadcast_to(scale, (rows, LANES))
    for i in range(DI // LANES):
        lanes = tile_of(i)
        nm_ref[0, :, lanes] = (g_ref[:, lanes] * scale * gain_ref[0:1, lanes]).astype(BF16)


def c_block(rows):
    return pl.BlockSpec((1, rows, NS), lambda s: (s, 0, (DI + NS) // NS))


def mix_finish(y, xbc, prev, cum, cols, z, gain, after=()):
    seqs, rows, _ = y.shape
    return call(
        mix_finish_kernel,
        "mix_finish",
        seqs,
        (y, xbc, prev, cum, cols, z, gain),
        [
            seq_block(rows, DI),
            c_block(rows),
            seq_block(NS, DI),
            seq_block(rows, LANES),
            seq_block(rows, LANES),
            seq_block(rows, DI),
            whole_block(1, DI),
        ],
        [((seqs, rows, DI), F32), ((seqs, rows, DI), BF16)],
        [seq_block(rows, DI), seq_block(rows, DI)],
        [pltpu.VMEM((rows, DI), F32)],
        after=after,
    )


def gated_back_kernel(
    dn_ref, mo_ref, z_ref, gain_ref, c_ref, cum_ref, cols_ref, dy_ref, dza_ref, dzb_ref, msg_ref, sig_ref
):
    rows = dn_ref.shape[1]
    squares = jnp.zeros((rows, LANES), F32)
    mixed = jnp.zeros((rows, LANES), F32)
    for i in range(DI // LANES):
        lanes = tile_of(i)
        z = z_ref[0, :, lanes]
        sig = sigmoid(z)
        sig_ref[:, lanes] = sig
        g = mo_ref[0, :, lanes] * (z * sig)
        squares = squares + g * g
        mixed = mixed + g * (dn_ref[0, :, lanes] * gain_ref[0:1, lanes])
    scale = lax.rsqrt(jnp.sum(squares, axis=1, keepdims=True) / DI + EPSILON)
    back = jnp.sum(mixed, axis=1, keepdims=True) / DI * scale * scale * scale
    scale = jnp.broadcast_to(scale, (rows, LANES))
    back = jnp.broadcast_to(back, (rows, LANES))
    cum = cum_ref[0]
    flow = jnp.exp(cum) * cols_ref[0, :, 4:5]
    msg_ref[0, NS:STATE_ROWS, :] = all_heads(jnp.exp(cum[rows - 1 : rows])).astype(BF16)
    c_turned = c_ref[0].T
    for i in range(DI // LANES):
        lanes = tile_of(i)
        z = z_ref[0, :, lanes]
        mo = mo_ref[0, :, lanes]
        sig = sig_ref[:, lanes]
        swish = z * sig
        g = mo * swish
        dn = dn_ref[0, :, lanes] * scale
        dg = dn * gain_ref[0:1, lanes] - g * back
        dy = (dg * swish).astype(BF16)
        dy_ref[0, :, lanes] = dy
        dz = (dg * mo * (sig + swish * (1.0 - sig))).astype(BF16)
        split = dza_ref.shape[2] // LANES
        if i < split:
            dza_ref[0, :, lanes] = dz
        else:
            dzb_ref[0, :, tile_of(i - split)] = dz
        flowed = (dy.astype(F32) * two_heads(flow, i)).astype(BF16)
        msg_ref[0, 0:NS, lanes] = dot_nn(c_turned, flowed).astype(BF16)


def gated_back(dn, mo, z, gain, xbc, cum, cols, split, after=()):
    seqs, rows, _ = dn.shape
    return call(
        gated_back_kernel,
        "gated_back",
        seqs,
        (dn, mo, z, gain, xbc, cum, cols),
        [
            seq_block(rows, DI),
            seq_block(rows, DI),
            seq_block(rows, DI),
            whole_block(1, DI),
            c_block(rows),
            seq_block(rows, LANES),
            seq_block(rows, LANES),
        ],
        [
            ((seqs, rows, DI), BF16),
            ((seqs, rows, split), BF16),
            ((seqs, rows, DI - split), BF16),
            ((seqs, STATE_ROWS, DI), BF16),
        ],
        [
            seq_block(rows, DI),
            seq_block(rows, split),
            seq_block(rows, DI - split),
            seq_block(STATE_ROWS, DI),
        ],
        [pltpu.VMEM((rows, DI), F32)],
        after=after,
    )


def inside_back_kernel(
    xbc_ref, xd_ref, cum_ref, cols_ref, rows_ref, skip_ref, spread_ref, dy_ref, mo_ref, prev_ref,
    dxd_ref, dbc_ref, sums_ref, dcouple_ref,
):
    rows = xbc_ref.shape[1]
    cum = cum_ref[0]
    flow = jnp.exp(cum) * cols_ref[0, :, 4:5]
    sums = jnp.zeros((rows, LANES), F32)
    dc = jnp.zeros((rows, NS), F32)
    for i in range(DI // LANES):
        lanes = tile_of(i)
        dy = dy_ref[0, :, lanes].astype(F32)
        plain = mo_ref[0, :, lanes] - xbc_ref[0, :, lanes].astype(F32) * skip_ref[0:1, lanes]
        sums = sums + sum_heads(dy * plain, spread_ref[:, lanes])
        dc = dc + dot_nt((dy * two_heads(flow, i)).astype(BF16), prev_ref[0, :, lanes])
    sums_ref[0] = sums
    b_rows, c_rows = xbc_ref[0, :, DI : DI + NS], xbc_ref[0, :, DI + NS :]
    seg_col, seg_row = cols_ref[0, :, 5:6], rows_ref[0, 0:1, :]
    row_at = lax.broadcasted_iota(jnp.int32, (rows, rows), 0)
    col_at = lax.broadcasted_iota(jnp.int32, (rows, rows), 1)
    keep = (seg_col == seg_row) & (row_at <= col_at)
    couple = jnp.where(keep, dot_nt(b_rows, c_rows), 0.0)
    dcouple_ref[...] = jnp.zeros_like(dcouple_ref)
    cum_rows = cum.T
    for first in range(0, H, 2):
        lanes = slice(first * P_SIZE, (first + 2) * P_SIZE)
        dy_sides = side_by_side(dy_ref[0, :, lanes])
        xd = xd_ref[0, :, lanes]
        for begin, end, _ in row_parts(rows):
            dxd, added = [], []
            for h, dy in zip((first, first + 1), dy_sides):
                decay = jnp.exp(jnp.minimum(cum_rows[h : h + 1, begin:] - cum[begin:end, h : h + 1], 0.0))
                mixing = (decay * couple[begin:end, begin:]).astype(BF16)
                dxd.append(dot_nn(mixing, dy[begin:]))
                added.append(dot_nt(xd[begin:end], dy[begin:]) * decay)
            dcouple_ref[begin:end, begin:] += added[0] + added[1]
            dxd_ref[0, begin:end, lanes] = dxd[0] + dxd[1]
    dcouple = jnp.where(keep, dcouple_ref[...], 0.0).astype(BF16)
    dbc_ref[0, :, :NS] = dot_nn(dcouple, c_rows)
    dbc_ref[0, :, NS:] = dc + dot_tn(dcouple, b_rows)


def inside_back(xbc, xd, cum, cols, rows_in, skip, spread, dy, mo, prev, after=()):
    seqs, rows, width = xbc.shape
    return call(
        inside_back_kernel,
        "inside_back",
        seqs,
        (xbc, xd, cum, cols, rows_in, skip, spread, dy, mo, prev),
        [
            seq_block(rows, width),
            seq_block(rows, DI),
            seq_block(rows, LANES),
            seq_block(rows, LANES),
            seq_block(8, rows),
            whole_block(8, DI),
            whole_block(LANES, DI),
            seq_block(rows, DI),
            seq_block(rows, DI),
            seq_block(NS, DI),
        ],
        [((seqs, rows, DI), F32), ((seqs, rows, 2 * NS), F32), ((seqs, rows, LANES), F32)],
        [seq_block(rows, DI), seq_block(rows, 2 * NS), seq_block(rows, LANES)],
        [pltpu.VMEM((rows, rows), F32)],
        after=after,
    )


def mix_end_kernel(
    left_ref, right_ref, halo_ref, xbc_ref, slope_ref, xd_ref, step_ref, cum_ref, cols_ref, heads_ref, skip_ref,
    conv_ref, spread_ref, dy_ref, dxd_ref, dbc_ref, sums_ref, later_ref, prev_ref,
    grad_ref, gconv_ref, gheads_ref, dco_ref, tops_ref,
):
    rows = xbc_ref.shape[1]
    cum = cum_ref[0]
    step = step_ref[0]
    masks = cols_ref[0]
    last = cum[rows - 1 : rows]
    ends = jnp.exp(last - cum) * masks[:, 3:4]
    b_rows = xbc_ref[0, :, DI : DI + NS]
    direct = jnp.zeros((rows, LANES), F32)
    columns = jnp.zeros((rows, LANES), F32)
    db = dbc_ref[0, :, :NS]
    for i in range(DI // LANES):
        lanes = tile_of(i)
        x = xbc_ref[0, :, lanes].astype(F32)
        xd = xd_ref[0, :, lanes].astype(F32)
        dy = dy_ref[0, :, lanes].astype(F32)
        later = later_ref[0, :, lanes]
        to_end = two_heads(ends, i)
        from_end = dot_nn(b_rows, later) * to_end
        dxd = dxd_ref[0, :, lanes] + from_end
        dco_ref[:, lanes] = dxd * two_heads(step, i) + dy * skip_ref[0:1, lanes]
        db = db + dot_nt((xd * to_end).astype(BF16), later)
        direct = direct + dot_nt((x * dxd).astype(BF16), spread_ref[:, lanes])
        columns = columns + sum_heads(xd * dxd, spread_ref[:, lanes])
        tops_ref[:, lanes] = jnp.concatenate(
            [
                jnp.sum(xd * from_end, axis=0, keepdims=True),
                jnp.sum(dy * x, axis=0, keepdims=True),
                jnp.sum(later.astype(F32) * prev_ref[0, :, lanes].astype(F32), axis=0, keepdims=True),
                jnp.zeros((13, LANES), F32),
            ],
            0,
        )
    dco_ref[:, DI : DI + NS] = db
    dco_ref[:, DI + NS :] = dbc_ref[0, :, NS:]
    tops = sum_heads(tops_ref[...], spread_ref[...])
    ended, skipped, carried = tops[0:1], tops[1:2], tops[2:3]
    at = lax.broadcasted_iota(jnp.int32, (rows, LANES), 0)
    dcum = sums_ref[0] - columns
    dcum = dcum + jnp.where(at == rows - 1, ended + jnp.exp(last) * carried, 0.0)
    da = exact_sum(triangle(rows, False), dcum)
    rate = heads_ref[1:2]
    graw = (direct + da * rate) * sigmoid(raw_tile(right_ref) + heads_ref[0:1])
    seqs = grad_ref.shape[0] // (rows + HALO)
    seq = pl.program_id(0)
    main = pl.ds(pl.multiple_of(seq * rows, rows), rows)
    edge = pl.ds(pl.multiple_of(seqs * rows + seq * HALO, HALO), HALO)
    end = CONV_WIDTH + LANES
    grad_ref[main, CONV_WIDTH:end] = graw.astype(BF16)
    grad_ref[edge, CONV_WIDTH:end] = jnp.zeros((HALO, LANES), BF16)
    grad_ref[main, end:] = jnp.zeros((rows, grad_ref.shape[1] - end), BF16)
    grad_ref[edge, end:] = jnp.zeros((HALO, grad_ref.shape[1] - end), BF16)
    gheads_ref[0] = jnp.concatenate(
        [
            jnp.sum(graw, axis=0, keepdims=True),
            jnp.sum(da * step, axis=0, keepdims=True) * rate,
            skipped,
            jnp.zeros((5, LANES), F32),
        ],
        0,
    )
    wide = [jnp.broadcast_to(masks[:, k : k + 1], (rows, LANES)) for k in range(KC - 1)]
    blank = jnp.zeros((HALO, LANES), F32)
    for i in range(CONV_WIDTH // LANES):
        lanes = tile_of(i)
        du = dco_ref[:, lanes] * slope_ref[0, :, lanes].astype(F32)
        own = conv_tile(left_ref, right_ref, i)
        ext = jnp.concatenate([halo_ref[0, :, lanes].astype(F32), own], 0)
        taps = conv_ref[:, lanes]
        grads = []
        total = jnp.zeros((rows + HALO, LANES), F32)
        for k in range(KC):
            part = du * wide[k] if k < KC - 1 else du
            at_ext = HALO - (KC - 1) + k
            grads.append(jnp.sum(part * ext[at_ext : at_ext + rows], axis=0, keepdims=True))
            padded = jnp.concatenate([blank, part, blank], 0)
            total = total + taps[k : k + 1] * padded[KC - 1 - k : KC - 1 - k + rows + HALO]
        grad_ref[main, lanes] = total[HALO:].astype(BF16)
        grad_ref[edge, lanes] = total[:HALO].astype(BF16)
        gconv_ref[0, :, lanes] = jnp.concatenate(
            grads + [jnp.sum(du, axis=0, keepdims=True), jnp.zeros((3, LANES), F32)], 0
        )


def mix_end(
    left, right, halo, xbc, slope, xd, step, cum, cols, heads, skip, conv, spread, dy, dxd, dbc, sums, later, prev,
    after=(),
):
    seqs, rows, width = xbc.shape
    tokens = seqs * (rows + HALO)
    return call(
        mix_end_kernel,
        "mix_end",
        seqs,
        (left, right, halo, xbc, slope, xd, step, cum, cols, heads, skip, conv, spread, dy, dxd, dbc, sums, later, prev),
        [
            seq_block(rows, LEFT),
            seq_block(rows, LEFT),
            seq_block(HALO, halo.shape[2]),
            seq_block(rows, width),
            seq_block(rows, width),
            seq_block(rows, DI),
            seq_block(rows, LANES),
            seq_block(rows, LANES),
            seq_block(rows, LANES),
            whole_block(8, LANES),
            whole_block(8, DI),
            whole_block(8, width),
            whole_block(LANES, DI),
            seq_block(rows, DI),
            seq_block(rows, DI),
            seq_block(rows, 2 * NS),
            seq_block(rows, LANES),
            seq_block(NS, DI),
            seq_block(NS, DI),
        ],
        [
            ((tokens, 2 * LEFT), BF16),
            ((seqs, 8, width), F32),
            ((seqs, 8, LANES), F32),
        ],
        [
            whole_block(tokens, 2 * LEFT),
            seq_block(8, width),
            seq_block(8, LANES),
        ],
        [pltpu.VMEM((rows, width), F32), pltpu.VMEM((16, DI), F32)],
        after=after,
    )


def attend_bias(slot, rest, cols_ref, rows_ref, kv_ref, offsets):
    rows = cols_ref.shape[1]
    found = []
    for before in range(slot + 1):
        for j, offset in enumerate(offsets):
            if before == slot and offset == 0:
                row_at = lax.broadcasted_iota(jnp.int32, (rows, rows), 0)
                col_at = lax.broadcasted_iota(jnp.int32, (rows, rows), 1)
                same = cols_ref[slot, :, 5:6] == rows_ref[slot, 0:1, :]
                allowed = same & (row_at >= col_at)
            else:
                keys = kv_ref[j][before, rows : rows + 16, :rows].astype(F32)[0:1]
                if before == slot:
                    keys = keys * jnp.where((rest ^ offset) < rest, 1.0, 0.0)
                allowed = cols_ref[slot, :, 4:5] * keys > 0.5
            found.append((j, before, jnp.where(allowed, 0.0, NEGATIVE)))
    return found


def swap_halves(pair):
    return jnp.concatenate([pair[:, P_SIZE:], pair[:, :P_SIZE]], 1)


def to_side(pair, group):
    pair_sides, swapped = side_by_side(pair), side_by_side(swap_halves(pair))
    return (pair_sides[0], swapped[0]) if group == 0 else (swapped[1], pair_sides[1])


def from_side(left, right, group):
    lane = lax.broadcasted_iota(jnp.int32, left.shape, 1)
    if group == 0:
        right = swap_halves(right)
    else:
        left = swap_halves(left)
    return jnp.where(lane < P_SIZE, left, right)


def attend_kernel(offsets, rest_ref, q_ref, cols_ref, rows_ref, *refs):
    kv_ref, (out_ref, lse_ref) = refs[:-2], refs[-2:]
    rows = q_ref.shape[1]
    for slot in range(SLOTS):
        blocks = attend_bias(slot, rest_ref[0], cols_ref, rows_ref, kv_ref, offsets)
        sums = []
        for i in range(QUERY_HEADS // 2):
            lanes, group = tile_of(i), (2 * i) // (QUERY_HEADS // KEY_VALUE_HEADS)
            outs = []
            for q in to_side(q_ref[slot, :, lanes] * jnp.asarray(HEAD_WIDTH**-0.5, BF16), group):
                scores = [dot_nt(q, kv_ref[j][n, :rows, :LANES]) + bias for j, n, bias in blocks]
                top = jnp.max(functools.reduce(jnp.maximum, scores), axis=1, keepdims=True)
                weights = [jnp.exp(s - top) for s in scores]
                total = jnp.sum(functools.reduce(jnp.add, weights), axis=1, keepdims=True)
                out = [
                    dot_nn(w.astype(BF16), kv_ref[j][n, :rows, LANES:]) for (j, n, _), w in zip(blocks, weights)
                ]
                outs.append(functools.reduce(jnp.add, out) / total)
                sums.append(top + jnp.log(total))
            out_ref[slot, :, lanes] = from_side(*outs, group).astype(BF16)
        lse_ref[slot] = jnp.concatenate(sums + [jnp.zeros((rows, LANES - QUERY_HEADS), F32)], 1)


def call_whole(kernel, name, scalars, ins, outs, scratch=(), after=()):
    vmem = pl.BlockSpec(memory_space=pltpu.VMEM)
    n_in = len(scalars) + len(ins)

    def run(*refs):
        kernel(*refs[:n_in], *refs[n_in + len(after) :])

    return pl.pallas_call(
        run,
        in_specs=[pl.BlockSpec(memory_space=pltpu.SMEM)] * len(scalars) + [vmem] * len(ins) + spec_any(len(after)),
        out_specs=[vmem] * len(outs),
        out_shape=[jax.ShapeDtypeStruct(s, d) for s, d in outs],
        scratch_shapes=list(scratch),
        compiler_params=pltpu.CompilerParams(vmem_limit_bytes=VMEM_LIMIT),
        name=name,
    )(*scalars, *ins, *after)


def attend(rest, q, kv, cols, rows_in, offsets, after=()):
    outs = [(q.shape, BF16), (q.shape[:2] + (LANES,), F32)]
    return call_whole(
        functools.partial(attend_kernel, offsets), "attend", (rest,), (q, cols, rows_in, *kv), outs, after=after
    )


def attend_back_kernel(
    offsets, rest_ref, q_ref, cols_ref, rows_ref, out_ref, lse_ref, dout_ref, *refs
):
    count = len(offsets)
    kv_ref, dq_ref, dkv_ref, acc_ref = refs[:count], refs[count], refs[count + 1 : -1], refs[-1]
    rows = q_ref.shape[1]
    scale = HEAD_WIDTH**-0.5
    acc_ref[...] = jnp.zeros_like(acc_ref)
    for slot in range(SLOTS):
        blocks = attend_bias(slot, rest_ref[0], cols_ref, rows_ref, kv_ref, offsets)
        for i in range(QUERY_HEADS // 2):
            lanes, group = tile_of(i), (2 * i) // (QUERY_HEADS // KEY_VALUE_HEADS)
            q_pair = q_ref[slot, :, lanes] * jnp.asarray(scale, BF16)
            dout_pair = dout_ref[slot, :, lanes]
            q_turned, dout_turned = q_pair.T, dout_pair.T
            product = dout_pair.astype(F32) * out_ref[slot, :, lanes].astype(F32)
            q_sides, dout_sides = to_side(q_pair, group), to_side(dout_pair, group)
            k_rows = slice(group * HEAD_WIDTH, (group + 1) * HEAD_WIDTH)
            v_rows = slice(LANES + group * HEAD_WIDTH, LANES + (group + 1) * HEAD_WIDTH)
            dqs = []
            for n in range(2):
                own = slice(n * HEAD_WIDTH, (n + 1) * HEAD_WIDTH)
                q, dout = q_sides[n], dout_sides[n]
                delta = jnp.sum(side_by_side(product)[n], axis=1, keepdims=True)
                lse = lse_ref[slot, :, 2 * i + n : 2 * i + n + 1]
                dq = None
                for j, before, bias in blocks:
                    k, v = kv_ref[j][before, :rows, :LANES], kv_ref[j][before, :rows, LANES:]
                    p = jnp.exp(dot_nt(q, k) + bias - lse)
                    ds = (p * (dot_nt(dout, v) - delta)).astype(BF16)
                    part = dot_nn(ds, k)
                    dq = part if dq is None else dq + part
                    acc_ref[j, before, k_rows, :] += dot_nn(q_turned[own], ds)
                    acc_ref[j, before, v_rows, :] += dot_nn(dout_turned[own], p.astype(BF16))
                dqs.append(dq * scale)
            dq_ref[slot, :, lanes] = from_side(*dqs, group).astype(BF16)
    for j in range(len(offsets)):
        for before in range(SLOTS):
            dkv_ref[j][before] = acc_ref[j, before].T.astype(BF16)


def attend_back(rest, q, kv, cols, rows_in, out, lse, dout, offsets, after=()):
    rows, blocks, (slots, _, kv_width) = q.shape[1], len(kv), kv[0].shape
    found = call_whole(
        functools.partial(attend_back_kernel, offsets),
        "attend_back",
        (rest,),
        (q, cols, rows_in, out, lse, dout, *kv),
        [(q.shape, BF16)] + [((slots, rows, kv_width), BF16)] * blocks,
        [pltpu.VMEM((blocks, slots, kv_width, rows), F32)],
        after=after,
    )
    return found[0], found[1:]


def pick_offset(rest, number, group, offsets, pieces, slot):
    wanted = (number % group) ^ rest
    found = None
    for offset, piece in zip(offsets, pieces):
        part = piece[slot].astype(F32)
        found = part if found is None else jnp.where(wanted == offset, part, found)
    return found


def halo_kernel(offsets, rest_ref, *refs):
    pieces, out_ref = refs[:-1], refs[-1]
    rest, group = rest_ref[0], len(pieces)
    for slot in range(SLOTS):
        found = jnp.zeros(out_ref.shape[1:], F32)
        for number in range(group * slot, group * (slot + 1)):
            if number > 0:
                before = number - 1
                part = pick_offset(rest, before, group, offsets, pieces, before // group)
                found = jnp.where(rest == number % group, part, found)
        out_ref[slot] = found.astype(out_ref.dtype)


def take_halo(rest, pieces, offsets):
    return call_whole(
        functools.partial(halo_kernel, offsets), "halo", (rest,), pieces, [(pieces[0].shape, pieces[0].dtype)]
    )[0]


def scan_kernel(offsets, from_earlier, rest_ref, *refs):
    pieces, out_ref = refs[:-1], refs[-1]
    rest, group = rest_ref[0], len(pieces)
    order = list(range(SLOTS * group))
    width = 4 * LANES

    def column(i, _):
        lanes = pl.ds(pl.multiple_of(i * width, width), width)
        state = jnp.zeros((NS, width), F32)
        found = [state] * SLOTS
        for number in order if from_earlier else order[::-1]:
            slot = number // group
            found[slot] = jnp.where(rest == number % group, state, found[slot])
            part = pick_offset(rest, number, group, offsets, [p.at[:, :, lanes] for p in pieces], slot)
            state = part[:NS] + part[NS : NS + 1] * state
        for slot in range(SLOTS):
            out_ref[slot, :, lanes] = found[slot].astype(BF16)
        return 0

    lax.fori_loop(0, DI // width, column, 0)


def scan_states(rest, pieces, offsets, from_earlier, after=()):
    return call_whole(
        functools.partial(scan_kernel, offsets, from_earlier),
        "scan_states",
        (rest,),
        pieces,
        [((SLOTS, NS, DI), BF16)],
        after=after,
    )[0]


def join_grads_kernel(za_ref, zb_ref, q_ref, own_ref, got_ref, out_ref):
    slots, rows, width = own_ref.shape
    at = 0
    for ref in (za_ref, zb_ref, q_ref):
        out_ref[:, at : at + ref.shape[1]] = ref[...]
        at += ref.shape[1]
    for s in range(slots):
        total = own_ref[s].astype(F32) + got_ref[s].astype(F32)
        out_ref[s * rows : (s + 1) * rows, at:] = total.astype(BF16)


def join_grads(za, zb, q, own, got, after=()):
    tokens = za.shape[0]
    width = za.shape[1] + zb.shape[1] + q.shape[1] + own.shape[2]
    return call_whole(
        join_grads_kernel, "join_grads", (), (za, zb, q, own, got), [((tokens, width), BF16)], after=after
    )[0]


def line_place(j, count, r):
    stride = LANES // -(-count // r)
    return j % r, stride * (j // r)


def pack_lines(rows_of, r):
    count = len(rows_of)
    stride = LANES // -(-count // r)
    groups = []
    for begin in range(0, count, r):
        part = [
            jnp.concatenate([v, jnp.zeros((1, stride - v.shape[1]), F32)], 1) for v in rows_of[begin : begin + r]
        ]
        if len(part) < r:
            part.append(jnp.zeros((r - len(part), stride), F32))
        groups.append(jnp.concatenate(part, 0))
    tile = jnp.concatenate(groups, 1) if len(groups) > 1 else groups[0]
    if tile.shape[1] < LANES:
        tile = jnp.concatenate([tile, jnp.zeros((r, LANES - tile.shape[1]), F32)], 1)
    return tile


def pack_first_kernel(xbc_ref, step_ref, conv_ref, bias_ref, mix_ref, one_ref, two_ref, out_ref):
    r = xbc_ref.shape[0]
    over = CONV_WIDTH - LEFT
    out_ref[0] = xbc_ref[:, :LEFT]
    out_ref[1, :, :over] = xbc_ref[:, LEFT:]
    blank = jnp.zeros((r, LANES - H), BF16)
    out_ref[1, :, over : over + LANES] = jnp.concatenate([step_ref[...], blank], 1)
    taps = conv_ref[...].astype(F32)
    vectors = [taps[k : k + 1] for k in range(KC)]
    vectors += [ref[...].astype(F32) for ref in (bias_ref, mix_ref, one_ref, two_ref)]
    out_ref[1, :, over + LANES :] = pack_lines(vectors, r).astype(BF16)


def pack_first(w_xbc, w_step, conv_weight, conv_bias, mixer_gain, norm1_gain, norm2_gain):
    r = w_xbc.shape[0]
    vmem = pl.BlockSpec(memory_space=pltpu.VMEM)
    return pl.pallas_call(
        pack_first_kernel,
        in_specs=[vmem] * 7,
        out_specs=vmem,
        out_shape=jax.ShapeDtypeStruct((2, r, LEFT), BF16),
        name="pack_first",
    )(w_xbc, w_step, conv_weight, conv_bias[None], mixer_gain[None], norm1_gain[None], norm2_gain[None])


def pack_two_kernel(z_ref, query_ref, kv_ref, mix_ref, attn_ref, two_ref):
    r = z_ref.shape[0]
    width = two_ref.shape[2] - MODEL_WIDTH
    two_ref[0, :, :width] = z_ref[:, :width]
    two_ref[1, :, : DI - width] = z_ref[:, width:]
    at = DI - width + query_ref.shape[1]
    two_ref[1, :, DI - width : at] = query_ref[...]
    two_ref[1, :, at:width] = kv_ref[...]
    more = mix_ref.shape[0] - r
    two_ref[0, :, width:] = mix_ref[:r]
    two_ref[1, :more, width:] = mix_ref[r:]
    two_ref[1, more:, width:] = attn_ref[...]


def pack_two(w_gate_z, w_query, key_value_weight, w_mix_out, w_attn_out, after=()):
    width = (DI + w_query.shape[1] + key_value_weight.shape[1]) // 2 + MODEL_WIDTH
    ins = (w_gate_z, w_query, key_value_weight, w_mix_out, w_attn_out)
    return call_whole(pack_two_kernel, "pack_two", (), ins, [((2, w_gate_z.shape[0], width), BF16)], after=after)[0]


def pack_units_kernel(gate_up_ref, down_ref, units_ref):
    r, half = gate_up_ref.shape[0], down_ref.shape[0] // 2
    for n in range(2):
        for q in range(2):
            column = (2 * n + q) * MODEL_WIDTH
            units_ref[n, q * r : (q + 1) * r] = gate_up_ref[:, column : column + MODEL_WIDTH]
        units_ref[n, 2 * r :] = down_ref[n * half : (n + 1) * half]


def pack_units(w_gate_up, w_down, after=()):
    shape = (2, 2 * w_gate_up.shape[0] + w_down.shape[0] // 2, MODEL_WIDTH)
    return call_whole(pack_units_kernel, "pack_units", (), (w_gate_up, w_down), [(shape, BF16)], after=after)[0]


def unpack_small_kernel(r, small_ref, conv_ref, mix_ref, gain_ref):
    count = small_ref.shape[0] // r
    widths = [CONV_WIDTH // count] * (KC + 1) + [DI // count] + [MODEL_WIDTH // count] * 2
    found = [[] for _ in widths]
    for i in range(count):
        tile = small_ref[i * r : (i + 1) * r, :].astype(F32)
        for j, width in enumerate(widths):
            row, lane = line_place(j, len(widths), r)
            found[j].append(tile[row : row + 1, lane : lane + width])
    found = [jnp.concatenate(v, 1) for v in found]
    conv_ref[...] = jnp.concatenate(found[: KC + 1] + [jnp.zeros((3, CONV_WIDTH), F32)], 0)
    mix_ref[...] = found[KC + 1]
    gain_ref[...] = jnp.concatenate(found[KC + 2 :], 0)


def unpack_small(small, r):
    vmem = pl.BlockSpec(memory_space=pltpu.VMEM)
    return pl.pallas_call(
        functools.partial(unpack_small_kernel, r),
        in_specs=[vmem],
        out_specs=[vmem] * 3,
        out_shape=[jax.ShapeDtypeStruct(s, F32) for s in ((8, CONV_WIDTH), (1, DI), (2, MODEL_WIDTH))],
        name="unpack_small",
    )(small)


def small_grads_kernel(r, offsets, place_ref, conv_ref, heads_ref, keep_ref, send_ref, tile_ref):
    count = tile_ref.shape[0]
    conv = jnp.sum(conv_ref[...], 0)
    heads = jnp.sum(heads_ref[...], 0)
    width = CONV_WIDTH // count
    shared = [heads[k : k + 1, :H] for k in range(3)]
    high = [v.astype(BF16).astype(F32) for v in shared]
    shared = high + [v - h for v, h in zip(shared, high)]
    for i in range(count):
        own = [conv[k : k + 1, i * width : (i + 1) * width] for k in range(KC + 1)]
        tile_ref[i] = pack_lines(own + shared, r)
    place = place_ref[0]
    for t, offset in enumerate(offsets):
        keep_ref[t * r : (t + 1) * r] = tile_ref[place ^ offset].astype(BF16)
        send_ref[t * r : (t + 1) * r] = tile_ref[place ^ (offset ^ 1)].astype(BF16)


def small_grads(r, conv, heads):
    bits = bit_count()
    count = 1 << bits
    vmem = pl.BlockSpec(memory_space=pltpu.VMEM)
    return pl.pallas_call(
        functools.partial(small_grads_kernel, r, turned_offsets(bits)),
        in_specs=[pl.BlockSpec(memory_space=pltpu.SMEM)] + [vmem] * 2,
        out_specs=[vmem] * 2,
        out_shape=[jax.ShapeDtypeStruct((count // 2 * r, LANES), BF16)] * 2,
        scratch_shapes=[pltpu.VMEM((count, r, LANES), F32)],
        name="small_grads",
    )(place_of().reshape(1).astype(jnp.int32), conv, heads)


def tiles_spec(shape, axis, width):
    block = tuple(width if n == axis else size for n, size in enumerate(shape))
    return pl.BlockSpec(block, lambda i: tuple(i if n == axis else 0 for n in range(len(shape))))


def fixed(*shape):
    return pl.BlockSpec(shape, lambda i: (0,) * len(shape))


def dense(kernel, name, steps, ins, in_specs, outs, out_specs, scratch=(), after=()):
    n_in, n_after = len(ins), len(after)

    def run(*refs):
        kernel(*refs[:n_in], *refs[n_in + n_after :])

    return pl.pallas_call(
        run,
        grid=(steps,),
        in_specs=list(in_specs) + spec_any(n_after),
        out_specs=out_specs,
        out_shape=[jax.ShapeDtypeStruct(s, d) for s, d in outs],
        scratch_shapes=list(scratch),
        compiler_params=pltpu.CompilerParams(vmem_limit_bytes=VMEM_LIMIT),
        name=name,
    )(*ins, *after)


def row_scale(values):
    return lax.rsqrt(jnp.mean(values * values, axis=1, keepdims=True) + EPSILON)


def first_proj_kernel(x_ref, gain_ref, left_w, right_w, cols_ref, normed_ref, left_ref, right_ref, tails_ref):
    step, tile = pl.program_id(0), left_w.shape[1]

    @pl.when(step == 0)
    def _():
        x = x_ref[...].astype(F32)
        normed_ref[...] = (x * row_scale(x) * gain_ref[...]).astype(BF16)

    left = dot_nn(normed_ref[...], left_w[...]).astype(BF16)
    right = dot_nn(normed_ref[...], right_w[...])
    left_ref[...] = left
    right_ref[...] = right
    slots, rows, _ = cols_ref.shape
    lanes = pl.ds(pl.multiple_of(step * tile, tile), tile)
    for s in range(slots):
        begin, end = (s + 1) * rows - HALO, (s + 1) * rows
        edge = cols_ref[s, rows - HALO :, 3:4]
        tails_ref[s, :, lanes] = (left[begin:end].astype(F32) * edge).astype(BF16)
        normed = normed_ref[begin:end, lanes].astype(F32)
        tails_ref[s, :, pl.ds(pl.multiple_of(CONV_WIDTH + step * tile, tile), tile)] = (normed * edge).astype(BF16)

        @pl.when(step < (CONV_WIDTH - LEFT) // tile)
        def _():
            at = pl.ds(pl.multiple_of(LEFT + step * tile, tile), tile)
            tails_ref[s, :, at] = (right[begin:end].astype(BF16).astype(F32) * edge).astype(BF16)


def first_proj(x, gain, left_full, right_full, cols, after=()):
    tokens, width = x.shape
    tile = LEFT // 4
    tails = (cols.shape[0], HALO, CONV_WIDTH + width)
    return dense(
        first_proj_kernel,
        "first_proj",
        4,
        (x, gain, left_full, right_full, cols),
        [
            fixed(tokens, width),
            fixed(1, width),
            tiles_spec((width, LEFT), 1, tile),
            tiles_spec((width, LEFT), 1, tile),
            fixed(*cols.shape),
        ],
        [((tokens, width), BF16), ((tokens, LEFT), BF16), ((tokens, LEFT), F32), (tails, BF16)],
        [
            fixed(tokens, width),
            tiles_spec((tokens, LEFT), 1, tile),
            tiles_spec((tokens, LEFT), 1, tile),
            fixed(*tails),
        ],
        after=after,
    )


def second_proj_kernel(normed_ref, z_w, qkv_w, rows_ref, z_ref, q_ref, kv_ref):
    step = pl.program_id(0)
    z_ref[...] = dot_nn(normed_ref[...], z_w[...])
    part = dot_nn(normed_ref[...], qkv_w[...]).astype(BF16)
    slots, extended, width = kv_ref.shape
    rows = extended - 16

    @pl.when(step < 2)
    def _():
        q_ref[...] = part

    @pl.when(step == 2)
    def _():
        for s in range(slots):
            kv_ref[s, :rows] = part[s * rows : (s + 1) * rows]
            keys = jnp.broadcast_to(rows_ref[s, 1:2], (16, rows))
            if rows < width:
                keys = jnp.concatenate([keys, jnp.zeros((16, width - rows), F32)], 1)
            kv_ref[s, rows:] = keys.astype(BF16)


def second_proj(normed, z_full, qkv_full, rows_in, after=()):
    tokens, width = normed.shape
    slots, _, rows = rows_in.shape
    query, kv = QUERY_HEADS * HEAD_WIDTH, 2 * KEY_VALUE_HEADS * HEAD_WIDTH
    return dense(
        second_proj_kernel,
        "second_proj",
        3,
        (normed, z_full, qkv_full, rows_in),
        [
            fixed(tokens, width),
            tiles_spec((width, DI), 1, DI // 3),
            tiles_spec((width, query + kv), 1, kv),
            fixed(slots, 8, rows),
        ],
        [((tokens, DI), F32), ((tokens, query), BF16), ((slots, rows + 16, kv), BF16)],
        [
            tiles_spec((tokens, DI), 1, DI // 3),
            pl.BlockSpec((tokens, kv), lambda i: (0, jnp.minimum(i, 1))),
            fixed(slots, rows + 16, kv),
        ],
        after=after,
    )


def out_proj_kernel(x_ref, nm_ref, attn_ref, mix_w, attn_w, gain_ref, resid_ref, normed_ref):
    step = pl.program_id(0)
    part = dot_nn(nm_ref[...], mix_w[...]) + dot_nn(attn_ref[...], attn_w[...])

    @pl.when(step == 0)
    def _():
        resid_ref[...] = x_ref[...].astype(F32) + part

    @pl.when(step > 0)
    def _():
        resid_ref[...] += part

    @pl.when(step == pl.num_programs(0) - 1)
    def _():
        resid = resid_ref[...]
        normed_ref[...] = (resid * row_scale(resid) * gain_ref[...]).astype(BF16)


def out_proj(x, nm, attn, mix_full, attn_full, gain, after=()):
    tokens, width = x.shape
    query = attn.shape[1]
    steps = 2
    return dense(
        out_proj_kernel,
        "out_proj",
        steps,
        (x, nm, attn, mix_full, attn_full, gain),
        [
            fixed(tokens, width),
            tiles_spec(nm.shape, 1, DI // steps),
            tiles_spec(attn.shape, 1, query // steps),
            tiles_spec(mix_full.shape, 0, DI // steps),
            tiles_spec(attn_full.shape, 0, query // steps),
            fixed(1, width),
        ],
        [((tokens, width), F32), ((tokens, width), BF16)],
        [fixed(tokens, width), fixed(tokens, width)],
        after=after,
    )


def gate_up_kernel(normed_ref, gate_w, up_w, act_ref, swish_ref, slope_ref):
    gate = dot_nn(normed_ref[...], gate_w[...])
    up = dot_nn(normed_ref[...], up_w[...])
    sig = sigmoid(gate)
    swish = gate * sig
    act_ref[...] = (swish * up).astype(BF16)
    swish_ref[...] = swish.astype(BF16)
    slope_ref[...] = ((sig + swish * (1.0 - sig)) * up).astype(BF16)


def gate_up(normed, gate_full, up_full, after=()):
    tokens, width = normed.shape
    tile = FF // 2
    spec = tiles_spec((tokens, FF), 1, tile)
    return dense(
        gate_up_kernel,
        "gate_up",
        2,
        (normed, gate_full, up_full),
        [fixed(tokens, width), tiles_spec((width, FF), 1, tile), tiles_spec((width, FF), 1, tile)],
        [((tokens, FF), BF16)] * 3,
        [spec] * 3,
        after=after,
    )


def down_kernel(act_ref, swish_ref, slope_ref, down_w, resid_ref, grad_ref, out_ref, dgate_ref, dup_ref, total_ref):
    step = pl.program_id(0)
    weights = down_w[...]
    part = dot_nn(act_ref[...], weights)

    @pl.when(step == 0)
    def _():
        total_ref[...] = resid_ref[...] + part

    @pl.when(step > 0)
    def _():
        total_ref[...] += part

    @pl.when(step == pl.num_programs(0) - 1)
    def _():
        out_ref[...] = total_ref[...].astype(BF16)

    dact = dot_nt(grad_ref[...], weights)
    dgate_ref[...] = (dact * slope_ref[...].astype(F32)).astype(BF16)
    dup_ref[...] = (dact * swish_ref[...].astype(F32)).astype(BF16)


def down(act, swish, slope, down_full, resid, grad_out, after=()):
    tokens, width = resid.shape
    tile = FF // 2
    spec = tiles_spec((tokens, FF), 1, tile)
    return dense(
        down_kernel,
        "down",
        2,
        (act, swish, slope, down_full, resid, grad_out),
        [spec, spec, spec, tiles_spec((FF, width), 0, tile), fixed(tokens, width), fixed(tokens, width)],
        [((tokens, width), BF16), ((tokens, FF), BF16), ((tokens, FF), BF16)],
        [fixed(tokens, width), spec, spec],
        [pltpu.VMEM((tokens, width), F32)],
        after=after,
    )


def gate_up_back_kernel(
    dgate_ref, dup_ref, gate_w, up_w, resid_ref, gain_ref, grad_ref, back_ref, branch_ref, total_ref
):
    step = pl.program_id(0)
    part = dot_nt(dgate_ref[...], gate_w[...]) + dot_nt(dup_ref[...], up_w[...])

    @pl.when(step == 0)
    def _():
        total_ref[...] = part

    @pl.when(step > 0)
    def _():
        total_ref[...] += part

    @pl.when(step == pl.num_programs(0) - 1)
    def _():
        resid = resid_ref[...]
        scale = row_scale(resid)
        scaled = resid * scale
        dnormed = total_ref[...]
        dscaled = dnormed * gain_ref[...]
        mean = jnp.mean(dscaled * scaled, axis=1, keepdims=True)
        back = grad_ref[...].astype(F32) + (dscaled - scaled * mean) * scale
        back_ref[...] = back
        branch_ref[...] = back.astype(BF16)


def gate_up_back(dgate, dup, gate_full, up_full, resid, gain, grad_out, after=()):
    tokens, width = resid.shape
    tile = FF // 2
    spec, w_spec, whole = tiles_spec((tokens, FF), 1, tile), tiles_spec((width, FF), 1, tile), fixed(tokens, width)
    return dense(
        gate_up_back_kernel,
        "gate_up_back",
        2,
        (dgate, dup, gate_full, up_full, resid, gain, grad_out),
        [spec, spec, w_spec, w_spec, whole, fixed(1, width), whole],
        [((tokens, width), F32), ((tokens, width), BF16)],
        [whole, whole],
        [pltpu.VMEM((tokens, width), F32)],
        after=after,
    )


def out_back_kernel(branch_ref, mix_w, attn_w, dnm_ref, dattn_ref):
    dnm_ref[...] = dot_nt(branch_ref[...], mix_w[...])
    dattn_ref[...] = dot_nt(branch_ref[...], attn_w[...]).astype(BF16)


def out_back(branch, mix_full, attn_full, after=()):
    tokens, width = branch.shape
    query = attn_full.shape[0]
    steps = 2
    return dense(
        out_back_kernel,
        "out_back",
        steps,
        (branch, mix_full, attn_full),
        [
            fixed(tokens, width),
            tiles_spec(mix_full.shape, 0, DI // steps),
            tiles_spec(attn_full.shape, 0, query // steps),
        ],
        [((tokens, DI), F32), ((tokens, query), BF16)],
        [tiles_spec((tokens, DI), 1, DI // steps), tiles_spec((tokens, query), 1, query // steps)],
        after=after,
    )


def second_back_kernel(grad_ref, z_w, qkv_w, out_ref):
    out_ref[...] = dot_nt(grad_ref[:, :DI], z_w[...]) + dot_nt(grad_ref[:, DI:], qkv_w[...])


def second_back(grad, z_full, qkv_full, after=()):
    tokens, width = grad.shape[0], z_full.shape[0]
    tile = width // 2
    return dense(
        second_back_kernel,
        "second_back",
        2,
        (grad, z_full, qkv_full),
        [fixed(*grad.shape), tiles_spec(z_full.shape, 0, tile), tiles_spec(qkv_full.shape, 0, tile)],
        [((tokens, width), F32)],
        [tiles_spec((tokens, width), 1, tile)],
        after=after,
    )[0]


def first_back_kernel(grad_ref, left_w, right_w, part_ref, out_ref, edge_ref):
    tokens = part_ref.shape[0]
    total = dot_nt(grad_ref[:, :LEFT], left_w[...]) + dot_nt(grad_ref[:, LEFT:], right_w[...])
    out_ref[...] = total[:tokens] + part_ref[...]
    edge_ref[...] = total[tokens:]


def first_back(grad, left_full, right_full, part, after=()):
    tokens, width = part.shape
    ext = grad.shape[0]
    tile = width // 2
    w_spec = tiles_spec((width, LEFT), 0, tile)
    return dense(
        first_back_kernel,
        "first_back",
        2,
        (grad, left_full, right_full, part),
        [fixed(*grad.shape), w_spec, w_spec, tiles_spec((tokens, width), 1, tile)],
        [((tokens, width), F32), ((ext - tokens, width), F32)],
        [tiles_spec((tokens, width), 1, tile), tiles_spec((ext - tokens, width), 1, tile)],
        after=after,
    )


def input_back_kernel(gn_ref, next_ref, x_ref, gain_ref, resid_ref, out_ref, low_ref):
    rows = gn_ref.shape[0]
    x = x_ref[...].astype(F32)
    scale = row_scale(x)
    scaled = x * scale
    tail = gn_ref[rows - HALO :] + next_ref[0]
    dscaled = jnp.concatenate([gn_ref[: rows - HALO], tail], 0) * gain_ref[...]
    mean = jnp.mean(dscaled * scaled, axis=1, keepdims=True)
    total = resid_ref[...] + (dscaled - scaled * mean) * scale
    out_ref[0] = total
    low_ref[0] = total.astype(BF16)


def input_back(gn, from_next, x, gain, resid, after=()):
    slots = from_next.shape[0]
    rows, width = gn.shape[0] // slots, gn.shape[1]
    spec = pl.BlockSpec((rows, width), lambda s: (s, 0))
    return dense(
        input_back_kernel,
        "input_back",
        slots,
        (gn, from_next, x, gain, resid),
        [spec, seq_block(HALO, width), spec, fixed(1, width), spec],
        [((slots, rows, width), F32), ((slots, rows, width), BF16)],
        [seq_block(rows, width)] * 2,
        after=after,
    )


def pick_kernel(index_ref, block_ref, out_ref):
    out_ref[...] = block_ref[0]


def pick(block, index, after=()):
    n_after = len(after)

    def run(index_ref, block_ref, *refs):
        pick_kernel(index_ref, block_ref, refs[n_after])

    return pl.pallas_call(
        run,
        grid_spec=pltpu.PrefetchScalarGridSpec(
            num_scalar_prefetch=1,
            grid=(1,),
            in_specs=[pl.BlockSpec((1,) + block.shape[1:], lambda i, index: (index[0], 0, 0))] + spec_any(n_after),
            out_specs=pl.BlockSpec(block.shape[1:], lambda i, index: (0, 0)),
        ),
        out_shape=jax.ShapeDtypeStruct(block.shape[1:], block.dtype),
        name="pick",
    )(index.reshape(1).astype(jnp.int32), block, *after)


def merge_kernel(side_ref, block_ref, got_ref, out_ref):
    keep = pl.program_id(0) == side_ref[0]

    @pl.when(keep)
    def _():
        out_ref[0] = block_ref[0]

    @pl.when(jnp.logical_not(keep))
    def _():
        out_ref[0] = got_ref[...]


def merge(block, got, side, after=()):
    slots, rows, width = block.shape
    n_after = len(after)

    def run(side_ref, block_ref, got_ref, *refs):
        merge_kernel(side_ref, block_ref, got_ref, refs[n_after])

    return pl.pallas_call(
        run,
        grid=(slots,),
        in_specs=[
            pl.BlockSpec(memory_space=pltpu.SMEM),
            seq_block(rows, width),
            pl.BlockSpec((rows, width), lambda s: (0, 0)),
        ]
        + spec_any(n_after),
        out_specs=seq_block(rows, width),
        out_shape=jax.ShapeDtypeStruct(block.shape, block.dtype),
        name="merge",
    )(side.reshape(1).astype(jnp.int32), block, got, *after)


def fsdp_bits():
    return lax.axis_size("fsdp").bit_length() - 1


def fsdp_exchange(block, bit):
    return lax.ppermute(block, "fsdp", [(i, i ^ (1 << bit)) for i in range(lax.axis_size("fsdp"))])


def side_of():
    return lax.axis_index("fsdp") >> (fsdp_bits() - 1)


def swap_start(block):
    return fsdp_exchange(lax.dynamic_index_in_dim(block, 1 - side_of(), 0, False), fsdp_bits() - 1)


def swap_end(block, got):
    return lax.dynamic_update_index_in_dim(block, got.astype(block.dtype), 1 - side_of(), 0)


def gather_sequence(block):
    pieces, offsets = [block], [0]
    for bit in range(fsdp_bits() - 1):
        pieces = pieces + [fsdp_exchange(a, bit) for a in pieces]
        offsets = offsets + [o ^ (1 << bit) for o in offsets]
    return pieces, tuple(offsets)


def sum_sequence(blocks):
    blocks = list(blocks)
    for bit in range(fsdp_bits() - 2, -1, -1):
        half = len(blocks) // 2
        got = [fsdp_exchange(a, bit) for a in blocks[half:]]
        if half > 1:
            blocks = [(a.astype(F32) + b.astype(F32)).astype(BF16) for a, b in zip(blocks, got)]
        else:
            blocks = [blocks[0], got[0]]
    return blocks


def rest_place():
    return lax.axis_index("fsdp") & (lax.axis_size("fsdp") // 2 - 1)


def from_next_part(block):
    pieces, offsets = gather_sequence(block)
    group, rest = len(pieces), rest_place()
    found = [jnp.zeros(block.shape[1:], block.dtype)] * SLOTS
    for number in range(SLOTS * group - 1):
        slot, after = number // group, number + 1
        for offset, piece in zip(offsets, pieces):
            match = (rest == number % group) & ((after % group) ^ rest == offset)
            found[slot] = jnp.where(match, piece[after // group], found[slot])
    return jnp.stack(found)


def sequence_masks(segs):
    slots, rows = segs.shape
    behind = (lax.iota(jnp.int32, slots)[:, None] > 0) | (rest_place() > 0)
    first = (segs == segs[:, :1]) & behind
    keep_end = segs == segs[:, -1:]
    columns = []
    for k in range(KC - 1):
        back = KC - 1 - k
        inside = segs[:, back:] == segs[:, : rows - back]
        columns.append(jnp.concatenate([first[:, :back], inside], 1).astype(F32))
    columns += [keep_end.astype(F32), first.astype(F32), segs.astype(F32)]
    cols = jnp.stack(columns, 2)
    cols = jnp.pad(cols, ((0, 0), (0, 0), (0, LANES - cols.shape[2])))
    rows_in = jnp.pad(jnp.stack([segs, keep_end.astype(segs.dtype)], 1).astype(F32), ((0, 0), (0, 6), (0, 0)))
    return cols, rows_in, keep_end


def per_device(
    hidden_in,
    segment_ids,
    norm1_gain,
    w_gate_z,
    w_xbc,
    w_step,
    conv_weight,
    conv_bias,
    step_bias,
    decay_log,
    skip_gain,
    mixer_gain,
    w_mix_out,
    w_query,
    key_value_weight,
    w_attn_out,
    norm2_gain,
    w_gate_up,
    w_down,
    out_grad,
):
    rows = hidden_in.shape[2]
    seqs = hidden_in.shape[0] * hidden_in.shape[1]
    flat_rows = seqs * rows
    count = lax.axis_size(BOTH)
    query_width = QUERY_HEADS * HEAD_WIDTH
    kv_width = 2 * KEY_VALUE_HEADS * HEAD_WIDTH
    by_seq = lambda a: a.reshape(seqs, rows, a.shape[1])
    flat = lambda a: a.reshape(flat_rows, a.shape[2])
    r, rm, ra, rd = w_xbc.shape[0], w_mix_out.shape[0], w_attn_out.shape[0], w_down.shape[0]
    bits = bit_count()
    top = list(range(bits - 1, 2, -1))
    half = (DI + query_width + kv_width) // 2

    heads = jnp.stack([step_bias, -jnp.exp(decay_log), skip_gain])
    heads = jnp.pad(heads, ((0, 5), (0, LANES - H)))
    spread = jnp.repeat(jnp.eye(LANES, H, dtype=BF16), P_SIZE, axis=1)
    skip_row = jnp.broadcast_to(jnp.repeat(skip_gain, P_SIZE)[None], (8, DI))
    picks = jnp.eye(LANES, 2 * LEFT, 2 * LEFT - LANES, dtype=BF16)
    rest = rest_place().reshape(1).astype(jnp.int32)

    first = Part(
        pack_first(w_xbc, w_step, conv_weight, conv_bias, mixer_gain, norm1_gain, norm2_gain)[None]
    )
    if len(top) == 2:
        first.direct((8, 16, 24))
    else:
        first.step(top[0])
    segs_got = swap_start(segment_ids[:, 0])
    x_got = fsdp_exchange(pick(in_hbm(hidden_in[:, 0]), 1 - side_of(), after=(segs_got,)), fsdp_bits() - 1)
    for bit in top[1:] if len(top) != 2 else ():
        join([first])
        first.step(bit)
    first_halves = join([first], split=(first,), after=(heads, spread, skip_row, picks))
    [p.step(bit) for p, bit in zip(first_halves, (2, 1))]
    two = Part(pack_two(w_gate_z, w_query, key_value_weight, w_mix_out, w_attn_out, after=(first_halves[0].pieces[0][0],))[None])
    two.step(top[0])
    cols, rows_in, keep_end = sequence_masks(swap_end(segment_ids[:, 0], segs_got))
    x = merge(in_hbm(hidden_in[:, 0]), x_got, side_of()).reshape(flat_rows, MODEL_WIDTH)
    join(first_halves + [two], after=(x,))
    [p.step(bit) for p, bit in zip(first_halves, (1, 2))]
    two.steps(top[1:])
    [p.core() for p in first_halves]
    two_halves = join([two], split=(two,), after=[p.pieces[1][0] for p in first_halves])
    [p.step(bit) for p, bit in zip(two_halves, (2, 1))]
    units = Part(pack_units(w_gate_up, w_down, after=(two_halves[0].pieces[0][0],))[None])
    units.step(top[0])
    left_full, right_full, small_full = assemble(
        first_halves,
        [(count, r, LEFT), (count, r, LEFT), (count, r, LANES)],
        [
            (0, 0, r, 0, LEFT, 0, 0, 0),
            (1, 0, r, 0, LEFT, 1, 0, 0),
            (1, 0, r, LEFT - LANES, LANES, 2, 0, 0),
        ],
        after=(units.pieces[0][0],),
    )

    conv, mix_gain, gains = unpack_small(small_full, r)
    gain_one, gain_two = gains[:1], gains[1:]
    normed, left, right, tails = first_proj(x, gain_one, left_full, right_full, cols, after=(rows_in,))
    left, right = by_seq(left), by_seq(right)
    tail_pieces, offsets = gather_sequence(tails)
    join(two_halves + [units], after=(left,))
    [p.step(bit) for p, bit in zip(two_halves, (1, 2))]
    units.steps(top[1:])
    halo = take_halo(rest, tail_pieces, offsets)
    xbc, slope, xd, step, cum, msg = mix_begin(
        left, right, halo, cols, heads, conv, after=(two_halves[0].pieces[0][0],)
    )
    msg_pieces, _ = gather_sequence(msg)
    units_halves = join([units], after=(cum,), split=(units,))
    (two_all,) = join_all(two_halves, after=(units_halves[0].pieces[0][0],))
    two_offsets = sum((o for _, o in two_halves[0].pieces), [])
    other_offsets = sum((o for _, o in two_halves[1].pieces), [])
    two_got = exchange(two_all, 0)
    [p.step(bit) for p, bit in zip(units_halves, (2, 1))]
    inside = mix_inside(xbc, xd, cum, cols, rows_in, skip_row, after=(two_all,))
    for n, (p, offsets_of) in enumerate(zip(two_halves, (two_offsets, other_offsets))):
        p.pieces = [(two_all, offsets_of, n), (two_got, [o ^ 1 for o in offsets_of], n)]
    z_full, qkv_full = assemble(
        two_halves,
        [(count, r, DI), (count, r, query_width + kv_width)],
        [
            (0, 0, r, 0, half, 0, 0, 0),
            (1, 0, r, 0, DI - half, 0, 0, half),
            (1, 0, r, DI - half, query_width + kv_width, 1, 0, 0),
        ],
        after=(inside,),
    )
    gate_z, queries, keyvals = second_proj(normed, z_full, qkv_full, rows_in)
    gate_z, queries = by_seq(gate_z), by_seq(queries)
    prev = scan_states(rest, msg_pieces, offsets, True, after=(gate_z,))
    join(units_halves, after=(prev,))
    [p.step(bit) for p, bit in zip(units_halves, (1, 2))]
    kv_pieces, _ = gather_sequence(keyvals)
    mixer_out, normed_mix = mix_finish(
        in_hbm(inside), xbc, prev, cum, cols, in_hbm(gate_z), mix_gain, after=(units_halves[0].pieces[0][0],)
    )
    attn_low, log_sums = attend(rest, queries, kv_pieces, cols, rows_in, offsets, after=(normed_mix,))

    out_keep, out_send = turn(flat(normed_mix), flat(attn_low))
    x_halo = halo[:, :, CONV_WIDTH:].reshape(seqs * HALO, MODEL_WIDTH)
    normed_keep, normed_send = turn(jnp.concatenate([normed, x_halo]), after=(out_keep,))

    mix_out_full, attn_out_full = assemble(
        two_halves,
        [(count, rm, MODEL_WIDTH), (count, ra, MODEL_WIDTH)],
        [
            (0, 0, r, half, MODEL_WIDTH, 0, 0, 0),
            (1, 0, rm - r, half, MODEL_WIDTH, 0, r, 0),
            (1, rm - r, ra, half, MODEL_WIDTH, 1, 0, 0),
        ],
        after=(normed_keep,),
    )
    residual, normed_two = out_proj(x, flat(normed_mix), flat(attn_low), mix_out_full, attn_out_full, gain_two)
    two_keep, two_send, *held = turn(normed_two, hold=[p.pieces[1][0] for p in units_halves])
    for p, got in zip(units_halves, held):
        p.pieces[1] = (got, p.pieces[1][1])
        p.core()
    moves = [(n, q * r, r, 0, MODEL_WIDTH, n, 0, q * MODEL_WIDTH) for n in range(2) for q in range(2)]
    moves += [(n, 2 * r, rd // 2, 0, MODEL_WIDTH, 2, n * (rd // 2), 0) for n in range(2)]
    gate_full, up_full, down_full = assemble(
        units_halves, [(count, r, FF), (count, r, FF), (count, rd, MODEL_WIDTH)], moves, after=(two_keep,), limit=60
    )
    out_turned = [out_keep, exchange(out_send, 0)]
    x_turned = [normed_keep, exchange(normed_send, 0)]
    two_turned = [two_keep, exchange(two_send, 0)]
    grad_got = fsdp_exchange(pick(in_hbm(out_grad[:, 0]), 1 - side_of(), after=(gate_full,)), fsdp_bits() - 1)
    act, swish, gate_slope = gate_up(
        normed_two, gate_full, up_full, after=(out_turned[1], x_turned[1], two_turned[1])
    )
    act_keep, act_send = turn(act)
    grad_out = merge(in_hbm(out_grad[:, 0]), grad_got, side_of(), after=(act_keep,)).reshape(flat_rows, MODEL_WIDTH)
    act_turned = [act_keep, exchange(act_send, 0)]
    grad_out_got = exchange(grad_out, 0)

    block_out, grad_gate, grad_up = down(
        act, swish, gate_slope, down_full, residual, grad_out, after=(act_keep,)
    )
    gate_got, up_got = exchange(grad_gate, 0), exchange(grad_up, 0)
    hidden_got = swap_start(by_seq(block_out))
    grad_resid, grad_branch = gate_up_back(
        grad_gate, grad_up, gate_full, up_full, residual, gain_two, grad_out, after=(block_out,)
    )
    sum_down = Sum(act_turned, [grad_out, grad_out_got], 1, after=(grad_branch,))
    sum_gate = Sum(two_turned, [grad_gate, gate_got], 0, after=(sum_down.send,))
    hidden_out = swap_end(by_seq(block_out), hidden_got)
    sum_up = Sum(two_turned, [grad_up, up_got], 1, after=(sum_gate.send, hidden_out))
    branch_got = exchange(grad_branch, 0)
    sum_gate.near(), sum_up.near()
    grad_normed_mix, grad_attn = out_back(
        grad_branch, mix_out_full, attn_out_full, after=(sum_up.send,)
    )
    grad_normed_mix, grad_attn = by_seq(grad_normed_mix), by_seq(grad_attn)
    sum_out = Sum(out_turned, [grad_branch, branch_got], 0, after=(grad_normed_mix,))

    grad_queries, grad_kv_pieces = attend_back(
        rest, queries, kv_pieces, cols, rows_in, attn_low, log_sums, grad_attn, offsets, after=(sum_out.send,)
    )
    advance([sum_gate, sum_up], after=(grad_queries,))
    sum_gate.second(), sum_up.second()
    kv_own, kv_got = sum_sequence(grad_kv_pieces)
    dy, grad_za, grad_zb, back_msg = gated_back(
        grad_normed_mix, mixer_out, gate_z, mix_gain, xbc, cum, cols, half, after=(sum_gate.send, sum_up.send)
    )
    (pair_gate_up,) = advance([(sum_gate, sum_up)], after=(dy,))
    grad_zq = join_grads(
        flat(grad_za), flat(grad_zb), flat(grad_queries), kv_own, kv_got, after=(pair_gate_up.send,)
    )
    zq_got = exchange(grad_zq, 0)
    back_pieces, _ = gather_sequence(back_msg)
    pair_gate_up.start(3)
    sum_out.near(), sum_down.near()
    dxd, dbc, sums = inside_back(
        xbc, xd, cum, cols, rows_in, skip_row, spread, dy, mixer_out, prev, after=(grad_zq,)
    )
    sum_z = Sum(x_turned, [grad_zq, zq_got], 0, after=(sums,), columns=(0, half))
    sum_zq = Sum(x_turned, [grad_zq, zq_got], 1, after=(sum_z.send,), columns=(half, half))
    later = scan_states(rest, back_pieces, offsets, False, after=(sum_zq.send,))
    for bit in range(4, bits):
        advance([sum_out, sum_down, pair_gate_up] if bit == 4 else [pair_gate_up], after=(later,))
        pair_gate_up.start(bit)
    sum_out.second(), sum_down.second()
    sum_z.near(), sum_zq.near()
    grad_second = second_back(grad_zq, z_full, qkv_full, after=(sum_out.send,))
    grad_first, conv_sums, head_sums = mix_end(
        left, right, halo, xbc, slope, xd, step, cum, cols, heads, skip_row, conv, spread,
        dy, dxd, dbc, sums, later, prev, after=(grad_second,),
    )
    _, _, pair_out_down = advance([sum_z, sum_zq, (sum_out, sum_down)], after=(head_sums,))
    (own_gate_up,) = finish([pair_gate_up], after=(pair_out_down.send,))
    small_keep, small_send = small_grads(r, conv_sums, head_sums)
    sum_x = Direct(
        [normed_keep, small_keep], [normed_send, small_send], [grad_first, picks], after=(own_gate_up,)
    )
    grad_normed, grad_halo = first_back(
        grad_first, left_full, right_full, grad_second, after=(sum_x.send,)
    )
    sum_x.core()
    sum_z.second(), sum_zq.second()
    pair_out_down.start(3)
    edge = keep_end[:, rows - HALO :, None]
    from_next = jnp.where(edge, from_next_part(grad_halo.reshape(seqs, HALO, MODEL_WIDTH)), 0.0)
    quarter = sum_x.planes(after=(grad_normed,))
    input_grad, input_low = input_back(grad_normed, from_next, x, gain_one, grad_resid, after=(quarter,))
    input_got = swap_start(input_low)
    input_grad = swap_end(input_grad, input_got)
    far = list(range(4, bits))
    (pair_z,) = advance([(sum_z, sum_zq)], after=(quarter,))
    pair_z.start(3)
    for bit in far:
        advance([pair_out_down], after=(input_low,))
        pair_out_down.start(bit)
    sum_x.lines(after=(pair_out_down.send, pair_z.send))
    (own_out_down,) = finish([pair_out_down], after=(sum_x.keep,))
    for bit in far:
        advance([pair_z], after=(sum_x.keep,))
        pair_z.start(bit)
    (own_zq,) = finish([pair_z], after=(sum_x.keep,))
    own_first = sum_x.done()
    own_small = own_first[:, 2 * LEFT - LANES :]
    widths = [conv_weight.shape[1]] * KC + [conv_bias.shape[0]] + [H] * 6
    own = []
    for j, width in enumerate(widths):
        row, lane = line_place(j, len(widths), r)
        own.append(own_small[row, lane : lane + width])
    gain_grad = lambda weights, grads, gain: sum(
        jnp.sum(w.astype(F32) * g, 1) for w, g in zip(weights, grads)
    ) / gain.astype(F32)
    zq = jnp.concatenate([own_zq[0], own_zq[1]], 1)
    grad_z, grad_query, grad_keyval = jnp.split(zq, (DI, DI + query_width), 1)
    grad_xbc = own_first[:, :CONV_WIDTH]
    grad_step = own_first[:, CONV_WIDTH : CONV_WIDTH + H]
    grad_gate_up = jnp.concatenate([own_gate_up[0], own_gate_up[1]], 1)
    grad_out_w, grad_down = own_out_down[0], own_out_down[1]
    first_w = (w_gate_z, w_xbc, w_step, w_query, key_value_weight)
    first_g = (grad_z, grad_xbc, grad_step, grad_query, grad_keyval)
    return (
        hidden_out.reshape(hidden_in.shape),
        input_grad.reshape(hidden_in.shape),
        gain_grad(first_w, first_g, norm1_gain),
        grad_z,
        grad_xbc,
        grad_step,
        jnp.stack(own[:KC]),
        own[KC],
        own[KC + 1] + own[KC + 4],
        own[KC + 2] + own[KC + 5],
        own[KC + 3] + own[KC + 6],
        gain_grad([w_mix_out], [grad_out_w[:rm]], mixer_gain),
        grad_out_w[:rm],
        grad_query,
        grad_keyval,
        grad_out_w[rm:],
        gain_grad([w_gate_up], [grad_gate_up], norm2_gain),
        grad_gate_up,
        grad_down,
    )


def solution(mesh):
    placed = (
        P(None, "dp", "fsdp", None),
        P(None, "dp", "fsdp"),
        P(("dp", "fsdp")),
        P(("dp", "fsdp"), None),
        P(("dp", "fsdp"), None),
        P(("dp", "fsdp"), None),
        P(None, ("dp", "fsdp")),
        P(("dp", "fsdp")),
        P(),
        P(),
        P(),
        P(("dp", "fsdp")),
        P(("dp", "fsdp"), None),
        P(("dp", "fsdp"), None),
        P(("dp", "fsdp"), None),
        P(("dp", "fsdp"), None),
        P(("dp", "fsdp")),
        P(("dp", "fsdp"), None),
        P(("dp", "fsdp"), None),
        P(None, "dp", "fsdp", None),
    )
    return jax.shard_map(
        per_device,
        mesh=mesh,
        in_specs=placed,
        out_specs=(
            P(None, "dp", "fsdp", None),
            P(None, "dp", "fsdp", None),
            P(("dp", "fsdp")),
            P(("dp", "fsdp"), None),
            P(("dp", "fsdp"), None),
            P(("dp", "fsdp"), None),
            P(None, ("dp", "fsdp")),
            P(("dp", "fsdp")),
            P(),
            P(),
            P(),
            P(("dp", "fsdp")),
            P(("dp", "fsdp"), None),
            P(("dp", "fsdp"), None),
            P(("dp", "fsdp"), None),
            P(("dp", "fsdp"), None),
            P(("dp", "fsdp")),
            P(("dp", "fsdp"), None),
            P(("dp", "fsdp"), None),
        ),
        check_vma=False,
    )
```

```python
import functools

import jax
import jax.numpy as jnp
from jax import lax
from jax.experimental import pallas as pl
from jax.experimental.pallas import tpu as pltpu
from jax.sharding import PartitionSpec as P

MODEL_WIDTH = 1024
FF = 2048
H = 24
P_SIZE = 64
NS = 128
QUERY_HEADS = 8
KEY_VALUE_HEADS = 2
HEAD_WIDTH = 64
KC = 4
DI = 1536


EPSILON = 1e-06
NEGATIVE = -1e30


def matmul(first_op, second_op):
    return jnp.dot(first_op, second_op, preferred_element_type=jnp.float32)


def left_t(first_op, second_op):
    return jnp.einsum("ti,tj->ij", first_op, second_op, preferred_element_type=jnp.float32)


def right_t(first_op, second_op):
    return jnp.einsum("ti,ji->tj", first_op, second_op, preferred_element_type=jnp.float32)


def rms_gain(values, gain_in):
    return values * lax.rsqrt(jnp.mean(values * values, axis=-1, keepdims=True) + EPSILON) * gain_in


def swiglu(gate_up):
    return jax.nn.silu(gate_up[:, :FF]) * gate_up[:, FF:]


BOTH = ("dp", "fsdp")


def exchange_mask(block, mask):
    count = lax.axis_size(BOTH)
    return lax.ppermute(block, BOTH, [(i, i ^ mask) for i in range(count)])


def exchange(block, bit):
    return exchange_mask(block, 1 << bit)


def bit_count():
    return lax.axis_size(BOTH).bit_length() - 1


def place_of():
    return lax.axis_index(BOTH)


def in_hbm(array):
    return pltpu.with_memory_space_constraint(array, pltpu.HBM)


def spec_any(count):
    return [pl.BlockSpec(memory_space=pl.ANY)] * count


def copies_kernel(n_in, n_after, n_out, n_hold, jobs, place_ref, *refs):
    ins, refs = refs[:n_in], refs[n_in + n_hold + n_after :]
    outs, refs = refs[:n_out], refs[n_out + n_hold :]
    held, sems, out_sems = refs[:n_out], refs[-2], refs[-1]
    place = place_ref[0]
    copies = [[] for _ in outs]
    for number, (out, source, source_at, target_at) in enumerate(jobs):
        copy = pltpu.make_async_copy(
            ins[source].at[source_at], held[out].at[target_at(place)], sems.at[number]
        )
        copy.start()
        copies[out].append(copy)
    back = []
    for out in range(n_out):
        for copy in copies[out]:
            copy.wait()
        copy = pltpu.make_async_copy(held[out], outs[out], out_sems.at[out])
        copy.start()
        back.append(copy)
    for copy in back:
        copy.wait()


def copies(name, ins, outs, jobs, after=(), hold=(), limit=24):
    jobs = sorted(jobs, key=lambda job: job[0])
    ins = [in_hbm(a) for a in ins]
    return pl.pallas_call(
        functools.partial(copies_kernel, len(ins), len(after), len(outs), len(hold), jobs),
        out_shape=[jax.ShapeDtypeStruct(s, jnp.bfloat16) for s in outs]
        + [jax.ShapeDtypeStruct(a.shape, a.dtype) for a in hold],
        in_specs=[pl.BlockSpec(memory_space=pltpu.SMEM)] + spec_any(len(ins) + len(hold) + len(after)),
        out_specs=spec_any(len(outs) + len(hold)),
        input_output_aliases={1 + len(ins) + n: len(outs) + n for n in range(len(hold))},
        scratch_shapes=[pltpu.VMEM(s, jnp.bfloat16) for s in outs]
        + [pltpu.SemaphoreType.DMA((len(jobs),)), pltpu.SemaphoreType.DMA((len(outs),))],
        compiler_params=pltpu.CompilerParams(vmem_limit_bytes=limit * 2**20),
        name=name,
    )(place_of().reshape(1).astype(jnp.int32), *ins, *hold, *after)


class Part:
    def __init__(self, block, offsets=(0,)):
        self.pieces = [(block, list(offsets))]

    def step(self, bit):
        ((block, offsets),) = self.pieces
        self.pieces.append((exchange(block, bit), [o ^ (1 << bit) for o in offsets]))

    def steps(self, bits):
        for n, bit in enumerate(bits):
            if n:
                join([self])
            self.step(bit)

    def direct(self, masks):
        ((block, offsets),) = self.pieces
        self.pieces += [(exchange_mask(block, mask), [o ^ mask for o in offsets]) for mask in masks]

    def core(self):
        self.pieces += [(exchange(a, 0), [o ^ 1 for o in offsets]) for a, offsets in self.pieces]


def join_all(parts, after=(), hold=()):
    ins, jobs = [], []
    for p, part in enumerate(parts):
        at = 0
        for array, own in part.pieces:
            target = (p, slice(at, at + len(own)))
            jobs.append((0, len(ins), (slice(None),), lambda place, target=target: target))
            ins.append(array)
            at += len(own)
    shape = (len(parts), at) + ins[0].shape[1:]
    return copies("join_all", ins, [shape], jobs, after, hold)


def join(parts, after=(), split=(), hold=()):
    ins, outs, jobs, made = [], [], [], []
    for part in parts:
        first = part.pieces[0][0]
        blocks = sum(len(offsets) for _, offsets in part.pieces)
        offsets = sum((o for _, o in part.pieces), [])
        halves = (0, 1) if part in split else (None,)
        for half in halves:
            at = 0
            for number, (array, own) in enumerate(part.pieces):
                source = len(ins) + number
                source_at = (slice(None),) if half is None else (slice(None), half)
                target = (slice(at, at + len(own)),)
                jobs.append((len(outs), source, source_at, lambda place, target=target: target))
                at += len(own)
            outs.append((blocks,) + (first.shape[1:] if half is None else first.shape[2:]))
            made.append((part, half, offsets))
        ins += [array for array, _ in part.pieces]
    cut = []
    held = [part.pieces[-1][0] for part in hold]
    found = copies("join", ins, outs, jobs, after, held)
    for array, part in zip(found[len(outs) :], hold):
        part.pieces[-1] = (array, part.pieces[-1][1])
    for array, (part, half, offsets) in zip(found, made):
        if half is None:
            part.pieces = [(array, offsets)]
        else:
            cut.append(Part(array, offsets))
    return cut


def assemble(parts, outs, moves, after=(), limit=24):
    ins, jobs = [], []
    for at, part in enumerate(parts):
        for piece, offsets, *of_part in part.pieces:
            for j, offset in enumerate(offsets):
                for of, r0, rows, c0, columns, out, row, column in moves:
                    if of == at:
                        source_at = (*of_part, j, pl.ds(r0, rows), pl.ds(c0, columns))
                        target = (pl.ds(row, rows), pl.ds(column, columns))
                        jobs.append(
                            (out, len(ins), source_at, lambda place, o=offset, t=target: (place ^ o,) + t)
                        )
            ins.append(piece)
    return [a.reshape(-1, a.shape[2]) for a in copies("assemble", ins, outs, jobs, after, limit=limit)]


def turned_offsets(bits):
    offsets = [0]
    for bit in list(range(bits - 1, 2, -1)) + [1, 2]:
        offsets = offsets + [o ^ (1 << bit) for o in offsets]
    return offsets


def turn_kernel(n_x, n_hold, n_after, rows, offsets, place_ref, *refs):
    xs, refs = refs[:n_x], refs[n_x + n_hold + n_after :]
    keep_ref, send_ref, turned = refs[0], refs[1], refs[2 + n_hold :]
    place = place_ref[0]
    total = sum(rows)
    for x_ref, t_ref in zip(xs, turned):
        t_ref[...] = x_ref[...].T
    for t, offset in enumerate(offsets):
        at = t * total
        for t_ref, size in zip(turned, rows):
            begin = pl.multiple_of((place ^ offset) * size, size)
            keep_ref[at : at + size] = t_ref[pl.ds(begin, size)]
            begin = pl.multiple_of((place ^ (offset ^ 1)) * size, size)
            send_ref[at : at + size] = t_ref[pl.ds(begin, size)]
            at += size


def turn(*xs, after=(), hold=()):
    bits = bit_count()
    rows = [x.shape[1] >> bits for x in xs]
    tokens, half = xs[0].shape[0], sum(x.shape[1] for x in xs) // 2
    if any(r % 16 for r in rows):
        blocks = jnp.concatenate([x.T.reshape(1 << bits, r, tokens) for x, r in zip(xs, rows)], 1)
        offsets = jnp.asarray(turned_offsets(bits), jnp.int32) ^ place_of()
        sides = [jnp.take(blocks, o, axis=0).reshape(half, tokens) for o in (offsets, offsets ^ 1)]
        return (*sides, *hold)
    vmem = pl.BlockSpec(memory_space=pltpu.VMEM)
    return pl.pallas_call(
        functools.partial(turn_kernel, len(xs), len(hold), len(after), rows, turned_offsets(bits)),
        in_specs=[pl.BlockSpec(memory_space=pltpu.SMEM)] + [vmem] * len(xs) + spec_any(len(hold) + len(after)),
        out_specs=[vmem] * 2 + spec_any(len(hold)),
        out_shape=[jax.ShapeDtypeStruct((half, tokens), jnp.bfloat16)] * 2
        + [jax.ShapeDtypeStruct(a.shape, a.dtype) for a in hold],
        input_output_aliases={1 + len(xs) + n: 2 + n for n in range(len(hold))},
        scratch_shapes=[pltpu.VMEM((x.shape[1], x.shape[0]), jnp.bfloat16) for x in xs],
        compiler_params=pltpu.CompilerParams(vmem_limit_bytes=24 * 2**20),
        name="turn",
    )(place_of().reshape(1).astype(jnp.int32), *xs, *hold, *after)


def grad_kernel(n_pairs, half, *refs):
    pairs, (keep_ref, send_ref) = refs[: 2 * n_pairs], refs[-2:]
    total = None
    for x_ref, g_ref in zip(pairs[:n_pairs], pairs[n_pairs:]):
        part = jnp.dot(x_ref[...], g_ref[...], preferred_element_type=jnp.float32)
        total = part if total is None else total + part
    total = total.astype(jnp.bfloat16)
    rows = keep_ref.shape[1]
    for second in range(2):
        for first, ref in enumerate((keep_ref, send_ref)):
            quarter = 2 * first + second if half == 0 else 2 * second + first
            ref[second] = total[quarter * rows : (quarter + 1) * rows]


def weight_grad(xs, gs, half, after=(), columns=None):
    k, (first, n) = xs[0].shape[0], columns or (0, gs[0].shape[1])
    width = next(w for w in (1024, 512, 384, 256, 128) if n % w == 0 and first % w == 0)
    at = first // width
    block = pl.BlockSpec((2, k // 4, width), lambda i: (0, 0, i))
    return pl.pallas_call(
        functools.partial(grad_kernel, len(xs), half),
        grid=(n // width,),
        in_specs=[pl.BlockSpec((k, g.shape[0]), lambda i: (0, 0)) for g in gs]
        + [pl.BlockSpec((g.shape[0], width), lambda i: (0, at + i)) for g in gs]
        + spec_any(len(after)),
        out_specs=[block, block],
        out_shape=[jax.ShapeDtypeStruct((2, k // 4, n), jnp.bfloat16)] * 2,
        compiler_params=pltpu.CompilerParams(vmem_limit_bytes=48 * 2**20),
        name="weight_grad",
    )(*xs, *gs, *after)


def both_kernel(n_pairs, half, *refs):
    outs = refs[-2:]
    gs = refs[2 * n_pairs : 3 * n_pairs]
    for xs, out_ref in ((refs[:n_pairs], outs[0]), (refs[n_pairs : 2 * n_pairs], outs[1])):
        total = None
        for x_ref, g_ref in zip(xs, gs):
            part = jnp.dot(x_ref[...], g_ref[...], preferred_element_type=jnp.float32)
            total = part if total is None else total + part
        total = total.astype(jnp.bfloat16)
        rows = out_ref.shape[1] // 4
        for quarter in range(4):
            place = quarter if half == 0 else 2 * (quarter % 2) + quarter // 2
            out_ref[0, place * rows : (place + 1) * rows] = total[quarter * rows : (quarter + 1) * rows]


def both_grads(keeps, sends, gs, half, after=()):
    k, n = keeps[0].shape[0], gs[0].shape[1]
    width = next(w for w in (512, 256, 128) if n % w == 0)
    block = pl.BlockSpec((1, k, width), lambda i: (0, 0, i))
    return pl.pallas_call(
        functools.partial(both_kernel, len(gs), half),
        grid=(n // width,),
        in_specs=[pl.BlockSpec((k, g.shape[0]), lambda i: (0, 0)) for g in gs] * 2
        + [pl.BlockSpec((g.shape[0], width), lambda i: (0, i)) for g in gs]
        + spec_any(len(after)),
        out_specs=[block, block],
        out_shape=[jax.ShapeDtypeStruct((1, k, n), jnp.bfloat16)] * 2,
        compiler_params=pltpu.CompilerParams(vmem_limit_bytes=48 * 2**20),
        name="both_grads",
    )(*keeps, *sends, *gs, *after)


def add_kernel(shape, last, n_after, *refs):
    n_in = sum(len(counts) for counts in shape)
    keeps, gots, outs = refs[:n_in], refs[n_in : 2 * n_in], refs[2 * n_in + n_after :]
    at = 0
    for item, counts in enumerate(shape):
        slot = 0
        for count in counts:
            for s in range(count):
                total = keeps[at][s].astype(jnp.float32) + gots[at][s].astype(jnp.float32)
                if last:
                    outs[item][slot] = total
                else:
                    total = total.astype(jnp.bfloat16)
                    half = total.shape[0] // 2
                    outs[2 * item][slot] = total[:half]
                    outs[2 * item + 1][slot] = total[half:]
                slot += 1
            at += 1


def add_up(items, after=(), last=False):
    shape = [[own.shape[0] for own, _ in item] for item in items]
    keeps = [own for item in items for own, _ in item]
    gots = [in_hbm(got) for item in items for _, got in item]
    widths = {a.shape[2] for a in keeps}
    steps = next(g for g in (2, 3, 1) if all(w % (g * 128) == 0 for w in widths))
    blocks, outs = [], []
    for a in keeps:
        blocks.append(pl.BlockSpec(a.shape[:2] + (a.shape[2] // steps,), lambda i: (0, 0, i)))
    out_blocks = []
    for item, counts in zip(items, shape):
        rows, n = item[0][0].shape[1:]
        rows = rows if last else rows // 2
        for _ in range(1 if last else 2):
            out_blocks.append(pl.BlockSpec((sum(counts), rows, n // steps), lambda i: (0, 0, i)))
            outs.append(
                jax.ShapeDtypeStruct((sum(counts), rows, n), jnp.float32 if last else jnp.bfloat16)
            )
    return pl.pallas_call(
        functools.partial(add_kernel, shape, last, len(after)),
        grid=(steps,),
        in_specs=blocks + blocks + spec_any(len(after)),
        out_specs=out_blocks,
        out_shape=outs,
        compiler_params=pltpu.CompilerParams(vmem_limit_bytes=48 * 2**20),
        name="add_up",
    )(*keeps, *gots, *after)


class Sum:
    def __init__(self, xs, gs, half, after=(), columns=None):
        self.first = (2, 1)[half]
        keep, send = weight_grad(xs, gs, half, after, columns)
        self.keep, self.send = (a.reshape(1, -1, a.shape[2]) for a in (keep, send))

    def start(self, bit):
        self.got = exchange(self.send, bit)

    def near(self):
        self.start(self.first)

    def second(self):
        self.start(3 - self.first)


class CoreSum(Sum):
    def __init__(self, keeps, sends, gs, half, after=()):
        self.first = (2, 1)[half]
        self.keep, self.send = both_grads(keeps, sends, gs, half, after)

    def core(self):
        self.start(0)


class Pair:
    def start(self, bit):
        self.got = exchange(self.send, bit)


def advance(steps, after=()):
    items = [[(s.keep, s.got) for s in (step if isinstance(step, tuple) else (step,))] for step in steps]
    found = add_up(items, after)
    made = []
    for n, step in enumerate(steps):
        step = Pair() if isinstance(step, tuple) else step
        step.keep, step.send = found[2 * n : 2 * n + 2]
        made.append(step)
    return made


def finish(pairs, after=()):
    return add_up([[(p.keep, p.got)] for p in pairs], after, last=True)


def parts_kernel(n_in, parts, n_skip, *refs):
    ins, outs = refs[:n_in], refs[n_in + n_skip :]
    total = ins[0][0].astype(jnp.float32)
    for ref in ins[1:]:
        total = total + ref[0].astype(jnp.float32)
    rows = total.shape[0] // parts
    for n in range(parts):
        outs[n][0] = total[n * rows : (n + 1) * rows].astype(outs[n].dtype)


def add_parts(arrays, parts, kind=jnp.bfloat16, after=(), hold=()):
    _, rows, n = arrays[0].shape
    steps = next(g for g in (2, 1) if n % (g * 128) == 0)
    spec = lambda rows: pl.BlockSpec((1, rows, n // steps), lambda i: (0, 0, i))
    return pl.pallas_call(
        functools.partial(parts_kernel, len(arrays), parts, len(hold) + len(after)),
        grid=(steps,),
        in_specs=[spec(rows)] * len(arrays) + spec_any(len(hold) + len(after)),
        out_specs=[spec(rows // parts)] * parts + spec_any(len(hold)),
        out_shape=[jax.ShapeDtypeStruct((1, rows // parts, n), kind)] * parts
        + [jax.ShapeDtypeStruct(a.shape, a.dtype) for a in hold],
        input_output_aliases={len(arrays) + n: parts + n for n in range(len(hold))},
        compiler_params=pltpu.CompilerParams(vmem_limit_bytes=48 * 2**20),
        name="add_parts",
    )(arrays[0], *[in_hbm(a) for a in arrays[1:]], *hold, *after)


class Direct:
    def __init__(self, keeps, sends, gs, after=()):
        self.keep, self.send = both_grads(keeps, sends, gs, 0, after)

    def core(self):
        self.got = [exchange(self.send, 0)]

    def planes(self, after=()):
        quarters = add_parts([self.keep] + self.got, 4, after=after)
        self.keep = quarters[0]
        self.got = [exchange_mask(q, mask) for q, mask in zip(quarters[1:], (2, 4, 6))]
        return quarters[0]

    def lines(self, after=(), hold=()):
        bits = bit_count()
        arrays = [self.keep] + self.got
        if bits == 5:
            quarters = add_parts(arrays, 4, after=after, hold=hold)
            self.keep = quarters[0]
            self.got = [exchange_mask(q, mask) for q, mask in zip(quarters[1:4], (16, 8, 24))]
            return quarters[4:]
        for bit in range(3, bits):
            self.keep, send = add_parts(arrays, 2, after=after)
            self.got = [exchange(send, bit)]
            arrays = [self.keep] + self.got
        return hold

    def done(self):
        return add_parts([self.keep] + self.got, 1, jnp.float32)[0][0]


F32 = jnp.float32
BF16 = jnp.bfloat16
LANES = 128
HALO = 16
STATE_ROWS = NS + 16
LEFT = 1024
SLOTS = 2
CONV_WIDTH = DI + 2 * NS
VMEM_LIMIT = 48 * 2**20


def dot_nn(a, b):
    return jnp.dot(a, b, preferred_element_type=F32)


def dot_nt(a, b):
    return lax.dot_general(a, b, (((1,), (1,)), ((), ())), preferred_element_type=F32)


def dot_tn(a, b):
    return lax.dot_general(a, b, (((0,), (0,)), ((), ())), preferred_element_type=F32)


def split_two(v):
    high = v.astype(BF16)
    return high, (v - high.astype(F32)).astype(BF16)


def sum_heads(v, spread):
    high, low = split_two(v)
    return dot_nt(high, spread) + dot_nt(low, spread)


def tile_of(i):
    return slice(i * LANES, (i + 1) * LANES)


def two_heads(v, i):
    rows = v.shape[0]
    lane = lax.broadcasted_iota(jnp.int32, (rows, LANES), 1)
    left = jnp.broadcast_to(v[:, 2 * i : 2 * i + 1], (rows, LANES))
    right = jnp.broadcast_to(v[:, 2 * i + 1 : 2 * i + 2], (rows, LANES))
    return jnp.where(lane < P_SIZE, left, right)


def all_heads(v):
    v = jnp.broadcast_to(v, (16, LANES))
    return jnp.concatenate([two_heads(v, i) for i in range(DI // LANES)], 1)


def triangle(size, lower):
    rows = lax.broadcasted_iota(jnp.int32, (size, size), 0)
    cols = lax.broadcasted_iota(jnp.int32, (size, size), 1)
    return jnp.where(rows >= cols if lower else rows <= cols, 1.0, 0.0).astype(BF16)


def exact_sum(ones, v):
    high = v.astype(BF16)
    rest = v - high.astype(F32)
    mid = rest.astype(BF16)
    low = (rest - mid.astype(F32)).astype(BF16)
    return dot_nn(ones, high) + (dot_nn(ones, mid) + dot_nn(ones, low))


def soft_plus(z):
    return jnp.maximum(z, 0.0) + jnp.log1p(jnp.exp(-jnp.abs(z)))


def sigmoid(v):
    return 0.5 * jnp.tanh(0.5 * v) + 0.5


def conv_tile(left_ref, right_ref, i):
    tiles = LEFT // LANES
    if i < tiles:
        return left_ref[0, :, tile_of(i)].astype(F32)
    return right_ref[0, :, tile_of(i - tiles)].astype(BF16).astype(F32)


def raw_tile(right_ref):
    return right_ref[0, :, CONV_WIDTH - LEFT : CONV_WIDTH - LEFT + LANES]


def mix_begin_kernel(
    left_ref, right_ref, halo_ref, cols_ref, heads_ref, conv_ref,
    xbc_ref, slope_ref, xd_ref, step_ref, cum_ref, msg_ref,
):
    rows = left_ref.shape[1]
    masks = cols_ref[0]
    step = soft_plus(raw_tile(right_ref) + heads_ref[0:1])
    cum = exact_sum(triangle(rows, True), step * heads_ref[1:2])
    step_ref[0] = step
    cum_ref[0] = cum
    last = cum[rows - 1 : rows]
    ends = jnp.exp(last - cum) * masks[:, 3:4]
    msg_ref[0, NS:STATE_ROWS, :] = all_heads(jnp.exp(last)).astype(BF16)
    wide = [jnp.broadcast_to(masks[:, k : k + 1], (rows, LANES)) for k in range(KC - 1)]

    def conv(i):
        lanes = tile_of(i)
        own = conv_tile(left_ref, right_ref, i)
        ext = jnp.concatenate([halo_ref[0, :, lanes].astype(F32), own], 0)
        taps = conv_ref[:, lanes]
        total = taps[4:5] + taps[3:4] * own
        for k in range(KC - 1):
            at = HALO - (KC - 1) + k
            total = total + taps[k : k + 1] * (ext[at : at + rows] * wide[k])
        sig = sigmoid(total)
        x = total * sig
        slope_ref[0, :, lanes] = (sig + x * (1.0 - sig)).astype(BF16)
        low = x.astype(BF16)
        xbc_ref[0, :, lanes] = low
        return x, low

    tiles = DI // LANES
    b_turned = conv(tiles)[1].T
    conv(tiles + 1)
    for i in range(tiles):
        xd = conv(i)[0] * two_heads(step, i)
        xd_ref[0, :, tile_of(i)] = xd.astype(BF16)
        weighted = (xd * two_heads(ends, i)).astype(BF16)
        msg_ref[0, 0:NS, tile_of(i)] = dot_nn(b_turned, weighted).astype(BF16)


def seq_block(*shape):
    return pl.BlockSpec((1,) + shape, lambda s: (s,) + (0,) * len(shape))


def whole_block(*shape):
    return pl.BlockSpec(shape, lambda s: (0,) * len(shape))


def call(kernel, name, seqs, ins, in_specs, outs, out_specs, scratch=(), after=()):
    n_in, n_after = len(ins), len(after)

    def run(*refs):
        kernel(*refs[:n_in], *refs[n_in + n_after :])

    ins = tuple(ins) + tuple(after)
    in_specs = list(in_specs) + [pl.BlockSpec(memory_space=pl.ANY)] * n_after
    return pl.pallas_call(
        run,
        grid=(seqs,),
        in_specs=in_specs,
        out_specs=out_specs,
        out_shape=[jax.ShapeDtypeStruct(s, d) for s, d in outs],
        scratch_shapes=list(scratch),
        compiler_params=pltpu.CompilerParams(vmem_limit_bytes=VMEM_LIMIT),
        name=name,
    )(*ins)


def mix_begin(left, right, halo, cols, heads, conv, after=()):
    seqs, rows, _ = left.shape
    width = CONV_WIDTH
    return call(
        mix_begin_kernel,
        "mix_begin",
        seqs,
        (left, right, halo, cols, heads, conv),
        [
            seq_block(rows, LEFT),
            seq_block(rows, LEFT),
            seq_block(HALO, halo.shape[2]),
            seq_block(rows, LANES),
            whole_block(8, LANES),
            whole_block(8, width),
        ],
        [
            ((seqs, rows, width), BF16),
            ((seqs, rows, width), BF16),
            ((seqs, rows, DI), BF16),
            ((seqs, rows, LANES), F32),
            ((seqs, rows, LANES), F32),
            ((seqs, STATE_ROWS, DI), BF16),
        ],
        [
            seq_block(rows, width),
            seq_block(rows, width),
            seq_block(rows, DI),
            seq_block(rows, LANES),
            seq_block(rows, LANES),
            seq_block(STATE_ROWS, DI),
        ],
        after=after,
    )


def row_parts(rows):
    if rows < 256:
        return [(0, rows, rows)]
    return [(a, a + LANES, a + LANES) for a in range(0, rows, LANES)]


def side_by_side(pair):
    lane = lax.broadcasted_iota(jnp.int32, pair.shape, 1)
    blank = jnp.zeros_like(pair)
    return jnp.where(lane < P_SIZE, pair, blank), jnp.where(lane < P_SIZE, blank, pair)


def mix_inside_kernel(xbc_ref, xd_ref, cum_ref, cols_ref, rows_ref, skip_ref, y_ref):
    rows = xbc_ref.shape[1]
    b_rows, c_rows = xbc_ref[0, :, DI : DI + NS], xbc_ref[0, :, DI + NS :]
    seg_col, seg_row = cols_ref[0, :, 5:6], rows_ref[0, 0:1, :]
    row_at = lax.broadcasted_iota(jnp.int32, (rows, rows), 0)
    col_at = lax.broadcasted_iota(jnp.int32, (rows, rows), 1)
    couple = jnp.where((seg_col == seg_row) & (row_at >= col_at), dot_nt(c_rows, b_rows), 0.0)
    cum = cum_ref[0]
    cum_rows = cum.T
    for first in range(0, H, 2):
        lanes = slice(first * P_SIZE, (first + 2) * P_SIZE)
        sides = side_by_side(xd_ref[0, :, lanes])
        for begin, end, upto in row_parts(rows):
            y = xbc_ref[0, begin:end, lanes].astype(F32) * skip_ref[0:1, lanes]
            for h, side in zip((first, first + 1), sides):
                gap = jnp.minimum(cum[begin:end, h : h + 1] - cum_rows[h : h + 1, :upto], 0.0)
                mixing = (jnp.exp(gap) * couple[begin:end, :upto]).astype(BF16)
                y = y + dot_nn(mixing, side[:upto])
            y_ref[0, begin:end, lanes] = y


def mix_inside(xbc, xd, cum, cols, rows_in, skip, after=()):
    seqs, rows, width = xbc.shape
    return call(
        mix_inside_kernel,
        "mix_inside",
        seqs,
        (xbc, xd, cum, cols, rows_in, skip),
        [
            seq_block(rows, width),
            seq_block(rows, DI),
            seq_block(rows, LANES),
            seq_block(rows, LANES),
            seq_block(8, rows),
            whole_block(8, DI),
        ],
        [((seqs, rows, DI), F32)],
        [seq_block(rows, DI)],
        after=after,
    )[0]


def mix_finish_kernel(y_ref, c_ref, prev_ref, cum_ref, cols_ref, z_ref, gain_ref, mo_ref, nm_ref, g_ref):
    rows = y_ref.shape[1]
    flow = jnp.exp(cum_ref[0]) * cols_ref[0, :, 4:5]
    c_rows = c_ref[0]
    total = jnp.zeros((rows, LANES), F32)
    for i in range(DI // LANES):
        lanes = tile_of(i)
        mo = y_ref[0, :, lanes] + dot_nn(c_rows, prev_ref[0, :, lanes]) * two_heads(flow, i)
        mo_ref[0, :, lanes] = mo
        z = z_ref[0, :, lanes]
        g = mo * (z * sigmoid(z))
        g_ref[:, lanes] = g
        total = total + g * g
    scale = lax.rsqrt(jnp.sum(total, axis=1, keepdims=True) / DI + EPSILON)
    scale = jnp.broadcast_to(scale, (rows, LANES))
    for i in range(DI // LANES):
        lanes = tile_of(i)
        nm_ref[0, :, lanes] = (g_ref[:, lanes] * scale * gain_ref[0:1, lanes]).astype(BF16)


def c_block(rows):
    return pl.BlockSpec((1, rows, NS), lambda s: (s, 0, (DI + NS) // NS))


def mix_finish(y, xbc, prev, cum, cols, z, gain, after=()):
    seqs, rows, _ = y.shape
    return call(
        mix_finish_kernel,
        "mix_finish",
        seqs,
        (y, xbc, prev, cum, cols, z, gain),
        [
            seq_block(rows, DI),
            c_block(rows),
            seq_block(NS, DI),
            seq_block(rows, LANES),
            seq_block(rows, LANES),
            seq_block(rows, DI),
            whole_block(1, DI),
        ],
        [((seqs, rows, DI), F32), ((seqs, rows, DI), BF16)],
        [seq_block(rows, DI), seq_block(rows, DI)],
        [pltpu.VMEM((rows, DI), F32)],
        after=after,
    )


def gated_back_kernel(
    dn_ref, mo_ref, z_ref, gain_ref, c_ref, cum_ref, cols_ref, dy_ref, dza_ref, dzb_ref, msg_ref, sig_ref
):
    rows = dn_ref.shape[1]
    squares = jnp.zeros((rows, LANES), F32)
    mixed = jnp.zeros((rows, LANES), F32)
    for i in range(DI // LANES):
        lanes = tile_of(i)
        z = z_ref[0, :, lanes]
        sig = sigmoid(z)
        sig_ref[:, lanes] = sig
        g = mo_ref[0, :, lanes] * (z * sig)
        squares = squares + g * g
        mixed = mixed + g * (dn_ref[0, :, lanes] * gain_ref[0:1, lanes])
    scale = lax.rsqrt(jnp.sum(squares, axis=1, keepdims=True) / DI + EPSILON)
    back = jnp.sum(mixed, axis=1, keepdims=True) / DI * scale * scale * scale
    scale = jnp.broadcast_to(scale, (rows, LANES))
    back = jnp.broadcast_to(back, (rows, LANES))
    cum = cum_ref[0]
    flow = jnp.exp(cum) * cols_ref[0, :, 4:5]
    msg_ref[0, NS:STATE_ROWS, :] = all_heads(jnp.exp(cum[rows - 1 : rows])).astype(BF16)
    c_turned = c_ref[0].T
    for i in range(DI // LANES):
        lanes = tile_of(i)
        z = z_ref[0, :, lanes]
        mo = mo_ref[0, :, lanes]
        sig = sig_ref[:, lanes]
        swish = z * sig
        g = mo * swish
        dn = dn_ref[0, :, lanes] * scale
        dg = dn * gain_ref[0:1, lanes] - g * back
        dy = (dg * swish).astype(BF16)
        dy_ref[0, :, lanes] = dy
        dz = (dg * mo * (sig + swish * (1.0 - sig))).astype(BF16)
        split = dza_ref.shape[2] // LANES
        if i < split:
            dza_ref[0, :, lanes] = dz
        else:
            dzb_ref[0, :, tile_of(i - split)] = dz
        flowed = (dy.astype(F32) * two_heads(flow, i)).astype(BF16)
        msg_ref[0, 0:NS, lanes] = dot_nn(c_turned, flowed).astype(BF16)


def gated_back(dn, mo, z, gain, xbc, cum, cols, split, after=()):
    seqs, rows, _ = dn.shape
    return call(
        gated_back_kernel,
        "gated_back",
        seqs,
        (dn, mo, z, gain, xbc, cum, cols),
        [
            seq_block(rows, DI),
            seq_block(rows, DI),
            seq_block(rows, DI),
            whole_block(1, DI),
            c_block(rows),
            seq_block(rows, LANES),
            seq_block(rows, LANES),
        ],
        [
            ((seqs, rows, DI), BF16),
            ((seqs, rows, split), BF16),
            ((seqs, rows, DI - split), BF16),
            ((seqs, STATE_ROWS, DI), BF16),
        ],
        [
            seq_block(rows, DI),
            seq_block(rows, split),
            seq_block(rows, DI - split),
            seq_block(STATE_ROWS, DI),
        ],
        [pltpu.VMEM((rows, DI), F32)],
        after=after,
    )


def inside_back_kernel(
    xbc_ref, xd_ref, cum_ref, cols_ref, rows_ref, skip_ref, spread_ref, dy_ref, mo_ref, prev_ref,
    dxd_ref, dbc_ref, sums_ref, dcouple_ref,
):
    rows = xbc_ref.shape[1]
    cum = cum_ref[0]
    flow = jnp.exp(cum) * cols_ref[0, :, 4:5]
    sums = jnp.zeros((rows, LANES), F32)
    dc = jnp.zeros((rows, NS), F32)
    for i in range(DI // LANES):
        lanes = tile_of(i)
        dy = dy_ref[0, :, lanes].astype(F32)
        plain = mo_ref[0, :, lanes] - xbc_ref[0, :, lanes].astype(F32) * skip_ref[0:1, lanes]
        sums = sums + sum_heads(dy * plain, spread_ref[:, lanes])
        dc = dc + dot_nt((dy * two_heads(flow, i)).astype(BF16), prev_ref[0, :, lanes])
    sums_ref[0] = sums
    b_rows, c_rows = xbc_ref[0, :, DI : DI + NS], xbc_ref[0, :, DI + NS :]
    seg_col, seg_row = cols_ref[0, :, 5:6], rows_ref[0, 0:1, :]
    row_at = lax.broadcasted_iota(jnp.int32, (rows, rows), 0)
    col_at = lax.broadcasted_iota(jnp.int32, (rows, rows), 1)
    keep = (seg_col == seg_row) & (row_at <= col_at)
    couple = jnp.where(keep, dot_nt(b_rows, c_rows), 0.0)
    dcouple_ref[...] = jnp.zeros_like(dcouple_ref)
    cum_rows = cum.T
    for first in range(0, H, 2):
        lanes = slice(first * P_SIZE, (first + 2) * P_SIZE)
        dy_sides = side_by_side(dy_ref[0, :, lanes])
        xd = xd_ref[0, :, lanes]
        for begin, end, _ in row_parts(rows):
            dxd, added = [], []
            for h, dy in zip((first, first + 1), dy_sides):
                decay = jnp.exp(jnp.minimum(cum_rows[h : h + 1, begin:] - cum[begin:end, h : h + 1], 0.0))
                mixing = (decay * couple[begin:end, begin:]).astype(BF16)
                dxd.append(dot_nn(mixing, dy[begin:]))
                added.append(dot_nt(xd[begin:end], dy[begin:]) * decay)
            dcouple_ref[begin:end, begin:] += added[0] + added[1]
            dxd_ref[0, begin:end, lanes] = dxd[0] + dxd[1]
    dcouple = jnp.where(keep, dcouple_ref[...], 0.0).astype(BF16)
    dbc_ref[0, :, :NS] = dot_nn(dcouple, c_rows)
    dbc_ref[0, :, NS:] = dc + dot_tn(dcouple, b_rows)


def inside_back(xbc, xd, cum, cols, rows_in, skip, spread, dy, mo, prev, after=()):
    seqs, rows, width = xbc.shape
    return call(
        inside_back_kernel,
        "inside_back",
        seqs,
        (xbc, xd, cum, cols, rows_in, skip, spread, dy, mo, prev),
        [
            seq_block(rows, width),
            seq_block(rows, DI),
            seq_block(rows, LANES),
            seq_block(rows, LANES),
            seq_block(8, rows),
            whole_block(8, DI),
            whole_block(LANES, DI),
            seq_block(rows, DI),
            seq_block(rows, DI),
            seq_block(NS, DI),
        ],
        [((seqs, rows, DI), F32), ((seqs, rows, 2 * NS), F32), ((seqs, rows, LANES), F32)],
        [seq_block(rows, DI), seq_block(rows, 2 * NS), seq_block(rows, LANES)],
        [pltpu.VMEM((rows, rows), F32)],
        after=after,
    )


def mix_end_kernel(
    left_ref, right_ref, halo_ref, xbc_ref, slope_ref, xd_ref, step_ref, cum_ref, cols_ref, heads_ref, skip_ref,
    conv_ref, spread_ref, dy_ref, dxd_ref, dbc_ref, sums_ref, later_ref, prev_ref,
    grad_ref, gconv_ref, gheads_ref, dco_ref, tops_ref,
):
    rows = xbc_ref.shape[1]
    cum = cum_ref[0]
    step = step_ref[0]
    masks = cols_ref[0]
    last = cum[rows - 1 : rows]
    ends = jnp.exp(last - cum) * masks[:, 3:4]
    b_rows = xbc_ref[0, :, DI : DI + NS]
    direct = jnp.zeros((rows, LANES), F32)
    columns = jnp.zeros((rows, LANES), F32)
    db = dbc_ref[0, :, :NS]
    for i in range(DI // LANES):
        lanes = tile_of(i)
        x = xbc_ref[0, :, lanes].astype(F32)
        xd = xd_ref[0, :, lanes].astype(F32)
        dy = dy_ref[0, :, lanes].astype(F32)
        later = later_ref[0, :, lanes]
        to_end = two_heads(ends, i)
        from_end = dot_nn(b_rows, later) * to_end
        dxd = dxd_ref[0, :, lanes] + from_end
        dco_ref[:, lanes] = dxd * two_heads(step, i) + dy * skip_ref[0:1, lanes]
        db = db + dot_nt((xd * to_end).astype(BF16), later)
        direct = direct + dot_nt((x * dxd).astype(BF16), spread_ref[:, lanes])
        columns = columns + sum_heads(xd * dxd, spread_ref[:, lanes])
        tops_ref[:, lanes] = jnp.concatenate(
            [
                jnp.sum(xd * from_end, axis=0, keepdims=True),
                jnp.sum(dy * x, axis=0, keepdims=True),
                jnp.sum(later.astype(F32) * prev_ref[0, :, lanes].astype(F32), axis=0, keepdims=True),
                jnp.zeros((13, LANES), F32),
            ],
            0,
        )
    dco_ref[:, DI : DI + NS] = db
    dco_ref[:, DI + NS :] = dbc_ref[0, :, NS:]
    tops = sum_heads(tops_ref[...], spread_ref[...])
    ended, skipped, carried = tops[0:1], tops[1:2], tops[2:3]
    at = lax.broadcasted_iota(jnp.int32, (rows, LANES), 0)
    dcum = sums_ref[0] - columns
    dcum = dcum + jnp.where(at == rows - 1, ended + jnp.exp(last) * carried, 0.0)
    da = exact_sum(triangle(rows, False), dcum)
    rate = heads_ref[1:2]
    graw = (direct + da * rate) * sigmoid(raw_tile(right_ref) + heads_ref[0:1])
    seqs = grad_ref.shape[0] // (rows + HALO)
    seq = pl.program_id(0)
    main = pl.ds(pl.multiple_of(seq * rows, rows), rows)
    edge = pl.ds(pl.multiple_of(seqs * rows + seq * HALO, HALO), HALO)
    end = CONV_WIDTH + LANES
    grad_ref[main, CONV_WIDTH:end] = graw.astype(BF16)
    grad_ref[edge, CONV_WIDTH:end] = jnp.zeros((HALO, LANES), BF16)
    grad_ref[main, end:] = jnp.zeros((rows, grad_ref.shape[1] - end), BF16)
    grad_ref[edge, end:] = jnp.zeros((HALO, grad_ref.shape[1] - end), BF16)
    gheads_ref[0] = jnp.concatenate(
        [
            jnp.sum(graw, axis=0, keepdims=True),
            jnp.sum(da * step, axis=0, keepdims=True) * rate,
            skipped,
            jnp.zeros((5, LANES), F32),
        ],
        0,
    )
    wide = [jnp.broadcast_to(masks[:, k : k + 1], (rows, LANES)) for k in range(KC - 1)]
    blank = jnp.zeros((HALO, LANES), F32)
    for i in range(CONV_WIDTH // LANES):
        lanes = tile_of(i)
        du = dco_ref[:, lanes] * slope_ref[0, :, lanes].astype(F32)
        own = conv_tile(left_ref, right_ref, i)
        ext = jnp.concatenate([halo_ref[0, :, lanes].astype(F32), own], 0)
        taps = conv_ref[:, lanes]
        grads = []
        total = jnp.zeros((rows + HALO, LANES), F32)
        for k in range(KC):
            part = du * wide[k] if k < KC - 1 else du
            at_ext = HALO - (KC - 1) + k
            grads.append(jnp.sum(part * ext[at_ext : at_ext + rows], axis=0, keepdims=True))
            padded = jnp.concatenate([blank, part, blank], 0)
            total = total + taps[k : k + 1] * padded[KC - 1 - k : KC - 1 - k + rows + HALO]
        grad_ref[main, lanes] = total[HALO:].astype(BF16)
        grad_ref[edge, lanes] = total[:HALO].astype(BF16)
        gconv_ref[0, :, lanes] = jnp.concatenate(
            grads + [jnp.sum(du, axis=0, keepdims=True), jnp.zeros((3, LANES), F32)], 0
        )


def mix_end(
    left, right, halo, xbc, slope, xd, step, cum, cols, heads, skip, conv, spread, dy, dxd, dbc, sums, later, prev,
    after=(),
):
    seqs, rows, width = xbc.shape
    tokens = seqs * (rows + HALO)
    return call(
        mix_end_kernel,
        "mix_end",
        seqs,
        (left, right, halo, xbc, slope, xd, step, cum, cols, heads, skip, conv, spread, dy, dxd, dbc, sums, later, prev),
        [
            seq_block(rows, LEFT),
            seq_block(rows, LEFT),
            seq_block(HALO, halo.shape[2]),
            seq_block(rows, width),
            seq_block(rows, width),
            seq_block(rows, DI),
            seq_block(rows, LANES),
            seq_block(rows, LANES),
            seq_block(rows, LANES),
            whole_block(8, LANES),
            whole_block(8, DI),
            whole_block(8, width),
            whole_block(LANES, DI),
            seq_block(rows, DI),
            seq_block(rows, DI),
            seq_block(rows, 2 * NS),
            seq_block(rows, LANES),
            seq_block(NS, DI),
            seq_block(NS, DI),
        ],
        [
            ((tokens, 2 * LEFT), BF16),
            ((seqs, 8, width), F32),
            ((seqs, 8, LANES), F32),
        ],
        [
            whole_block(tokens, 2 * LEFT),
            seq_block(8, width),
            seq_block(8, LANES),
        ],
        [pltpu.VMEM((rows, width), F32), pltpu.VMEM((16, DI), F32)],
        after=after,
    )


def attend_bias(slot, rest, cols_ref, rows_ref, kv_ref, offsets):
    rows = cols_ref.shape[1]
    found = []
    for before in range(slot + 1):
        for j, offset in enumerate(offsets):
            if before == slot and offset == 0:
                row_at = lax.broadcasted_iota(jnp.int32, (rows, rows), 0)
                col_at = lax.broadcasted_iota(jnp.int32, (rows, rows), 1)
                same = cols_ref[slot, :, 5:6] == rows_ref[slot, 0:1, :]
                allowed = same & (row_at >= col_at)
            else:
                keys = kv_ref[j][before, rows : rows + 16, :rows].astype(F32)[0:1]
                if before == slot:
                    keys = keys * jnp.where((rest ^ offset) < rest, 1.0, 0.0)
                allowed = cols_ref[slot, :, 4:5] * keys > 0.5
            found.append((j, before, jnp.where(allowed, 0.0, NEGATIVE)))
    return found


def swap_halves(pair):
    return jnp.concatenate([pair[:, P_SIZE:], pair[:, :P_SIZE]], 1)


def to_side(pair, group):
    pair_sides, swapped = side_by_side(pair), side_by_side(swap_halves(pair))
    return (pair_sides[0], swapped[0]) if group == 0 else (swapped[1], pair_sides[1])


def from_side(left, right, group):
    lane = lax.broadcasted_iota(jnp.int32, left.shape, 1)
    if group == 0:
        right = swap_halves(right)
    else:
        left = swap_halves(left)
    return jnp.where(lane < P_SIZE, left, right)


def attend_kernel(offsets, rest_ref, q_ref, cols_ref, rows_ref, *refs):
    kv_ref, (out_ref, lse_ref) = refs[:-2], refs[-2:]
    rows = q_ref.shape[1]
    for slot in range(SLOTS):
        blocks = attend_bias(slot, rest_ref[0], cols_ref, rows_ref, kv_ref, offsets)
        sums = []
        for i in range(QUERY_HEADS // 2):
            lanes, group = tile_of(i), (2 * i) // (QUERY_HEADS // KEY_VALUE_HEADS)
            outs = []
            for q in to_side(q_ref[slot, :, lanes] * jnp.asarray(HEAD_WIDTH**-0.5, BF16), group):
                scores = [dot_nt(q, kv_ref[j][n, :rows, :LANES]) + bias for j, n, bias in blocks]
                top = jnp.max(functools.reduce(jnp.maximum, scores), axis=1, keepdims=True)
                weights = [jnp.exp(s - top) for s in scores]
                total = jnp.sum(functools.reduce(jnp.add, weights), axis=1, keepdims=True)
                out = [
                    dot_nn(w.astype(BF16), kv_ref[j][n, :rows, LANES:]) for (j, n, _), w in zip(blocks, weights)
                ]
                outs.append(functools.reduce(jnp.add, out) / total)
                sums.append(top + jnp.log(total))
            out_ref[slot, :, lanes] = from_side(*outs, group).astype(BF16)
        lse_ref[slot] = jnp.concatenate(sums + [jnp.zeros((rows, LANES - QUERY_HEADS), F32)], 1)


def call_whole(kernel, name, scalars, ins, outs, scratch=(), after=()):
    vmem = pl.BlockSpec(memory_space=pltpu.VMEM)
    n_in = len(scalars) + len(ins)

    def run(*refs):
        kernel(*refs[:n_in], *refs[n_in + len(after) :])

    return pl.pallas_call(
        run,
        in_specs=[pl.BlockSpec(memory_space=pltpu.SMEM)] * len(scalars) + [vmem] * len(ins) + spec_any(len(after)),
        out_specs=[vmem] * len(outs),
        out_shape=[jax.ShapeDtypeStruct(s, d) for s, d in outs],
        scratch_shapes=list(scratch),
        compiler_params=pltpu.CompilerParams(vmem_limit_bytes=VMEM_LIMIT),
        name=name,
    )(*scalars, *ins, *after)


def attend(rest, q, kv, cols, rows_in, offsets, after=()):
    outs = [(q.shape, BF16), (q.shape[:2] + (LANES,), F32)]
    return call_whole(
        functools.partial(attend_kernel, offsets), "attend", (rest,), (q, cols, rows_in, *kv), outs, after=after
    )


def attend_back_kernel(
    offsets, rest_ref, q_ref, cols_ref, rows_ref, out_ref, lse_ref, dout_ref, *refs
):
    count = len(offsets)
    kv_ref, dq_ref, dkv_ref, acc_ref = refs[:count], refs[count], refs[count + 1 : -1], refs[-1]
    rows = q_ref.shape[1]
    scale = HEAD_WIDTH**-0.5
    acc_ref[...] = jnp.zeros_like(acc_ref)
    for slot in range(SLOTS):
        blocks = attend_bias(slot, rest_ref[0], cols_ref, rows_ref, kv_ref, offsets)
        for i in range(QUERY_HEADS // 2):
            lanes, group = tile_of(i), (2 * i) // (QUERY_HEADS // KEY_VALUE_HEADS)
            q_pair = q_ref[slot, :, lanes] * jnp.asarray(scale, BF16)
            dout_pair = dout_ref[slot, :, lanes]
            q_turned, dout_turned = q_pair.T, dout_pair.T
            product = dout_pair.astype(F32) * out_ref[slot, :, lanes].astype(F32)
            q_sides, dout_sides = to_side(q_pair, group), to_side(dout_pair, group)
            k_rows = slice(group * HEAD_WIDTH, (group + 1) * HEAD_WIDTH)
            v_rows = slice(LANES + group * HEAD_WIDTH, LANES + (group + 1) * HEAD_WIDTH)
            dqs = []
            for n in range(2):
                own = slice(n * HEAD_WIDTH, (n + 1) * HEAD_WIDTH)
                q, dout = q_sides[n], dout_sides[n]
                delta = jnp.sum(side_by_side(product)[n], axis=1, keepdims=True)
                lse = lse_ref[slot, :, 2 * i + n : 2 * i + n + 1]
                dq = None
                for j, before, bias in blocks:
                    k, v = kv_ref[j][before, :rows, :LANES], kv_ref[j][before, :rows, LANES:]
                    p = jnp.exp(dot_nt(q, k) + bias - lse)
                    ds = (p * (dot_nt(dout, v) - delta)).astype(BF16)
                    part = dot_nn(ds, k)
                    dq = part if dq is None else dq + part
                    acc_ref[j, before, k_rows, :] += dot_nn(q_turned[own], ds)
                    acc_ref[j, before, v_rows, :] += dot_nn(dout_turned[own], p.astype(BF16))
                dqs.append(dq * scale)
            dq_ref[slot, :, lanes] = from_side(*dqs, group).astype(BF16)
    for j in range(len(offsets)):
        for before in range(SLOTS):
            dkv_ref[j][before] = acc_ref[j, before].T.astype(BF16)


def attend_back(rest, q, kv, cols, rows_in, out, lse, dout, offsets, after=()):
    rows, blocks, (slots, _, kv_width) = q.shape[1], len(kv), kv[0].shape
    found = call_whole(
        functools.partial(attend_back_kernel, offsets),
        "attend_back",
        (rest,),
        (q, cols, rows_in, out, lse, dout, *kv),
        [(q.shape, BF16)] + [((slots, rows, kv_width), BF16)] * blocks,
        [pltpu.VMEM((blocks, slots, kv_width, rows), F32)],
        after=after,
    )
    return found[0], found[1:]


def pick_offset(rest, number, group, offsets, pieces, slot):
    wanted = (number % group) ^ rest
    found = None
    for offset, piece in zip(offsets, pieces):
        part = piece[slot].astype(F32)
        found = part if found is None else jnp.where(wanted == offset, part, found)
    return found


def halo_kernel(offsets, rest_ref, *refs):
    pieces, out_ref = refs[:-1], refs[-1]
    rest, group = rest_ref[0], len(pieces)
    for slot in range(SLOTS):
        found = jnp.zeros(out_ref.shape[1:], F32)
        for number in range(group * slot, group * (slot + 1)):
            if number > 0:
                before = number - 1
                part = pick_offset(rest, before, group, offsets, pieces, before // group)
                found = jnp.where(rest == number % group, part, found)
        out_ref[slot] = found.astype(out_ref.dtype)


def take_halo(rest, pieces, offsets):
    return call_whole(
        functools.partial(halo_kernel, offsets), "halo", (rest,), pieces, [(pieces[0].shape, pieces[0].dtype)]
    )[0]


def scan_kernel(offsets, from_earlier, rest_ref, *refs):
    pieces, out_ref = refs[:-1], refs[-1]
    rest, group = rest_ref[0], len(pieces)
    order = list(range(SLOTS * group))
    width = 4 * LANES

    def column(i, _):
        lanes = pl.ds(pl.multiple_of(i * width, width), width)
        state = jnp.zeros((NS, width), F32)
        found = [state] * SLOTS
        for number in order if from_earlier else order[::-1]:
            slot = number // group
            found[slot] = jnp.where(rest == number % group, state, found[slot])
            part = pick_offset(rest, number, group, offsets, [p.at[:, :, lanes] for p in pieces], slot)
            state = part[:NS] + part[NS : NS + 1] * state
        for slot in range(SLOTS):
            out_ref[slot, :, lanes] = found[slot].astype(BF16)
        return 0

    lax.fori_loop(0, DI // width, column, 0)


def scan_states(rest, pieces, offsets, from_earlier, after=()):
    return call_whole(
        functools.partial(scan_kernel, offsets, from_earlier),
        "scan_states",
        (rest,),
        pieces,
        [((SLOTS, NS, DI), BF16)],
        after=after,
    )[0]


def join_grads_kernel(za_ref, zb_ref, q_ref, own_ref, got_ref, out_ref):
    slots, rows, width = own_ref.shape
    at = 0
    for ref in (za_ref, zb_ref, q_ref):
        out_ref[:, at : at + ref.shape[1]] = ref[...]
        at += ref.shape[1]
    for s in range(slots):
        total = own_ref[s].astype(F32) + got_ref[s].astype(F32)
        out_ref[s * rows : (s + 1) * rows, at:] = total.astype(BF16)


def join_grads(za, zb, q, own, got, after=()):
    tokens = za.shape[0]
    width = za.shape[1] + zb.shape[1] + q.shape[1] + own.shape[2]
    return call_whole(
        join_grads_kernel, "join_grads", (), (za, zb, q, own, got), [((tokens, width), BF16)], after=after
    )[0]


def line_place(j, count, r):
    stride = LANES // -(-count // r)
    return j % r, stride * (j // r)


def pack_lines(rows_of, r):
    count = len(rows_of)
    stride = LANES // -(-count // r)
    groups = []
    for begin in range(0, count, r):
        part = [
            jnp.concatenate([v, jnp.zeros((1, stride - v.shape[1]), F32)], 1) for v in rows_of[begin : begin + r]
        ]
        if len(part) < r:
            part.append(jnp.zeros((r - len(part), stride), F32))
        groups.append(jnp.concatenate(part, 0))
    tile = jnp.concatenate(groups, 1) if len(groups) > 1 else groups[0]
    if tile.shape[1] < LANES:
        tile = jnp.concatenate([tile, jnp.zeros((r, LANES - tile.shape[1]), F32)], 1)
    return tile


def pack_first_kernel(xbc_ref, step_ref, conv_ref, bias_ref, mix_ref, one_ref, two_ref, out_ref):
    r = xbc_ref.shape[0]
    over = CONV_WIDTH - LEFT
    out_ref[0] = xbc_ref[:, :LEFT]
    out_ref[1, :, :over] = xbc_ref[:, LEFT:]
    blank = jnp.zeros((r, LANES - H), BF16)
    out_ref[1, :, over : over + LANES] = jnp.concatenate([step_ref[...], blank], 1)
    taps = conv_ref[...].astype(F32)
    vectors = [taps[k : k + 1] for k in range(KC)]
    vectors += [ref[...].astype(F32) for ref in (bias_ref, mix_ref, one_ref, two_ref)]
    out_ref[1, :, over + LANES :] = pack_lines(vectors, r).astype(BF16)


def pack_first(w_xbc, w_step, conv_weight, conv_bias, mixer_gain, norm1_gain, norm2_gain):
    r = w_xbc.shape[0]
    vmem = pl.BlockSpec(memory_space=pltpu.VMEM)
    return pl.pallas_call(
        pack_first_kernel,
        in_specs=[vmem] * 7,
        out_specs=vmem,
        out_shape=jax.ShapeDtypeStruct((2, r, LEFT), BF16),
        name="pack_first",
    )(w_xbc, w_step, conv_weight, conv_bias[None], mixer_gain[None], norm1_gain[None], norm2_gain[None])


def pack_two_kernel(z_ref, query_ref, kv_ref, mix_ref, attn_ref, two_ref):
    r = z_ref.shape[0]
    width = two_ref.shape[2] - MODEL_WIDTH
    two_ref[0, :, :width] = z_ref[:, :width]
    two_ref[1, :, : DI - width] = z_ref[:, width:]
    at = DI - width + query_ref.shape[1]
    two_ref[1, :, DI - width : at] = query_ref[...]
    two_ref[1, :, at:width] = kv_ref[...]
    more = mix_ref.shape[0] - r
    two_ref[0, :, width:] = mix_ref[:r]
    two_ref[1, :more, width:] = mix_ref[r:]
    two_ref[1, more:, width:] = attn_ref[...]


def pack_two(w_gate_z, w_query, key_value_weight, w_mix_out, w_attn_out, after=()):
    width = (DI + w_query.shape[1] + key_value_weight.shape[1]) // 2 + MODEL_WIDTH
    ins = (w_gate_z, w_query, key_value_weight, w_mix_out, w_attn_out)
    return call_whole(pack_two_kernel, "pack_two", (), ins, [((2, w_gate_z.shape[0], width), BF16)], after=after)[0]


def pack_units_kernel(gate_up_ref, down_ref, units_ref):
    r, half = gate_up_ref.shape[0], down_ref.shape[0] // 2
    for n in range(2):
        for q in range(2):
            column = (2 * n + q) * MODEL_WIDTH
            units_ref[n, q * r : (q + 1) * r] = gate_up_ref[:, column : column + MODEL_WIDTH]
        units_ref[n, 2 * r :] = down_ref[n * half : (n + 1) * half]


def pack_units(w_gate_up, w_down, after=()):
    shape = (2, 2 * w_gate_up.shape[0] + w_down.shape[0] // 2, MODEL_WIDTH)
    return call_whole(pack_units_kernel, "pack_units", (), (w_gate_up, w_down), [(shape, BF16)], after=after)[0]


def unpack_small_kernel(r, small_ref, conv_ref, mix_ref, gain_ref):
    count = small_ref.shape[0] // r
    widths = [CONV_WIDTH // count] * (KC + 1) + [DI // count] + [MODEL_WIDTH // count] * 2
    found = [[] for _ in widths]
    for i in range(count):
        tile = small_ref[i * r : (i + 1) * r, :].astype(F32)
        for j, width in enumerate(widths):
            row, lane = line_place(j, len(widths), r)
            found[j].append(tile[row : row + 1, lane : lane + width])
    found = [jnp.concatenate(v, 1) for v in found]
    conv_ref[...] = jnp.concatenate(found[: KC + 1] + [jnp.zeros((3, CONV_WIDTH), F32)], 0)
    mix_ref[...] = found[KC + 1]
    gain_ref[...] = jnp.concatenate(found[KC + 2 :], 0)


def unpack_small(small, r):
    vmem = pl.BlockSpec(memory_space=pltpu.VMEM)
    return pl.pallas_call(
        functools.partial(unpack_small_kernel, r),
        in_specs=[vmem],
        out_specs=[vmem] * 3,
        out_shape=[jax.ShapeDtypeStruct(s, F32) for s in ((8, CONV_WIDTH), (1, DI), (2, MODEL_WIDTH))],
        name="unpack_small",
    )(small)


def small_grads_kernel(r, offsets, place_ref, conv_ref, heads_ref, keep_ref, send_ref, tile_ref):
    count = tile_ref.shape[0]
    conv = jnp.sum(conv_ref[...], 0)
    heads = jnp.sum(heads_ref[...], 0)
    width = CONV_WIDTH // count
    shared = [heads[k : k + 1, :H] for k in range(3)]
    high = [v.astype(BF16).astype(F32) for v in shared]
    shared = high + [v - h for v, h in zip(shared, high)]
    for i in range(count):
        own = [conv[k : k + 1, i * width : (i + 1) * width] for k in range(KC + 1)]
        tile_ref[i] = pack_lines(own + shared, r)
    place = place_ref[0]
    for t, offset in enumerate(offsets):
        keep_ref[t * r : (t + 1) * r] = tile_ref[place ^ offset].astype(BF16)
        send_ref[t * r : (t + 1) * r] = tile_ref[place ^ (offset ^ 1)].astype(BF16)


def small_grads(r, conv, heads):
    bits = bit_count()
    count = 1 << bits
    vmem = pl.BlockSpec(memory_space=pltpu.VMEM)
    return pl.pallas_call(
        functools.partial(small_grads_kernel, r, turned_offsets(bits)),
        in_specs=[pl.BlockSpec(memory_space=pltpu.SMEM)] + [vmem] * 2,
        out_specs=[vmem] * 2,
        out_shape=[jax.ShapeDtypeStruct((count // 2 * r, LANES), BF16)] * 2,
        scratch_shapes=[pltpu.VMEM((count, r, LANES), F32)],
        name="small_grads",
    )(place_of().reshape(1).astype(jnp.int32), conv, heads)


def tiles_spec(shape, axis, width):
    block = tuple(width if n == axis else size for n, size in enumerate(shape))
    return pl.BlockSpec(block, lambda i: tuple(i if n == axis else 0 for n in range(len(shape))))


def fixed(*shape):
    return pl.BlockSpec(shape, lambda i: (0,) * len(shape))


def dense(kernel, name, steps, ins, in_specs, outs, out_specs, scratch=(), after=()):
    n_in, n_after = len(ins), len(after)

    def run(*refs):
        kernel(*refs[:n_in], *refs[n_in + n_after :])

    return pl.pallas_call(
        run,
        grid=(steps,),
        in_specs=list(in_specs) + spec_any(n_after),
        out_specs=out_specs,
        out_shape=[jax.ShapeDtypeStruct(s, d) for s, d in outs],
        scratch_shapes=list(scratch),
        compiler_params=pltpu.CompilerParams(vmem_limit_bytes=VMEM_LIMIT),
        name=name,
    )(*ins, *after)


def row_scale(values):
    return lax.rsqrt(jnp.mean(values * values, axis=1, keepdims=True) + EPSILON)


def first_proj_kernel(x_ref, gain_ref, left_w, right_w, cols_ref, normed_ref, left_ref, right_ref, tails_ref):
    step, tile = pl.program_id(0), left_w.shape[1]

    @pl.when(step == 0)
    def _():
        x = x_ref[...].astype(F32)
        normed_ref[...] = (x * row_scale(x) * gain_ref[...]).astype(BF16)

    left = dot_nn(normed_ref[...], left_w[...]).astype(BF16)
    right = dot_nn(normed_ref[...], right_w[...])
    left_ref[...] = left
    right_ref[...] = right
    slots, rows, _ = cols_ref.shape
    lanes = pl.ds(pl.multiple_of(step * tile, tile), tile)
    for s in range(slots):
        begin, end = (s + 1) * rows - HALO, (s + 1) * rows
        edge = cols_ref[s, rows - HALO :, 3:4]
        tails_ref[s, :, lanes] = (left[begin:end].astype(F32) * edge).astype(BF16)
        normed = normed_ref[begin:end, lanes].astype(F32)
        tails_ref[s, :, pl.ds(pl.multiple_of(CONV_WIDTH + step * tile, tile), tile)] = (normed * edge).astype(BF16)

        @pl.when(step < (CONV_WIDTH - LEFT) // tile)
        def _():
            at = pl.ds(pl.multiple_of(LEFT + step * tile, tile), tile)
            tails_ref[s, :, at] = (right[begin:end].astype(BF16).astype(F32) * edge).astype(BF16)


def first_proj(x, gain, left_full, right_full, cols, after=()):
    tokens, width = x.shape
    tile = LEFT // 4
    tails = (cols.shape[0], HALO, CONV_WIDTH + width)
    return dense(
        first_proj_kernel,
        "first_proj",
        4,
        (x, gain, left_full, right_full, cols),
        [
            fixed(tokens, width),
            fixed(1, width),
            tiles_spec((width, LEFT), 1, tile),
            tiles_spec((width, LEFT), 1, tile),
            fixed(*cols.shape),
        ],
        [((tokens, width), BF16), ((tokens, LEFT), BF16), ((tokens, LEFT), F32), (tails, BF16)],
        [
            fixed(tokens, width),
            tiles_spec((tokens, LEFT), 1, tile),
            tiles_spec((tokens, LEFT), 1, tile),
            fixed(*tails),
        ],
        after=after,
    )


def second_proj_kernel(normed_ref, z_w, qkv_w, rows_ref, z_ref, q_ref, kv_ref):
    step = pl.program_id(0)
    z_ref[...] = dot_nn(normed_ref[...], z_w[...])
    part = dot_nn(normed_ref[...], qkv_w[...]).astype(BF16)
    slots, extended, width = kv_ref.shape
    rows = extended - 16

    @pl.when(step < 2)
    def _():
        q_ref[...] = part

    @pl.when(step == 2)
    def _():
        for s in range(slots):
            kv_ref[s, :rows] = part[s * rows : (s + 1) * rows]
            keys = jnp.broadcast_to(rows_ref[s, 1:2], (16, rows))
            if rows < width:
                keys = jnp.concatenate([keys, jnp.zeros((16, width - rows), F32)], 1)
            kv_ref[s, rows:] = keys.astype(BF16)


def second_proj(normed, z_full, qkv_full, rows_in, after=()):
    tokens, width = normed.shape
    slots, _, rows = rows_in.shape
    query, kv = QUERY_HEADS * HEAD_WIDTH, 2 * KEY_VALUE_HEADS * HEAD_WIDTH
    return dense(
        second_proj_kernel,
        "second_proj",
        3,
        (normed, z_full, qkv_full, rows_in),
        [
            fixed(tokens, width),
            tiles_spec((width, DI), 1, DI // 3),
            tiles_spec((width, query + kv), 1, kv),
            fixed(slots, 8, rows),
        ],
        [((tokens, DI), F32), ((tokens, query), BF16), ((slots, rows + 16, kv), BF16)],
        [
            tiles_spec((tokens, DI), 1, DI // 3),
            pl.BlockSpec((tokens, kv), lambda i: (0, jnp.minimum(i, 1))),
            fixed(slots, rows + 16, kv),
        ],
        after=after,
    )


def out_proj_kernel(x_ref, nm_ref, attn_ref, mix_w, attn_w, gain_ref, resid_ref, normed_ref):
    step = pl.program_id(0)
    part = dot_nn(nm_ref[...], mix_w[...]) + dot_nn(attn_ref[...], attn_w[...])

    @pl.when(step == 0)
    def _():
        resid_ref[...] = x_ref[...].astype(F32) + part

    @pl.when(step > 0)
    def _():
        resid_ref[...] += part

    @pl.when(step == pl.num_programs(0) - 1)
    def _():
        resid = resid_ref[...]
        normed_ref[...] = (resid * row_scale(resid) * gain_ref[...]).astype(BF16)


def out_proj(x, nm, attn, mix_full, attn_full, gain, after=()):
    tokens, width = x.shape
    query = attn.shape[1]
    steps = 2
    return dense(
        out_proj_kernel,
        "out_proj",
        steps,
        (x, nm, attn, mix_full, attn_full, gain),
        [
            fixed(tokens, width),
            tiles_spec(nm.shape, 1, DI // steps),
            tiles_spec(attn.shape, 1, query // steps),
            tiles_spec(mix_full.shape, 0, DI // steps),
            tiles_spec(attn_full.shape, 0, query // steps),
            fixed(1, width),
        ],
        [((tokens, width), F32), ((tokens, width), BF16)],
        [fixed(tokens, width), fixed(tokens, width)],
        after=after,
    )


def gate_up_kernel(normed_ref, gate_w, up_w, act_ref, swish_ref, slope_ref):
    gate = dot_nn(normed_ref[...], gate_w[...])
    up = dot_nn(normed_ref[...], up_w[...])
    sig = sigmoid(gate)
    swish = gate * sig
    act_ref[...] = (swish * up).astype(BF16)
    swish_ref[...] = swish.astype(BF16)
    slope_ref[...] = ((sig + swish * (1.0 - sig)) * up).astype(BF16)


def gate_up(normed, gate_full, up_full, after=()):
    tokens, width = normed.shape
    tile = FF // 2
    spec = tiles_spec((tokens, FF), 1, tile)
    return dense(
        gate_up_kernel,
        "gate_up",
        2,
        (normed, gate_full, up_full),
        [fixed(tokens, width), tiles_spec((width, FF), 1, tile), tiles_spec((width, FF), 1, tile)],
        [((tokens, FF), BF16)] * 3,
        [spec] * 3,
        after=after,
    )


def down_kernel(act_ref, swish_ref, slope_ref, down_w, resid_ref, grad_ref, out_ref, dgate_ref, dup_ref, total_ref):
    step = pl.program_id(0)
    weights = down_w[...]
    part = dot_nn(act_ref[...], weights)

    @pl.when(step == 0)
    def _():
        total_ref[...] = resid_ref[...] + part

    @pl.when(step > 0)
    def _():
        total_ref[...] += part

    @pl.when(step == pl.num_programs(0) - 1)
    def _():
        out_ref[...] = total_ref[...].astype(BF16)

    dact = dot_nt(grad_ref[...], weights)
    dgate_ref[...] = (dact * slope_ref[...].astype(F32)).astype(BF16)
    dup_ref[...] = (dact * swish_ref[...].astype(F32)).astype(BF16)


def down(act, swish, slope, down_full, resid, grad_out, after=()):
    tokens, width = resid.shape
    tile = FF // 2
    spec = tiles_spec((tokens, FF), 1, tile)
    return dense(
        down_kernel,
        "down",
        2,
        (act, swish, slope, down_full, resid, grad_out),
        [spec, spec, spec, tiles_spec((FF, width), 0, tile), fixed(tokens, width), fixed(tokens, width)],
        [((tokens, width), BF16), ((tokens, FF), BF16), ((tokens, FF), BF16)],
        [fixed(tokens, width), spec, spec],
        [pltpu.VMEM((tokens, width), F32)],
        after=after,
    )


def gate_up_back_kernel(
    dgate_ref, dup_ref, gate_w, up_w, resid_ref, gain_ref, grad_ref, back_ref, branch_ref, total_ref
):
    step = pl.program_id(0)
    part = dot_nt(dgate_ref[...], gate_w[...]) + dot_nt(dup_ref[...], up_w[...])

    @pl.when(step == 0)
    def _():
        total_ref[...] = part

    @pl.when(step > 0)
    def _():
        total_ref[...] += part

    @pl.when(step == pl.num_programs(0) - 1)
    def _():
        resid = resid_ref[...]
        scale = row_scale(resid)
        scaled = resid * scale
        dnormed = total_ref[...]
        dscaled = dnormed * gain_ref[...]
        mean = jnp.mean(dscaled * scaled, axis=1, keepdims=True)
        back = grad_ref[...].astype(F32) + (dscaled - scaled * mean) * scale
        back_ref[...] = back
        branch_ref[...] = back.astype(BF16)


def gate_up_back(dgate, dup, gate_full, up_full, resid, gain, grad_out, after=()):
    tokens, width = resid.shape
    tile = FF // 2
    spec, w_spec, whole = tiles_spec((tokens, FF), 1, tile), tiles_spec((width, FF), 1, tile), fixed(tokens, width)
    return dense(
        gate_up_back_kernel,
        "gate_up_back",
        2,
        (dgate, dup, gate_full, up_full, resid, gain, grad_out),
        [spec, spec, w_spec, w_spec, whole, fixed(1, width), whole],
        [((tokens, width), F32), ((tokens, width), BF16)],
        [whole, whole],
        [pltpu.VMEM((tokens, width), F32)],
        after=after,
    )


def out_back_kernel(branch_ref, mix_w, attn_w, dnm_ref, dattn_ref):
    dnm_ref[...] = dot_nt(branch_ref[...], mix_w[...])
    dattn_ref[...] = dot_nt(branch_ref[...], attn_w[...]).astype(BF16)


def out_back(branch, mix_full, attn_full, after=()):
    tokens, width = branch.shape
    query = attn_full.shape[0]
    steps = 2
    return dense(
        out_back_kernel,
        "out_back",
        steps,
        (branch, mix_full, attn_full),
        [
            fixed(tokens, width),
            tiles_spec(mix_full.shape, 0, DI // steps),
            tiles_spec(attn_full.shape, 0, query // steps),
        ],
        [((tokens, DI), F32), ((tokens, query), BF16)],
        [tiles_spec((tokens, DI), 1, DI // steps), tiles_spec((tokens, query), 1, query // steps)],
        after=after,
    )


def second_back_kernel(grad_ref, z_w, qkv_w, out_ref):
    out_ref[...] = dot_nt(grad_ref[:, :DI], z_w[...]) + dot_nt(grad_ref[:, DI:], qkv_w[...])


def second_back(grad, z_full, qkv_full, after=()):
    tokens, width = grad.shape[0], z_full.shape[0]
    tile = width // 2
    return dense(
        second_back_kernel,
        "second_back",
        2,
        (grad, z_full, qkv_full),
        [fixed(*grad.shape), tiles_spec(z_full.shape, 0, tile), tiles_spec(qkv_full.shape, 0, tile)],
        [((tokens, width), F32)],
        [tiles_spec((tokens, width), 1, tile)],
        after=after,
    )[0]


def first_back_kernel(grad_ref, left_w, right_w, part_ref, out_ref, edge_ref):
    tokens = part_ref.shape[0]
    total = dot_nt(grad_ref[:, :LEFT], left_w[...]) + dot_nt(grad_ref[:, LEFT:], right_w[...])
    out_ref[...] = total[:tokens] + part_ref[...]
    edge_ref[...] = total[tokens:]


def first_back(grad, left_full, right_full, part, after=()):
    tokens, width = part.shape
    ext = grad.shape[0]
    tile = width // 2
    w_spec = tiles_spec((width, LEFT), 0, tile)
    return dense(
        first_back_kernel,
        "first_back",
        2,
        (grad, left_full, right_full, part),
        [fixed(*grad.shape), w_spec, w_spec, tiles_spec((tokens, width), 1, tile)],
        [((tokens, width), F32), ((ext - tokens, width), F32)],
        [tiles_spec((tokens, width), 1, tile), tiles_spec((ext - tokens, width), 1, tile)],
        after=after,
    )


def input_back_kernel(gn_ref, next_ref, x_ref, gain_ref, resid_ref, out_ref, low_ref):
    rows = gn_ref.shape[0]
    x = x_ref[...].astype(F32)
    scale = row_scale(x)
    scaled = x * scale
    tail = gn_ref[rows - HALO :] + next_ref[0]
    dscaled = jnp.concatenate([gn_ref[: rows - HALO], tail], 0) * gain_ref[...]
    mean = jnp.mean(dscaled * scaled, axis=1, keepdims=True)
    total = resid_ref[...] + (dscaled - scaled * mean) * scale
    out_ref[0] = total
    low_ref[0] = total.astype(BF16)


def input_back(gn, from_next, x, gain, resid, after=()):
    slots = from_next.shape[0]
    rows, width = gn.shape[0] // slots, gn.shape[1]
    spec = pl.BlockSpec((rows, width), lambda s: (s, 0))
    return dense(
        input_back_kernel,
        "input_back",
        slots,
        (gn, from_next, x, gain, resid),
        [spec, seq_block(HALO, width), spec, fixed(1, width), spec],
        [((slots, rows, width), F32), ((slots, rows, width), BF16)],
        [seq_block(rows, width)] * 2,
        after=after,
    )


def pick_kernel(index_ref, block_ref, out_ref):
    out_ref[...] = block_ref[0]


def pick(block, index, after=()):
    n_after = len(after)

    def run(index_ref, block_ref, *refs):
        pick_kernel(index_ref, block_ref, refs[n_after])

    return pl.pallas_call(
        run,
        grid_spec=pltpu.PrefetchScalarGridSpec(
            num_scalar_prefetch=1,
            grid=(1,),
            in_specs=[pl.BlockSpec((1,) + block.shape[1:], lambda i, index: (index[0], 0, 0))] + spec_any(n_after),
            out_specs=pl.BlockSpec(block.shape[1:], lambda i, index: (0, 0)),
        ),
        out_shape=jax.ShapeDtypeStruct(block.shape[1:], block.dtype),
        name="pick",
    )(index.reshape(1).astype(jnp.int32), block, *after)


def merge_kernel(side_ref, block_ref, got_ref, out_ref):
    keep = pl.program_id(0) == side_ref[0]

    @pl.when(keep)
    def _():
        out_ref[0] = block_ref[0]

    @pl.when(jnp.logical_not(keep))
    def _():
        out_ref[0] = got_ref[...]


def merge(block, got, side, after=()):
    slots, rows, width = block.shape
    n_after = len(after)

    def run(side_ref, block_ref, got_ref, *refs):
        merge_kernel(side_ref, block_ref, got_ref, refs[n_after])

    return pl.pallas_call(
        run,
        grid=(slots,),
        in_specs=[
            pl.BlockSpec(memory_space=pltpu.SMEM),
            seq_block(rows, width),
            pl.BlockSpec((rows, width), lambda s: (0, 0)),
        ]
        + spec_any(n_after),
        out_specs=seq_block(rows, width),
        out_shape=jax.ShapeDtypeStruct(block.shape, block.dtype),
        name="merge",
    )(side.reshape(1).astype(jnp.int32), block, got, *after)


def units_kernel(n_in, jobs, place_ref, normed_ref, *refs):
    ins, refs = refs[:n_in], refs[n_in:]
    act_ref, swish_ref, slope_ref = refs[:3]
    fulls, held, sems, out_sems = refs[3:6], refs[6:9], refs[9], refs[10]
    place = place_ref[0]
    waits = {}
    for number, (group, out, source, source_at, target_at) in enumerate(jobs):
        copy = pltpu.make_async_copy(
            ins[source].at[source_at], held[out].at[target_at(place)], sems.at[number]
        )
        copy.start()
        waits.setdefault(group, []).append(copy)
    normed = normed_ref[...]
    blocks, r, width = held[0].shape
    chunk_width = 512
    for q in range(width // MODEL_WIDTH):
        for copy in waits[q]:
            copy.wait()
        for at in range(q * MODEL_WIDTH, (q + 1) * MODEL_WIDTH, chunk_width):
            lanes = slice(at, at + chunk_width)
            gate = dot_nn(normed, held[0][:, :, lanes].reshape(blocks * r, chunk_width))
            up = dot_nn(normed, held[1][:, :, lanes].reshape(blocks * r, chunk_width))
            sig = sigmoid(gate)
            swish = gate * sig
            act_ref[:, lanes] = (swish * up).astype(BF16)
            swish_ref[:, lanes] = swish.astype(BF16)
            slope_ref[:, lanes] = ((sig + swish * (1.0 - sig)) * up).astype(BF16)
    back = []
    for out in range(3):
        if out == 2:
            for copy in waits[width // MODEL_WIDTH]:
                copy.wait()
        copy = pltpu.make_async_copy(held[out], fulls[out], out_sems.at[out])
        copy.start()
        back.append(copy)
    for copy in back:
        copy.wait()


def gate_up_pieces(normed, parts, r, rd, after=()):
    count, mw = lax.axis_size(BOTH), MODEL_WIDTH
    ins, jobs = [], []
    for n, part in enumerate(parts):
        for piece, offsets in part.pieces:
            for j, offset in enumerate(offsets):
                for q in range(2):
                    source_at = (j, pl.ds(q * r, r))
                    target = lambda place, o=offset, q=q: (place ^ o, slice(None), pl.ds(q * mw, mw))
                    jobs.append((q, n, len(ins), source_at, target))
                source_at = (j, pl.ds(2 * r, rd // 2))
                target = lambda place, o=offset, n=n: (place ^ o, pl.ds(n * (rd // 2), rd // 2))
                jobs.append((2, 2, len(ins), source_at, target))
            ins.append(in_hbm(piece))
    jobs.sort(key=lambda job: job[0])
    tokens = normed.shape[0]
    shapes = [(count, r, FF), (count, r, FF), (count, rd, mw)]
    vmem = pl.BlockSpec(memory_space=pltpu.VMEM)
    n_after = len(after)

    def run(place_ref, normed_ref, *refs):
        units_kernel(len(ins), jobs, place_ref, normed_ref, *refs[: len(ins)], *refs[len(ins) + n_after :])

    found = pl.pallas_call(
        run,
        in_specs=[pl.BlockSpec(memory_space=pltpu.SMEM), vmem] + spec_any(len(ins) + n_after),
        out_specs=[vmem] * 3 + spec_any(3),
        out_shape=[jax.ShapeDtypeStruct((tokens, FF), BF16)] * 3 + [jax.ShapeDtypeStruct(s, BF16) for s in shapes],
        scratch_shapes=[pltpu.VMEM(s, BF16) for s in shapes]
        + [pltpu.SemaphoreType.DMA((len(jobs),)), pltpu.SemaphoreType.DMA((3,))],
        compiler_params=pltpu.CompilerParams(vmem_limit_bytes=UNITS_LIMIT * 2**20),
        name="gate_up_pieces",
    )(place_of().reshape(1).astype(jnp.int32), normed, *ins, *after)
    return list(found[:3]) + [a.reshape(-1, a.shape[2]) for a in found[3:]]


UNITS_LIMIT = 48


def piece_jobs(parts, moves):
    ins, jobs = [], []
    for at, part in enumerate(parts):
        for piece, offsets, *of_part in part.pieces:
            for j, offset in enumerate(offsets):
                for of, r0, rows, c0, columns, out, row, column in moves:
                    if of == at:
                        source_at = (*of_part, j, pl.ds(r0, rows), pl.ds(c0, columns))
                        target = (pl.ds(row, rows), pl.ds(column, columns))
                        jobs.append(
                            (out, len(ins), source_at, lambda place, o=offset, t=target: (place ^ o,) + t)
                        )
            ins.append(in_hbm(piece))
    return ins, sorted(jobs, key=lambda job: job[0])


def start_pieces(jobs, place, ins, held, sems):
    waits = [[] for _ in held]
    for number, (out, source, source_at, target_at) in enumerate(jobs):
        copy = pltpu.make_async_copy(
            ins[source].at[source_at], held[out].at[target_at(place)], sems.at[number]
        )
        copy.start()
        waits[out].append(copy)
    return waits


def land(waits, held, full, sem):
    for copy in waits:
        copy.wait()
    copy = pltpu.make_async_copy(held, full, sem)
    copy.start()
    return copy


def pieces_call(kernel, name, parts, moves, shapes, ins, outs, after=()):
    pieces, jobs = piece_jobs(parts, moves)
    n_in, n_pieces, n_out, n_full = len(ins), len(pieces), len(outs), len(shapes)

    def run(place_ref, *refs):
        arrays, refs = refs[:n_in], refs[n_in:]
        sources, refs = refs[:n_pieces], refs[n_pieces + len(after) :]
        results, fulls, refs = refs[:n_out], refs[n_out : n_out + n_full], refs[n_out + n_full :]
        held, sems, out_sems = refs[:n_full], refs[n_full], refs[n_full + 1]
        waits = start_pieces(jobs, place_ref[0], sources, held, sems)
        kernel(waits, held, fulls, out_sems, *arrays, *results)

    vmem = pl.BlockSpec(memory_space=pltpu.VMEM)
    found = pl.pallas_call(
        run,
        in_specs=[pl.BlockSpec(memory_space=pltpu.SMEM)] + [vmem] * n_in + spec_any(n_pieces + len(after)),
        out_specs=[vmem] * n_out + spec_any(n_full),
        out_shape=[jax.ShapeDtypeStruct(s, d) for s, d in outs] + [jax.ShapeDtypeStruct(s, BF16) for s in shapes],
        scratch_shapes=[pltpu.VMEM(s, BF16) for s in shapes]
        + [pltpu.SemaphoreType.DMA((len(jobs),)), pltpu.SemaphoreType.DMA((n_full,))],
        compiler_params=pltpu.CompilerParams(vmem_limit_bytes=VMEM_LIMIT),
        name=name,
    )(place_of().reshape(1).astype(jnp.int32), *ins, *pieces, *after)
    return list(found[:n_out]) + [a.reshape(-1, a.shape[2]) for a in found[n_out:]]


def whole_of(held, lanes):
    blocks, r, _ = held.shape
    return held[:, :, lanes].reshape(blocks * r, lanes.stop - lanes.start)


def first_pieces_kernel(
    waits, held, fulls, sems, x_ref, cols_ref,
    normed_ref, left_ref, right_ref, tails_ref, conv_ref, mix_ref, gain_ref,
):
    back = [land(waits[1], held[1], fulls[1], sems.at[1])]
    count, r, _ = held[1].shape
    widths = [CONV_WIDTH // count] * (KC + 1) + [DI // count] + [MODEL_WIDTH // count] * 2
    found = [[] for _ in widths]
    for i in range(count):
        tile = held[1][i, :, LEFT - LANES :].astype(F32)
        for j, width in enumerate(widths):
            row, lane = line_place(j, len(widths), r)
            found[j].append(tile[row : row + 1, lane : lane + width])
    found = [jnp.concatenate(v, 1) for v in found]
    conv_ref[...] = jnp.concatenate(found[: KC + 1] + [jnp.zeros((3, CONV_WIDTH), F32)], 0)
    mix_ref[...] = found[KC + 1]
    gain_ref[...] = jnp.concatenate(found[KC + 2 :], 0)
    x = x_ref[...].astype(F32)
    normed_ref[...] = (x * row_scale(x) * found[KC + 2]).astype(BF16)
    normed = normed_ref[...]
    for at in range(0, LEFT, 512):
        lanes = slice(at, at + 512)
        right_ref[:, lanes] = dot_nn(normed, whole_of(held[1], lanes))
    back.append(land(waits[0], held[0], fulls[0], sems.at[0]))
    for at in range(0, LEFT, 512):
        lanes = slice(at, at + 512)
        left_ref[:, lanes] = dot_nn(normed, whole_of(held[0], lanes)).astype(BF16)
    slots, rows, _ = cols_ref.shape
    over = CONV_WIDTH - LEFT
    for s in range(slots):
        begin, end = (s + 1) * rows - HALO, (s + 1) * rows
        edge = cols_ref[s, rows - HALO :, 3:4]
        tails_ref[s, :, :LEFT] = (left_ref[begin:end].astype(F32) * edge).astype(BF16)
        right = right_ref[begin:end, :over].astype(BF16).astype(F32)
        tails_ref[s, :, LEFT:CONV_WIDTH] = (right * edge).astype(BF16)
        tails_ref[s, :, CONV_WIDTH:] = (normed_ref[begin:end].astype(F32) * edge).astype(BF16)
    for copy in back:
        copy.wait()


def first_pieces(x, cols, parts, r, after=()):
    tokens, width = x.shape
    count = lax.axis_size(BOTH)
    moves = [(0, 0, r, 0, LEFT, 0, 0, 0), (1, 0, r, 0, LEFT, 1, 0, 0)]
    outs = [
        ((tokens, width), BF16),
        ((tokens, LEFT), BF16),
        ((tokens, LEFT), F32),
        ((cols.shape[0], HALO, CONV_WIDTH + width), BF16),
        ((8, CONV_WIDTH), F32),
        ((1, DI), F32),
        ((2, width), F32),
    ]
    return pieces_call(
        first_pieces_kernel, "first_pieces", parts, moves, [(count, r, LEFT)] * 2, (x, cols), outs, after
    )


def second_pieces_kernel(waits, held, fulls, sems, normed_ref, rows_ref, z_ref, q_ref, kv_ref):
    normed = normed_ref[...]
    back = [land(waits[1], held[1], fulls[1], sems.at[1])]
    query = q_ref.shape[1]
    slots, extended, width = kv_ref.shape
    rows = extended - 16
    q_ref[...] = dot_nn(normed, whole_of(held[1], slice(0, query))).astype(BF16)
    part = dot_nn(normed, whole_of(held[1], slice(query, query + width))).astype(BF16)
    for s in range(slots):
        kv_ref[s, :rows] = part[s * rows : (s + 1) * rows]
        keys = jnp.broadcast_to(rows_ref[s, 1:2], (16, rows))
        if rows < width:
            keys = jnp.concatenate([keys, jnp.zeros((16, width - rows), F32)], 1)
        kv_ref[s, rows:] = keys.astype(BF16)
    back.append(land(waits[0], held[0], fulls[0], sems.at[0]))
    for at in range(0, DI, 512):
        lanes = slice(at, at + 512)
        z_ref[:, lanes] = dot_nn(normed, whole_of(held[0], lanes))
    for copy in back:
        copy.wait()


def second_pieces(normed, rows_in, parts, moves, r, after=()):
    tokens, width = normed.shape
    slots, _, rows = rows_in.shape
    count = lax.axis_size(BOTH)
    query, kv = QUERY_HEADS * HEAD_WIDTH, 2 * KEY_VALUE_HEADS * HEAD_WIDTH
    outs = [((tokens, DI), F32), ((tokens, query), BF16), ((slots, rows + 16, kv), BF16)]
    shapes = [(count, r, DI), (count, r, query + kv)]
    return pieces_call(
        second_pieces_kernel, "second_pieces", parts, moves, shapes, (normed, rows_in), outs, after
    )


def fsdp_bits():
    return lax.axis_size("fsdp").bit_length() - 1


def fsdp_exchange(block, bit):
    return lax.ppermute(block, "fsdp", [(i, i ^ (1 << bit)) for i in range(lax.axis_size("fsdp"))])


def side_of():
    return lax.axis_index("fsdp") >> (fsdp_bits() - 1)


def swap_start(block):
    return fsdp_exchange(lax.dynamic_index_in_dim(block, 1 - side_of(), 0, False), fsdp_bits() - 1)


def swap_end(block, got):
    return lax.dynamic_update_index_in_dim(block, got.astype(block.dtype), 1 - side_of(), 0)


def gather_sequence(block):
    pieces, offsets = [block], [0]
    for bit in range(fsdp_bits() - 1):
        pieces = pieces + [fsdp_exchange(a, bit) for a in pieces]
        offsets = offsets + [o ^ (1 << bit) for o in offsets]
    return pieces, tuple(offsets)


def sum_sequence(blocks):
    blocks = list(blocks)
    for bit in range(fsdp_bits() - 2, -1, -1):
        half = len(blocks) // 2
        got = [fsdp_exchange(a, bit) for a in blocks[half:]]
        if half > 1:
            blocks = [(a.astype(F32) + b.astype(F32)).astype(BF16) for a, b in zip(blocks, got)]
        else:
            blocks = [blocks[0], got[0]]
    return blocks


def rest_place():
    return lax.axis_index("fsdp") & (lax.axis_size("fsdp") // 2 - 1)


def from_next_part(block):
    pieces, offsets = gather_sequence(block)
    group, rest = len(pieces), rest_place()
    found = [jnp.zeros(block.shape[1:], block.dtype)] * SLOTS
    for number in range(SLOTS * group - 1):
        slot, after = number // group, number + 1
        for offset, piece in zip(offsets, pieces):
            match = (rest == number % group) & ((after % group) ^ rest == offset)
            found[slot] = jnp.where(match, piece[after // group], found[slot])
    return jnp.stack(found)


def sequence_masks(segs):
    slots, rows = segs.shape
    behind = (lax.iota(jnp.int32, slots)[:, None] > 0) | (rest_place() > 0)
    first = (segs == segs[:, :1]) & behind
    keep_end = segs == segs[:, -1:]
    columns = []
    for k in range(KC - 1):
        back = KC - 1 - k
        inside = segs[:, back:] == segs[:, : rows - back]
        columns.append(jnp.concatenate([first[:, :back], inside], 1).astype(F32))
    columns += [keep_end.astype(F32), first.astype(F32), segs.astype(F32)]
    cols = jnp.stack(columns, 2)
    cols = jnp.pad(cols, ((0, 0), (0, 0), (0, LANES - cols.shape[2])))
    rows_in = jnp.pad(jnp.stack([segs, keep_end.astype(segs.dtype)], 1).astype(F32), ((0, 0), (0, 6), (0, 0)))
    return cols, rows_in, keep_end


def per_device(
    hidden_in,
    segment_ids,
    norm1_gain,
    w_gate_z,
    w_xbc,
    w_step,
    conv_weight,
    conv_bias,
    step_bias,
    decay_log,
    skip_gain,
    mixer_gain,
    w_mix_out,
    w_query,
    key_value_weight,
    w_attn_out,
    norm2_gain,
    w_gate_up,
    w_down,
    out_grad,
):
    rows = hidden_in.shape[2]
    seqs = hidden_in.shape[0] * hidden_in.shape[1]
    flat_rows = seqs * rows
    count = lax.axis_size(BOTH)
    query_width = QUERY_HEADS * HEAD_WIDTH
    kv_width = 2 * KEY_VALUE_HEADS * HEAD_WIDTH
    by_seq = lambda a: a.reshape(seqs, rows, a.shape[1])
    flat = lambda a: a.reshape(flat_rows, a.shape[2])
    r, rm, ra, rd = w_xbc.shape[0], w_mix_out.shape[0], w_attn_out.shape[0], w_down.shape[0]
    bits = bit_count()
    top = list(range(bits - 1, 2, -1))
    half = (DI + query_width + kv_width) // 2

    heads = jnp.stack([step_bias, -jnp.exp(decay_log), skip_gain])
    heads = jnp.pad(heads, ((0, 5), (0, LANES - H)))
    spread = jnp.repeat(jnp.eye(LANES, H, dtype=BF16), P_SIZE, axis=1)
    skip_row = jnp.broadcast_to(jnp.repeat(skip_gain, P_SIZE)[None], (8, DI))
    picks = jnp.eye(LANES, 2 * LEFT, 2 * LEFT - LANES, dtype=BF16)
    rest = rest_place().reshape(1).astype(jnp.int32)

    first = Part(
        pack_first(w_xbc, w_step, conv_weight, conv_bias, mixer_gain, norm1_gain, norm2_gain)[None]
    )
    if len(top) == 2:
        first.direct((8, 16, 24))
    else:
        first.step(top[0])
    segs_got = swap_start(segment_ids[:, 0])
    x_got = fsdp_exchange(pick(in_hbm(hidden_in[:, 0]), 1 - side_of(), after=(segs_got,)), fsdp_bits() - 1)
    for bit in top[1:] if len(top) != 2 else ():
        join([first])
        first.step(bit)
    first_halves = join([first], split=(first,), after=(heads, spread, skip_row, picks))
    [p.step(bit) for p, bit in zip(first_halves, (2, 1))]
    two = Part(pack_two(w_gate_z, w_query, key_value_weight, w_mix_out, w_attn_out, after=(first_halves[0].pieces[0][0],))[None])
    two.step(top[0])
    cols, rows_in, keep_end = sequence_masks(swap_end(segment_ids[:, 0], segs_got))
    x = merge(in_hbm(hidden_in[:, 0]), x_got, side_of()).reshape(flat_rows, MODEL_WIDTH)
    join(first_halves + [two], after=(x,))
    [p.step(bit) for p, bit in zip(first_halves, (1, 2))]
    two.steps(top[1:])
    [p.core() for p in first_halves]
    two_halves = join([two], split=(two,), after=[p.pieces[1][0] for p in first_halves])
    [p.step(bit) for p, bit in zip(two_halves, (2, 1))]
    units = Part(pack_units(w_gate_up, w_down, after=(two_halves[0].pieces[0][0],))[None])
    units.step(top[0])
    if r % 16:
        left_full, right_full, small_full = assemble(
            first_halves,
            [(count, r, LEFT), (count, r, LEFT), (count, r, LANES)],
            [
                (0, 0, r, 0, LEFT, 0, 0, 0),
                (1, 0, r, 0, LEFT, 1, 0, 0),
                (1, 0, r, LEFT - LANES, LANES, 2, 0, 0),
            ],
            after=(units.pieces[0][0],),
        )

        conv, mix_gain, gains = unpack_small(small_full, r)
        gain_one, gain_two = gains[:1], gains[1:]
        normed, left, right, tails = first_proj(x, gain_one, left_full, right_full, cols, after=(rows_in,))
    else:
        normed, left, right, tails, conv, mix_gain, gains, left_full, right_full = first_pieces(
            x, cols, first_halves, r, after=(units.pieces[0][0], rows_in)
        )
        gain_one, gain_two = gains[:1], gains[1:]
    left, right = by_seq(left), by_seq(right)
    tail_pieces, offsets = gather_sequence(tails)
    join(two_halves + [units], after=(left,))
    [p.step(bit) for p, bit in zip(two_halves, (1, 2))]
    units.steps(top[1:])
    halo = take_halo(rest, tail_pieces, offsets)
    xbc, slope, xd, step, cum, msg = mix_begin(
        left, right, halo, cols, heads, conv, after=(two_halves[0].pieces[0][0],)
    )
    msg_pieces, _ = gather_sequence(msg)
    units_halves = join([units], after=(cum,), split=(units,))
    (two_all,) = join_all(two_halves, after=(units_halves[0].pieces[0][0],))
    two_offsets = sum((o for _, o in two_halves[0].pieces), [])
    other_offsets = sum((o for _, o in two_halves[1].pieces), [])
    two_got = exchange(two_all, 0)
    [p.step(bit) for p, bit in zip(units_halves, (2, 1))]
    inside = mix_inside(xbc, xd, cum, cols, rows_in, skip_row, after=(two_all,))
    for n, (p, offsets_of) in enumerate(zip(two_halves, (two_offsets, other_offsets))):
        p.pieces = [(two_all, offsets_of, n), (two_got, [o ^ 1 for o in offsets_of], n)]
    second_moves = [
        (0, 0, r, 0, half, 0, 0, 0),
        (1, 0, r, 0, DI - half, 0, 0, half),
        (1, 0, r, DI - half, query_width + kv_width, 1, 0, 0),
    ]
    if r % 16:
        z_full, qkv_full = assemble(
            two_halves,
            [(count, r, DI), (count, r, query_width + kv_width)],
            second_moves,
            after=(inside,),
        )
        gate_z, queries, keyvals = second_proj(normed, z_full, qkv_full, rows_in)
    else:
        gate_z, queries, keyvals, z_full, qkv_full = second_pieces(
            normed, rows_in, two_halves, second_moves, r, after=(inside,)
        )
    gate_z, queries = by_seq(gate_z), by_seq(queries)
    prev = scan_states(rest, msg_pieces, offsets, True, after=(gate_z,))
    join(units_halves, after=(prev,))
    [p.step(bit) for p, bit in zip(units_halves, (1, 2))]
    kv_pieces, _ = gather_sequence(keyvals)
    mixer_out, normed_mix = mix_finish(
        in_hbm(inside), xbc, prev, cum, cols, in_hbm(gate_z), mix_gain, after=(units_halves[0].pieces[0][0],)
    )
    attn_low, log_sums = attend(rest, queries, kv_pieces, cols, rows_in, offsets, after=(normed_mix,))

    out_keep, out_send = turn(flat(normed_mix), flat(attn_low))
    x_halo = halo[:, :, CONV_WIDTH:].reshape(seqs * HALO, MODEL_WIDTH)
    normed_keep, normed_send = turn(jnp.concatenate([normed, x_halo]), after=(out_keep,))

    mix_out_full, attn_out_full = assemble(
        two_halves,
        [(count, rm, MODEL_WIDTH), (count, ra, MODEL_WIDTH)],
        [
            (0, 0, r, half, MODEL_WIDTH, 0, 0, 0),
            (1, 0, rm - r, half, MODEL_WIDTH, 0, r, 0),
            (1, rm - r, ra, half, MODEL_WIDTH, 1, 0, 0),
        ],
        after=(normed_keep,),
    )
    residual, normed_two = out_proj(x, flat(normed_mix), flat(attn_low), mix_out_full, attn_out_full, gain_two)
    two_keep, two_send, *held = turn(normed_two, hold=[p.pieces[1][0] for p in units_halves])
    for p, got in zip(units_halves, held):
        p.pieces[1] = (got, p.pieces[1][1])
        p.core()
    if r % 16:
        moves = [(n, q * r, r, 0, MODEL_WIDTH, n, 0, q * MODEL_WIDTH) for n in range(2) for q in range(2)]
        moves += [(n, 2 * r, rd // 2, 0, MODEL_WIDTH, 2, n * (rd // 2), 0) for n in range(2)]
        gate_full, up_full, down_full = assemble(
            units_halves, [(count, r, FF), (count, r, FF), (count, rd, MODEL_WIDTH)], moves, after=(two_keep,), limit=60
        )
        act, swish, gate_slope = gate_up(normed_two, gate_full, up_full)
    else:
        act, swish, gate_slope, gate_full, up_full, down_full = gate_up_pieces(
            normed_two, units_halves, r, rd, after=(two_keep,)
        )
    out_turned = [out_keep, exchange(out_send, 0)]
    x_turned = [normed_keep, exchange(normed_send, 0)]
    two_turned = [two_keep, exchange(two_send, 0)]
    grad_got = fsdp_exchange(pick(in_hbm(out_grad[:, 0]), 1 - side_of(), after=(two_keep,)), fsdp_bits() - 1)
    act_keep, act_send = turn(act, after=(out_turned[1], x_turned[1], two_turned[1]))
    grad_out = merge(in_hbm(out_grad[:, 0]), grad_got, side_of(), after=(act_keep,)).reshape(flat_rows, MODEL_WIDTH)
    act_turned = [act_keep, exchange(act_send, 0)]
    grad_out_got = exchange(grad_out, 0)

    block_out, grad_gate, grad_up = down(
        act, swish, gate_slope, down_full, residual, grad_out, after=(act_keep,)
    )
    gate_got, up_got = exchange(grad_gate, 0), exchange(grad_up, 0)
    hidden_got = swap_start(by_seq(block_out))
    grad_resid, grad_branch = gate_up_back(
        grad_gate, grad_up, gate_full, up_full, residual, gain_two, grad_out, after=(block_out,)
    )
    sum_down = Sum(act_turned, [grad_out, grad_out_got], 1, after=(grad_branch,))
    sum_gate = Sum(two_turned, [grad_gate, gate_got], 0, after=(sum_down.send,))
    hidden_out = swap_end(by_seq(block_out), hidden_got)
    sum_up = Sum(two_turned, [grad_up, up_got], 1, after=(sum_gate.send, hidden_out))
    branch_got = exchange(grad_branch, 0)
    sum_gate.near(), sum_up.near()
    grad_normed_mix, grad_attn = out_back(
        grad_branch, mix_out_full, attn_out_full, after=(sum_up.send,)
    )
    grad_normed_mix, grad_attn = by_seq(grad_normed_mix), by_seq(grad_attn)
    sum_out = Sum(out_turned, [grad_branch, branch_got], 0, after=(grad_normed_mix,))

    grad_queries, grad_kv_pieces = attend_back(
        rest, queries, kv_pieces, cols, rows_in, attn_low, log_sums, grad_attn, offsets, after=(sum_out.send,)
    )
    advance([sum_gate, sum_up], after=(grad_queries,))
    sum_gate.second(), sum_up.second()
    kv_own, kv_got = sum_sequence(grad_kv_pieces)
    dy, grad_za, grad_zb, back_msg = gated_back(
        grad_normed_mix, mixer_out, gate_z, mix_gain, xbc, cum, cols, half, after=(sum_gate.send, sum_up.send)
    )
    (pair_gate_up,) = advance([(sum_gate, sum_up)], after=(dy,))
    grad_zq = join_grads(
        flat(grad_za), flat(grad_zb), flat(grad_queries), kv_own, kv_got, after=(pair_gate_up.send,)
    )
    zq_got = exchange(grad_zq, 0)
    back_pieces, _ = gather_sequence(back_msg)
    pair_gate_up.start(3)
    sum_out.near(), sum_down.near()
    dxd, dbc, sums = inside_back(
        xbc, xd, cum, cols, rows_in, skip_row, spread, dy, mixer_out, prev, after=(grad_zq,)
    )
    sum_z = Sum(x_turned, [grad_zq, zq_got], 0, after=(sums,), columns=(0, half))
    sum_zq = Sum(x_turned, [grad_zq, zq_got], 1, after=(sum_z.send,), columns=(half, half))
    later = scan_states(rest, back_pieces, offsets, False, after=(sum_zq.send,))
    for bit in range(4, bits):
        advance([sum_out, sum_down, pair_gate_up] if bit == 4 else [pair_gate_up], after=(later,))
        pair_gate_up.start(bit)
    sum_out.second(), sum_down.second()
    sum_z.near(), sum_zq.near()
    grad_second = second_back(grad_zq, z_full, qkv_full, after=(sum_out.send,))
    grad_first, conv_sums, head_sums = mix_end(
        left, right, halo, xbc, slope, xd, step, cum, cols, heads, skip_row, conv, spread,
        dy, dxd, dbc, sums, later, prev, after=(grad_second,),
    )
    _, _, pair_out_down = advance([sum_z, sum_zq, (sum_out, sum_down)], after=(head_sums,))
    (own_gate_up,) = finish([pair_gate_up], after=(pair_out_down.send,))
    small_keep, small_send = small_grads(r, conv_sums, head_sums)
    sum_x = Direct(
        [normed_keep, small_keep], [normed_send, small_send], [grad_first, picks], after=(own_gate_up,)
    )
    grad_normed, grad_halo = first_back(
        grad_first, left_full, right_full, grad_second, after=(sum_x.send,)
    )
    sum_x.core()
    sum_z.second(), sum_zq.second()
    pair_out_down.start(3)
    edge = keep_end[:, rows - HALO :, None]
    from_next = jnp.where(edge, from_next_part(grad_halo.reshape(seqs, HALO, MODEL_WIDTH)), 0.0)
    quarter = sum_x.planes(after=(grad_normed,))
    input_grad, input_low = input_back(grad_normed, from_next, x, gain_one, grad_resid, after=(quarter,))
    input_got = swap_start(input_low)
    input_grad = swap_end(input_grad, input_got)
    far = list(range(4, bits))
    (pair_z,) = advance([(sum_z, sum_zq)], after=(quarter,))
    pair_z.start(3)
    for bit in far:
        advance([pair_out_down], after=(input_low,))
        pair_out_down.start(bit)
    sum_x.lines(after=(pair_out_down.send, pair_z.send))
    (own_out_down,) = finish([pair_out_down], after=(sum_x.keep,))
    for bit in far:
        advance([pair_z], after=(sum_x.keep,))
        pair_z.start(bit)
    (own_zq,) = finish([pair_z], after=(sum_x.keep,))
    own_first = sum_x.done()
    own_small = own_first[:, 2 * LEFT - LANES :]
    widths = [conv_weight.shape[1]] * KC + [conv_bias.shape[0]] + [H] * 6
    own = []
    for j, width in enumerate(widths):
        row, lane = line_place(j, len(widths), r)
        own.append(own_small[row, lane : lane + width])
    gain_grad = lambda weights, grads, gain: sum(
        jnp.sum(w.astype(F32) * g, 1) for w, g in zip(weights, grads)
    ) / gain.astype(F32)
    zq = jnp.concatenate([own_zq[0], own_zq[1]], 1)
    grad_z, grad_query, grad_keyval = jnp.split(zq, (DI, DI + query_width), 1)
    grad_xbc = own_first[:, :CONV_WIDTH]
    grad_step = own_first[:, CONV_WIDTH : CONV_WIDTH + H]
    grad_gate_up = jnp.concatenate([own_gate_up[0], own_gate_up[1]], 1)
    grad_out_w, grad_down = own_out_down[0], own_out_down[1]
    first_w = (w_gate_z, w_xbc, w_step, w_query, key_value_weight)
    first_g = (grad_z, grad_xbc, grad_step, grad_query, grad_keyval)
    return (
        hidden_out.reshape(hidden_in.shape),
        input_grad.reshape(hidden_in.shape),
        gain_grad(first_w, first_g, norm1_gain),
        grad_z,
        grad_xbc,
        grad_step,
        jnp.stack(own[:KC]),
        own[KC],
        own[KC + 1] + own[KC + 4],
        own[KC + 2] + own[KC + 5],
        own[KC + 3] + own[KC + 6],
        gain_grad([w_mix_out], [grad_out_w[:rm]], mixer_gain),
        grad_out_w[:rm],
        grad_query,
        grad_keyval,
        grad_out_w[rm:],
        gain_grad([w_gate_up], [grad_gate_up], norm2_gain),
        grad_gate_up,
        grad_down,
    )


def solution(mesh):
    placed = (
        P(None, "dp", "fsdp", None),
        P(None, "dp", "fsdp"),
        P(("dp", "fsdp")),
        P(("dp", "fsdp"), None),
        P(("dp", "fsdp"), None),
        P(("dp", "fsdp"), None),
        P(None, ("dp", "fsdp")),
        P(("dp", "fsdp")),
        P(),
        P(),
        P(),
        P(("dp", "fsdp")),
        P(("dp", "fsdp"), None),
        P(("dp", "fsdp"), None),
        P(("dp", "fsdp"), None),
        P(("dp", "fsdp"), None),
        P(("dp", "fsdp")),
        P(("dp", "fsdp"), None),
        P(("dp", "fsdp"), None),
        P(None, "dp", "fsdp", None),
    )
    return jax.shard_map(
        per_device,
        mesh=mesh,
        in_specs=placed,
        out_specs=(
            P(None, "dp", "fsdp", None),
            P(None, "dp", "fsdp", None),
            P(("dp", "fsdp")),
            P(("dp", "fsdp"), None),
            P(("dp", "fsdp"), None),
            P(("dp", "fsdp"), None),
            P(None, ("dp", "fsdp")),
            P(("dp", "fsdp")),
            P(),
            P(),
            P(),
            P(("dp", "fsdp")),
            P(("dp", "fsdp"), None),
            P(("dp", "fsdp"), None),
            P(("dp", "fsdp"), None),
            P(("dp", "fsdp"), None),
            P(("dp", "fsdp")),
            P(("dp", "fsdp"), None),
            P(("dp", "fsdp"), None),
        ),
        check_vma=False,
    )
```

```python
import functools

import jax
import jax.numpy as jnp
from jax import lax
from jax.experimental import pallas as pl
from jax.experimental.pallas import tpu as pltpu
from jax.sharding import PartitionSpec as P

MODEL_WIDTH = 1024
FF = 2048
H = 24
P_SIZE = 64
NS = 128
QUERY_HEADS = 8
KEY_VALUE_HEADS = 2
HEAD_WIDTH = 64
KC = 4
DI = 1536


EPSILON = 1e-06
NEGATIVE = -1e30


def matmul(first_op, second_op):
    return jnp.dot(first_op, second_op, preferred_element_type=jnp.float32)


def left_t(first_op, second_op):
    return jnp.einsum("ti,tj->ij", first_op, second_op, preferred_element_type=jnp.float32)


def right_t(first_op, second_op):
    return jnp.einsum("ti,ji->tj", first_op, second_op, preferred_element_type=jnp.float32)


def rms_gain(values, gain_in):
    return values * lax.rsqrt(jnp.mean(values * values, axis=-1, keepdims=True) + EPSILON) * gain_in


def swiglu(gate_up):
    return jax.nn.silu(gate_up[:, :FF]) * gate_up[:, FF:]


BOTH = ("dp", "fsdp")


def exchange_mask(block, mask):
    count = lax.axis_size(BOTH)
    return lax.ppermute(block, BOTH, [(i, i ^ mask) for i in range(count)])


def exchange(block, bit):
    return exchange_mask(block, 1 << bit)


def bit_count():
    return lax.axis_size(BOTH).bit_length() - 1


def place_of():
    return lax.axis_index(BOTH)


def in_hbm(array):
    return pltpu.with_memory_space_constraint(array, pltpu.HBM)


def spec_any(count):
    return [pl.BlockSpec(memory_space=pl.ANY)] * count


def copies_kernel(n_in, n_after, n_out, n_hold, jobs, place_ref, *refs):
    ins, refs = refs[:n_in], refs[n_in + n_hold + n_after :]
    outs, refs = refs[:n_out], refs[n_out + n_hold :]
    held, sems, out_sems = refs[:n_out], refs[-2], refs[-1]
    place = place_ref[0]
    copies = [[] for _ in outs]
    for number, (out, source, source_at, target_at) in enumerate(jobs):
        copy = pltpu.make_async_copy(
            ins[source].at[source_at], held[out].at[target_at(place)], sems.at[number]
        )
        copy.start()
        copies[out].append(copy)
    back = []
    for out in range(n_out):
        for copy in copies[out]:
            copy.wait()
        copy = pltpu.make_async_copy(held[out], outs[out], out_sems.at[out])
        copy.start()
        back.append(copy)
    for copy in back:
        copy.wait()


def copies(name, ins, outs, jobs, after=(), hold=(), limit=24):
    jobs = sorted(jobs, key=lambda job: job[0])
    ins = [in_hbm(a) for a in ins]
    return pl.pallas_call(
        functools.partial(copies_kernel, len(ins), len(after), len(outs), len(hold), jobs),
        out_shape=[jax.ShapeDtypeStruct(s, jnp.bfloat16) for s in outs]
        + [jax.ShapeDtypeStruct(a.shape, a.dtype) for a in hold],
        in_specs=[pl.BlockSpec(memory_space=pltpu.SMEM)] + spec_any(len(ins) + len(hold) + len(after)),
        out_specs=spec_any(len(outs) + len(hold)),
        input_output_aliases={1 + len(ins) + n: len(outs) + n for n in range(len(hold))},
        scratch_shapes=[pltpu.VMEM(s, jnp.bfloat16) for s in outs]
        + [pltpu.SemaphoreType.DMA((len(jobs),)), pltpu.SemaphoreType.DMA((len(outs),))],
        compiler_params=pltpu.CompilerParams(vmem_limit_bytes=limit * 2**20),
        name=name,
    )(place_of().reshape(1).astype(jnp.int32), *ins, *hold, *after)


class Part:
    def __init__(self, block, offsets=(0,)):
        self.pieces = [(block, list(offsets))]

    def step(self, bit):
        ((block, offsets),) = self.pieces
        self.pieces.append((exchange(block, bit), [o ^ (1 << bit) for o in offsets]))

    def steps(self, bits):
        for n, bit in enumerate(bits):
            if n:
                join([self])
            self.step(bit)

    def direct(self, masks):
        ((block, offsets),) = self.pieces
        self.pieces += [(exchange_mask(block, mask), [o ^ mask for o in offsets]) for mask in masks]

    def core(self):
        self.pieces += [(exchange(a, 0), [o ^ 1 for o in offsets]) for a, offsets in self.pieces]


def join_all(parts, after=(), hold=()):
    ins, jobs = [], []
    for p, part in enumerate(parts):
        at = 0
        for array, own in part.pieces:
            target = (p, slice(at, at + len(own)))
            jobs.append((0, len(ins), (slice(None),), lambda place, target=target: target))
            ins.append(array)
            at += len(own)
    shape = (len(parts), at) + ins[0].shape[1:]
    return copies("join_all", ins, [shape], jobs, after, hold)


def join(parts, after=(), split=(), hold=()):
    ins, outs, jobs, made = [], [], [], []
    for part in parts:
        first = part.pieces[0][0]
        blocks = sum(len(offsets) for _, offsets in part.pieces)
        offsets = sum((o for _, o in part.pieces), [])
        halves = (0, 1) if part in split else (None,)
        for half in halves:
            at = 0
            for number, (array, own) in enumerate(part.pieces):
                source = len(ins) + number
                source_at = (slice(None),) if half is None else (slice(None), half)
                target = (slice(at, at + len(own)),)
                jobs.append((len(outs), source, source_at, lambda place, target=target: target))
                at += len(own)
            outs.append((blocks,) + (first.shape[1:] if half is None else first.shape[2:]))
            made.append((part, half, offsets))
        ins += [array for array, _ in part.pieces]
    cut = []
    held = [part.pieces[-1][0] for part in hold]
    found = copies("join", ins, outs, jobs, after, held)
    for array, part in zip(found[len(outs) :], hold):
        part.pieces[-1] = (array, part.pieces[-1][1])
    for array, (part, half, offsets) in zip(found, made):
        if half is None:
            part.pieces = [(array, offsets)]
        else:
            cut.append(Part(array, offsets))
    return cut


def assemble(parts, outs, moves, after=(), limit=24):
    ins, jobs = [], []
    for at, part in enumerate(parts):
        for piece, offsets, *of_part in part.pieces:
            for j, offset in enumerate(offsets):
                for of, r0, rows, c0, columns, out, row, column in moves:
                    if of == at:
                        source_at = (*of_part, j, pl.ds(r0, rows), pl.ds(c0, columns))
                        target = (pl.ds(row, rows), pl.ds(column, columns))
                        jobs.append(
                            (out, len(ins), source_at, lambda place, o=offset, t=target: (place ^ o,) + t)
                        )
            ins.append(piece)
    return [a.reshape(-1, a.shape[2]) for a in copies("assemble", ins, outs, jobs, after, limit=limit)]


def turned_offsets(bits):
    offsets = [0]
    for bit in list(range(bits - 1, 2, -1)) + [1, 2]:
        offsets = offsets + [o ^ (1 << bit) for o in offsets]
    return offsets


def turn_kernel(n_x, n_hold, n_after, rows, offsets, place_ref, *refs):
    xs, refs = refs[:n_x], refs[n_x + n_hold + n_after :]
    keep_ref, send_ref, turned = refs[0], refs[1], refs[2 + n_hold :]
    place = place_ref[0]
    total = sum(rows)
    for x_ref, t_ref in zip(xs, turned):
        t_ref[...] = x_ref[...].T
    for t, offset in enumerate(offsets):
        at = t * total
        for t_ref, size in zip(turned, rows):
            begin = pl.multiple_of((place ^ offset) * size, size)
            keep_ref[at : at + size] = t_ref[pl.ds(begin, size)]
            begin = pl.multiple_of((place ^ (offset ^ 1)) * size, size)
            send_ref[at : at + size] = t_ref[pl.ds(begin, size)]
            at += size


def turn(*xs, after=(), hold=()):
    bits = bit_count()
    rows = [x.shape[1] >> bits for x in xs]
    tokens, half = xs[0].shape[0], sum(x.shape[1] for x in xs) // 2
    if any(r % 16 for r in rows):
        blocks = jnp.concatenate([x.T.reshape(1 << bits, r, tokens) for x, r in zip(xs, rows)], 1)
        offsets = jnp.asarray(turned_offsets(bits), jnp.int32) ^ place_of()
        sides = [jnp.take(blocks, o, axis=0).reshape(half, tokens) for o in (offsets, offsets ^ 1)]
        return (*sides, *hold)
    vmem = pl.BlockSpec(memory_space=pltpu.VMEM)
    return pl.pallas_call(
        functools.partial(turn_kernel, len(xs), len(hold), len(after), rows, turned_offsets(bits)),
        in_specs=[pl.BlockSpec(memory_space=pltpu.SMEM)] + [vmem] * len(xs) + spec_any(len(hold) + len(after)),
        out_specs=[vmem] * 2 + spec_any(len(hold)),
        out_shape=[jax.ShapeDtypeStruct((half, tokens), jnp.bfloat16)] * 2
        + [jax.ShapeDtypeStruct(a.shape, a.dtype) for a in hold],
        input_output_aliases={1 + len(xs) + n: 2 + n for n in range(len(hold))},
        scratch_shapes=[pltpu.VMEM((x.shape[1], x.shape[0]), jnp.bfloat16) for x in xs],
        compiler_params=pltpu.CompilerParams(vmem_limit_bytes=24 * 2**20),
        name="turn",
    )(place_of().reshape(1).astype(jnp.int32), *xs, *hold, *after)


def grad_kernel(n_pairs, half, *refs):
    pairs, (keep_ref, send_ref) = refs[: 2 * n_pairs], refs[-2:]
    total = None
    for x_ref, g_ref in zip(pairs[:n_pairs], pairs[n_pairs:]):
        part = jnp.dot(x_ref[...], g_ref[...], preferred_element_type=jnp.float32)
        total = part if total is None else total + part
    total = total.astype(jnp.bfloat16)
    rows = keep_ref.shape[1]
    for second in range(2):
        for first, ref in enumerate((keep_ref, send_ref)):
            quarter = 2 * first + second if half == 0 else 2 * second + first
            ref[second] = total[quarter * rows : (quarter + 1) * rows]


def weight_grad(xs, gs, half, after=(), columns=None):
    k, (first, n) = xs[0].shape[0], columns or (0, gs[0].shape[1])
    width = next(w for w in (1024, 512, 384, 256, 128) if n % w == 0 and first % w == 0)
    at = first // width
    block = pl.BlockSpec((2, k // 4, width), lambda i: (0, 0, i))
    return pl.pallas_call(
        functools.partial(grad_kernel, len(xs), half),
        grid=(n // width,),
        in_specs=[pl.BlockSpec((k, g.shape[0]), lambda i: (0, 0)) for g in gs]
        + [pl.BlockSpec((g.shape[0], width), lambda i: (0, at + i)) for g in gs]
        + spec_any(len(after)),
        out_specs=[block, block],
        out_shape=[jax.ShapeDtypeStruct((2, k // 4, n), jnp.bfloat16)] * 2,
        compiler_params=pltpu.CompilerParams(vmem_limit_bytes=48 * 2**20),
        name="weight_grad",
    )(*xs, *gs, *after)


def both_kernel(n_pairs, half, *refs):
    outs = refs[-2:]
    gs = refs[2 * n_pairs : 3 * n_pairs]
    for xs, out_ref in ((refs[:n_pairs], outs[0]), (refs[n_pairs : 2 * n_pairs], outs[1])):
        total = None
        for x_ref, g_ref in zip(xs, gs):
            part = jnp.dot(x_ref[...], g_ref[...], preferred_element_type=jnp.float32)
            total = part if total is None else total + part
        total = total.astype(jnp.bfloat16)
        rows = out_ref.shape[1] // 4
        for quarter in range(4):
            place = quarter if half == 0 else 2 * (quarter % 2) + quarter // 2
            out_ref[0, place * rows : (place + 1) * rows] = total[quarter * rows : (quarter + 1) * rows]


def both_grads(keeps, sends, gs, half, after=()):
    k, n = keeps[0].shape[0], gs[0].shape[1]
    width = next(w for w in (512, 256, 128) if n % w == 0)
    block = pl.BlockSpec((1, k, width), lambda i: (0, 0, i))
    return pl.pallas_call(
        functools.partial(both_kernel, len(gs), half),
        grid=(n // width,),
        in_specs=[pl.BlockSpec((k, g.shape[0]), lambda i: (0, 0)) for g in gs] * 2
        + [pl.BlockSpec((g.shape[0], width), lambda i: (0, i)) for g in gs]
        + spec_any(len(after)),
        out_specs=[block, block],
        out_shape=[jax.ShapeDtypeStruct((1, k, n), jnp.bfloat16)] * 2,
        compiler_params=pltpu.CompilerParams(vmem_limit_bytes=48 * 2**20),
        name="both_grads",
    )(*keeps, *sends, *gs, *after)


def add_kernel(shape, last, n_after, *refs):
    n_in = sum(len(counts) for counts in shape)
    keeps, gots, outs = refs[:n_in], refs[n_in : 2 * n_in], refs[2 * n_in + n_after :]
    at = 0
    for item, counts in enumerate(shape):
        slot = 0
        for count in counts:
            for s in range(count):
                total = keeps[at][s].astype(jnp.float32) + gots[at][s].astype(jnp.float32)
                if last:
                    outs[item][slot] = total
                else:
                    total = total.astype(jnp.bfloat16)
                    half = total.shape[0] // 2
                    outs[2 * item][slot] = total[:half]
                    outs[2 * item + 1][slot] = total[half:]
                slot += 1
            at += 1


def add_up(items, after=(), last=False):
    shape = [[own.shape[0] for own, _ in item] for item in items]
    keeps = [own for item in items for own, _ in item]
    gots = [in_hbm(got) for item in items for _, got in item]
    widths = {a.shape[2] for a in keeps}
    steps = next(g for g in (2, 3, 1) if all(w % (g * 128) == 0 for w in widths))
    blocks, outs = [], []
    for a in keeps:
        blocks.append(pl.BlockSpec(a.shape[:2] + (a.shape[2] // steps,), lambda i: (0, 0, i)))
    out_blocks = []
    for item, counts in zip(items, shape):
        rows, n = item[0][0].shape[1:]
        rows = rows if last else rows // 2
        for _ in range(1 if last else 2):
            out_blocks.append(pl.BlockSpec((sum(counts), rows, n // steps), lambda i: (0, 0, i)))
            outs.append(
                jax.ShapeDtypeStruct((sum(counts), rows, n), jnp.float32 if last else jnp.bfloat16)
            )
    return pl.pallas_call(
        functools.partial(add_kernel, shape, last, len(after)),
        grid=(steps,),
        in_specs=blocks + blocks + spec_any(len(after)),
        out_specs=out_blocks,
        out_shape=outs,
        compiler_params=pltpu.CompilerParams(vmem_limit_bytes=48 * 2**20),
        name="add_up",
    )(*keeps, *gots, *after)


class Sum:
    def __init__(self, xs, gs, half, after=(), columns=None):
        self.first = (2, 1)[half]
        keep, send = weight_grad(xs, gs, half, after, columns)
        self.keep, self.send = (a.reshape(1, -1, a.shape[2]) for a in (keep, send))

    def start(self, bit):
        self.got = exchange(self.send, bit)

    def near(self):
        self.start(self.first)

    def second(self):
        self.start(3 - self.first)


class CoreSum(Sum):
    def __init__(self, keeps, sends, gs, half, after=()):
        self.first = (2, 1)[half]
        self.keep, self.send = both_grads(keeps, sends, gs, half, after)

    def core(self):
        self.start(0)


class Pair:
    def start(self, bit):
        self.got = exchange(self.send, bit)


def advance(steps, after=()):
    items = [[(s.keep, s.got) for s in (step if isinstance(step, tuple) else (step,))] for step in steps]
    found = add_up(items, after)
    made = []
    for n, step in enumerate(steps):
        step = Pair() if isinstance(step, tuple) else step
        step.keep, step.send = found[2 * n : 2 * n + 2]
        made.append(step)
    return made


def finish(pairs, after=()):
    return add_up([[(p.keep, p.got)] for p in pairs], after, last=True)


def parts_kernel(n_in, parts, n_skip, *refs):
    ins, outs = refs[:n_in], refs[n_in + n_skip :]
    total = ins[0][0].astype(jnp.float32)
    for ref in ins[1:]:
        total = total + ref[0].astype(jnp.float32)
    rows = total.shape[0] // parts
    for n in range(parts):
        outs[n][0] = total[n * rows : (n + 1) * rows].astype(outs[n].dtype)


def add_parts(arrays, parts, kind=jnp.bfloat16, after=(), hold=()):
    _, rows, n = arrays[0].shape
    steps = next(g for g in (2, 1) if n % (g * 128) == 0)
    spec = lambda rows: pl.BlockSpec((1, rows, n // steps), lambda i: (0, 0, i))
    return pl.pallas_call(
        functools.partial(parts_kernel, len(arrays), parts, len(hold) + len(after)),
        grid=(steps,),
        in_specs=[spec(rows)] * len(arrays) + spec_any(len(hold) + len(after)),
        out_specs=[spec(rows // parts)] * parts + spec_any(len(hold)),
        out_shape=[jax.ShapeDtypeStruct((1, rows // parts, n), kind)] * parts
        + [jax.ShapeDtypeStruct(a.shape, a.dtype) for a in hold],
        input_output_aliases={len(arrays) + n: parts + n for n in range(len(hold))},
        compiler_params=pltpu.CompilerParams(vmem_limit_bytes=48 * 2**20),
        name="add_parts",
    )(arrays[0], *[in_hbm(a) for a in arrays[1:]], *hold, *after)


class Direct:
    def __init__(self, keeps, sends, gs, after=()):
        self.keep, self.send = both_grads(keeps, sends, gs, 0, after)

    def core(self):
        self.got = [exchange(self.send, 0)]

    def planes(self, after=()):
        quarters = add_parts([self.keep] + self.got, 4, after=after)
        self.keep = quarters[0]
        self.got = [exchange_mask(q, mask) for q, mask in zip(quarters[1:], (2, 4, 6))]
        return quarters[0]

    def lines(self, after=(), hold=()):
        bits = bit_count()
        arrays = [self.keep] + self.got
        if bits == 5:
            quarters = add_parts(arrays, 4, after=after, hold=hold)
            self.keep = quarters[0]
            self.got = [exchange_mask(q, mask) for q, mask in zip(quarters[1:4], (16, 8, 24))]
            return quarters[4:]
        for bit in range(3, bits):
            self.keep, send = add_parts(arrays, 2, after=after)
            self.got = [exchange(send, bit)]
            arrays = [self.keep] + self.got
        return hold

    def done(self):
        return add_parts([self.keep] + self.got, 1, jnp.float32)[0][0]


F32 = jnp.float32
BF16 = jnp.bfloat16
LANES = 128
HALO = 16
STATE_ROWS = NS + 16
LEFT = 1024
SLOTS = 2
CONV_WIDTH = DI + 2 * NS
VMEM_LIMIT = 48 * 2**20


def dot_nn(a, b):
    return jnp.dot(a, b, preferred_element_type=F32)


def dot_nt(a, b):
    return lax.dot_general(a, b, (((1,), (1,)), ((), ())), preferred_element_type=F32)


def dot_tn(a, b):
    return lax.dot_general(a, b, (((0,), (0,)), ((), ())), preferred_element_type=F32)


def split_two(v):
    high = v.astype(BF16)
    return high, (v - high.astype(F32)).astype(BF16)


def sum_heads(v, spread):
    high, low = split_two(v)
    return dot_nt(high, spread) + dot_nt(low, spread)


def tile_of(i):
    return slice(i * LANES, (i + 1) * LANES)


def two_heads(v, i):
    rows = v.shape[0]
    lane = lax.broadcasted_iota(jnp.int32, (rows, LANES), 1)
    left = jnp.broadcast_to(v[:, 2 * i : 2 * i + 1], (rows, LANES))
    right = jnp.broadcast_to(v[:, 2 * i + 1 : 2 * i + 2], (rows, LANES))
    return jnp.where(lane < P_SIZE, left, right)


def all_heads(v):
    v = jnp.broadcast_to(v, (16, LANES))
    return jnp.concatenate([two_heads(v, i) for i in range(DI // LANES)], 1)


def triangle(size, lower):
    rows = lax.broadcasted_iota(jnp.int32, (size, size), 0)
    cols = lax.broadcasted_iota(jnp.int32, (size, size), 1)
    return jnp.where(rows >= cols if lower else rows <= cols, 1.0, 0.0).astype(BF16)


def exact_sum(ones, v):
    high = v.astype(BF16)
    rest = v - high.astype(F32)
    mid = rest.astype(BF16)
    low = (rest - mid.astype(F32)).astype(BF16)
    return dot_nn(ones, high) + (dot_nn(ones, mid) + dot_nn(ones, low))


def soft_plus(z):
    return jnp.maximum(z, 0.0) + jnp.log1p(jnp.exp(-jnp.abs(z)))


def sigmoid(v):
    return 0.5 * jnp.tanh(0.5 * v) + 0.5


def conv_tile(left_ref, right_ref, i):
    tiles = LEFT // LANES
    if i < tiles:
        return left_ref[0, :, tile_of(i)].astype(F32)
    return right_ref[0, :, tile_of(i - tiles)].astype(BF16).astype(F32)


def raw_tile(right_ref):
    return right_ref[0, :, CONV_WIDTH - LEFT : CONV_WIDTH - LEFT + LANES]


def mix_begin_kernel(
    left_ref, right_ref, halo_ref, cols_ref, heads_ref, conv_ref,
    xbc_ref, slope_ref, xd_ref, step_ref, cum_ref, msg_ref,
):
    rows = left_ref.shape[1]
    masks = cols_ref[0]
    step = soft_plus(raw_tile(right_ref) + heads_ref[0:1])
    cum = exact_sum(triangle(rows, True), step * heads_ref[1:2])
    step_ref[0] = step
    cum_ref[0] = cum
    last = cum[rows - 1 : rows]
    ends = jnp.exp(last - cum) * masks[:, 3:4]
    msg_ref[0, NS:STATE_ROWS, :] = all_heads(jnp.exp(last)).astype(BF16)
    wide = [jnp.broadcast_to(masks[:, k : k + 1], (rows, LANES)) for k in range(KC - 1)]

    def conv(i):
        lanes = tile_of(i)
        own = conv_tile(left_ref, right_ref, i)
        ext = jnp.concatenate([halo_ref[0, :, lanes].astype(F32), own], 0)
        taps = conv_ref[:, lanes]
        total = taps[4:5] + taps[3:4] * own
        for k in range(KC - 1):
            at = HALO - (KC - 1) + k
            total = total + taps[k : k + 1] * (ext[at : at + rows] * wide[k])
        sig = sigmoid(total)
        x = total * sig
        slope_ref[0, :, lanes] = (sig + x * (1.0 - sig)).astype(BF16)
        low = x.astype(BF16)
        xbc_ref[0, :, lanes] = low
        return x, low

    tiles = DI // LANES
    b_turned = conv(tiles)[1].T
    conv(tiles + 1)
    for i in range(tiles):
        xd = conv(i)[0] * two_heads(step, i)
        xd_ref[0, :, tile_of(i)] = xd.astype(BF16)
        weighted = (xd * two_heads(ends, i)).astype(BF16)
        msg_ref[0, 0:NS, tile_of(i)] = dot_nn(b_turned, weighted).astype(BF16)


def seq_block(*shape):
    return pl.BlockSpec((1,) + shape, lambda s: (s,) + (0,) * len(shape))


def whole_block(*shape):
    return pl.BlockSpec(shape, lambda s: (0,) * len(shape))


def call(kernel, name, seqs, ins, in_specs, outs, out_specs, scratch=(), after=()):
    n_in, n_after = len(ins), len(after)

    def run(*refs):
        kernel(*refs[:n_in], *refs[n_in + n_after :])

    ins = tuple(ins) + tuple(after)
    in_specs = list(in_specs) + [pl.BlockSpec(memory_space=pl.ANY)] * n_after
    return pl.pallas_call(
        run,
        grid=(seqs,),
        in_specs=in_specs,
        out_specs=out_specs,
        out_shape=[jax.ShapeDtypeStruct(s, d) for s, d in outs],
        scratch_shapes=list(scratch),
        compiler_params=pltpu.CompilerParams(vmem_limit_bytes=VMEM_LIMIT),
        name=name,
    )(*ins)


def mix_begin(left, right, halo, cols, heads, conv, after=()):
    seqs, rows, _ = left.shape
    width = CONV_WIDTH
    return call(
        mix_begin_kernel,
        "mix_begin",
        seqs,
        (left, right, halo, cols, heads, conv),
        [
            seq_block(rows, LEFT),
            seq_block(rows, LEFT),
            seq_block(HALO, halo.shape[2]),
            seq_block(rows, LANES),
            whole_block(8, LANES),
            whole_block(8, width),
        ],
        [
            ((seqs, rows, width), BF16),
            ((seqs, rows, width), BF16),
            ((seqs, rows, DI), BF16),
            ((seqs, rows, LANES), F32),
            ((seqs, rows, LANES), F32),
            ((seqs, STATE_ROWS, DI), BF16),
        ],
        [
            seq_block(rows, width),
            seq_block(rows, width),
            seq_block(rows, DI),
            seq_block(rows, LANES),
            seq_block(rows, LANES),
            seq_block(STATE_ROWS, DI),
        ],
        after=after,
    )


def row_parts(rows):
    if rows < 256:
        return [(0, rows, rows)]
    return [(a, a + LANES, a + LANES) for a in range(0, rows, LANES)]


def side_by_side(pair):
    lane = lax.broadcasted_iota(jnp.int32, pair.shape, 1)
    blank = jnp.zeros_like(pair)
    return jnp.where(lane < P_SIZE, pair, blank), jnp.where(lane < P_SIZE, blank, pair)


def mix_inside_kernel(xbc_ref, xd_ref, cum_ref, cols_ref, rows_ref, skip_ref, y_ref):
    rows = xbc_ref.shape[1]
    b_rows, c_rows = xbc_ref[0, :, DI : DI + NS], xbc_ref[0, :, DI + NS :]
    seg_col, seg_row = cols_ref[0, :, 5:6], rows_ref[0, 0:1, :]
    row_at = lax.broadcasted_iota(jnp.int32, (rows, rows), 0)
    col_at = lax.broadcasted_iota(jnp.int32, (rows, rows), 1)
    couple = jnp.where((seg_col == seg_row) & (row_at >= col_at), dot_nt(c_rows, b_rows), 0.0)
    cum = cum_ref[0]
    cum_rows = cum.T
    for first in range(0, H, 2):
        lanes = slice(first * P_SIZE, (first + 2) * P_SIZE)
        sides = side_by_side(xd_ref[0, :, lanes])
        for begin, end, upto in row_parts(rows):
            y = xbc_ref[0, begin:end, lanes].astype(F32) * skip_ref[0:1, lanes]
            for h, side in zip((first, first + 1), sides):
                gap = jnp.minimum(cum[begin:end, h : h + 1] - cum_rows[h : h + 1, :upto], 0.0)
                mixing = (jnp.exp(gap) * couple[begin:end, :upto]).astype(BF16)
                y = y + dot_nn(mixing, side[:upto])
            y_ref[0, begin:end, lanes] = y


def mix_inside(xbc, xd, cum, cols, rows_in, skip, after=()):
    seqs, rows, width = xbc.shape
    return call(
        mix_inside_kernel,
        "mix_inside",
        seqs,
        (xbc, xd, cum, cols, rows_in, skip),
        [
            seq_block(rows, width),
            seq_block(rows, DI),
            seq_block(rows, LANES),
            seq_block(rows, LANES),
            seq_block(8, rows),
            whole_block(8, DI),
        ],
        [((seqs, rows, DI), F32)],
        [seq_block(rows, DI)],
        after=after,
    )[0]


def mix_finish_kernel(y_ref, c_ref, prev_ref, cum_ref, cols_ref, z_ref, gain_ref, mo_ref, nm_ref, g_ref):
    rows = y_ref.shape[1]
    flow = jnp.exp(cum_ref[0]) * cols_ref[0, :, 4:5]
    c_rows = c_ref[0]
    total = jnp.zeros((rows, LANES), F32)
    for i in range(DI // LANES):
        lanes = tile_of(i)
        mo = y_ref[0, :, lanes] + dot_nn(c_rows, prev_ref[0, :, lanes]) * two_heads(flow, i)
        mo_ref[0, :, lanes] = mo
        z = z_ref[0, :, lanes]
        g = mo * (z * sigmoid(z))
        g_ref[:, lanes] = g
        total = total + g * g
    scale = lax.rsqrt(jnp.sum(total, axis=1, keepdims=True) / DI + EPSILON)
    scale = jnp.broadcast_to(scale, (rows, LANES))
    for i in range(DI // LANES):
        lanes = tile_of(i)
        nm_ref[0, :, lanes] = (g_ref[:, lanes] * scale * gain_ref[0:1, lanes]).astype(BF16)


def c_block(rows):
    return pl.BlockSpec((1, rows, NS), lambda s: (s, 0, (DI + NS) // NS))


def mix_finish(y, xbc, prev, cum, cols, z, gain, after=()):
    seqs, rows, _ = y.shape
    return call(
        mix_finish_kernel,
        "mix_finish",
        seqs,
        (y, xbc, prev, cum, cols, z, gain),
        [
            seq_block(rows, DI),
            c_block(rows),
            seq_block(NS, DI),
            seq_block(rows, LANES),
            seq_block(rows, LANES),
            seq_block(rows, DI),
            whole_block(1, DI),
        ],
        [((seqs, rows, DI), F32), ((seqs, rows, DI), BF16)],
        [seq_block(rows, DI), seq_block(rows, DI)],
        [pltpu.VMEM((rows, DI), F32)],
        after=after,
    )


def gated_back_kernel(
    dn_ref, mo_ref, z_ref, gain_ref, c_ref, cum_ref, cols_ref, dy_ref, dza_ref, dzb_ref, msg_ref, sig_ref
):
    rows = dn_ref.shape[1]
    squares = jnp.zeros((rows, LANES), F32)
    mixed = jnp.zeros((rows, LANES), F32)
    for i in range(DI // LANES):
        lanes = tile_of(i)
        z = z_ref[0, :, lanes]
        sig = sigmoid(z)
        sig_ref[:, lanes] = sig
        g = mo_ref[0, :, lanes] * (z * sig)
        squares = squares + g * g
        mixed = mixed + g * (dn_ref[0, :, lanes] * gain_ref[0:1, lanes])
    scale = lax.rsqrt(jnp.sum(squares, axis=1, keepdims=True) / DI + EPSILON)
    back = jnp.sum(mixed, axis=1, keepdims=True) / DI * scale * scale * scale
    scale = jnp.broadcast_to(scale, (rows, LANES))
    back = jnp.broadcast_to(back, (rows, LANES))
    cum = cum_ref[0]
    flow = jnp.exp(cum) * cols_ref[0, :, 4:5]
    msg_ref[0, NS:STATE_ROWS, :] = all_heads(jnp.exp(cum[rows - 1 : rows])).astype(BF16)
    c_turned = c_ref[0].T
    for i in range(DI // LANES):
        lanes = tile_of(i)
        z = z_ref[0, :, lanes]
        mo = mo_ref[0, :, lanes]
        sig = sig_ref[:, lanes]
        swish = z * sig
        g = mo * swish
        dn = dn_ref[0, :, lanes] * scale
        dg = dn * gain_ref[0:1, lanes] - g * back
        dy = (dg * swish).astype(BF16)
        dy_ref[0, :, lanes] = dy
        dz = (dg * mo * (sig + swish * (1.0 - sig))).astype(BF16)
        split = dza_ref.shape[2] // LANES
        if i < split:
            dza_ref[0, :, lanes] = dz
        else:
            dzb_ref[0, :, tile_of(i - split)] = dz
        flowed = (dy.astype(F32) * two_heads(flow, i)).astype(BF16)
        msg_ref[0, 0:NS, lanes] = dot_nn(c_turned, flowed).astype(BF16)


def gated_back(dn, mo, z, gain, xbc, cum, cols, split, after=()):
    seqs, rows, _ = dn.shape
    return call(
        gated_back_kernel,
        "gated_back",
        seqs,
        (dn, mo, z, gain, xbc, cum, cols),
        [
            seq_block(rows, DI),
            seq_block(rows, DI),
            seq_block(rows, DI),
            whole_block(1, DI),
            c_block(rows),
            seq_block(rows, LANES),
            seq_block(rows, LANES),
        ],
        [
            ((seqs, rows, DI), BF16),
            ((seqs, rows, split), BF16),
            ((seqs, rows, DI - split), BF16),
            ((seqs, STATE_ROWS, DI), BF16),
        ],
        [
            seq_block(rows, DI),
            seq_block(rows, split),
            seq_block(rows, DI - split),
            seq_block(STATE_ROWS, DI),
        ],
        [pltpu.VMEM((rows, DI), F32)],
        after=after,
    )


def inside_back_kernel(
    xbc_ref, xd_ref, cum_ref, cols_ref, rows_ref, skip_ref, spread_ref, dy_ref, mo_ref, prev_ref,
    dxd_ref, dbc_ref, sums_ref, dcouple_ref,
):
    rows = xbc_ref.shape[1]
    cum = cum_ref[0]
    flow = jnp.exp(cum) * cols_ref[0, :, 4:5]
    sums = jnp.zeros((rows, LANES), F32)
    dc = jnp.zeros((rows, NS), F32)
    for i in range(DI // LANES):
        lanes = tile_of(i)
        dy = dy_ref[0, :, lanes].astype(F32)
        plain = mo_ref[0, :, lanes] - xbc_ref[0, :, lanes].astype(F32) * skip_ref[0:1, lanes]
        sums = sums + sum_heads(dy * plain, spread_ref[:, lanes])
        dc = dc + dot_nt((dy * two_heads(flow, i)).astype(BF16), prev_ref[0, :, lanes])
    sums_ref[0] = sums
    b_rows, c_rows = xbc_ref[0, :, DI : DI + NS], xbc_ref[0, :, DI + NS :]
    seg_col, seg_row = cols_ref[0, :, 5:6], rows_ref[0, 0:1, :]
    row_at = lax.broadcasted_iota(jnp.int32, (rows, rows), 0)
    col_at = lax.broadcasted_iota(jnp.int32, (rows, rows), 1)
    keep = (seg_col == seg_row) & (row_at <= col_at)
    couple = jnp.where(keep, dot_nt(b_rows, c_rows), 0.0)
    dcouple_ref[...] = jnp.zeros_like(dcouple_ref)
    cum_rows = cum.T
    for first in range(0, H, 2):
        lanes = slice(first * P_SIZE, (first + 2) * P_SIZE)
        dy_sides = side_by_side(dy_ref[0, :, lanes])
        xd = xd_ref[0, :, lanes]
        for begin, end, _ in row_parts(rows):
            dxd, added = [], []
            for h, dy in zip((first, first + 1), dy_sides):
                decay = jnp.exp(jnp.minimum(cum_rows[h : h + 1, begin:] - cum[begin:end, h : h + 1], 0.0))
                mixing = (decay * couple[begin:end, begin:]).astype(BF16)
                dxd.append(dot_nn(mixing, dy[begin:]))
                added.append(dot_nt(xd[begin:end], dy[begin:]) * decay)
            dcouple_ref[begin:end, begin:] += added[0] + added[1]
            dxd_ref[0, begin:end, lanes] = dxd[0] + dxd[1]
    dcouple = jnp.where(keep, dcouple_ref[...], 0.0).astype(BF16)
    dbc_ref[0, :, :NS] = dot_nn(dcouple, c_rows)
    dbc_ref[0, :, NS:] = dc + dot_tn(dcouple, b_rows)


def inside_back(xbc, xd, cum, cols, rows_in, skip, spread, dy, mo, prev, after=()):
    seqs, rows, width = xbc.shape
    return call(
        inside_back_kernel,
        "inside_back",
        seqs,
        (xbc, xd, cum, cols, rows_in, skip, spread, dy, mo, prev),
        [
            seq_block(rows, width),
            seq_block(rows, DI),
            seq_block(rows, LANES),
            seq_block(rows, LANES),
            seq_block(8, rows),
            whole_block(8, DI),
            whole_block(LANES, DI),
            seq_block(rows, DI),
            seq_block(rows, DI),
            seq_block(NS, DI),
        ],
        [((seqs, rows, DI), F32), ((seqs, rows, 2 * NS), F32), ((seqs, rows, LANES), F32)],
        [seq_block(rows, DI), seq_block(rows, 2 * NS), seq_block(rows, LANES)],
        [pltpu.VMEM((rows, rows), F32)],
        after=after,
    )


def mix_end_kernel(
    left_ref, right_ref, halo_ref, xbc_ref, slope_ref, xd_ref, step_ref, cum_ref, cols_ref, heads_ref, skip_ref,
    conv_ref, spread_ref, dy_ref, dxd_ref, dbc_ref, sums_ref, later_ref, prev_ref,
    grad_ref, gconv_ref, gheads_ref, dco_ref, tops_ref,
):
    rows = xbc_ref.shape[1]
    cum = cum_ref[0]
    step = step_ref[0]
    masks = cols_ref[0]
    last = cum[rows - 1 : rows]
    ends = jnp.exp(last - cum) * masks[:, 3:4]
    b_rows = xbc_ref[0, :, DI : DI + NS]
    direct = jnp.zeros((rows, LANES), F32)
    columns = jnp.zeros((rows, LANES), F32)
    db = dbc_ref[0, :, :NS]
    for i in range(DI // LANES):
        lanes = tile_of(i)
        x = xbc_ref[0, :, lanes].astype(F32)
        xd = xd_ref[0, :, lanes].astype(F32)
        dy = dy_ref[0, :, lanes].astype(F32)
        later = later_ref[0, :, lanes]
        to_end = two_heads(ends, i)
        from_end = dot_nn(b_rows, later) * to_end
        dxd = dxd_ref[0, :, lanes] + from_end
        dco_ref[:, lanes] = dxd * two_heads(step, i) + dy * skip_ref[0:1, lanes]
        db = db + dot_nt((xd * to_end).astype(BF16), later)
        direct = direct + dot_nt((x * dxd).astype(BF16), spread_ref[:, lanes])
        columns = columns + sum_heads(xd * dxd, spread_ref[:, lanes])
        tops_ref[:, lanes] = jnp.concatenate(
            [
                jnp.sum(xd * from_end, axis=0, keepdims=True),
                jnp.sum(dy * x, axis=0, keepdims=True),
                jnp.sum(later.astype(F32) * prev_ref[0, :, lanes].astype(F32), axis=0, keepdims=True),
                jnp.zeros((13, LANES), F32),
            ],
            0,
        )
    dco_ref[:, DI : DI + NS] = db
    dco_ref[:, DI + NS :] = dbc_ref[0, :, NS:]
    tops = sum_heads(tops_ref[...], spread_ref[...])
    ended, skipped, carried = tops[0:1], tops[1:2], tops[2:3]
    at = lax.broadcasted_iota(jnp.int32, (rows, LANES), 0)
    dcum = sums_ref[0] - columns
    dcum = dcum + jnp.where(at == rows - 1, ended + jnp.exp(last) * carried, 0.0)
    da = exact_sum(triangle(rows, False), dcum)
    rate = heads_ref[1:2]
    graw = (direct + da * rate) * sigmoid(raw_tile(right_ref) + heads_ref[0:1])
    seqs = grad_ref.shape[0] // (rows + HALO)
    seq = pl.program_id(0)
    main = pl.ds(pl.multiple_of(seq * rows, rows), rows)
    edge = pl.ds(pl.multiple_of(seqs * rows + seq * HALO, HALO), HALO)
    end = CONV_WIDTH + LANES
    grad_ref[main, CONV_WIDTH:end] = graw.astype(BF16)
    grad_ref[edge, CONV_WIDTH:end] = jnp.zeros((HALO, LANES), BF16)
    grad_ref[main, end:] = jnp.zeros((rows, grad_ref.shape[1] - end), BF16)
    grad_ref[edge, end:] = jnp.zeros((HALO, grad_ref.shape[1] - end), BF16)
    gheads_ref[0] = jnp.concatenate(
        [
            jnp.sum(graw, axis=0, keepdims=True),
            jnp.sum(da * step, axis=0, keepdims=True) * rate,
            skipped,
            jnp.zeros((5, LANES), F32),
        ],
        0,
    )
    wide = [jnp.broadcast_to(masks[:, k : k + 1], (rows, LANES)) for k in range(KC - 1)]
    blank = jnp.zeros((HALO, LANES), F32)
    for i in range(CONV_WIDTH // LANES):
        lanes = tile_of(i)
        du = dco_ref[:, lanes] * slope_ref[0, :, lanes].astype(F32)
        own = conv_tile(left_ref, right_ref, i)
        ext = jnp.concatenate([halo_ref[0, :, lanes].astype(F32), own], 0)
        taps = conv_ref[:, lanes]
        grads = []
        total = jnp.zeros((rows + HALO, LANES), F32)
        for k in range(KC):
            part = du * wide[k] if k < KC - 1 else du
            at_ext = HALO - (KC - 1) + k
            grads.append(jnp.sum(part * ext[at_ext : at_ext + rows], axis=0, keepdims=True))
            padded = jnp.concatenate([blank, part, blank], 0)
            total = total + taps[k : k + 1] * padded[KC - 1 - k : KC - 1 - k + rows + HALO]
        grad_ref[main, lanes] = total[HALO:].astype(BF16)
        grad_ref[edge, lanes] = total[:HALO].astype(BF16)
        gconv_ref[0, :, lanes] = jnp.concatenate(
            grads + [jnp.sum(du, axis=0, keepdims=True), jnp.zeros((3, LANES), F32)], 0
        )


def mix_end(
    left, right, halo, xbc, slope, xd, step, cum, cols, heads, skip, conv, spread, dy, dxd, dbc, sums, later, prev,
    after=(),
):
    seqs, rows, width = xbc.shape
    tokens = seqs * (rows + HALO)
    return call(
        mix_end_kernel,
        "mix_end",
        seqs,
        (left, right, halo, xbc, slope, xd, step, cum, cols, heads, skip, conv, spread, dy, dxd, dbc, sums, later, prev),
        [
            seq_block(rows, LEFT),
            seq_block(rows, LEFT),
            seq_block(HALO, halo.shape[2]),
            seq_block(rows, width),
            seq_block(rows, width),
            seq_block(rows, DI),
            seq_block(rows, LANES),
            seq_block(rows, LANES),
            seq_block(rows, LANES),
            whole_block(8, LANES),
            whole_block(8, DI),
            whole_block(8, width),
            whole_block(LANES, DI),
            seq_block(rows, DI),
            seq_block(rows, DI),
            seq_block(rows, 2 * NS),
            seq_block(rows, LANES),
            seq_block(NS, DI),
            seq_block(NS, DI),
        ],
        [
            ((tokens, 2 * LEFT), BF16),
            ((seqs, 8, width), F32),
            ((seqs, 8, LANES), F32),
        ],
        [
            whole_block(tokens, 2 * LEFT),
            seq_block(8, width),
            seq_block(8, LANES),
        ],
        [pltpu.VMEM((rows, width), F32), pltpu.VMEM((16, DI), F32)],
        after=after,
    )


def attend_bias(slot, rest, cols_ref, rows_ref, kv_ref, offsets):
    rows = cols_ref.shape[1]
    found = []
    for before in range(slot + 1):
        for j, offset in enumerate(offsets):
            if before == slot and offset == 0:
                row_at = lax.broadcasted_iota(jnp.int32, (rows, rows), 0)
                col_at = lax.broadcasted_iota(jnp.int32, (rows, rows), 1)
                same = cols_ref[slot, :, 5:6] == rows_ref[slot, 0:1, :]
                allowed = same & (row_at >= col_at)
            else:
                keys = kv_ref[j][before, rows : rows + 16, :rows].astype(F32)[0:1]
                if before == slot:
                    keys = keys * jnp.where((rest ^ offset) < rest, 1.0, 0.0)
                allowed = cols_ref[slot, :, 4:5] * keys > 0.5
            found.append((j, before, jnp.where(allowed, 0.0, NEGATIVE)))
    return found


def swap_halves(pair):
    return jnp.concatenate([pair[:, P_SIZE:], pair[:, :P_SIZE]], 1)


def to_side(pair, group):
    pair_sides, swapped = side_by_side(pair), side_by_side(swap_halves(pair))
    return (pair_sides[0], swapped[0]) if group == 0 else (swapped[1], pair_sides[1])


def from_side(left, right, group):
    lane = lax.broadcasted_iota(jnp.int32, left.shape, 1)
    if group == 0:
        right = swap_halves(right)
    else:
        left = swap_halves(left)
    return jnp.where(lane < P_SIZE, left, right)


def attend_kernel(offsets, rest_ref, q_ref, cols_ref, rows_ref, *refs):
    kv_ref, (out_ref, lse_ref) = refs[:-2], refs[-2:]
    rows = q_ref.shape[1]
    for slot in range(SLOTS):
        blocks = attend_bias(slot, rest_ref[0], cols_ref, rows_ref, kv_ref, offsets)
        sums = []
        for i in range(QUERY_HEADS // 2):
            lanes, group = tile_of(i), (2 * i) // (QUERY_HEADS // KEY_VALUE_HEADS)
            outs = []
            for q in to_side(q_ref[slot, :, lanes] * jnp.asarray(HEAD_WIDTH**-0.5, BF16), group):
                scores = [dot_nt(q, kv_ref[j][n, :rows, :LANES]) + bias for j, n, bias in blocks]
                top = jnp.max(functools.reduce(jnp.maximum, scores), axis=1, keepdims=True)
                weights = [jnp.exp(s - top) for s in scores]
                total = jnp.sum(functools.reduce(jnp.add, weights), axis=1, keepdims=True)
                out = [
                    dot_nn(w.astype(BF16), kv_ref[j][n, :rows, LANES:]) for (j, n, _), w in zip(blocks, weights)
                ]
                outs.append(functools.reduce(jnp.add, out) / total)
                sums.append(top + jnp.log(total))
            out_ref[slot, :, lanes] = from_side(*outs, group).astype(BF16)
        lse_ref[slot] = jnp.concatenate(sums + [jnp.zeros((rows, LANES - QUERY_HEADS), F32)], 1)


def call_whole(kernel, name, scalars, ins, outs, scratch=(), after=()):
    vmem = pl.BlockSpec(memory_space=pltpu.VMEM)
    n_in = len(scalars) + len(ins)

    def run(*refs):
        kernel(*refs[:n_in], *refs[n_in + len(after) :])

    return pl.pallas_call(
        run,
        in_specs=[pl.BlockSpec(memory_space=pltpu.SMEM)] * len(scalars) + [vmem] * len(ins) + spec_any(len(after)),
        out_specs=[vmem] * len(outs),
        out_shape=[jax.ShapeDtypeStruct(s, d) for s, d in outs],
        scratch_shapes=list(scratch),
        compiler_params=pltpu.CompilerParams(vmem_limit_bytes=VMEM_LIMIT),
        name=name,
    )(*scalars, *ins, *after)


def attend(rest, q, kv, cols, rows_in, offsets, after=()):
    outs = [(q.shape, BF16), (q.shape[:2] + (LANES,), F32)]
    return call_whole(
        functools.partial(attend_kernel, offsets), "attend", (rest,), (q, cols, rows_in, *kv), outs, after=after
    )


def attend_back_kernel(
    offsets, rest_ref, q_ref, cols_ref, rows_ref, out_ref, lse_ref, dout_ref, *refs
):
    count = len(offsets)
    kv_ref, dq_ref, dkv_ref, acc_ref = refs[:count], refs[count], refs[count + 1 : -1], refs[-1]
    rows = q_ref.shape[1]
    scale = HEAD_WIDTH**-0.5
    acc_ref[...] = jnp.zeros_like(acc_ref)
    for slot in range(SLOTS):
        blocks = attend_bias(slot, rest_ref[0], cols_ref, rows_ref, kv_ref, offsets)
        for i in range(QUERY_HEADS // 2):
            lanes, group = tile_of(i), (2 * i) // (QUERY_HEADS // KEY_VALUE_HEADS)
            q_pair = q_ref[slot, :, lanes] * jnp.asarray(scale, BF16)
            dout_pair = dout_ref[slot, :, lanes]
            q_turned, dout_turned = q_pair.T, dout_pair.T
            product = dout_pair.astype(F32) * out_ref[slot, :, lanes].astype(F32)
            q_sides, dout_sides = to_side(q_pair, group), to_side(dout_pair, group)
            k_rows = slice(group * HEAD_WIDTH, (group + 1) * HEAD_WIDTH)
            v_rows = slice(LANES + group * HEAD_WIDTH, LANES + (group + 1) * HEAD_WIDTH)
            dqs = []
            for n in range(2):
                own = slice(n * HEAD_WIDTH, (n + 1) * HEAD_WIDTH)
                q, dout = q_sides[n], dout_sides[n]
                delta = jnp.sum(side_by_side(product)[n], axis=1, keepdims=True)
                lse = lse_ref[slot, :, 2 * i + n : 2 * i + n + 1]
                dq = None
                for j, before, bias in blocks:
                    k, v = kv_ref[j][before, :rows, :LANES], kv_ref[j][before, :rows, LANES:]
                    p = jnp.exp(dot_nt(q, k) + bias - lse)
                    ds = (p * (dot_nt(dout, v) - delta)).astype(BF16)
                    part = dot_nn(ds, k)
                    dq = part if dq is None else dq + part
                    acc_ref[j, before, k_rows, :] += dot_nn(q_turned[own], ds)
                    acc_ref[j, before, v_rows, :] += dot_nn(dout_turned[own], p.astype(BF16))
                dqs.append(dq * scale)
            dq_ref[slot, :, lanes] = from_side(*dqs, group).astype(BF16)
    for j in range(len(offsets)):
        for before in range(SLOTS):
            dkv_ref[j][before] = acc_ref[j, before].T.astype(BF16)


def attend_back(rest, q, kv, cols, rows_in, out, lse, dout, offsets, after=()):
    rows, blocks, (slots, _, kv_width) = q.shape[1], len(kv), kv[0].shape
    found = call_whole(
        functools.partial(attend_back_kernel, offsets),
        "attend_back",
        (rest,),
        (q, cols, rows_in, out, lse, dout, *kv),
        [(q.shape, BF16)] + [((slots, rows, kv_width), BF16)] * blocks,
        [pltpu.VMEM((blocks, slots, kv_width, rows), F32)],
        after=after,
    )
    return found[0], found[1:]


def pick_offset(rest, number, group, offsets, pieces, slot):
    wanted = (number % group) ^ rest
    found = None
    for offset, piece in zip(offsets, pieces):
        part = piece[slot].astype(F32)
        found = part if found is None else jnp.where(wanted == offset, part, found)
    return found


def halo_kernel(offsets, rest_ref, *refs):
    pieces, out_ref = refs[:-1], refs[-1]
    rest, group = rest_ref[0], len(pieces)
    for slot in range(SLOTS):
        found = jnp.zeros(out_ref.shape[1:], F32)
        for number in range(group * slot, group * (slot + 1)):
            if number > 0:
                before = number - 1
                part = pick_offset(rest, before, group, offsets, pieces, before // group)
                found = jnp.where(rest == number % group, part, found)
        out_ref[slot] = found.astype(out_ref.dtype)


def take_halo(rest, pieces, offsets):
    return call_whole(
        functools.partial(halo_kernel, offsets), "halo", (rest,), pieces, [(pieces[0].shape, pieces[0].dtype)]
    )[0]


def scan_kernel(offsets, from_earlier, rest_ref, *refs):
    pieces, out_ref = refs[:-1], refs[-1]
    rest, group = rest_ref[0], len(pieces)
    order = list(range(SLOTS * group))
    width = 4 * LANES

    def column(i, _):
        lanes = pl.ds(pl.multiple_of(i * width, width), width)
        state = jnp.zeros((NS, width), F32)
        found = [state] * SLOTS
        for number in order if from_earlier else order[::-1]:
            slot = number // group
            found[slot] = jnp.where(rest == number % group, state, found[slot])
            part = pick_offset(rest, number, group, offsets, [p.at[:, :, lanes] for p in pieces], slot)
            state = part[:NS] + part[NS : NS + 1] * state
        for slot in range(SLOTS):
            out_ref[slot, :, lanes] = found[slot].astype(BF16)
        return 0

    lax.fori_loop(0, DI // width, column, 0)


def scan_states(rest, pieces, offsets, from_earlier, after=()):
    return call_whole(
        functools.partial(scan_kernel, offsets, from_earlier),
        "scan_states",
        (rest,),
        pieces,
        [((SLOTS, NS, DI), BF16)],
        after=after,
    )[0]


def join_grads_kernel(za_ref, zb_ref, q_ref, own_ref, got_ref, out_ref):
    slots, rows, width = own_ref.shape
    at = 0
    for ref in (za_ref, zb_ref, q_ref):
        out_ref[:, at : at + ref.shape[1]] = ref[...]
        at += ref.shape[1]
    for s in range(slots):
        total = own_ref[s].astype(F32) + got_ref[s].astype(F32)
        out_ref[s * rows : (s + 1) * rows, at:] = total.astype(BF16)


def join_grads(za, zb, q, own, got, after=()):
    tokens = za.shape[0]
    width = za.shape[1] + zb.shape[1] + q.shape[1] + own.shape[2]
    return call_whole(
        join_grads_kernel, "join_grads", (), (za, zb, q, own, got), [((tokens, width), BF16)], after=after
    )[0]


def line_place(j, count, r):
    stride = LANES // -(-count // r)
    return j % r, stride * (j // r)


def pack_lines(rows_of, r):
    count = len(rows_of)
    stride = LANES // -(-count // r)
    groups = []
    for begin in range(0, count, r):
        part = [
            jnp.concatenate([v, jnp.zeros((1, stride - v.shape[1]), F32)], 1) for v in rows_of[begin : begin + r]
        ]
        if len(part) < r:
            part.append(jnp.zeros((r - len(part), stride), F32))
        groups.append(jnp.concatenate(part, 0))
    tile = jnp.concatenate(groups, 1) if len(groups) > 1 else groups[0]
    if tile.shape[1] < LANES:
        tile = jnp.concatenate([tile, jnp.zeros((r, LANES - tile.shape[1]), F32)], 1)
    return tile


def pack_first_kernel(xbc_ref, step_ref, conv_ref, bias_ref, mix_ref, one_ref, two_ref, out_ref):
    r = xbc_ref.shape[0]
    over = CONV_WIDTH - LEFT
    out_ref[0] = xbc_ref[:, :LEFT]
    out_ref[1, :, :over] = xbc_ref[:, LEFT:]
    blank = jnp.zeros((r, LANES - H), BF16)
    out_ref[1, :, over : over + LANES] = jnp.concatenate([step_ref[...], blank], 1)
    taps = conv_ref[...].astype(F32)
    vectors = [taps[k : k + 1] for k in range(KC)]
    vectors += [ref[...].astype(F32) for ref in (bias_ref, mix_ref, one_ref, two_ref)]
    out_ref[1, :, over + LANES :] = pack_lines(vectors, r).astype(BF16)


def pack_first(w_xbc, w_step, conv_weight, conv_bias, mixer_gain, norm1_gain, norm2_gain):
    r = w_xbc.shape[0]
    vmem = pl.BlockSpec(memory_space=pltpu.VMEM)
    return pl.pallas_call(
        pack_first_kernel,
        in_specs=[vmem] * 7,
        out_specs=vmem,
        out_shape=jax.ShapeDtypeStruct((2, r, LEFT), BF16),
        name="pack_first",
    )(w_xbc, w_step, conv_weight, conv_bias[None], mixer_gain[None], norm1_gain[None], norm2_gain[None])


def pack_two_kernel(z_ref, query_ref, kv_ref, mix_ref, attn_ref, two_ref):
    r = z_ref.shape[0]
    width = two_ref.shape[2] - MODEL_WIDTH
    two_ref[0, :, :width] = z_ref[:, :width]
    two_ref[1, :, : DI - width] = z_ref[:, width:]
    at = DI - width + query_ref.shape[1]
    two_ref[1, :, DI - width : at] = query_ref[...]
    two_ref[1, :, at:width] = kv_ref[...]
    more = mix_ref.shape[0] - r
    two_ref[0, :, width:] = mix_ref[:r]
    two_ref[1, :more, width:] = mix_ref[r:]
    two_ref[1, more:, width:] = attn_ref[...]


def pack_two(w_gate_z, w_query, key_value_weight, w_mix_out, w_attn_out, after=()):
    width = (DI + w_query.shape[1] + key_value_weight.shape[1]) // 2 + MODEL_WIDTH
    ins = (w_gate_z, w_query, key_value_weight, w_mix_out, w_attn_out)
    return call_whole(pack_two_kernel, "pack_two", (), ins, [((2, w_gate_z.shape[0], width), BF16)], after=after)[0]


def pack_units_kernel(gate_up_ref, down_ref, units_ref):
    r, half = gate_up_ref.shape[0], down_ref.shape[0] // 2
    for n in range(2):
        for q in range(2):
            column = (2 * n + q) * MODEL_WIDTH
            units_ref[n, q * r : (q + 1) * r] = gate_up_ref[:, column : column + MODEL_WIDTH]
        units_ref[n, 2 * r :] = down_ref[n * half : (n + 1) * half]


def pack_units(w_gate_up, w_down, after=()):
    shape = (2, 2 * w_gate_up.shape[0] + w_down.shape[0] // 2, MODEL_WIDTH)
    return call_whole(pack_units_kernel, "pack_units", (), (w_gate_up, w_down), [(shape, BF16)], after=after)[0]


def unpack_small_kernel(r, small_ref, conv_ref, mix_ref, gain_ref):
    count = small_ref.shape[0] // r
    widths = [CONV_WIDTH // count] * (KC + 1) + [DI // count] + [MODEL_WIDTH // count] * 2
    found = [[] for _ in widths]
    for i in range(count):
        tile = small_ref[i * r : (i + 1) * r, :].astype(F32)
        for j, width in enumerate(widths):
            row, lane = line_place(j, len(widths), r)
            found[j].append(tile[row : row + 1, lane : lane + width])
    found = [jnp.concatenate(v, 1) for v in found]
    conv_ref[...] = jnp.concatenate(found[: KC + 1] + [jnp.zeros((3, CONV_WIDTH), F32)], 0)
    mix_ref[...] = found[KC + 1]
    gain_ref[...] = jnp.concatenate(found[KC + 2 :], 0)


def unpack_small(small, r):
    vmem = pl.BlockSpec(memory_space=pltpu.VMEM)
    return pl.pallas_call(
        functools.partial(unpack_small_kernel, r),
        in_specs=[vmem],
        out_specs=[vmem] * 3,
        out_shape=[jax.ShapeDtypeStruct(s, F32) for s in ((8, CONV_WIDTH), (1, DI), (2, MODEL_WIDTH))],
        name="unpack_small",
    )(small)


def small_grads_kernel(r, offsets, place_ref, conv_ref, heads_ref, keep_ref, send_ref, tile_ref):
    count = tile_ref.shape[0]
    conv = jnp.sum(conv_ref[...], 0)
    heads = jnp.sum(heads_ref[...], 0)
    width = CONV_WIDTH // count
    shared = [heads[k : k + 1, :H] for k in range(3)]
    high = [v.astype(BF16).astype(F32) for v in shared]
    shared = high + [v - h for v, h in zip(shared, high)]
    for i in range(count):
        own = [conv[k : k + 1, i * width : (i + 1) * width] for k in range(KC + 1)]
        tile_ref[i] = pack_lines(own + shared, r)
    place = place_ref[0]
    for t, offset in enumerate(offsets):
        keep_ref[t * r : (t + 1) * r] = tile_ref[place ^ offset].astype(BF16)
        send_ref[t * r : (t + 1) * r] = tile_ref[place ^ (offset ^ 1)].astype(BF16)


def small_grads(r, conv, heads):
    bits = bit_count()
    count = 1 << bits
    vmem = pl.BlockSpec(memory_space=pltpu.VMEM)
    return pl.pallas_call(
        functools.partial(small_grads_kernel, r, turned_offsets(bits)),
        in_specs=[pl.BlockSpec(memory_space=pltpu.SMEM)] + [vmem] * 2,
        out_specs=[vmem] * 2,
        out_shape=[jax.ShapeDtypeStruct((count // 2 * r, LANES), BF16)] * 2,
        scratch_shapes=[pltpu.VMEM((count, r, LANES), F32)],
        name="small_grads",
    )(place_of().reshape(1).astype(jnp.int32), conv, heads)


def tiles_spec(shape, axis, width):
    block = tuple(width if n == axis else size for n, size in enumerate(shape))
    return pl.BlockSpec(block, lambda i: tuple(i if n == axis else 0 for n in range(len(shape))))


def fixed(*shape):
    return pl.BlockSpec(shape, lambda i: (0,) * len(shape))


def dense(kernel, name, steps, ins, in_specs, outs, out_specs, scratch=(), after=()):
    n_in, n_after = len(ins), len(after)

    def run(*refs):
        kernel(*refs[:n_in], *refs[n_in + n_after :])

    return pl.pallas_call(
        run,
        grid=(steps,),
        in_specs=list(in_specs) + spec_any(n_after),
        out_specs=out_specs,
        out_shape=[jax.ShapeDtypeStruct(s, d) for s, d in outs],
        scratch_shapes=list(scratch),
        compiler_params=pltpu.CompilerParams(vmem_limit_bytes=VMEM_LIMIT),
        name=name,
    )(*ins, *after)


def row_scale(values):
    return lax.rsqrt(jnp.mean(values * values, axis=1, keepdims=True) + EPSILON)


def first_proj_kernel(x_ref, gain_ref, left_w, right_w, cols_ref, normed_ref, left_ref, right_ref, tails_ref):
    step, tile = pl.program_id(0), left_w.shape[1]

    @pl.when(step == 0)
    def _():
        x = x_ref[...].astype(F32)
        normed_ref[...] = (x * row_scale(x) * gain_ref[...]).astype(BF16)

    left = dot_nn(normed_ref[...], left_w[...]).astype(BF16)
    right = dot_nn(normed_ref[...], right_w[...])
    left_ref[...] = left
    right_ref[...] = right
    slots, rows, _ = cols_ref.shape
    lanes = pl.ds(pl.multiple_of(step * tile, tile), tile)
    for s in range(slots):
        begin, end = (s + 1) * rows - HALO, (s + 1) * rows
        edge = cols_ref[s, rows - HALO :, 3:4]
        tails_ref[s, :, lanes] = (left[begin:end].astype(F32) * edge).astype(BF16)
        normed = normed_ref[begin:end, lanes].astype(F32)
        tails_ref[s, :, pl.ds(pl.multiple_of(CONV_WIDTH + step * tile, tile), tile)] = (normed * edge).astype(BF16)

        @pl.when(step < (CONV_WIDTH - LEFT) // tile)
        def _():
            at = pl.ds(pl.multiple_of(LEFT + step * tile, tile), tile)
            tails_ref[s, :, at] = (right[begin:end].astype(BF16).astype(F32) * edge).astype(BF16)


def first_proj(x, gain, left_full, right_full, cols, after=()):
    tokens, width = x.shape
    tile = LEFT // 4
    tails = (cols.shape[0], HALO, CONV_WIDTH + width)
    return dense(
        first_proj_kernel,
        "first_proj",
        4,
        (x, gain, left_full, right_full, cols),
        [
            fixed(tokens, width),
            fixed(1, width),
            tiles_spec((width, LEFT), 1, tile),
            tiles_spec((width, LEFT), 1, tile),
            fixed(*cols.shape),
        ],
        [((tokens, width), BF16), ((tokens, LEFT), BF16), ((tokens, LEFT), F32), (tails, BF16)],
        [
            fixed(tokens, width),
            tiles_spec((tokens, LEFT), 1, tile),
            tiles_spec((tokens, LEFT), 1, tile),
            fixed(*tails),
        ],
        after=after,
    )


def second_proj_kernel(normed_ref, z_w, qkv_w, rows_ref, z_ref, q_ref, kv_ref):
    step = pl.program_id(0)
    z_ref[...] = dot_nn(normed_ref[...], z_w[...])
    part = dot_nn(normed_ref[...], qkv_w[...]).astype(BF16)
    slots, extended, width = kv_ref.shape
    rows = extended - 16

    @pl.when(step < 2)
    def _():
        q_ref[...] = part

    @pl.when(step == 2)
    def _():
        for s in range(slots):
            kv_ref[s, :rows] = part[s * rows : (s + 1) * rows]
            keys = jnp.broadcast_to(rows_ref[s, 1:2], (16, rows))
            if rows < width:
                keys = jnp.concatenate([keys, jnp.zeros((16, width - rows), F32)], 1)
            kv_ref[s, rows:] = keys.astype(BF16)


def second_proj(normed, z_full, qkv_full, rows_in, after=()):
    tokens, width = normed.shape
    slots, _, rows = rows_in.shape
    query, kv = QUERY_HEADS * HEAD_WIDTH, 2 * KEY_VALUE_HEADS * HEAD_WIDTH
    return dense(
        second_proj_kernel,
        "second_proj",
        3,
        (normed, z_full, qkv_full, rows_in),
        [
            fixed(tokens, width),
            tiles_spec((width, DI), 1, DI // 3),
            tiles_spec((width, query + kv), 1, kv),
            fixed(slots, 8, rows),
        ],
        [((tokens, DI), F32), ((tokens, query), BF16), ((slots, rows + 16, kv), BF16)],
        [
            tiles_spec((tokens, DI), 1, DI // 3),
            pl.BlockSpec((tokens, kv), lambda i: (0, jnp.minimum(i, 1))),
            fixed(slots, rows + 16, kv),
        ],
        after=after,
    )


def out_proj_kernel(x_ref, nm_ref, attn_ref, mix_w, attn_w, gain_ref, resid_ref, normed_ref):
    step = pl.program_id(0)
    part = dot_nn(nm_ref[...], mix_w[...]) + dot_nn(attn_ref[...], attn_w[...])

    @pl.when(step == 0)
    def _():
        resid_ref[...] = x_ref[...].astype(F32) + part

    @pl.when(step > 0)
    def _():
        resid_ref[...] += part

    @pl.when(step == pl.num_programs(0) - 1)
    def _():
        resid = resid_ref[...]
        normed_ref[...] = (resid * row_scale(resid) * gain_ref[...]).astype(BF16)


def out_proj(x, nm, attn, mix_full, attn_full, gain, after=()):
    tokens, width = x.shape
    query = attn.shape[1]
    steps = 2
    return dense(
        out_proj_kernel,
        "out_proj",
        steps,
        (x, nm, attn, mix_full, attn_full, gain),
        [
            fixed(tokens, width),
            tiles_spec(nm.shape, 1, DI // steps),
            tiles_spec(attn.shape, 1, query // steps),
            tiles_spec(mix_full.shape, 0, DI // steps),
            tiles_spec(attn_full.shape, 0, query // steps),
            fixed(1, width),
        ],
        [((tokens, width), F32), ((tokens, width), BF16)],
        [fixed(tokens, width), fixed(tokens, width)],
        after=after,
    )


def gate_up_kernel(normed_ref, gate_w, up_w, act_ref, swish_ref, slope_ref):
    gate = dot_nn(normed_ref[...], gate_w[...])
    up = dot_nn(normed_ref[...], up_w[...])
    sig = sigmoid(gate)
    swish = gate * sig
    act_ref[...] = (swish * up).astype(BF16)
    swish_ref[...] = swish.astype(BF16)
    slope_ref[...] = ((sig + swish * (1.0 - sig)) * up).astype(BF16)


def gate_up(normed, gate_full, up_full, after=()):
    tokens, width = normed.shape
    tile = FF // 2
    spec = tiles_spec((tokens, FF), 1, tile)
    return dense(
        gate_up_kernel,
        "gate_up",
        2,
        (normed, gate_full, up_full),
        [fixed(tokens, width), tiles_spec((width, FF), 1, tile), tiles_spec((width, FF), 1, tile)],
        [((tokens, FF), BF16)] * 3,
        [spec] * 3,
        after=after,
    )


def down_kernel(act_ref, swish_ref, slope_ref, down_w, resid_ref, grad_ref, out_ref, dgate_ref, dup_ref, total_ref):
    step = pl.program_id(0)
    weights = down_w[...]
    part = dot_nn(act_ref[...], weights)

    @pl.when(step == 0)
    def _():
        total_ref[...] = resid_ref[...] + part

    @pl.when(step > 0)
    def _():
        total_ref[...] += part

    @pl.when(step == pl.num_programs(0) - 1)
    def _():
        out_ref[...] = total_ref[...].astype(BF16)

    dact = dot_nt(grad_ref[...], weights)
    dgate_ref[...] = (dact * slope_ref[...].astype(F32)).astype(BF16)
    dup_ref[...] = (dact * swish_ref[...].astype(F32)).astype(BF16)


def down(act, swish, slope, down_full, resid, grad_out, after=()):
    tokens, width = resid.shape
    tile = FF // 2
    spec = tiles_spec((tokens, FF), 1, tile)
    return dense(
        down_kernel,
        "down",
        2,
        (act, swish, slope, down_full, resid, grad_out),
        [spec, spec, spec, tiles_spec((FF, width), 0, tile), fixed(tokens, width), fixed(tokens, width)],
        [((tokens, width), BF16), ((tokens, FF), BF16), ((tokens, FF), BF16)],
        [fixed(tokens, width), spec, spec],
        [pltpu.VMEM((tokens, width), F32)],
        after=after,
    )


def gate_up_back_kernel(
    dgate_ref, dup_ref, gate_w, up_w, resid_ref, gain_ref, grad_ref, back_ref, branch_ref, total_ref
):
    step = pl.program_id(0)
    part = dot_nt(dgate_ref[...], gate_w[...]) + dot_nt(dup_ref[...], up_w[...])

    @pl.when(step == 0)
    def _():
        total_ref[...] = part

    @pl.when(step > 0)
    def _():
        total_ref[...] += part

    @pl.when(step == pl.num_programs(0) - 1)
    def _():
        resid = resid_ref[...]
        scale = row_scale(resid)
        scaled = resid * scale
        dnormed = total_ref[...]
        dscaled = dnormed * gain_ref[...]
        mean = jnp.mean(dscaled * scaled, axis=1, keepdims=True)
        back = grad_ref[...].astype(F32) + (dscaled - scaled * mean) * scale
        back_ref[...] = back
        branch_ref[...] = back.astype(BF16)


def gate_up_back(dgate, dup, gate_full, up_full, resid, gain, grad_out, after=()):
    tokens, width = resid.shape
    tile = FF // 2
    spec, w_spec, whole = tiles_spec((tokens, FF), 1, tile), tiles_spec((width, FF), 1, tile), fixed(tokens, width)
    return dense(
        gate_up_back_kernel,
        "gate_up_back",
        2,
        (dgate, dup, gate_full, up_full, resid, gain, grad_out),
        [spec, spec, w_spec, w_spec, whole, fixed(1, width), whole],
        [((tokens, width), F32), ((tokens, width), BF16)],
        [whole, whole],
        [pltpu.VMEM((tokens, width), F32)],
        after=after,
    )


def out_back_kernel(branch_ref, mix_w, attn_w, dnm_ref, dattn_ref):
    dnm_ref[...] = dot_nt(branch_ref[...], mix_w[...])
    dattn_ref[...] = dot_nt(branch_ref[...], attn_w[...]).astype(BF16)


def out_back(branch, mix_full, attn_full, after=()):
    tokens, width = branch.shape
    query = attn_full.shape[0]
    steps = 2
    return dense(
        out_back_kernel,
        "out_back",
        steps,
        (branch, mix_full, attn_full),
        [
            fixed(tokens, width),
            tiles_spec(mix_full.shape, 0, DI // steps),
            tiles_spec(attn_full.shape, 0, query // steps),
        ],
        [((tokens, DI), F32), ((tokens, query), BF16)],
        [tiles_spec((tokens, DI), 1, DI // steps), tiles_spec((tokens, query), 1, query // steps)],
        after=after,
    )


def second_back_kernel(grad_ref, z_w, qkv_w, out_ref):
    out_ref[...] = dot_nt(grad_ref[:, :DI], z_w[...]) + dot_nt(grad_ref[:, DI:], qkv_w[...])


def second_back(grad, z_full, qkv_full, after=()):
    tokens, width = grad.shape[0], z_full.shape[0]
    tile = width // 2
    return dense(
        second_back_kernel,
        "second_back",
        2,
        (grad, z_full, qkv_full),
        [fixed(*grad.shape), tiles_spec(z_full.shape, 0, tile), tiles_spec(qkv_full.shape, 0, tile)],
        [((tokens, width), F32)],
        [tiles_spec((tokens, width), 1, tile)],
        after=after,
    )[0]


def first_back_kernel(grad_ref, left_w, right_w, part_ref, out_ref, edge_ref):
    tokens = part_ref.shape[0]
    total = dot_nt(grad_ref[:, :LEFT], left_w[...]) + dot_nt(grad_ref[:, LEFT:], right_w[...])
    out_ref[...] = total[:tokens] + part_ref[...]
    edge_ref[...] = total[tokens:]


def first_back(grad, left_full, right_full, part, after=()):
    tokens, width = part.shape
    ext = grad.shape[0]
    tile = width // 2
    w_spec = tiles_spec((width, LEFT), 0, tile)
    return dense(
        first_back_kernel,
        "first_back",
        2,
        (grad, left_full, right_full, part),
        [fixed(*grad.shape), w_spec, w_spec, tiles_spec((tokens, width), 1, tile)],
        [((tokens, width), F32), ((ext - tokens, width), F32)],
        [tiles_spec((tokens, width), 1, tile), tiles_spec((ext - tokens, width), 1, tile)],
        after=after,
    )


def input_back_kernel(gn_ref, next_ref, x_ref, gain_ref, resid_ref, out_ref, low_ref):
    rows = gn_ref.shape[0]
    x = x_ref[...].astype(F32)
    scale = row_scale(x)
    scaled = x * scale
    tail = gn_ref[rows - HALO :] + next_ref[0]
    dscaled = jnp.concatenate([gn_ref[: rows - HALO], tail], 0) * gain_ref[...]
    mean = jnp.mean(dscaled * scaled, axis=1, keepdims=True)
    total = resid_ref[...] + (dscaled - scaled * mean) * scale
    out_ref[0] = total
    low_ref[0] = total.astype(BF16)


def input_back(gn, from_next, x, gain, resid, after=()):
    slots = from_next.shape[0]
    rows, width = gn.shape[0] // slots, gn.shape[1]
    spec = pl.BlockSpec((rows, width), lambda s: (s, 0))
    return dense(
        input_back_kernel,
        "input_back",
        slots,
        (gn, from_next, x, gain, resid),
        [spec, seq_block(HALO, width), spec, fixed(1, width), spec],
        [((slots, rows, width), F32), ((slots, rows, width), BF16)],
        [seq_block(rows, width)] * 2,
        after=after,
    )


def pick_kernel(index_ref, block_ref, out_ref):
    out_ref[...] = block_ref[0]


def pick(block, index, after=()):
    n_after = len(after)

    def run(index_ref, block_ref, *refs):
        pick_kernel(index_ref, block_ref, refs[n_after])

    return pl.pallas_call(
        run,
        grid_spec=pltpu.PrefetchScalarGridSpec(
            num_scalar_prefetch=1,
            grid=(1,),
            in_specs=[pl.BlockSpec((1,) + block.shape[1:], lambda i, index: (index[0], 0, 0))] + spec_any(n_after),
            out_specs=pl.BlockSpec(block.shape[1:], lambda i, index: (0, 0)),
        ),
        out_shape=jax.ShapeDtypeStruct(block.shape[1:], block.dtype),
        name="pick",
    )(index.reshape(1).astype(jnp.int32), block, *after)


def merge_kernel(side_ref, block_ref, got_ref, out_ref):
    keep = pl.program_id(0) == side_ref[0]

    @pl.when(keep)
    def _():
        out_ref[0] = block_ref[0]

    @pl.when(jnp.logical_not(keep))
    def _():
        out_ref[0] = got_ref[...]


def merge(block, got, side, after=()):
    slots, rows, width = block.shape
    n_after = len(after)

    def run(side_ref, block_ref, got_ref, *refs):
        merge_kernel(side_ref, block_ref, got_ref, refs[n_after])

    return pl.pallas_call(
        run,
        grid=(slots,),
        in_specs=[
            pl.BlockSpec(memory_space=pltpu.SMEM),
            seq_block(rows, width),
            pl.BlockSpec((rows, width), lambda s: (0, 0)),
        ]
        + spec_any(n_after),
        out_specs=seq_block(rows, width),
        out_shape=jax.ShapeDtypeStruct(block.shape, block.dtype),
        name="merge",
    )(side.reshape(1).astype(jnp.int32), block, got, *after)


def units_kernel(n_in, jobs, place_ref, normed_ref, *refs):
    ins, refs = refs[:n_in], refs[n_in:]
    act_ref, swish_ref, slope_ref = refs[:3]
    fulls, held, sems, out_sems = refs[3:6], refs[6:9], refs[9], refs[10]
    place = place_ref[0]
    waits = {}
    for number, (group, out, source, source_at, target_at) in enumerate(jobs):
        copy = pltpu.make_async_copy(
            ins[source].at[source_at], held[out].at[target_at(place)], sems.at[number]
        )
        copy.start()
        waits.setdefault(group, []).append(copy)
    normed = normed_ref[...]
    blocks, r, width = held[0].shape
    chunk_width = 512
    for q in range(width // MODEL_WIDTH):
        for copy in waits[q]:
            copy.wait()
        for at in range(q * MODEL_WIDTH, (q + 1) * MODEL_WIDTH, chunk_width):
            lanes = slice(at, at + chunk_width)
            gate = dot_nn(normed, held[0][:, :, lanes].reshape(blocks * r, chunk_width))
            up = dot_nn(normed, held[1][:, :, lanes].reshape(blocks * r, chunk_width))
            sig = sigmoid(gate)
            swish = gate * sig
            act_ref[:, lanes] = (swish * up).astype(BF16)
            swish_ref[:, lanes] = swish.astype(BF16)
            slope_ref[:, lanes] = ((sig + swish * (1.0 - sig)) * up).astype(BF16)
    back = []
    for out in range(3):
        if out == 2:
            for copy in waits[width // MODEL_WIDTH]:
                copy.wait()
        copy = pltpu.make_async_copy(held[out], fulls[out], out_sems.at[out])
        copy.start()
        back.append(copy)
    for copy in back:
        copy.wait()


def gate_up_pieces(normed, parts, r, rd, after=()):
    count, mw = lax.axis_size(BOTH), MODEL_WIDTH
    ins, jobs = [], []
    for n, part in enumerate(parts):
        for piece, offsets in part.pieces:
            for j, offset in enumerate(offsets):
                for q in range(2):
                    source_at = (j, pl.ds(q * r, r))
                    target = lambda place, o=offset, q=q: (place ^ o, slice(None), pl.ds(q * mw, mw))
                    jobs.append((q, n, len(ins), source_at, target))
                source_at = (j, pl.ds(2 * r, rd // 2))
                target = lambda place, o=offset, n=n: (place ^ o, pl.ds(n * (rd // 2), rd // 2))
                jobs.append((2, 2, len(ins), source_at, target))
            ins.append(in_hbm(piece))
    jobs.sort(key=lambda job: job[0])
    tokens = normed.shape[0]
    shapes = [(count, r, FF), (count, r, FF), (count, rd, mw)]
    vmem = pl.BlockSpec(memory_space=pltpu.VMEM)
    n_after = len(after)

    def run(place_ref, normed_ref, *refs):
        units_kernel(len(ins), jobs, place_ref, normed_ref, *refs[: len(ins)], *refs[len(ins) + n_after :])

    found = pl.pallas_call(
        run,
        in_specs=[pl.BlockSpec(memory_space=pltpu.SMEM), vmem] + spec_any(len(ins) + n_after),
        out_specs=[vmem] * 3 + spec_any(3),
        out_shape=[jax.ShapeDtypeStruct((tokens, FF), BF16)] * 3 + [jax.ShapeDtypeStruct(s, BF16) for s in shapes],
        scratch_shapes=[pltpu.VMEM(s, BF16) for s in shapes]
        + [pltpu.SemaphoreType.DMA((len(jobs),)), pltpu.SemaphoreType.DMA((3,))],
        compiler_params=pltpu.CompilerParams(vmem_limit_bytes=UNITS_LIMIT * 2**20),
        name="gate_up_pieces",
    )(place_of().reshape(1).astype(jnp.int32), normed, *ins, *after)
    return list(found[:3]) + [a.reshape(-1, a.shape[2]) for a in found[3:]]


UNITS_LIMIT = 48


def piece_jobs(parts, moves):
    ins, jobs = [], []
    for at, part in enumerate(parts):
        for piece, offsets, *of_part in part.pieces:
            for j, offset in enumerate(offsets):
                for of, r0, rows, c0, columns, out, row, column in moves:
                    if of == at:
                        source_at = (*of_part, j, pl.ds(r0, rows), pl.ds(c0, columns))
                        target = (pl.ds(row, rows), pl.ds(column, columns))
                        jobs.append(
                            (out, len(ins), source_at, lambda place, o=offset, t=target: (place ^ o,) + t)
                        )
            ins.append(in_hbm(piece))
    return ins, sorted(jobs, key=lambda job: job[0])


def start_pieces(jobs, place, ins, held, sems):
    waits = [[] for _ in held]
    for number, (out, source, source_at, target_at) in enumerate(jobs):
        copy = pltpu.make_async_copy(
            ins[source].at[source_at], held[out].at[target_at(place)], sems.at[number]
        )
        copy.start()
        waits[out].append(copy)
    return waits


def land(waits, held, full, sem):
    for copy in waits:
        copy.wait()
    copy = pltpu.make_async_copy(held, full, sem)
    copy.start()
    return copy


def pieces_call(kernel, name, parts, moves, shapes, ins, outs, after=()):
    pieces, jobs = piece_jobs(parts, moves)
    n_in, n_pieces, n_out, n_full = len(ins), len(pieces), len(outs), len(shapes)

    def run(place_ref, *refs):
        arrays, refs = refs[:n_in], refs[n_in:]
        sources, refs = refs[:n_pieces], refs[n_pieces + len(after) :]
        results, fulls, refs = refs[:n_out], refs[n_out : n_out + n_full], refs[n_out + n_full :]
        held, sems, out_sems = refs[:n_full], refs[n_full], refs[n_full + 1]
        waits = start_pieces(jobs, place_ref[0], sources, held, sems)
        kernel(waits, held, fulls, out_sems, *arrays, *results)

    vmem = pl.BlockSpec(memory_space=pltpu.VMEM)
    found = pl.pallas_call(
        run,
        in_specs=[pl.BlockSpec(memory_space=pltpu.SMEM)] + [vmem] * n_in + spec_any(n_pieces + len(after)),
        out_specs=[vmem] * n_out + spec_any(n_full),
        out_shape=[jax.ShapeDtypeStruct(s, d) for s, d in outs] + [jax.ShapeDtypeStruct(s, BF16) for s in shapes],
        scratch_shapes=[pltpu.VMEM(s, BF16) for s in shapes]
        + [pltpu.SemaphoreType.DMA((len(jobs),)), pltpu.SemaphoreType.DMA((n_full,))],
        compiler_params=pltpu.CompilerParams(vmem_limit_bytes=VMEM_LIMIT),
        name=name,
    )(place_of().reshape(1).astype(jnp.int32), *ins, *pieces, *after)
    return list(found[:n_out]) + [a.reshape(-1, a.shape[2]) for a in found[n_out:]]


def whole_of(held, lanes):
    blocks, r, _ = held.shape
    return held[:, :, lanes].reshape(blocks * r, lanes.stop - lanes.start)


def first_pieces_kernel(
    waits, held, fulls, sems, x_ref, cols_ref,
    normed_ref, left_ref, right_ref, tails_ref, conv_ref, mix_ref, gain_ref,
):
    back = [land(waits[1], held[1], fulls[1], sems.at[1])]
    count, r, _ = held[1].shape
    widths = [CONV_WIDTH // count] * (KC + 1) + [DI // count] + [MODEL_WIDTH // count] * 2
    found = [[] for _ in widths]
    for i in range(count):
        tile = held[1][i, :, LEFT - LANES :].astype(F32)
        for j, width in enumerate(widths):
            row, lane = line_place(j, len(widths), r)
            found[j].append(tile[row : row + 1, lane : lane + width])
    found = [jnp.concatenate(v, 1) for v in found]
    conv_ref[...] = jnp.concatenate(found[: KC + 1] + [jnp.zeros((3, CONV_WIDTH), F32)], 0)
    mix_ref[...] = found[KC + 1]
    gain_ref[...] = jnp.concatenate(found[KC + 2 :], 0)
    x = x_ref[...].astype(F32)
    normed_ref[...] = (x * row_scale(x) * found[KC + 2]).astype(BF16)
    normed = normed_ref[...]
    for at in range(0, LEFT, 512):
        lanes = slice(at, at + 512)
        right_ref[:, lanes] = dot_nn(normed, whole_of(held[1], lanes))
    back.append(land(waits[0], held[0], fulls[0], sems.at[0]))
    for at in range(0, LEFT, 512):
        lanes = slice(at, at + 512)
        left_ref[:, lanes] = dot_nn(normed, whole_of(held[0], lanes)).astype(BF16)
    slots, rows, _ = cols_ref.shape
    over = CONV_WIDTH - LEFT
    for s in range(slots):
        begin, end = (s + 1) * rows - HALO, (s + 1) * rows
        edge = cols_ref[s, rows - HALO :, 3:4]
        tails_ref[s, :, :LEFT] = (left_ref[begin:end].astype(F32) * edge).astype(BF16)
        right = right_ref[begin:end, :over].astype(BF16).astype(F32)
        tails_ref[s, :, LEFT:CONV_WIDTH] = (right * edge).astype(BF16)
        tails_ref[s, :, CONV_WIDTH:] = (normed_ref[begin:end].astype(F32) * edge).astype(BF16)
    for copy in back:
        copy.wait()


def first_pieces(x, cols, parts, r, after=()):
    tokens, width = x.shape
    count = lax.axis_size(BOTH)
    moves = [(0, 0, r, 0, LEFT, 0, 0, 0), (1, 0, r, 0, LEFT, 1, 0, 0)]
    outs = [
        ((tokens, width), BF16),
        ((tokens, LEFT), BF16),
        ((tokens, LEFT), F32),
        ((cols.shape[0], HALO, CONV_WIDTH + width), BF16),
        ((8, CONV_WIDTH), F32),
        ((1, DI), F32),
        ((2, width), F32),
    ]
    return pieces_call(
        first_pieces_kernel, "first_pieces", parts, moves, [(count, r, LEFT)] * 2, (x, cols), outs, after
    )


def second_pieces_kernel(waits, held, fulls, sems, normed_ref, rows_ref, z_ref, q_ref, kv_ref):
    normed = normed_ref[...]
    back = [land(waits[1], held[1], fulls[1], sems.at[1])]
    query = q_ref.shape[1]
    slots, extended, width = kv_ref.shape
    rows = extended - 16
    q_ref[...] = dot_nn(normed, whole_of(held[1], slice(0, query))).astype(BF16)
    part = dot_nn(normed, whole_of(held[1], slice(query, query + width))).astype(BF16)
    for s in range(slots):
        kv_ref[s, :rows] = part[s * rows : (s + 1) * rows]
        keys = jnp.broadcast_to(rows_ref[s, 1:2], (16, rows))
        if rows < width:
            keys = jnp.concatenate([keys, jnp.zeros((16, width - rows), F32)], 1)
        kv_ref[s, rows:] = keys.astype(BF16)
    back.append(land(waits[0], held[0], fulls[0], sems.at[0]))
    for at in range(0, DI, 512):
        lanes = slice(at, at + 512)
        z_ref[:, lanes] = dot_nn(normed, whole_of(held[0], lanes))
    for copy in back:
        copy.wait()


def second_pieces(normed, rows_in, parts, moves, r, after=()):
    tokens, width = normed.shape
    slots, _, rows = rows_in.shape
    count = lax.axis_size(BOTH)
    query, kv = QUERY_HEADS * HEAD_WIDTH, 2 * KEY_VALUE_HEADS * HEAD_WIDTH
    outs = [((tokens, DI), F32), ((tokens, query), BF16), ((slots, rows + 16, kv), BF16)]
    shapes = [(count, r, DI), (count, r, query + kv)]
    return pieces_call(
        second_pieces_kernel, "second_pieces", parts, moves, shapes, (normed, rows_in), outs, after
    )


def fsdp_bits():
    return lax.axis_size("fsdp").bit_length() - 1


def fsdp_exchange(block, bit):
    return lax.ppermute(block, "fsdp", [(i, i ^ (1 << bit)) for i in range(lax.axis_size("fsdp"))])


def side_of():
    return lax.axis_index("fsdp") >> (fsdp_bits() - 1)


def swap_start(block):
    return fsdp_exchange(lax.dynamic_index_in_dim(block, 1 - side_of(), 0, False), fsdp_bits() - 1)


def swap_end(block, got):
    return lax.dynamic_update_index_in_dim(block, got.astype(block.dtype), 1 - side_of(), 0)


def gather_sequence(block):
    pieces, offsets = [block], [0]
    for bit in range(fsdp_bits() - 1):
        pieces = pieces + [fsdp_exchange(a, bit) for a in pieces]
        offsets = offsets + [o ^ (1 << bit) for o in offsets]
    return pieces, tuple(offsets)


def sum_sequence(blocks):
    blocks = list(blocks)
    for bit in range(fsdp_bits() - 2, -1, -1):
        half = len(blocks) // 2
        got = [fsdp_exchange(a, bit) for a in blocks[half:]]
        if half > 1:
            blocks = [(a.astype(F32) + b.astype(F32)).astype(BF16) for a, b in zip(blocks, got)]
        else:
            blocks = [blocks[0], got[0]]
    return blocks


def rest_place():
    return lax.axis_index("fsdp") & (lax.axis_size("fsdp") // 2 - 1)


def from_next_part(block):
    pieces, offsets = gather_sequence(block)
    group, rest = len(pieces), rest_place()
    found = [jnp.zeros(block.shape[1:], block.dtype)] * SLOTS
    for number in range(SLOTS * group - 1):
        slot, after = number // group, number + 1
        for offset, piece in zip(offsets, pieces):
            match = (rest == number % group) & ((after % group) ^ rest == offset)
            found[slot] = jnp.where(match, piece[after // group], found[slot])
    return jnp.stack(found)


def sequence_masks(segs):
    slots, rows = segs.shape
    behind = (lax.iota(jnp.int32, slots)[:, None] > 0) | (rest_place() > 0)
    first = (segs == segs[:, :1]) & behind
    keep_end = segs == segs[:, -1:]
    columns = []
    for k in range(KC - 1):
        back = KC - 1 - k
        inside = segs[:, back:] == segs[:, : rows - back]
        columns.append(jnp.concatenate([first[:, :back], inside], 1).astype(F32))
    columns += [keep_end.astype(F32), first.astype(F32), segs.astype(F32)]
    cols = jnp.stack(columns, 2)
    cols = jnp.pad(cols, ((0, 0), (0, 0), (0, LANES - cols.shape[2])))
    rows_in = jnp.pad(jnp.stack([segs, keep_end.astype(segs.dtype)], 1).astype(F32), ((0, 0), (0, 6), (0, 0)))
    return cols, rows_in, keep_end


def per_device(
    hidden_in,
    segment_ids,
    norm1_gain,
    w_gate_z,
    w_xbc,
    w_step,
    conv_weight,
    conv_bias,
    step_bias,
    decay_log,
    skip_gain,
    mixer_gain,
    w_mix_out,
    w_query,
    key_value_weight,
    w_attn_out,
    norm2_gain,
    w_gate_up,
    w_down,
    out_grad,
):
    rows = hidden_in.shape[2]
    seqs = hidden_in.shape[0] * hidden_in.shape[1]
    flat_rows = seqs * rows
    count = lax.axis_size(BOTH)
    query_width = QUERY_HEADS * HEAD_WIDTH
    kv_width = 2 * KEY_VALUE_HEADS * HEAD_WIDTH
    by_seq = lambda a: a.reshape(seqs, rows, a.shape[1])
    flat = lambda a: a.reshape(flat_rows, a.shape[2])
    r, rm, ra, rd = w_xbc.shape[0], w_mix_out.shape[0], w_attn_out.shape[0], w_down.shape[0]
    bits = bit_count()
    top = list(range(bits - 1, 2, -1))
    half = (DI + query_width + kv_width) // 2

    heads = jnp.stack([step_bias, -jnp.exp(decay_log), skip_gain])
    heads = jnp.pad(heads, ((0, 5), (0, LANES - H)))
    spread = jnp.repeat(jnp.eye(LANES, H, dtype=BF16), P_SIZE, axis=1)
    skip_row = jnp.broadcast_to(jnp.repeat(skip_gain, P_SIZE)[None], (8, DI))
    picks = jnp.eye(LANES, 2 * LEFT, 2 * LEFT - LANES, dtype=BF16)
    rest = rest_place().reshape(1).astype(jnp.int32)

    first = Part(
        pack_first(w_xbc, w_step, conv_weight, conv_bias, mixer_gain, norm1_gain, norm2_gain)[None]
    )
    if len(top) == 2:
        first.direct((8, 16, 24))
    else:
        first.step(top[0])
    segs_got = swap_start(segment_ids[:, 0])
    x_got = fsdp_exchange(pick(in_hbm(hidden_in[:, 0]), 1 - side_of(), after=(segs_got,)), fsdp_bits() - 1)
    for bit in top[1:] if len(top) != 2 else ():
        join([first])
        first.step(bit)
    first_halves = join([first], split=(first,), after=(heads, spread, skip_row, picks))
    [p.step(bit) for p, bit in zip(first_halves, (2, 1))]
    two = Part(pack_two(w_gate_z, w_query, key_value_weight, w_mix_out, w_attn_out, after=(first_halves[0].pieces[0][0],))[None])
    two.step(top[0])
    cols, rows_in, keep_end = sequence_masks(swap_end(segment_ids[:, 0], segs_got))
    x = merge(in_hbm(hidden_in[:, 0]), x_got, side_of()).reshape(flat_rows, MODEL_WIDTH)
    join(first_halves + [two], after=(x,))
    [p.step(bit) for p, bit in zip(first_halves, (1, 2))]
    two.steps(top[1:])
    [p.core() for p in first_halves]
    two_halves = join([two], split=(two,), after=[p.pieces[1][0] for p in first_halves])
    [p.step(bit) for p, bit in zip(two_halves, (2, 1))]
    units = Part(pack_units(w_gate_up, w_down, after=(two_halves[0].pieces[0][0],))[None])
    units.step(top[0])
    if r % 16:
        left_full, right_full, small_full = assemble(
            first_halves,
            [(count, r, LEFT), (count, r, LEFT), (count, r, LANES)],
            [
                (0, 0, r, 0, LEFT, 0, 0, 0),
                (1, 0, r, 0, LEFT, 1, 0, 0),
                (1, 0, r, LEFT - LANES, LANES, 2, 0, 0),
            ],
            after=(units.pieces[0][0],),
        )

        conv, mix_gain, gains = unpack_small(small_full, r)
        gain_one, gain_two = gains[:1], gains[1:]
        normed, left, right, tails = first_proj(x, gain_one, left_full, right_full, cols, after=(rows_in,))
    else:
        normed, left, right, tails, conv, mix_gain, gains, left_full, right_full = first_pieces(
            x, cols, first_halves, r, after=(units.pieces[0][0], rows_in)
        )
        gain_one, gain_two = gains[:1], gains[1:]
    left, right = by_seq(left), by_seq(right)
    tail_pieces, offsets = gather_sequence(tails)
    join(two_halves + [units], after=(left,))
    [p.step(bit) for p, bit in zip(two_halves, (1, 2))]
    units.steps(top[1:])
    halo = take_halo(rest, tail_pieces, offsets)
    xbc, slope, xd, step, cum, msg = mix_begin(
        left, right, halo, cols, heads, conv, after=(two_halves[0].pieces[0][0],)
    )
    msg_pieces, _ = gather_sequence(msg)
    units_halves = join([units], after=(cum,), split=(units,))
    (two_all,) = join_all(two_halves, after=(units_halves[0].pieces[0][0],))
    two_offsets = sum((o for _, o in two_halves[0].pieces), [])
    other_offsets = sum((o for _, o in two_halves[1].pieces), [])
    two_got = exchange(two_all, 0)
    [p.step(bit) for p, bit in zip(units_halves, (2, 1))]
    inside = mix_inside(xbc, xd, cum, cols, rows_in, skip_row, after=(two_all,))
    for n, (p, offsets_of) in enumerate(zip(two_halves, (two_offsets, other_offsets))):
        p.pieces = [(two_all, offsets_of, n), (two_got, [o ^ 1 for o in offsets_of], n)]
    second_moves = [
        (0, 0, r, 0, half, 0, 0, 0),
        (1, 0, r, 0, DI - half, 0, 0, half),
        (1, 0, r, DI - half, query_width + kv_width, 1, 0, 0),
    ]
    if r % 16:
        z_full, qkv_full = assemble(
            two_halves,
            [(count, r, DI), (count, r, query_width + kv_width)],
            second_moves,
            after=(inside,),
        )
        gate_z, queries, keyvals = second_proj(normed, z_full, qkv_full, rows_in)
    else:
        gate_z, queries, keyvals, z_full, qkv_full = second_pieces(
            normed, rows_in, two_halves, second_moves, r, after=(inside,)
        )
    gate_z, queries = by_seq(gate_z), by_seq(queries)
    prev = scan_states(rest, msg_pieces, offsets, True, after=(gate_z,))
    join(units_halves, after=(prev,))
    [p.step(bit) for p, bit in zip(units_halves, (1, 2))]
    kv_pieces, _ = gather_sequence(keyvals)
    mixer_out, normed_mix = mix_finish(
        in_hbm(inside), xbc, prev, cum, cols, gate_z, mix_gain, after=(units_halves[0].pieces[0][0],)
    )
    attn_low, log_sums = attend(rest, queries, kv_pieces, cols, rows_in, offsets, after=(normed_mix,))

    out_keep, out_send = turn(flat(normed_mix), flat(attn_low))
    x_halo = halo[:, :, CONV_WIDTH:].reshape(seqs * HALO, MODEL_WIDTH)
    normed_keep, normed_send = turn(jnp.concatenate([normed, x_halo]), after=(out_keep,))

    mix_out_full, attn_out_full = assemble(
        two_halves,
        [(count, rm, MODEL_WIDTH), (count, ra, MODEL_WIDTH)],
        [
            (0, 0, r, half, MODEL_WIDTH, 0, 0, 0),
            (1, 0, rm - r, half, MODEL_WIDTH, 0, r, 0),
            (1, rm - r, ra, half, MODEL_WIDTH, 1, 0, 0),
        ],
        after=(normed_keep,),
    )
    residual, normed_two = out_proj(x, flat(normed_mix), flat(attn_low), mix_out_full, attn_out_full, gain_two)
    two_keep, two_send, *held = turn(normed_two, hold=[p.pieces[1][0] for p in units_halves])
    for p, got in zip(units_halves, held):
        p.pieces[1] = (got, p.pieces[1][1])
        p.core()
    if r % 16:
        moves = [(n, q * r, r, 0, MODEL_WIDTH, n, 0, q * MODEL_WIDTH) for n in range(2) for q in range(2)]
        moves += [(n, 2 * r, rd // 2, 0, MODEL_WIDTH, 2, n * (rd // 2), 0) for n in range(2)]
        gate_full, up_full, down_full = assemble(
            units_halves, [(count, r, FF), (count, r, FF), (count, rd, MODEL_WIDTH)], moves, after=(two_keep,), limit=60
        )
        act, swish, gate_slope = gate_up(normed_two, gate_full, up_full)
    else:
        act, swish, gate_slope, gate_full, up_full, down_full = gate_up_pieces(
            normed_two, units_halves, r, rd, after=(two_keep,)
        )
    out_turned = [out_keep, exchange(out_send, 0)]
    x_turned = [normed_keep, exchange(normed_send, 0)]
    two_turned = [two_keep, exchange(two_send, 0)]
    grad_got = fsdp_exchange(pick(in_hbm(out_grad[:, 0]), 1 - side_of(), after=(two_keep,)), fsdp_bits() - 1)
    act_keep, act_send = turn(act, after=(out_turned[1], x_turned[1], two_turned[1]))
    grad_out = merge(in_hbm(out_grad[:, 0]), grad_got, side_of(), after=(act_keep,)).reshape(flat_rows, MODEL_WIDTH)
    act_turned = [act_keep, exchange(act_send, 0)]
    grad_out_got = exchange(grad_out, 0)

    block_out, grad_gate, grad_up = down(
        act, swish, gate_slope, down_full, residual, grad_out, after=(act_keep,)
    )
    gate_got, up_got = exchange(grad_gate, 0), exchange(grad_up, 0)
    hidden_got = swap_start(by_seq(block_out))
    grad_resid, grad_branch = gate_up_back(
        grad_gate, grad_up, gate_full, up_full, residual, gain_two, grad_out, after=(block_out,)
    )
    sum_down = Sum(act_turned, [grad_out, grad_out_got], 1, after=(grad_branch,))
    sum_gate = Sum(two_turned, [grad_gate, gate_got], 0, after=(sum_down.send,))
    hidden_out = swap_end(by_seq(block_out), hidden_got)
    sum_up = Sum(two_turned, [grad_up, up_got], 1, after=(sum_gate.send, hidden_out))
    branch_got = exchange(grad_branch, 0)
    sum_gate.near(), sum_up.near()
    grad_normed_mix, grad_attn = out_back(
        grad_branch, mix_out_full, attn_out_full, after=(sum_up.send,)
    )
    grad_normed_mix, grad_attn = by_seq(grad_normed_mix), by_seq(grad_attn)
    sum_out = Sum(out_turned, [grad_branch, branch_got], 0, after=(grad_normed_mix,))

    grad_queries, grad_kv_pieces = attend_back(
        rest, queries, kv_pieces, cols, rows_in, attn_low, log_sums, grad_attn, offsets, after=(sum_out.send,)
    )
    advance([sum_gate, sum_up], after=(grad_queries,))
    sum_gate.second(), sum_up.second()
    kv_own, kv_got = sum_sequence(grad_kv_pieces)
    dy, grad_za, grad_zb, back_msg = gated_back(
        grad_normed_mix, mixer_out, gate_z, mix_gain, xbc, cum, cols, half, after=(sum_gate.send, sum_up.send)
    )
    (pair_gate_up,) = advance([(sum_gate, sum_up)], after=(dy,))
    grad_zq = join_grads(
        flat(grad_za), flat(grad_zb), flat(grad_queries), kv_own, kv_got, after=(pair_gate_up.send,)
    )
    zq_got = exchange(grad_zq, 0)
    back_pieces, _ = gather_sequence(back_msg)
    pair_gate_up.start(3)
    sum_out.near(), sum_down.near()
    dxd, dbc, sums = inside_back(
        xbc, xd, cum, cols, rows_in, skip_row, spread, dy, mixer_out, prev, after=(grad_zq,)
    )
    sum_z = Sum(x_turned, [grad_zq, zq_got], 0, after=(sums,), columns=(0, half))
    sum_zq = Sum(x_turned, [grad_zq, zq_got], 1, after=(sum_z.send,), columns=(half, half))
    later = scan_states(rest, back_pieces, offsets, False, after=(sum_zq.send,))
    for bit in range(4, bits):
        advance([sum_out, sum_down, pair_gate_up] if bit == 4 else [pair_gate_up], after=(later,))
        pair_gate_up.start(bit)
    sum_out.second(), sum_down.second()
    sum_z.near(), sum_zq.near()
    grad_second = second_back(grad_zq, z_full, qkv_full, after=(sum_out.send,))
    grad_first, conv_sums, head_sums = mix_end(
        left, right, halo, xbc, slope, xd, step, cum, cols, heads, skip_row, conv, spread,
        dy, dxd, dbc, sums, later, prev, after=(grad_second,),
    )
    _, _, pair_out_down = advance([sum_z, sum_zq, (sum_out, sum_down)], after=(head_sums,))
    (own_gate_up,) = finish([pair_gate_up], after=(pair_out_down.send,))
    small_keep, small_send = small_grads(r, conv_sums, head_sums)
    sum_x = Direct(
        [normed_keep, small_keep], [normed_send, small_send], [grad_first, picks], after=(own_gate_up,)
    )
    grad_normed, grad_halo = first_back(
        grad_first, left_full, right_full, grad_second, after=(sum_x.send,)
    )
    sum_x.core()
    sum_z.second(), sum_zq.second()
    pair_out_down.start(3)
    edge = keep_end[:, rows - HALO :, None]
    from_next = jnp.where(edge, from_next_part(grad_halo.reshape(seqs, HALO, MODEL_WIDTH)), 0.0)
    quarter = sum_x.planes(after=(grad_normed,))
    input_grad, input_low = input_back(grad_normed, from_next, x, gain_one, grad_resid, after=(quarter,))
    input_got = swap_start(input_low)
    input_grad = swap_end(input_grad, input_got)
    far = list(range(4, bits))
    (pair_z,) = advance([(sum_z, sum_zq)], after=(quarter,))
    pair_z.start(3)
    for bit in far:
        advance([pair_out_down], after=(input_low,))
        pair_out_down.start(bit)
    sum_x.lines(after=(pair_out_down.send, pair_z.send))
    (own_out_down,) = finish([pair_out_down], after=(sum_x.keep,))
    for bit in far:
        advance([pair_z], after=(sum_x.keep,))
        pair_z.start(bit)
    (own_zq,) = finish([pair_z], after=(sum_x.keep,))
    own_first = sum_x.done()
    own_small = own_first[:, 2 * LEFT - LANES :]
    widths = [conv_weight.shape[1]] * KC + [conv_bias.shape[0]] + [H] * 6
    own = []
    for j, width in enumerate(widths):
        row, lane = line_place(j, len(widths), r)
        own.append(own_small[row, lane : lane + width])
    gain_grad = lambda weights, grads, gain: sum(
        jnp.sum(w.astype(F32) * g, 1) for w, g in zip(weights, grads)
    ) / gain.astype(F32)
    zq = jnp.concatenate([own_zq[0], own_zq[1]], 1)
    grad_z, grad_query, grad_keyval = jnp.split(zq, (DI, DI + query_width), 1)
    grad_xbc = own_first[:, :CONV_WIDTH]
    grad_step = own_first[:, CONV_WIDTH : CONV_WIDTH + H]
    grad_gate_up = jnp.concatenate([own_gate_up[0], own_gate_up[1]], 1)
    grad_out_w, grad_down = own_out_down[0], own_out_down[1]
    first_w = (w_gate_z, w_xbc, w_step, w_query, key_value_weight)
    first_g = (grad_z, grad_xbc, grad_step, grad_query, grad_keyval)
    return (
        hidden_out.reshape(hidden_in.shape),
        input_grad.reshape(hidden_in.shape),
        gain_grad(first_w, first_g, norm1_gain),
        grad_z,
        grad_xbc,
        grad_step,
        jnp.stack(own[:KC]),
        own[KC],
        own[KC + 1] + own[KC + 4],
        own[KC + 2] + own[KC + 5],
        own[KC + 3] + own[KC + 6],
        gain_grad([w_mix_out], [grad_out_w[:rm]], mixer_gain),
        grad_out_w[:rm],
        grad_query,
        grad_keyval,
        grad_out_w[rm:],
        gain_grad([w_gate_up], [grad_gate_up], norm2_gain),
        grad_gate_up,
        grad_down,
    )


def solution(mesh):
    placed = (
        P(None, "dp", "fsdp", None),
        P(None, "dp", "fsdp"),
        P(("dp", "fsdp")),
        P(("dp", "fsdp"), None),
        P(("dp", "fsdp"), None),
        P(("dp", "fsdp"), None),
        P(None, ("dp", "fsdp")),
        P(("dp", "fsdp")),
        P(),
        P(),
        P(),
        P(("dp", "fsdp")),
        P(("dp", "fsdp"), None),
        P(("dp", "fsdp"), None),
        P(("dp", "fsdp"), None),
        P(("dp", "fsdp"), None),
        P(("dp", "fsdp")),
        P(("dp", "fsdp"), None),
        P(("dp", "fsdp"), None),
        P(None, "dp", "fsdp", None),
    )
    return jax.shard_map(
        per_device,
        mesh=mesh,
        in_specs=placed,
        out_specs=(
            P(None, "dp", "fsdp", None),
            P(None, "dp", "fsdp", None),
            P(("dp", "fsdp")),
            P(("dp", "fsdp"), None),
            P(("dp", "fsdp"), None),
            P(("dp", "fsdp"), None),
            P(None, ("dp", "fsdp")),
            P(("dp", "fsdp")),
            P(),
            P(),
            P(),
            P(("dp", "fsdp")),
            P(("dp", "fsdp"), None),
            P(("dp", "fsdp"), None),
            P(("dp", "fsdp"), None),
            P(("dp", "fsdp"), None),
            P(("dp", "fsdp")),
            P(("dp", "fsdp"), None),
            P(("dp", "fsdp"), None),
        ),
        check_vma=False,
    )
```
